32 devices in a mesh: enc: 4 (over y, x), seq: 8 (over z, core).
Axes of the slice: x: 2, y: 2, z: 4, core: 2. Of those that a mesh axis runs over, the one named last changes fastest.
Arguments:
- qkv: bfloat16 [16, 512, 3840], P('enc', 'seq'), may hold values from -6 to 6
- resid: bfloat16 [16, 512, 1280], P('enc', 'seq'), may hold values from -6 to 6
- block_count: int32 [4, 8], P('enc', 'seq'), may hold values from 2 to 4, as said below
- send_count: int32 [4, 8], P('enc', 'seq'), may hold values from 0 to 1, as said below
- send_slot: int32 [4, 384], P('enc', 'seq'), may hold values from 0 to 47, as said below
- lm_row: int32 [4, 384], P('enc', 'seq'), may hold values from -1 to 47, as said below
- out_weight: bfloat16 [1280, 1280], replicated, may hold values from -0.15625 to 0.15625
- out_bias: bfloat16 [1280], replicated, may hold values from -3 to 3
- norm_gain: bfloat16 [1280], replicated, may hold values from 0.25 to 1.75
Outputs:
- lm_tokens: bfloat16 [4, 384, 5120], P('enc', 'seq')
The draws below stay inside these ranges and needn't reach their ends.
Inputs may be any that keep to these rules, and one draw needn't show every extreme that they name: send_count is at most 1; a device's live slots come first. block_count[e, g] = 3 + send_count[e, g] - send_count[(e - 1) mod 4, g]. `send_slot`: values of one device are distinct; with o = (s - g) mod 8 and finv(o) = 2 * o for o < 4, else 2 * (o - 4) + 1, the device at seq index g uses slot s * 6 + k exactly when k * 8 + finv(o) < 48. `lm_row`: at seq index s, with o and finv as for send_slot, arriving slot g * 6 + k holds -1 exactly when k * 8 + finv((s - g) mod 8) >= 48; the other slots hold each of 0 to 47 once.
All inputs are finite; a program needn't handle non-finite values.
Results may differ from the reference program's by a relative error of at most 0.0036.
Values may be sent and summed in bfloat16 or wider, within the bound.
No kernel may reach another device: no remote copies, remote signals or barrier semaphores. Data moves between devices by JAX's collectives and lax.ppermute only.
A program may use at most 64 MiB of HBM per device.

```python
import math
import jax
import jax.numpy as jnp
from jax import lax

D = 1280
HEADS = 16
WIN = 64
SPARE = 1
BLOCKS = 3
SLOTS = 4
ROWS_OUT = 48
CAP = 6
N_ENC = 4
N_SEQ = 8


def lent_table(key):
    lent_count = jax.random.randint(jax.random.fold_in(key, 7), (N_ENC, N_SEQ), 0, SPARE + 1)
    lent_count = lent_count.at[0, 0].set(SPARE).at[1, 0].set(0).at[N_ENC - 1, 0].set(0)
    return lent_count.astype(jnp.int32)


def draw_send_count(key, part):
    return lent_table(key)


def draw_block_count(key, part):
    lent_count = lent_table(key)
    return (BLOCKS + lent_count - jnp.roll(lent_count, 1, axis=0)).astype(jnp.int32)


def spread_offset(index_in):
    return index_in // 2 + index_in % 2 * (N_SEQ // 2)


def spread_inverse(offset):
    return jnp.where(offset < N_SEQ // 2, 2 * offset, 2 * (offset - N_SEQ // 2) + 1)


def draw_send_slot(key, part):
    row_ids = jnp.arange(ROWS_OUT, dtype=jnp.int32)
    scores = jax.random.randint(key, (N_ENC, N_SEQ, ROWS_OUT), 0, 1 << 20) * ROWS_OUT + row_ids
    ranks = jnp.argsort(scores, axis=-1).astype(jnp.int32)
    offset = spread_offset(ranks % N_SEQ)
    seq_ids = jnp.arange(N_SEQ, dtype=jnp.int32)[None, :, None]
    target = (seq_ids + offset) % N_SEQ
    return (target * CAP + ranks // N_SEQ).reshape(N_ENC, N_SEQ * ROWS_OUT).astype(jnp.int32)


def draw_lm_row(key, part):
    slot_total = N_SEQ * CAP
    slot_ids = jnp.arange(slot_total, dtype=jnp.int32)
    sender = slot_ids // CAP
    rank_k = slot_ids % CAP
    seq_ids = jnp.arange(N_SEQ, dtype=jnp.int32)[:, None]
    offset = (seq_ids - sender[None, :]) % N_SEQ
    filled = rank_k[None, :] * N_SEQ + spread_inverse(offset) < ROWS_OUT
    scores = jax.random.randint(key, (N_ENC, N_SEQ, slot_total), 0, 1 << 20) * slot_total + slot_ids
    scores = jnp.where(filled[None], scores, (1 << 20) * slot_total + slot_ids)
    position = jnp.argsort(jnp.argsort(scores, axis=-1), axis=-1).astype(jnp.int32)
    return jnp.where(filled[None], position, -1).reshape(N_ENC, N_SEQ * slot_total).astype(jnp.int32)


def draw_qkv(key, part):
    head_size = D // HEADS
    shape = (N_ENC * SLOTS, N_SEQ, WIN, 3, HEADS, head_size)
    values = jnp.clip(jax.random.normal(key, shape), -4.0, 4.0)
    return values.reshape(N_ENC * SLOTS, N_SEQ * WIN, 3 * D).astype(jnp.bfloat16)


def block_levels(own_key, extent, cuts, low, largest):
    def one(dim, parts):
        draws = jax.random.uniform(jax.random.fold_in(jax.random.fold_in(own_key, 6), dim), (parts,), jnp.float32, low / len(cuts), largest / len(cuts))
        return jnp.repeat(jnp.exp(draws), extent[dim] // parts).reshape((-1,) + (1,) * (len(extent) - dim - 1))

    level = one(*cuts[0])
    for cut in cuts[1:]:
        level = level * one(*cut)
    return level


def normal_values(key, dims, width, limit, cuts=(), kind=jnp.bfloat16):
    entries = jax.random.normal(key, dims, jnp.float32) * width
    if len(cuts) > 0:
        entries = block_levels(key, dims, cuts, -0.22, 0.18) * entries
    return jnp.clip(entries, min=-limit, max=limit).astype(kind)


def setup_inputs(seed: int = 0) -> dict:
    keys = jax.random.split(jax.random.key(seed), 10)
    return {
        "qkv": draw_qkv(jax.random.fold_in(keys[9], 71), 0),
        "resid": normal_values(keys[1], (N_ENC * SLOTS, N_SEQ * WIN, D), 1.0, 6.0, ((0, 4), (1, 8))),
        "block_count": draw_block_count(jax.random.fold_in(keys[9], 71), 0),
        "send_count": draw_send_count(jax.random.fold_in(keys[9], 71), 0),
        "send_slot": draw_send_slot(jax.random.fold_in(keys[9], 71), 0),
        "lm_row": draw_lm_row(jax.random.fold_in(keys[9], 71), 0),
        "out_weight": normal_values(keys[6], (D, D), D ** -0.5, 0.15625),
        "out_bias": normal_values(keys[7], (D,), 0.5, 3.0),
        "norm_gain": jnp.clip(1.0 + 0.15 * jax.random.normal(keys[8], (D,), jnp.float32), 0.25, 1.75).astype(jnp.bfloat16),
    }


def encode_blocks(qkv_blocks, resid_blocks, out_weight, out_bias, norm_gain):
    block_total = qkv_blocks.shape[0]
    window_len = qkv_blocks.shape[1]
    model_width = resid_blocks.shape[2]
    head_size = model_width // HEADS
    packed = qkv_blocks.astype(jnp.float32).reshape(block_total, window_len, 3, HEADS, head_size)
    queries = packed[:, :, 0]
    key_rows = packed[:, :, 1]
    value_rows = packed[:, :, 2]
    scores = jnp.einsum('bqhd,bkhd->bhqk', queries, key_rows) * (1.0 / math.sqrt(head_size))
    exp_scores = jnp.exp(scores - lax.optimization_barrier(jnp.max(scores, axis=-1, keepdims=True)))
    probabilities = (exp_scores / lax.optimization_barrier(jnp.sum(exp_scores, axis=-1, keepdims=True))).astype(jnp.bfloat16)
    attended = jnp.einsum('bhqk,bkhd->bqhd', probabilities.astype(jnp.float32), value_rows).astype(jnp.bfloat16)
    flat_rows = attended.reshape(block_total * window_len, model_width)
    hidden = jnp.dot(flat_rows, out_weight, preferred_element_type=jnp.float32)
    hidden = hidden + out_bias.astype(jnp.float32) + resid_blocks.reshape(block_total * window_len, model_width).astype(jnp.float32)
    inv_rms = lax.rsqrt(lax.optimization_barrier(jnp.mean(hidden * hidden, axis=-1, keepdims=True)) + 1e-06)
    normed = (hidden * inv_rms * norm_gain.astype(jnp.float32)).astype(jnp.bfloat16)
    return normed.reshape(block_total, window_len // 4, 4 * model_width)

def reference(qkv, resid, block_count, send_count, send_slot, lm_row, out_weight, out_bias, norm_gain):
    qkv_dev = qkv.reshape(N_ENC, SLOTS * N_SEQ, WIN, 3 * D)
    resid_dev = resid.reshape(N_ENC, SLOTS * N_SEQ, WIN, D)

    def per_enc(pair):
        return encode_blocks(pair[0], pair[1], out_weight, out_bias, norm_gain)
    merged_all = lax.map(per_enc, (qkv_dev, resid_dev))
    merged_all = merged_all.reshape(N_ENC, SLOTS, N_SEQ, WIN // 4, 4 * D)
    enc_ids = jnp.arange(N_ENC, dtype=jnp.int32)[:, None, None]
    seq_ids = jnp.arange(N_SEQ, dtype=jnp.int32)[None, :, None]
    work_ids = jnp.arange(BLOCKS, dtype=jnp.int32)[None, None, :]
    kept_blocks = (block_count - send_count)[:, :, None]
    prev_count = jnp.roll(block_count, 1, axis=0)[:, :, None]
    prev_send = jnp.roll(send_count, 1, axis=0)[:, :, None]
    own_block = work_ids < kept_blocks
    src_enc = jnp.where(own_block, enc_ids, (enc_ids - 1) % N_ENC)
    src_slot = jnp.where(own_block, work_ids, prev_count - prev_send + work_ids - kept_blocks)
    seq_full = jnp.broadcast_to(seq_ids, src_slot.shape)
    work_rows = merged_all[src_enc, src_slot, seq_full]
    work_rows = work_rows.reshape(N_ENC, N_SEQ, ROWS_OUT, 4 * D)
    slot_value = send_slot.reshape(N_ENC, N_SEQ, ROWS_OUT)
    dest_seq = slot_value // CAP
    arrive_slot = seq_ids * CAP + slot_value % CAP
    flat_index = (dest_seq * (N_SEQ * CAP) + arrive_slot).reshape(N_ENC, N_SEQ * ROWS_OUT)
    place_row = jnp.take_along_axis(lm_row, flat_index, axis=1).reshape(N_ENC, N_SEQ, ROWS_OUT)
    final_row = dest_seq * ROWS_OUT + place_row
    lm_tokens = jnp.zeros((N_ENC, N_SEQ * ROWS_OUT, 4 * D), jnp.bfloat16)
    lm_tokens = lm_tokens.at[jnp.broadcast_to(enc_ids, final_row.shape), final_row].set(work_rows)
    return lm_tokens
```

```python
import functools
import math

import jax
import jax.numpy as jnp
from jax import lax
from jax.experimental import pallas as pl
from jax.experimental.pallas import tpu as pltpu
from jax.sharding import PartitionSpec as P

HEADS = 16
WIN = 64
LANES = 128
GROUP = 4
EPS = 1e-6

NT = (((1,), (1,)), ((), ()))


def dot32(a, b):
    return jnp.dot(a, b, preferred_element_type=jnp.float32)


def attend(q, k, v, out_ref, row0, width):
    head = width // HEADS
    rate = 1.0 / math.sqrt(head)
    totals = [None] * (width // LANES)
    sums = [None] * (width // LANES)
    first_half = lax.broadcasted_iota(jnp.int32, (WIN, 2 * WIN), 1) < WIN
    for pair in range(HEADS // 2):
        start = 2 * pair * head
        lo = start // LANES * LANES
        hi = -(-(start + 2 * head) // LANES) * LANES
        column = lax.broadcasted_iota(jnp.int32, (2 * WIN, hi - lo), 1) + lo
        row = lax.broadcasted_iota(jnp.int32, (2 * WIN, hi - lo), 0)
        begin = jnp.where(row < WIN, start, start + head)
        mask = ((column >= begin) & (column < begin + head)).astype(jnp.float32).astype(jnp.bfloat16)
        kw, vw = k(lo, hi), v(lo, hi)
        keys = jnp.concatenate([kw, kw], axis=0) * mask
        values = jnp.concatenate([vw, vw], axis=0) * mask
        scores = lax.dot_general(q(lo, hi), keys, NT, preferred_element_type=jnp.float32)
        top0 = jnp.max(jnp.where(first_half, scores, -jnp.inf), axis=1, keepdims=True)
        top1 = jnp.max(jnp.where(first_half, -jnp.inf, scores), axis=1, keepdims=True)
        raised = jnp.exp((scores - jnp.where(first_half, top0, top1)) * rate).astype(jnp.bfloat16)
        part = dot32(raised, values)
        norm = dot32(raised, mask)
        for tile in range(lo // LANES, hi // LANES):
            at = slice(tile * LANES - lo, (tile + 1) * LANES - lo)
            totals[tile] = part[:, at] if totals[tile] is None else totals[tile] + part[:, at]
            sums[tile] = norm[:, at] if sums[tile] is None else sums[tile] + norm[:, at]
    for tile in range(width // LANES):
        out_ref[row0 : row0 + WIN, tile * LANES : (tile + 1) * LANES] = (totals[tile] / sums[tile]).astype(
            jnp.bfloat16
        )


def encode_kernel(
    lend, count_ref, qkv_hbm, resid_hbm, weight_hbm, bias_ref, gain_ref, out_ref,
    qkv, resid, weight, attended, hidden, sems,
):
    blocks = qkv.shape[0]
    width = resid.shape[2]
    if lend:
        at = pl.ds(count_ref[0, 0] - 1, 1)
    else:
        at = pl.ds(0, blocks)
    qkv_copy = pltpu.make_async_copy(qkv_hbm.at[at], qkv, sems.at[0])
    weight_copy = pltpu.make_async_copy(weight_hbm, weight, sems.at[1])
    resid_copy = pltpu.make_async_copy(resid_hbm.at[at], resid, sems.at[2])
    qkv_copy.start()
    weight_copy.start()
    resid_copy.start()
    qkv_copy.wait()
    for b in range(blocks):
        attend(
            lambda lo, hi, b=b: qkv[b, :, lo:hi],
            lambda lo, hi, b=b: qkv[b, :, width + lo : width + hi],
            lambda lo, hi, b=b: qkv[b, :, 2 * width + lo : 2 * width + hi],
            attended, b * WIN, width,
        )
    weight_copy.wait()
    resid_copy.wait()
    rows = blocks * WIN
    squares = jnp.zeros((rows, 1), jnp.float32)
    step = 2 * LANES
    for lo in range(0, width, step):
        cols = slice(lo, lo + step)
        h = dot32(attended[...], weight[:, cols])
        h = h + bias_ref[:, cols].astype(jnp.float32)
        h = h + resid[:, :, cols].reshape(rows, step).astype(jnp.float32)
        hidden[:, cols] = h
        squares = squares + jnp.sum(h * h, axis=1, keepdims=True)
    scale = lax.rsqrt(squares * (1.0 / width) + EPS)
    for lo in range(0, width, step):
        cols = slice(lo, lo + step)
        out_ref[:, cols] = (hidden[:, cols] * scale * gain_ref[:, cols].astype(jnp.float32)).astype(jnp.bfloat16)


def encode(lend, blocks, count, qkv, resid, weight, bias, gain):
    width = resid.shape[2]
    rows = blocks * WIN
    vmem = pl.BlockSpec(memory_space=pltpu.VMEM)
    hbm = pl.BlockSpec(memory_space=pl.ANY)
    return pl.pallas_call(
        functools.partial(encode_kernel, lend),
        out_shape=jax.ShapeDtypeStruct((rows, width), jnp.bfloat16),
        in_specs=[pl.BlockSpec(memory_space=pltpu.SMEM), hbm, hbm, hbm, vmem, vmem],
        out_specs=vmem,
        scratch_shapes=[
            pltpu.VMEM((blocks, WIN, 3 * width), jnp.bfloat16),
            pltpu.VMEM((blocks, WIN, width), jnp.bfloat16),
            pltpu.VMEM((width, width), jnp.bfloat16),
            pltpu.VMEM((rows, width), jnp.bfloat16),
            pltpu.VMEM((rows, width), jnp.float32),
            pltpu.SemaphoreType.DMA((3,)),
        ],
        compiler_params=pltpu.CompilerParams(vmem_limit_bytes=24 << 20),
        cost_estimate=pl.CostEstimate(
            flops=2 * rows * width * width + 8 * rows * WIN * width,
            bytes_accessed=2 * (width * width + 5 * rows * width),
            transcendentals=rows * WIN * HEADS,
        ),
    )(count, qkv, resid, weight, bias, gain)


def pack_kernel(cap, row_slot_ref, col_slot_ref, own_ref, borrowed_ref, out_ref):
    own_rows = own_ref.shape[0]
    pick = (row_slot_ref[...] == col_slot_ref[...]).astype(jnp.float32).astype(jnp.bfloat16)
    picked = dot32(pick[:, :own_rows], own_ref[...]) + dot32(pick[:, own_rows:], borrowed_ref[...])
    out_ref[...] = picked.astype(jnp.bfloat16)


def place_kernel(row_ref, part_ref, in_ref, out_ref):
    width = in_ref.shape[1]
    rows_out = out_ref.shape[0]
    slots = in_ref.shape[0]
    row_ids = lax.broadcasted_iota(jnp.int32, (rows_out, slots), 0)
    here = row_ref[...] == row_ids
    for j in range(GROUP):
        pick = (here & (part_ref[...] == j)).astype(jnp.float32).astype(jnp.bfloat16)
        out_ref[:, j * width : (j + 1) * width] = dot32(pick, in_ref[...]).astype(jnp.bfloat16)


def per_device(
    qkv, resid, block_count, send_count, send_slot, lm_row, out_weight, out_bias, norm_gain
):
    width = resid.shape[2]
    row_total = send_slot.shape[1]
    tokens = WIN // GROUP
    blocks = row_total // tokens
    n_seq = lax.axis_size("seq")
    n_enc = lax.axis_size("enc")
    slots = lm_row.shape[1]
    cap = slots // n_seq
    bias = out_bias.reshape(1, width)
    gain = norm_gain.reshape(1, width)
    vmem = pl.BlockSpec(memory_space=pltpu.VMEM)

    lent = encode(True, 1, block_count, qkv, resid, out_weight, bias, gain)
    route = [((i - 1) % n_enc, i) for i in range(n_enc)]
    borrowed = lax.ppermute(lent, "enc", route)
    own = encode(False, blocks, block_count, qkv, resid, out_weight, bias, gain)

    kept = block_count[0, 0] - send_count[0, 0]
    source = send_slot.reshape(blocks, tokens, 1)
    live = jnp.arange(blocks, dtype=jnp.int32)[:, None, None] < kept
    parts = jnp.arange(GROUP, dtype=jnp.int32)[None, None, :]
    own_code = jnp.where(live, source * GROUP + parts, -1).reshape(1, blocks * WIN)
    borrowed_code = jnp.where(live[-1:], -1, source[-1:] * GROUP + parts).reshape(1, WIN)
    col_code = jnp.concatenate([own_code, borrowed_code], axis=1)
    dest = jnp.arange(n_seq, dtype=jnp.int32)[:, None, None]
    part = jnp.arange(GROUP, dtype=jnp.int32)[None, :, None]
    rank = jnp.arange(cap, dtype=jnp.int32)[None, None, :]
    row_code = ((dest * cap + rank) * GROUP + part).reshape(slots * GROUP, 1)

    packed = pl.pallas_call(
        functools.partial(pack_kernel, cap),
        out_shape=jax.ShapeDtypeStruct((slots * GROUP, width), jnp.bfloat16),
        in_specs=[vmem] * 4,
        out_specs=vmem,
    )(row_code, col_code, own, borrowed)

    arrived = lax.all_to_all(
        packed.reshape(n_seq, GROUP * cap, width), "seq", split_axis=0, concat_axis=0, tiled=True
    ).reshape(slots * GROUP, width)

    filled = jnp.broadcast_to(lm_row.reshape(n_seq, 1, cap), (n_seq, GROUP, cap)).reshape(1, slots * GROUP)
    part_of = jnp.broadcast_to(part, (n_seq, GROUP, cap)).reshape(1, slots * GROUP)
    placed = pl.pallas_call(
        place_kernel,
        out_shape=jax.ShapeDtypeStruct((row_total, GROUP * width), jnp.bfloat16),
        in_specs=[vmem] * 3,
        out_specs=vmem,
    )(filled, part_of, arrived)
    return placed[None]


def solution(mesh):
    placed = (
        P("enc", "seq", None),
        P("enc", "seq", None),
        P("enc", "seq"),
        P("enc", "seq"),
        P("enc", "seq"),
        P("enc", "seq"),
        P(),
        P(),
        P(),
    )
    return jax.shard_map(
        per_device, mesh=mesh, in_specs=placed, out_specs=P("enc", "seq", None), check_vma=False
    )
```

```python
import functools
import math

import jax
import jax.numpy as jnp
from jax import lax
from jax.experimental import pallas as pl
from jax.experimental.pallas import tpu as pltpu
from jax.sharding import PartitionSpec as P

HEADS = 16
WIN = 64
LANES = 128
GROUP = 4
EPS = 1e-6
CORES = 2

NT = (((1,), (1,)), ((), ()))


def dot32(a, b):
    return jnp.dot(a, b, preferred_element_type=jnp.float32)


def one_hot(match):
    return match.astype(jnp.float32).astype(jnp.bfloat16)


def attend(q, k, v, out_ref, row0, width):
    head = width // HEADS
    rate = 1.0 / math.sqrt(head)
    totals = [None] * (width // LANES)
    sums = [None] * (width // LANES)
    first_half = lax.broadcasted_iota(jnp.int32, (WIN, 2 * WIN), 1) < WIN
    for pair in range(HEADS // 2):
        start = 2 * pair * head
        lo = start // LANES * LANES
        hi = -(-(start + 2 * head) // LANES) * LANES
        column = lax.broadcasted_iota(jnp.int32, (2 * WIN, hi - lo), 1) + lo
        row = lax.broadcasted_iota(jnp.int32, (2 * WIN, hi - lo), 0)
        begin = jnp.where(row < WIN, start, start + head)
        mask = one_hot((column >= begin) & (column < begin + head))
        kw, vw = k(lo, hi), v(lo, hi)
        keys = jnp.concatenate([kw, kw], axis=0) * mask
        values = jnp.concatenate([vw, vw], axis=0) * mask
        scores = lax.dot_general(q(lo, hi), keys, NT, preferred_element_type=jnp.float32)
        top0 = jnp.max(jnp.where(first_half, scores, -jnp.inf), axis=1, keepdims=True)
        top1 = jnp.max(jnp.where(first_half, -jnp.inf, scores), axis=1, keepdims=True)
        raised = jnp.exp((scores - jnp.where(first_half, top0, top1)) * rate).astype(jnp.bfloat16)
        part = dot32(raised, values)
        norm = dot32(raised, mask)
        for tile in range(lo // LANES, hi // LANES):
            at = slice(tile * LANES - lo, (tile + 1) * LANES - lo)
            totals[tile] = part[:, at] if totals[tile] is None else totals[tile] + part[:, at]
            sums[tile] = norm[:, at] if sums[tile] is None else sums[tile] + norm[:, at]
    for tile in range(width // LANES):
        out_ref[row0 : row0 + WIN, tile * LANES : (tile + 1) * LANES] = (totals[tile] / sums[tile]).astype(
            jnp.bfloat16
        )


def encode(
    slot, qkv_hbm, resid_hbm, weight_hbm, bias_hbm, gain_hbm, out_ref,
    qkv, resid, weight, attended, hidden, bias_ref, gain_ref, sems,
):
    blocks = qkv.shape[0]
    width = resid.shape[2]
    at = pl.ds(slot, blocks)
    pairs = [
        (qkv_hbm.at[at], qkv), (weight_hbm, weight), (resid_hbm.at[at], resid), (bias_hbm, bias_ref), (gain_hbm, gain_ref)
    ]
    copies = [pltpu.make_async_copy(a, b, sems.at[i]) for i, (a, b) in enumerate(pairs)]
    for copy in copies:
        copy.start()
    copies[0].wait()
    for b in range(blocks):
        attend(
            lambda lo, hi, b=b: qkv[b, :, lo:hi],
            lambda lo, hi, b=b: qkv[b, :, width + lo : width + hi],
            lambda lo, hi, b=b: qkv[b, :, 2 * width + lo : 2 * width + hi],
            attended, b * WIN, width,
        )
    for copy in copies[1:]:
        copy.wait()
    rows = blocks * WIN
    squares = jnp.zeros((rows, 1), jnp.float32)
    step = 2 * LANES
    for lo in range(0, width, step):
        cols = slice(lo, lo + step)
        h = dot32(attended[...], weight[:, cols])
        h = h + bias_ref[cols].astype(jnp.float32).reshape(1, step)
        h = h + resid[:, :, cols].reshape(rows, step).astype(jnp.float32)
        hidden[:, cols] = h
        squares = squares + jnp.sum(h * h, axis=1, keepdims=True)
    scale = lax.rsqrt(squares * (1.0 / width) + EPS)
    for lo in range(0, width, step):
        cols = slice(lo, lo + step)
        gain = gain_ref[cols].astype(jnp.float32).reshape(1, step)
        out_ref[:, cols] = (hidden[:, cols] * scale * gain).astype(jnp.bfloat16)


def lent_kernel(count_ref, qkv_hbm, resid_hbm, weight_hbm, bias_hbm, gain_hbm, out_ref, *scratch):
    encode(count_ref[0, 0] - 1, qkv_hbm, resid_hbm, weight_hbm, bias_hbm, gain_hbm, out_ref, *scratch)


def split_index(index, n_seq, cap):
    step = index // (GROUP * cap)
    rest = index - step * (GROUP * cap)
    patch = rest // cap
    return step, patch, rest - patch * cap


def own_kernel(
    n_seq, cap, peer, count_ref, send_ref, me_ref, slot_ref, row_ref,
    qkv_hbm, resid_hbm, weight_hbm, bias_hbm, gain_hbm,
    packed_ref, borrow_ref, place_ref, normed, *scratch,
):
    rows = normed.shape[0]
    slots = n_seq * cap
    sent = slots * GROUP
    tokens = rows // GROUP
    me = me_ref[0, 0]
    encode(0, qkv_hbm, resid_hbm, weight_hbm, bias_hbm, gain_hbm, normed, *scratch)

    step, patch, rank = split_index(lax.broadcasted_iota(jnp.int32, (sent, 1), 0), n_seq, cap)
    row_code = (peer(me, step, 1) * cap + rank) * GROUP + patch
    token = lax.broadcasted_iota(jnp.int32, (tokens, rows), 0)
    column = lax.broadcasted_iota(jnp.int32, (tokens, rows), 1)
    spread = one_hot((column >= token * GROUP) & (column < (token + 1) * GROUP))
    slot = jnp.broadcast_to(slot_ref[...].astype(jnp.float32), (16, tokens)).astype(jnp.bfloat16)
    slot = dot32(slot, spread)[:1].astype(jnp.int32)
    index = lax.broadcasted_iota(jnp.int32, (1, rows), 1)
    col_code = slot * GROUP + jnp.bitwise_and(index, GROUP - 1)
    kept = (count_ref[0, 0] - send_ref[0, 0]) * WIN
    last = rows - WIN
    own = one_hot(row_code == jnp.where(index < kept, col_code, -1))
    packed_ref[...] = dot32(own, normed[...]).astype(jnp.bfloat16)
    borrow_ref[...] = one_hot(row_code == jnp.where(kept > last, -1, col_code[:, last:]))

    step, patch, rank = split_index(lax.broadcasted_iota(jnp.int32, (1, sent), 1), n_seq, cap)
    arrive = peer(me, step, -1) * cap + rank
    pick = one_hot(lax.broadcasted_iota(jnp.int32, (slots, sent), 0) == arrive)
    target = jnp.broadcast_to(row_ref[...].astype(jnp.float32), (16, slots)).astype(jnp.bfloat16)
    target = dot32(target, pick)[:1].astype(jnp.int32)
    out_row = lax.broadcasted_iota(jnp.int32, (tokens, sent), 0)
    for j in range(GROUP):
        place_ref[j * tokens : (j + 1) * tokens, :] = one_hot((target == out_row) & (patch == j))


def encode_call(kernel, blocks, scalars, slots, qkv, resid, weight, bias, gain, out_shape, extra):
    width = resid.shape[2]
    rows = blocks * WIN
    vmem = pl.BlockSpec(memory_space=pltpu.VMEM)
    smem = pl.BlockSpec(memory_space=pltpu.SMEM)
    hbm = pl.BlockSpec(memory_space=pltpu.HBM)
    return pl.pallas_call(
        kernel,
        out_shape=out_shape,
        in_specs=[smem] * len(scalars) + [vmem] * len(slots) + [hbm] * 5,
        out_specs=jax.tree.map(lambda _: vmem, out_shape),
        scratch_shapes=extra
        + [
            pltpu.VMEM((blocks, WIN, 3 * width), jnp.bfloat16),
            pltpu.VMEM((blocks, WIN, width), jnp.bfloat16),
            pltpu.VMEM((width, width), jnp.bfloat16),
            pltpu.VMEM((rows, width), jnp.bfloat16),
            pltpu.VMEM((rows, width), jnp.float32),
            pltpu.VMEM((width,), jnp.bfloat16),
            pltpu.VMEM((width,), jnp.bfloat16),
            pltpu.SemaphoreType.DMA((5,)),
        ],
        compiler_params=pltpu.CompilerParams(vmem_limit_bytes=24 << 20),
        cost_estimate=pl.CostEstimate(
            flops=2 * rows * width * width + 8 * rows * WIN * width,
            bytes_accessed=2 * (width * width + 5 * rows * width),
            transcendentals=rows * WIN * HEADS,
        ),
    )(*scalars, *slots, *(pltpu.with_memory_space_constraint(a, pltpu.HBM) for a in (qkv, resid, weight, bias, gain)))


def pack_kernel(packed_ref, borrow_ref, borrowed_ref, *out_refs):
    total = packed_ref[...].astype(jnp.float32) + dot32(borrow_ref[...], borrowed_ref[...])
    chunk = out_refs[0].shape[0]
    for step, out_ref in enumerate(out_refs):
        out_ref[...] = total[step * chunk : (step + 1) * chunk].astype(jnp.bfloat16)


def place_kernel(place_ref, *refs):
    out_ref = refs[-1]
    tokens = out_ref.shape[0]
    chunks = [ref[...].astype(jnp.float32) for ref in refs[:-1]]
    arrived = chunks[0] if len(chunks) == 1 else jnp.concatenate(chunks, axis=0)
    arrived = arrived.astype(jnp.bfloat16)
    width = arrived.shape[1]
    for j in range(GROUP):
        rows = dot32(place_ref[j * tokens : (j + 1) * tokens, :], arrived)
        out_ref[:, j * width : (j + 1) * width] = rows.astype(jnp.bfloat16)


def chip_peer(n_seq, me, step, sign):
    n_z = n_seq // CORES
    z = me // CORES + sign * (step // CORES)
    z = jnp.where(z >= n_z, z - n_z, jnp.where(z < 0, z + n_z, z))
    return z * CORES + jnp.bitwise_xor(jnp.bitwise_and(me, 1), jnp.bitwise_and(step, 1))


def per_device(
    qkv, resid, block_count, send_count, send_slot, lm_row, out_weight, out_bias, norm_gain
):
    width = resid.shape[2]
    row_total = send_slot.shape[1]
    tokens = WIN // GROUP
    blocks = row_total // tokens
    n_seq = lax.axis_size("seq")
    n_enc = lax.axis_size("enc")
    slots = lm_row.shape[1]
    cap = slots // n_seq
    chunk = GROUP * cap
    sent = slots * GROUP
    vmem = pl.BlockSpec(memory_space=pltpu.VMEM)
    small = pltpu.CompilerParams(vmem_limit_bytes=16 << 20)

    def rows_of(count, columns=width):
        return jax.ShapeDtypeStruct((count, columns), jnp.bfloat16)

    data = (qkv, resid, out_weight, out_bias, norm_gain)
    lent = encode_call(lent_kernel, 1, [block_count], [], *data, rows_of(WIN), [])
    borrowed = lax.ppermute(lent, "enc", [((i - 1) % n_enc, i) for i in range(n_enc)])

    by_steps = chunk % 8 == 0 and n_seq % CORES == 0
    peer = functools.partial(chip_peer, n_seq) if by_steps else lambda me, step, sign: step
    me = lax.axis_index("seq").astype(jnp.int32).reshape(1, 1)
    packed, borrow, place = encode_call(
        functools.partial(own_kernel, n_seq, cap, peer), blocks,
        [block_count, send_count, me], [send_slot, lm_row], *data,
        (rows_of(sent), rows_of(sent, WIN), rows_of(GROUP * row_total, sent)),
        [pltpu.VMEM((row_total * GROUP, width), jnp.bfloat16)],
    )
    pieces = n_seq if by_steps else 1
    outgoing = pl.pallas_call(
        pack_kernel,
        out_shape=[rows_of(sent // pieces)] * pieces,
        in_specs=[vmem] * 3,
        out_specs=[vmem] * pieces,
        compiler_params=small,
    )(packed, borrow, borrowed)

    if by_steps:
        n_z = n_seq // CORES
        arrived = [outgoing[0]] + [None] * (n_seq - 1)
        for step in sorted(range(1, n_seq), key=lambda s: (abs(s // CORES - n_z / 2), s)):
            route = [
                (i, (i // CORES + step // CORES) % n_z * CORES + (i ^ step) % CORES) for i in range(n_seq)
            ]
            arrived[step] = lax.ppermute(outgoing[step], "seq", route)
    else:
        arrived = [
            lax.all_to_all(
                outgoing[0].reshape(n_seq, chunk, width), "seq", split_axis=0, concat_axis=0, tiled=True
            ).reshape(sent, width)
        ]
    placed = pl.pallas_call(
        place_kernel,
        out_shape=rows_of(row_total, GROUP * width),
        in_specs=[vmem] * (1 + pieces),
        out_specs=vmem,
        compiler_params=small,
    )(place, *arrived)
    return placed[None]


def solution(mesh):
    placed = (
        P("enc", "seq", None),
        P("enc", "seq", None),
        P("enc", "seq"),
        P("enc", "seq"),
        P("enc", "seq"),
        P("enc", "seq"),
        P(),
        P(),
        P(),
    )
    return jax.shard_map(
        per_device, mesh=mesh, in_specs=placed, out_specs=P("enc", "seq", None), check_vma=False
    )
```

```python
import functools
import math

import jax
import jax.numpy as jnp
from jax import lax
from jax.experimental import pallas as pl
from jax.experimental.pallas import tpu as pltpu
from jax.sharding import PartitionSpec as P

HEADS = 16
WIN = 64
LANES = 128
GROUP = 4
EPS = 1e-6
CORES = 2

NT = (((1,), (1,)), ((), ()))


def dot32(a, b):
    return jnp.dot(a, b, preferred_element_type=jnp.float32)


def one_hot(match):
    return match.astype(jnp.float32).astype(jnp.bfloat16)


def attend(q, k, v, out_ref, row0, width):
    head = width // HEADS
    rate = 1.0 / math.sqrt(head)
    totals = [None] * (width // LANES)
    sums = [None] * (width // LANES)
    first_half = lax.broadcasted_iota(jnp.int32, (WIN, 2 * WIN), 1) < WIN
    for pair in range(HEADS // 2):
        start = 2 * pair * head
        lo = start // LANES * LANES
        hi = -(-(start + 2 * head) // LANES) * LANES
        column = lax.broadcasted_iota(jnp.int32, (2 * WIN, hi - lo), 1) + lo
        row = lax.broadcasted_iota(jnp.int32, (2 * WIN, hi - lo), 0)
        begin = jnp.where(row < WIN, start, start + head)
        mask = one_hot((column >= begin) & (column < begin + head))
        kw, vw = k(lo, hi), v(lo, hi)
        keys = jnp.concatenate([kw, kw], axis=0) * mask
        values = jnp.concatenate([vw, vw], axis=0) * mask
        scores = lax.dot_general(q(lo, hi), keys, NT, preferred_element_type=jnp.float32)
        top0 = jnp.max(jnp.where(first_half, scores, -jnp.inf), axis=1, keepdims=True)
        top1 = jnp.max(jnp.where(first_half, -jnp.inf, scores), axis=1, keepdims=True)
        raised = jnp.exp((scores - jnp.where(first_half, top0, top1)) * rate).astype(jnp.bfloat16)
        part = dot32(raised, values)
        norm = dot32(raised, mask)
        for tile in range(lo // LANES, hi // LANES):
            at = slice(tile * LANES - lo, (tile + 1) * LANES - lo)
            totals[tile] = part[:, at] if totals[tile] is None else totals[tile] + part[:, at]
            sums[tile] = norm[:, at] if sums[tile] is None else sums[tile] + norm[:, at]
    for tile in range(width // LANES):
        out_ref[row0 : row0 + WIN, tile * LANES : (tile + 1) * LANES] = (totals[tile] / sums[tile]).astype(
            jnp.bfloat16
        )


def encode(
    slot, qkv_hbm, resid_hbm, weight_hbm, bias_hbm, gain_hbm, out_ref,
    qkv, resid, weight, attended, hidden, bias_ref, gain_ref, sems,
):
    blocks = qkv.shape[0]
    width = resid.shape[2]
    at = pl.ds(slot, blocks)
    pairs = [
        (qkv_hbm.at[at], qkv), (weight_hbm, weight), (resid_hbm.at[at], resid), (bias_hbm, bias_ref), (gain_hbm, gain_ref)
    ]
    copies = [pltpu.make_async_copy(a, b, sems.at[i]) for i, (a, b) in enumerate(pairs)]
    for copy in copies:
        copy.start()
    copies[0].wait()
    for b in range(blocks):
        attend(
            lambda lo, hi, b=b: qkv[b, :, lo:hi],
            lambda lo, hi, b=b: qkv[b, :, width + lo : width + hi],
            lambda lo, hi, b=b: qkv[b, :, 2 * width + lo : 2 * width + hi],
            attended, b * WIN, width,
        )
    for copy in copies[1:]:
        copy.wait()
    rows = blocks * WIN
    squares = jnp.zeros((rows, 1), jnp.float32)
    step = 2 * LANES
    for lo in range(0, width, step):
        cols = slice(lo, lo + step)
        h = dot32(attended[...], weight[:, cols])
        h = h + bias_ref[cols].astype(jnp.float32).reshape(1, step)
        h = h + resid[:, :, cols].reshape(rows, step).astype(jnp.float32)
        hidden[:, cols] = h
        squares = squares + jnp.sum(h * h, axis=1, keepdims=True)
    scale = lax.rsqrt(squares * (1.0 / width) + EPS)
    for lo in range(0, width, step):
        cols = slice(lo, lo + step)
        gain = gain_ref[cols].astype(jnp.float32).reshape(1, step)
        out_ref[:, cols] = (hidden[:, cols] * scale * gain).astype(jnp.bfloat16)


def lent_kernel(count_ref, qkv_hbm, resid_hbm, weight_hbm, bias_hbm, gain_hbm, out_ref, *scratch):
    encode(count_ref[0, 0] - 1, qkv_hbm, resid_hbm, weight_hbm, bias_hbm, gain_hbm, out_ref, *scratch)


def split_index(index, n_seq, cap):
    step = index // (GROUP * cap)
    rest = index - step * (GROUP * cap)
    patch = rest // cap
    return step, patch, rest - patch * cap


def own_kernel(
    n_seq, cap, peer, count_ref, send_ref, me_ref, slot_ref, row_ref,
    qkv_hbm, resid_hbm, weight_hbm, bias_hbm, gain_hbm,
    packed_ref, borrow_ref, place_ref, normed, *scratch,
):
    rows = normed.shape[0]
    slots = n_seq * cap
    sent = slots * GROUP
    tokens = rows // GROUP
    me = me_ref[0, 0]
    encode(0, qkv_hbm, resid_hbm, weight_hbm, bias_hbm, gain_hbm, normed, *scratch)

    step, patch, rank = split_index(lax.broadcasted_iota(jnp.int32, (sent, 1), 0), n_seq, cap)
    row_code = (peer(me, step, 1) * cap + rank) * GROUP + patch
    token = lax.broadcasted_iota(jnp.int32, (tokens, rows), 0)
    column = lax.broadcasted_iota(jnp.int32, (tokens, rows), 1)
    spread = one_hot((column >= token * GROUP) & (column < (token + 1) * GROUP))
    slot = jnp.broadcast_to(slot_ref[...].astype(jnp.float32), (16, tokens)).astype(jnp.bfloat16)
    slot = dot32(slot, spread)[:1].astype(jnp.int32)
    index = lax.broadcasted_iota(jnp.int32, (1, rows), 1)
    col_code = slot * GROUP + jnp.bitwise_and(index, GROUP - 1)
    kept = (count_ref[0, 0] - send_ref[0, 0]) * WIN
    last = rows - WIN
    own = one_hot(row_code == jnp.where(index < kept, col_code, -1))
    packed_ref[...] = dot32(own, normed[...]).astype(jnp.bfloat16)
    borrow_ref[...] = one_hot(row_code == jnp.where(kept > last, -1, col_code[:, last:]))

    step, patch, rank = split_index(lax.broadcasted_iota(jnp.int32, (1, sent), 1), n_seq, cap)
    arrive = peer(me, step, -1) * cap + rank
    pick = one_hot(lax.broadcasted_iota(jnp.int32, (slots, sent), 0) == arrive)
    target = jnp.broadcast_to(row_ref[...].astype(jnp.float32), (16, slots)).astype(jnp.bfloat16)
    target = dot32(target, pick)[:1].astype(jnp.int32)
    out_row = lax.broadcasted_iota(jnp.int32, (tokens, sent), 0)
    for j in range(GROUP):
        place_ref[j * tokens : (j + 1) * tokens, :] = one_hot((target == out_row) & (patch == j))


def encode_call(kernel, blocks, scalars, slots, qkv, resid, weight, bias, gain, out_shape, extra):
    width = resid.shape[2]
    rows = blocks * WIN
    vmem = pl.BlockSpec(memory_space=pltpu.VMEM)
    smem = pl.BlockSpec(memory_space=pltpu.SMEM)
    hbm = pl.BlockSpec(memory_space=pltpu.HBM)
    return pl.pallas_call(
        kernel,
        out_shape=out_shape,
        in_specs=[smem] * len(scalars) + [vmem] * len(slots) + [hbm] * 5,
        out_specs=jax.tree.map(lambda _: vmem, out_shape),
        scratch_shapes=extra
        + [
            pltpu.VMEM((blocks, WIN, 3 * width), jnp.bfloat16),
            pltpu.VMEM((blocks, WIN, width), jnp.bfloat16),
            pltpu.VMEM((width, width), jnp.bfloat16),
            pltpu.VMEM((rows, width), jnp.bfloat16),
            pltpu.VMEM((rows, width), jnp.float32),
            pltpu.VMEM((width,), jnp.bfloat16),
            pltpu.VMEM((width,), jnp.bfloat16),
            pltpu.SemaphoreType.DMA((5,)),
        ],
        compiler_params=pltpu.CompilerParams(vmem_limit_bytes=24 << 20),
        cost_estimate=pl.CostEstimate(
            flops=2 * rows * width * width + 8 * rows * WIN * width,
            bytes_accessed=2 * (width * width + 5 * rows * width),
            transcendentals=rows * WIN * HEADS,
        ),
    )(*scalars, *slots, *(pltpu.with_memory_space_constraint(a, pltpu.HBM) for a in (qkv, resid, weight, bias, gain)))


def pack_kernel(packed_ref, borrow_ref, borrowed_ref, *out_refs):
    total = packed_ref[...].astype(jnp.float32) + dot32(borrow_ref[...], borrowed_ref[...])
    chunk = out_refs[0].shape[0]
    for step, out_ref in enumerate(out_refs):
        out_ref[...] = total[step * chunk : (step + 1) * chunk].astype(jnp.bfloat16)


def place_kernel(place_ref, *refs):
    out_ref = refs[-1]
    tokens = out_ref.shape[0]
    chunks = [ref[...].astype(jnp.float32) for ref in refs[:-1]]
    arrived = chunks[0] if len(chunks) == 1 else jnp.concatenate(chunks, axis=0)
    arrived = arrived.astype(jnp.bfloat16)
    width = arrived.shape[1]
    for j in range(GROUP):
        rows = dot32(place_ref[j * tokens : (j + 1) * tokens, :], arrived)
        out_ref[:, j * width : (j + 1) * width] = rows.astype(jnp.bfloat16)


def exchange_steps(n_seq):
    n_z = n_seq // CORES
    steps = [(dz, dc) for dz in range(n_z) for dc in range(CORES) if (dz, dc) != (0, 0)]
    return [(0, 0)] + sorted(steps, key=lambda s: (abs(s[0] - n_z / 2), s[1], s[0]))


def chip_peer(n_seq, me, step, sign):
    n_z = n_seq // CORES
    offset = jnp.zeros_like(step)
    flip = jnp.zeros_like(step)
    for i, (dz, dc) in enumerate(exchange_steps(n_seq)):
        offset = jnp.where(step == i, dz, offset)
        flip = jnp.where(step == i, dc, flip)
    z = me // CORES + sign * offset
    z = jnp.where(z >= n_z, z - n_z, jnp.where(z < 0, z + n_z, z))
    return z * CORES + jnp.bitwise_xor(jnp.bitwise_and(me, 1), flip)


def per_device(
    qkv, resid, block_count, send_count, send_slot, lm_row, out_weight, out_bias, norm_gain
):
    width = resid.shape[2]
    row_total = send_slot.shape[1]
    tokens = WIN // GROUP
    blocks = row_total // tokens
    n_seq = lax.axis_size("seq")
    n_enc = lax.axis_size("enc")
    slots = lm_row.shape[1]
    cap = slots // n_seq
    chunk = GROUP * cap
    sent = slots * GROUP
    vmem = pl.BlockSpec(memory_space=pltpu.VMEM)
    small = pltpu.CompilerParams(vmem_limit_bytes=16 << 20)

    def rows_of(count, columns=width):
        return jax.ShapeDtypeStruct((count, columns), jnp.bfloat16)

    data = (qkv, resid, out_weight, out_bias, norm_gain)
    lent = encode_call(lent_kernel, 1, [block_count], [], *data, rows_of(WIN), [])
    borrowed = lax.ppermute(lent, "enc", [((i - 1) % n_enc, i) for i in range(n_enc)])

    by_steps = chunk % 8 == 0 and n_seq % CORES == 0
    peer = functools.partial(chip_peer, n_seq) if by_steps else lambda me, step, sign: step
    me = lax.axis_index("seq").astype(jnp.int32).reshape(1, 1)
    packed, borrow, place = encode_call(
        functools.partial(own_kernel, n_seq, cap, peer), blocks,
        [block_count, send_count, me], [send_slot, lm_row], *data,
        (rows_of(sent), rows_of(sent, WIN), rows_of(GROUP * row_total, sent)),
        [pltpu.VMEM((row_total * GROUP, width), jnp.bfloat16)],
    )
    pieces = n_seq if by_steps else 1
    outgoing = pl.pallas_call(
        pack_kernel,
        out_shape=[rows_of(sent // pieces)] * pieces,
        in_specs=[vmem] * 3,
        out_specs=[vmem] * pieces,
        compiler_params=small,
    )(packed, borrow, borrowed)

    if by_steps:
        n_z = n_seq // CORES
        arrived = [outgoing[0]]
        for part, (dz, dc) in list(zip(outgoing, exchange_steps(n_seq)))[1:]:
            route = [(i, (i // CORES + dz) % n_z * CORES + (i + dc) % CORES) for i in range(n_seq)]
            arrived.append(lax.ppermute(part, "seq", route))
    else:
        arrived = [
            lax.all_to_all(
                outgoing[0].reshape(n_seq, chunk, width), "seq", split_axis=0, concat_axis=0, tiled=True
            ).reshape(sent, width)
        ]
    placed = pl.pallas_call(
        place_kernel,
        out_shape=rows_of(row_total, GROUP * width),
        in_specs=[vmem] * (1 + pieces),
        out_specs=vmem,
        compiler_params=small,
    )(place, *arrived)
    return placed[None]


def solution(mesh):
    placed = (
        P("enc", "seq", None),
        P("enc", "seq", None),
        P("enc", "seq"),
        P("enc", "seq"),
        P("enc", "seq"),
        P("enc", "seq"),
        P(),
        P(),
        P(),
    )
    return jax.shard_map(
        per_device, mesh=mesh, in_specs=placed, out_specs=P("enc", "seq", None), check_vma=False
    )
```

```python
import functools
import math

import jax
import jax.numpy as jnp
from jax import lax
from jax.experimental import pallas as pl
from jax.experimental.pallas import tpu as pltpu
from jax.sharding import PartitionSpec as P

HEADS = 16
WIN = 64
LANES = 128
GROUP = 4
EPS = 1e-6
CORES = 2

NT = (((1,), (1,)), ((), ()))


def dot32(a, b):
    return jnp.dot(a, b, preferred_element_type=jnp.float32)


def one_hot(match):
    return match.astype(jnp.float32).astype(jnp.bfloat16)


def attend(q, k, v, out_ref, row0, width):
    head = width // HEADS
    rate = 1.0 / math.sqrt(head)
    totals = [None] * (width // LANES)
    sums = [None] * (width // LANES)
    first_half = lax.broadcasted_iota(jnp.int32, (WIN, 2 * WIN), 1) < WIN
    for pair in range(HEADS // 2):
        start = 2 * pair * head
        lo = start // LANES * LANES
        hi = -(-(start + 2 * head) // LANES) * LANES
        column = lax.broadcasted_iota(jnp.int32, (2 * WIN, hi - lo), 1) + lo
        row = lax.broadcasted_iota(jnp.int32, (2 * WIN, hi - lo), 0)
        begin = jnp.where(row < WIN, start, start + head)
        mask = one_hot((column >= begin) & (column < begin + head))
        kw, vw = k(lo, hi), v(lo, hi)
        keys = jnp.concatenate([kw, kw], axis=0) * mask
        values = jnp.concatenate([vw, vw], axis=0) * mask
        scores = lax.dot_general(q(lo, hi), keys, NT, preferred_element_type=jnp.float32)
        top0 = jnp.max(jnp.where(first_half, scores, -jnp.inf), axis=1, keepdims=True)
        top1 = jnp.max(jnp.where(first_half, -jnp.inf, scores), axis=1, keepdims=True)
        raised = jnp.exp((scores - jnp.where(first_half, top0, top1)) * rate).astype(jnp.bfloat16)
        part = dot32(raised, values)
        norm = dot32(raised, mask)
        for tile in range(lo // LANES, hi // LANES):
            at = slice(tile * LANES - lo, (tile + 1) * LANES - lo)
            totals[tile] = part[:, at] if totals[tile] is None else totals[tile] + part[:, at]
            sums[tile] = norm[:, at] if sums[tile] is None else sums[tile] + norm[:, at]
    for tile in range(width // LANES):
        out_ref[row0 : row0 + WIN, tile * LANES : (tile + 1) * LANES] = (totals[tile] / sums[tile]).astype(
            jnp.bfloat16
        )


def encode_kernel(
    count_hbm, qkv_hbm, resid_hbm, weight_hbm, bias_hbm, gain_hbm, rows_ref, lent_ref, count,
    qkv, resid, weight, bias, gain, attended, hidden, slot_sems, weight_sems, sems,
):
    slots = qkv.shape[0]
    width = resid.shape[2]
    step = 2 * LANES
    chunks = [slice(lo, lo + step) for lo in range(0, width, step)]
    count_copy = pltpu.make_async_copy(count_hbm, count, sems.at[0])
    slot_copies = [pltpu.make_async_copy(qkv_hbm.at[b], qkv.at[b], slot_sems.at[b]) for b in range(slots)]
    weight_copies = [
        pltpu.make_async_copy(weight_hbm.at[:, cols], weight.at[:, cols], weight_sems.at[i])
        for i, cols in enumerate(chunks)
    ]
    other_copies = [
        pltpu.make_async_copy(a, b, sems.at[i + 1])
        for i, (a, b) in enumerate([(resid_hbm, resid), (bias_hbm, bias), (gain_hbm, gain)])
    ]
    for copy in slot_copies + weight_copies + other_copies + [count_copy]:
        copy.start()
    for b in range(slots):
        slot_copies[b].wait()
        attend(
            lambda lo, hi, b=b: qkv[b, :, lo:hi],
            lambda lo, hi, b=b: qkv[b, :, width + lo : width + hi],
            lambda lo, hi, b=b: qkv[b, :, 2 * width + lo : 2 * width + hi],
            attended, b * WIN, width,
        )
    rows = slots * WIN
    squares = jnp.zeros((rows, 1), jnp.float32)
    for i, cols in enumerate(chunks):
        weight_copies[i].wait()
        h = dot32(attended[...], weight[:, cols])
        if i == 0:
            for copy in other_copies:
                copy.wait()
        h = h + bias[cols].astype(jnp.float32).reshape(1, step)
        h = h + resid[:, :, cols].reshape(rows, step).astype(jnp.float32)
        hidden[:, cols] = h
        squares = squares + jnp.sum(h * h, axis=1, keepdims=True)
    scale = lax.rsqrt(squares * (1.0 / width) + EPS)
    for cols in chunks:
        rows_ref[:, cols] = (hidden[:, cols] * scale * gain[cols].astype(jnp.float32).reshape(1, step)).astype(jnp.bfloat16)
    count_copy.wait()
    last = pl.multiple_of((count[0, 0] - 1) * WIN, WIN)
    lent_ref[...] = rows_ref[pl.ds(last, WIN), :]


def split_index(index, n_seq, cap):
    step = index // (GROUP * cap)
    rest = index - step * (GROUP * cap)
    patch = rest // cap
    return step, patch, rest - patch * cap


def own_kernel(n_seq, cap, peer, count_ref, send_ref, me_ref, slot_ref, row_ref, rows_ref, packed_ref, borrow_ref, place_ref):
    slots = n_seq * cap
    sent = slots * GROUP
    tokens = slot_ref.shape[1]
    rows = tokens * GROUP
    me = me_ref[0, 0]

    step, patch, rank = split_index(lax.broadcasted_iota(jnp.int32, (sent, 1), 0), n_seq, cap)
    row_code = (peer(me, step, 1) * cap + rank) * GROUP + patch
    token = lax.broadcasted_iota(jnp.int32, (tokens, rows), 0)
    column = lax.broadcasted_iota(jnp.int32, (tokens, rows), 1)
    spread = one_hot((column >= token * GROUP) & (column < (token + 1) * GROUP))
    slot = jnp.broadcast_to(slot_ref[...].astype(jnp.float32), (16, tokens)).astype(jnp.bfloat16)
    slot = dot32(slot, spread)[:1].astype(jnp.int32)
    index = lax.broadcasted_iota(jnp.int32, (1, rows), 1)
    col_code = slot * GROUP + jnp.bitwise_and(index, GROUP - 1)
    kept = (count_ref[0, 0] - send_ref[0, 0]) * WIN
    last = rows - WIN
    own = one_hot(row_code == jnp.where(index < kept, col_code, -1))
    packed_ref[...] = dot32(own, rows_ref[:rows, :]).astype(jnp.bfloat16)
    borrow_ref[...] = one_hot(row_code == jnp.where(kept > last, -1, col_code[:, last:]))

    step, patch, rank = split_index(lax.broadcasted_iota(jnp.int32, (1, sent), 1), n_seq, cap)
    arrive = peer(me, step, -1) * cap + rank
    pick = one_hot(lax.broadcasted_iota(jnp.int32, (slots, sent), 0) == arrive)
    target = jnp.broadcast_to(row_ref[...].astype(jnp.float32), (16, slots)).astype(jnp.bfloat16)
    target = dot32(target, pick)[:1].astype(jnp.int32)
    out_row = lax.broadcasted_iota(jnp.int32, (tokens, sent), 0)
    for j in range(GROUP):
        place_ref[j * tokens : (j + 1) * tokens, :] = one_hot((target == out_row) & (patch == j))


def encode_all(count, qkv, resid, weight, bias, gain):
    slots, _, width = resid.shape
    rows = slots * WIN
    chunks = width // (2 * LANES)
    vmem = pl.BlockSpec(memory_space=pltpu.VMEM)
    inputs = (count, qkv, resid, weight, bias, gain)
    return pl.pallas_call(
        encode_kernel,
        out_shape=(
            jax.ShapeDtypeStruct((rows, width), jnp.bfloat16),
            jax.ShapeDtypeStruct((WIN, width), jnp.bfloat16),
            jax.ShapeDtypeStruct((1, 1), jnp.int32),
        ),
        in_specs=[pl.BlockSpec(memory_space=pltpu.HBM)] * len(inputs),
        out_specs=(vmem, vmem, pl.BlockSpec(memory_space=pltpu.SMEM)),
        scratch_shapes=[
            pltpu.VMEM((slots, WIN, 3 * width), jnp.bfloat16),
            pltpu.VMEM((slots, WIN, width), jnp.bfloat16),
            pltpu.VMEM((width, width), jnp.bfloat16),
            pltpu.VMEM((width,), jnp.bfloat16),
            pltpu.VMEM((width,), jnp.bfloat16),
            pltpu.VMEM((rows, width), jnp.bfloat16),
            pltpu.VMEM((rows, width), jnp.float32),
            pltpu.SemaphoreType.DMA((slots,)),
            pltpu.SemaphoreType.DMA((chunks,)),
            pltpu.SemaphoreType.DMA((4,)),
        ],
        compiler_params=pltpu.CompilerParams(vmem_limit_bytes=24 << 20),
        cost_estimate=pl.CostEstimate(
            flops=2 * rows * width * width + 8 * rows * WIN * width,
            bytes_accessed=2 * (width * width + 5 * rows * width),
            transcendentals=rows * WIN * HEADS,
        ),
    )(count, *(pltpu.with_memory_space_constraint(a, pltpu.HBM) for a in inputs[1:]))


def pack_kernel(packed_ref, borrow_ref, borrowed_ref, *out_refs):
    total = packed_ref[...].astype(jnp.float32) + dot32(borrow_ref[...], borrowed_ref[...])
    chunk = out_refs[0].shape[0]
    for step, out_ref in enumerate(out_refs):
        out_ref[...] = total[step * chunk : (step + 1) * chunk].astype(jnp.bfloat16)


def place_kernel(place_ref, *refs):
    *in_refs, out_hbm, out, sems = refs
    tokens = out.shape[0]
    chunks = [ref[...].astype(jnp.float32) for ref in in_refs]
    arrived = chunks[0] if len(chunks) == 1 else jnp.concatenate(chunks, axis=0)
    arrived = arrived.astype(jnp.bfloat16)
    width = arrived.shape[1]
    copies = []
    for j in range(GROUP):
        cols = slice(j * width, (j + 1) * width)
        out[:, cols] = dot32(place_ref[j * tokens : (j + 1) * tokens, :], arrived).astype(jnp.bfloat16)
        copies.append(pltpu.make_async_copy(out.at[:, cols], out_hbm.at[:, cols], sems.at[j]))
        copies[-1].start()
    for copy in copies:
        copy.wait()


def exchange_steps(n_seq):
    n_z = n_seq // CORES
    steps = [(dz, dc) for dz in range(n_z) for dc in range(CORES) if (dz, dc) != (0, 0)]
    return [(0, 0)] + sorted(steps, key=lambda s: (abs(s[0] - n_z / 2), s[1], s[0]))


def chip_peer(n_seq, me, step, sign):
    n_z = n_seq // CORES
    offset = jnp.zeros_like(step)
    flip = jnp.zeros_like(step)
    for i, (dz, dc) in enumerate(exchange_steps(n_seq)):
        offset = jnp.where(step == i, dz, offset)
        flip = jnp.where(step == i, dc, flip)
    z = me // CORES + sign * offset
    z = jnp.where(z >= n_z, z - n_z, jnp.where(z < 0, z + n_z, z))
    return z * CORES + jnp.bitwise_xor(jnp.bitwise_and(me, 1), flip)


def per_device(
    qkv, resid, block_count, send_count, send_slot, lm_row, out_weight, out_bias, norm_gain
):
    width = resid.shape[2]
    row_total = send_slot.shape[1]
    n_seq = lax.axis_size("seq")
    n_enc = lax.axis_size("enc")
    slots = lm_row.shape[1]
    cap = slots // n_seq
    chunk = GROUP * cap
    sent = slots * GROUP
    vmem = pl.BlockSpec(memory_space=pltpu.VMEM)
    smem = pl.BlockSpec(memory_space=pltpu.SMEM)
    small = pltpu.CompilerParams(vmem_limit_bytes=16 << 20)

    def rows_of(count, columns=width):
        return jax.ShapeDtypeStruct((count, columns), jnp.bfloat16)

    encoded, lent, count = encode_all(block_count, qkv, resid, out_weight, out_bias, norm_gain)
    borrowed = lax.ppermute(lent, "enc", [((i - 1) % n_enc, i) for i in range(n_enc)])

    by_steps = chunk % 8 == 0 and n_seq % CORES == 0
    peer = functools.partial(chip_peer, n_seq) if by_steps else lambda me, step, sign: step
    me = lax.axis_index("seq").astype(jnp.int32).reshape(1, 1)
    packed, borrow, place = pl.pallas_call(
        functools.partial(own_kernel, n_seq, cap, peer),
        out_shape=(rows_of(sent), rows_of(sent, WIN), rows_of(GROUP * row_total, sent)),
        in_specs=[smem] * 3 + [vmem] * 3,
        out_specs=(vmem, vmem, vmem),
        compiler_params=small,
        cost_estimate=pl.CostEstimate(flops=2 * sent * row_total * GROUP * width, bytes_accessed=2 << 20, transcendentals=0),
    )(count, send_count, me, send_slot, lm_row, encoded)
    pieces = n_seq if by_steps else 1
    outgoing = pl.pallas_call(
        pack_kernel,
        out_shape=[rows_of(sent // pieces)] * pieces,
        in_specs=[vmem] * 3,
        out_specs=[vmem] * pieces,
        compiler_params=small,
    )(packed, borrow, borrowed)

    if by_steps:
        n_z = n_seq // CORES
        arrived = [outgoing[0]]
        for part, (dz, dc) in list(zip(outgoing, exchange_steps(n_seq)))[1:]:
            route = [(i, (i // CORES + dz) % n_z * CORES + (i + dc) % CORES) for i in range(n_seq)]
            arrived.append(lax.ppermute(part, "seq", route))
    else:
        arrived = [
            lax.all_to_all(
                outgoing[0].reshape(n_seq, chunk, width), "seq", split_axis=0, concat_axis=0, tiled=True
            ).reshape(sent, width)
        ]
    placed = pl.pallas_call(
        place_kernel,
        out_shape=rows_of(row_total, GROUP * width),
        in_specs=[vmem] * (1 + pieces),
        out_specs=pl.BlockSpec(memory_space=pltpu.HBM),
        scratch_shapes=[pltpu.VMEM((row_total, GROUP * width), jnp.bfloat16), pltpu.SemaphoreType.DMA((GROUP,))],
        compiler_params=small,
    )(place, *arrived)
    return placed[None]


def solution(mesh):
    placed = (
        P("enc", "seq", None),
        P("enc", "seq", None),
        P("enc", "seq"),
        P("enc", "seq"),
        P("enc", "seq"),
        P("enc", "seq"),
        P(),
        P(),
        P(),
    )
    return jax.shard_map(
        per_device, mesh=mesh, in_specs=placed, out_specs=P("enc", "seq", None), check_vma=False
    )
```

```python
import functools
import math

import jax
import jax.numpy as jnp
from jax import lax
from jax.experimental import pallas as pl
from jax.experimental.pallas import tpu as pltpu
from jax.sharding import PartitionSpec as P

HEADS = 16
WIN = 64
LANES = 128
GROUP = 4
EPS = 1e-6
CORES = 2

NT = (((1,), (1,)), ((), ()))


def dot32(a, b):
    return jnp.dot(a, b, preferred_element_type=jnp.float32)


def one_hot(match):
    return match.astype(jnp.float32).astype(jnp.bfloat16)


def attend(q, k, v, out_ref, row0, width):
    head = width // HEADS
    rate = 1.0 / math.sqrt(head)
    totals = [None] * (width // LANES)
    sums = [None] * (width // LANES)
    first_half = lax.broadcasted_iota(jnp.int32, (WIN, 2 * WIN), 1) < WIN
    for pair in range(HEADS // 2):
        start = 2 * pair * head
        lo = start // LANES * LANES
        hi = -(-(start + 2 * head) // LANES) * LANES
        column = lax.broadcasted_iota(jnp.int32, (2 * WIN, hi - lo), 1) + lo
        row = lax.broadcasted_iota(jnp.int32, (2 * WIN, hi - lo), 0)
        begin = jnp.where(row < WIN, start, start + head)
        mask = one_hot((column >= begin) & (column < begin + head))
        kw, vw = k(lo, hi), v(lo, hi)
        keys = jnp.concatenate([kw, kw], axis=0) * mask
        values = jnp.concatenate([vw, vw], axis=0) * mask
        scores = lax.dot_general(q(lo, hi), keys, NT, preferred_element_type=jnp.float32)
        top0 = jnp.max(jnp.where(first_half, scores, -jnp.inf), axis=1, keepdims=True)
        top1 = jnp.max(jnp.where(first_half, -jnp.inf, scores), axis=1, keepdims=True)
        raised = jnp.exp((scores - jnp.where(first_half, top0, top1)) * rate).astype(jnp.bfloat16)
        part = dot32(raised, values)
        norm = dot32(raised, mask)
        for tile in range(lo // LANES, hi // LANES):
            at = slice(tile * LANES - lo, (tile + 1) * LANES - lo)
            totals[tile] = part[:, at] if totals[tile] is None else totals[tile] + part[:, at]
            sums[tile] = norm[:, at] if sums[tile] is None else sums[tile] + norm[:, at]
    for tile in range(width // LANES):
        out_ref[row0 : row0 + WIN, tile * LANES : (tile + 1) * LANES] = (totals[tile] / sums[tile]).astype(
            jnp.bfloat16
        )


def attend_all(qkv, attended, width):
    for b in range(qkv.shape[0]):
        attend(
            lambda lo, hi, b=b: qkv[b, :, lo:hi],
            lambda lo, hi, b=b: qkv[b, :, width + lo : width + hi],
            lambda lo, hi, b=b: qkv[b, :, 2 * width + lo : 2 * width + hi],
            attended, b * WIN, width,
        )


def project(attended, resid, weight, bias, gain, hidden, out_ref):
    rows, width = hidden.shape
    step = 2 * LANES
    chunks = [slice(lo, lo + step) for lo in range(0, width, step)]
    squares = jnp.zeros((rows, 1), jnp.float32)
    for cols in chunks:
        h = dot32(attended[...], weight[:, cols])
        h = h + bias[cols].astype(jnp.float32).reshape(1, step)
        h = h + resid[:, :, cols].reshape(rows, step).astype(jnp.float32)
        hidden[:, cols] = h
        squares = squares + jnp.sum(h * h, axis=1, keepdims=True)
    scale = lax.rsqrt(squares * (1.0 / width) + EPS)
    for cols in chunks:
        out_ref[:, cols] = (hidden[:, cols] * scale * gain[cols].astype(jnp.float32).reshape(1, step)).astype(jnp.bfloat16)


def lent_kernel(
    count_ref, qkv_hbm, resid_hbm, weight_hbm, bias_hbm, gain_hbm, out_ref,
    qkv, resid, weight, attended, hidden, bias, gain, sems, weight_sems,
):
    width = resid.shape[2]
    at = pl.ds(count_ref[0, 0] - 1, 1)
    step = width // weight_sems.shape[0]
    chunks = [slice(lo, lo + step) for lo in range(0, width, step)]
    qkv_copy = pltpu.make_async_copy(qkv_hbm.at[at], qkv, sems.at[0])
    weight_copies = [
        pltpu.make_async_copy(weight_hbm.at[part], weight.at[part], weight_sems.at[i]) for i, part in enumerate(chunks)
    ]
    pairs = [(resid_hbm.at[at], resid), (bias_hbm, bias), (gain_hbm, gain)]
    other_copies = [pltpu.make_async_copy(a, b, sems.at[i + 1]) for i, (a, b) in enumerate(pairs)]
    for copy in [qkv_copy] + weight_copies[:-1] + other_copies + weight_copies[-1:]:
        copy.start()
    qkv_copy.wait()
    attend_all(qkv, attended, width)
    for copy, part in list(zip(weight_copies, chunks))[:-1]:
        copy.wait()
        for cols in chunks:
            h = dot32(attended[:, part], weight[part, cols])
            hidden[:, cols] = h if part.start == 0 else hidden[:, cols] + h
    for copy in other_copies:
        copy.wait()
    for cols in chunks:
        h = hidden[:, cols] + bias[cols].astype(jnp.float32).reshape(1, step)
        hidden[:, cols] = h + resid[0, :, cols].astype(jnp.float32)
    weight_copies[-1].wait()
    squares = jnp.zeros((WIN, 1), jnp.float32)
    for cols in chunks:
        h = hidden[:, cols] + dot32(attended[:, chunks[-1]], weight[chunks[-1], cols])
        hidden[:, cols] = h
        squares = squares + jnp.sum(h * h, axis=1, keepdims=True)
    scale = lax.rsqrt(squares * (1.0 / width) + EPS)
    for cols in chunks:
        out_ref[:, cols] = (hidden[:, cols] * scale * gain[cols].astype(jnp.float32).reshape(1, step)).astype(jnp.bfloat16)


def encode(qkv_hbm, resid_hbm, weight_hbm, bias_hbm, gain_hbm, out_ref, qkv, resid, weight, attended, hidden, bias, gain, sems):
    at = pl.ds(0, qkv.shape[0])
    pairs = [(qkv_hbm.at[at], qkv), (weight_hbm, weight), (resid_hbm.at[at], resid), (bias_hbm, bias), (gain_hbm, gain)]
    copies = [pltpu.make_async_copy(a, b, sems.at[i]) for i, (a, b) in enumerate(pairs)]
    for copy in copies:
        copy.start()
    copies[0].wait()
    attend_all(qkv, attended, resid.shape[2])
    for copy in copies[1:]:
        copy.wait()
    project(attended, resid, weight, bias, gain, hidden, out_ref)


def split_index(index, n_seq, cap):
    step = index // (GROUP * cap)
    rest = index - step * (GROUP * cap)
    patch = rest // cap
    return step, patch, rest - patch * cap


def own_kernel(
    n_seq, cap, peer, count_ref, send_ref, me_ref, slot_ref, row_ref,
    qkv_hbm, resid_hbm, weight_hbm, bias_hbm, gain_hbm,
    packed_ref, borrow_ref, place_ref, normed, *scratch,
):
    rows = normed.shape[0]
    slots = n_seq * cap
    sent = slots * GROUP
    tokens = rows // GROUP
    me = me_ref[0, 0]
    encode(qkv_hbm, resid_hbm, weight_hbm, bias_hbm, gain_hbm, normed, *scratch)

    step, patch, rank = split_index(lax.broadcasted_iota(jnp.int32, (sent, 1), 0), n_seq, cap)
    row_code = (peer(me, step, 1) * cap + rank) * GROUP + patch
    token = lax.broadcasted_iota(jnp.int32, (tokens, rows), 0)
    column = lax.broadcasted_iota(jnp.int32, (tokens, rows), 1)
    spread = one_hot((column >= token * GROUP) & (column < (token + 1) * GROUP))
    slot = jnp.broadcast_to(slot_ref[...].astype(jnp.float32), (16, tokens)).astype(jnp.bfloat16)
    slot = dot32(slot, spread)[:1].astype(jnp.int32)
    index = lax.broadcasted_iota(jnp.int32, (1, rows), 1)
    col_code = slot * GROUP + jnp.bitwise_and(index, GROUP - 1)
    kept = (count_ref[0, 0] - send_ref[0, 0]) * WIN
    last = rows - WIN
    own = one_hot(row_code == jnp.where(index < kept, col_code, -1))
    packed_ref[...] = dot32(own, normed[...]).astype(jnp.bfloat16)
    borrow_ref[...] = one_hot(row_code == jnp.where(kept > last, -1, col_code[:, last:]))

    step, patch, rank = split_index(lax.broadcasted_iota(jnp.int32, (1, sent), 1), n_seq, cap)
    arrive = peer(me, step, -1) * cap + rank
    pick = one_hot(lax.broadcasted_iota(jnp.int32, (slots, sent), 0) == arrive)
    target = jnp.broadcast_to(row_ref[...].astype(jnp.float32), (16, slots)).astype(jnp.bfloat16)
    target = dot32(target, pick)[:1].astype(jnp.int32)
    out_row = lax.broadcasted_iota(jnp.int32, (tokens, sent), 0)
    for j in range(GROUP):
        place_ref[j * tokens : (j + 1) * tokens, :] = one_hot((target == out_row) & (patch == j))


def in_hbm(*arrays):
    return [pltpu.with_memory_space_constraint(a, pltpu.HBM) for a in arrays]


def encode_call(kernel, blocks, scalars, slots, qkv, resid, weight, bias, gain, out_shape, before=(), after=()):
    width = resid.shape[2]
    rows = blocks * WIN
    vmem = pl.BlockSpec(memory_space=pltpu.VMEM)
    smem = pl.BlockSpec(memory_space=pltpu.SMEM)
    hbm = pl.BlockSpec(memory_space=pltpu.HBM)
    return pl.pallas_call(
        kernel,
        out_shape=out_shape,
        in_specs=[smem] * len(scalars) + [vmem] * len(slots) + [hbm] * 5,
        out_specs=jax.tree.map(lambda _: vmem, out_shape),
        scratch_shapes=[
            *before,
            pltpu.VMEM((blocks, WIN, 3 * width), jnp.bfloat16),
            pltpu.VMEM((blocks, WIN, width), jnp.bfloat16),
            pltpu.VMEM((width, width), jnp.bfloat16),
            pltpu.VMEM((rows, width), jnp.bfloat16),
            pltpu.VMEM((rows, width), jnp.float32),
            pltpu.VMEM((width,), jnp.bfloat16),
            pltpu.VMEM((width,), jnp.bfloat16),
            pltpu.SemaphoreType.DMA((5,)),
            *after,
        ],
        compiler_params=pltpu.CompilerParams(vmem_limit_bytes=24 << 20),
        cost_estimate=pl.CostEstimate(
            flops=2 * rows * width * width + 8 * rows * WIN * width,
            bytes_accessed=2 * (width * width + 5 * rows * width),
            transcendentals=rows * WIN * HEADS,
        ),
    )(*scalars, *slots, *in_hbm(qkv, resid, weight, bias, gain))


def pack_kernel(packed_ref, borrow_ref, borrowed_ref, *out_refs):
    total = packed_ref[...].astype(jnp.float32) + dot32(borrow_ref[...], borrowed_ref[...])
    chunk = out_refs[0].shape[0]
    for step, out_ref in enumerate(out_refs):
        out_ref[...] = total[step * chunk : (step + 1) * chunk].astype(jnp.bfloat16)


def place_kernel(place_ref, *refs):
    *in_refs, out_hbm, out, sems = refs
    tokens = out.shape[0]
    chunks = [ref[...].astype(jnp.float32) for ref in in_refs]
    arrived = chunks[0] if len(chunks) == 1 else jnp.concatenate(chunks, axis=0)
    arrived = arrived.astype(jnp.bfloat16)
    width = arrived.shape[1]
    copies = []
    for j in range(GROUP):
        cols = slice(j * width, (j + 1) * width)
        out[:, cols] = dot32(place_ref[j * tokens : (j + 1) * tokens, :], arrived).astype(jnp.bfloat16)
        copies.append(pltpu.make_async_copy(out.at[:, cols], out_hbm.at[:, cols], sems.at[j]))
        copies[-1].start()
    for copy in copies:
        copy.wait()


def exchange_steps(n_seq):
    n_z = n_seq // CORES
    steps = [(dz, dc) for dz in range(n_z) for dc in range(CORES) if (dz, dc) != (0, 0)]
    return [(0, 0)] + sorted(steps, key=lambda s: (abs(s[0] - n_z / 2), s[1], s[0]))


def chip_peer(n_seq, me, step, sign):
    n_z = n_seq // CORES
    offset = jnp.zeros_like(step)
    flip = jnp.zeros_like(step)
    for i, (dz, dc) in enumerate(exchange_steps(n_seq)):
        offset = jnp.where(step == i, dz, offset)
        flip = jnp.where(step == i, dc, flip)
    z = me // CORES + sign * offset
    z = jnp.where(z >= n_z, z - n_z, jnp.where(z < 0, z + n_z, z))
    return z * CORES + jnp.bitwise_xor(jnp.bitwise_and(me, 1), flip)


def per_device(
    qkv, resid, block_count, send_count, send_slot, lm_row, out_weight, out_bias, norm_gain
):
    width = resid.shape[2]
    row_total = send_slot.shape[1]
    tokens = WIN // GROUP
    blocks = row_total // tokens
    n_seq = lax.axis_size("seq")
    n_enc = lax.axis_size("enc")
    slots = lm_row.shape[1]
    cap = slots // n_seq
    chunk = GROUP * cap
    sent = slots * GROUP
    vmem = pl.BlockSpec(memory_space=pltpu.VMEM)
    small = pltpu.CompilerParams(vmem_limit_bytes=16 << 20)

    def rows_of(count, columns=width):
        return jax.ShapeDtypeStruct((count, columns), jnp.bfloat16)

    data = (qkv, resid, out_weight, out_bias, norm_gain)
    weight_parts = [pltpu.SemaphoreType.DMA((width // (2 * LANES),))]
    lent = encode_call(lent_kernel, 1, [block_count], [], *data, rows_of(WIN), after=weight_parts)
    borrowed = lax.ppermute(lent, "enc", [((i - 1) % n_enc, i) for i in range(n_enc)])

    by_steps = chunk % 8 == 0 and n_seq % CORES == 0
    peer = functools.partial(chip_peer, n_seq) if by_steps else lambda me, step, sign: step
    me = lax.axis_index("seq").astype(jnp.int32).reshape(1, 1)
    packed, borrow, place = encode_call(
        functools.partial(own_kernel, n_seq, cap, peer), blocks,
        [block_count, send_count, me], [send_slot, lm_row], *data,
        (rows_of(sent), rows_of(sent, WIN), rows_of(GROUP * row_total, sent)),
        [pltpu.VMEM((row_total * GROUP, width), jnp.bfloat16)],
    )
    pieces = n_seq if by_steps else 1
    outgoing = pl.pallas_call(
        pack_kernel,
        out_shape=[rows_of(sent // pieces)] * pieces,
        in_specs=[vmem] * 3,
        out_specs=[vmem] * pieces,
        compiler_params=small,
    )(packed, borrow, borrowed)

    if by_steps:
        n_z = n_seq // CORES
        arrived = [outgoing[0]]
        for part, (dz, dc) in list(zip(outgoing, exchange_steps(n_seq)))[1:]:
            route = [(i, (i // CORES + dz) % n_z * CORES + (i + dc) % CORES) for i in range(n_seq)]
            arrived.append(lax.ppermute(part, "seq", route))
    else:
        arrived = [
            lax.all_to_all(
                outgoing[0].reshape(n_seq, chunk, width), "seq", split_axis=0, concat_axis=0, tiled=True
            ).reshape(sent, width)
        ]
    placed = pl.pallas_call(
        place_kernel,
        out_shape=rows_of(row_total, GROUP * width),
        in_specs=[vmem] * (1 + pieces),
        out_specs=pl.BlockSpec(memory_space=pltpu.HBM),
        scratch_shapes=[pltpu.VMEM((row_total, GROUP * width), jnp.bfloat16), pltpu.SemaphoreType.DMA((GROUP,))],
        compiler_params=small,
    )(place, *arrived)
    return placed[None]


def solution(mesh):
    placed = (
        P("enc", "seq", None),
        P("enc", "seq", None),
        P("enc", "seq"),
        P("enc", "seq"),
        P("enc", "seq"),
        P("enc", "seq"),
        P(),
        P(),
        P(),
    )
    return jax.shard_map(
        per_device, mesh=mesh, in_specs=placed, out_specs=P("enc", "seq", None), check_vma=False
    )
```

```python
import functools
import math

import jax
import jax.numpy as jnp
from jax import lax
from jax.experimental import pallas as pl
from jax.experimental.pallas import tpu as pltpu
from jax.sharding import PartitionSpec as P

HEADS = 16
WIN = 64
LANES = 128
GROUP = 4
EPS = 1e-6
CORES = 2

NT = (((1,), (1,)), ((), ()))


def dot32(a, b):
    return jnp.dot(a, b, preferred_element_type=jnp.float32)


def one_hot(match):
    return match.astype(jnp.float32).astype(jnp.bfloat16)


def head_pairs(width):
    head = width // HEADS
    spans = []
    for start in range(0, width, 2 * head):
        lo = start // LANES * LANES
        spans.append((start, lo, -(-(start + 2 * head) // LANES) * LANES))
    return spans


def mask_period(width):
    return LANES // math.gcd(LANES, 2 * (width // HEADS))


def mask_scratch(width):
    return pltpu.VMEM((mask_period(width), 2 * WIN, 2 * LANES), jnp.bfloat16)


def make_masks(masks, width):
    head = width // HEADS
    for i in range(masks.shape[0]):
        start, lo, hi = head_pairs(width)[i]
        column = lax.broadcasted_iota(jnp.int32, masks.shape[1:], 1) + lo
        row = lax.broadcasted_iota(jnp.int32, masks.shape[1:], 0)
        begin = jnp.where(row < WIN, start, start + head)
        masks[i] = one_hot((column >= begin) & (column < begin + head))


def attend(qkv, b, masks, out_ref, width):
    rate = math.log2(math.e) / math.sqrt(width // HEADS)
    totals = [None] * (width // LANES)
    first = lax.broadcasted_iota(jnp.int32, (WIN, 2 * WIN), 1) < WIN
    for pair, (_, lo, hi) in enumerate(head_pairs(width)):
        mask = masks[pair % masks.shape[0]]
        kw = qkv[b, :, width + lo : width + hi]
        vw = qkv[b, :, 2 * width + lo : 2 * width + hi]
        keys = jnp.concatenate([kw, kw], axis=0) * mask
        values = jnp.concatenate([vw, vw], axis=0) * mask
        scores = lax.dot_general(qkv[b, :, lo:hi], keys, NT, preferred_element_type=jnp.float32)
        top0 = jnp.max(jnp.where(first, scores, -jnp.inf), axis=1, keepdims=True)
        top1 = jnp.max(jnp.where(first, -jnp.inf, scores), axis=1, keepdims=True)
        raised = jnp.exp2((scores - jnp.where(first, top0, top1)) * rate)
        sum0 = jnp.sum(jnp.where(first, raised, 0.0), axis=1, keepdims=True)
        sum1 = jnp.sum(jnp.where(first, 0.0, raised), axis=1, keepdims=True)
        probs = (raised * jnp.where(first, 1.0 / sum0, 1.0 / sum1)).astype(jnp.bfloat16)
        part = dot32(probs, values)
        for tile in range(lo // LANES, hi // LANES):
            piece = part[:, tile * LANES - lo : (tile + 1) * LANES - lo]
            totals[tile] = piece if totals[tile] is None else totals[tile] + piece
    for tile, total in enumerate(totals):
        out_ref[b * WIN : (b + 1) * WIN, tile * LANES : (tile + 1) * LANES] = total.astype(jnp.bfloat16)


def project(attended, resid, weight, bias, gain, hidden, out_ref):
    rows, width = hidden.shape
    step = 2 * LANES
    chunks = [slice(lo, lo + step) for lo in range(0, width, step)]
    squares = jnp.zeros((rows, 1), jnp.float32)
    for cols in chunks:
        h = dot32(attended[...], weight[:, cols])
        h = h + bias[cols].astype(jnp.float32).reshape(1, step)
        h = h + resid[:, :, cols].reshape(rows, step).astype(jnp.float32)
        hidden[:, cols] = h
        squares = squares + jnp.sum(h * h, axis=1, keepdims=True)
    scale = lax.rsqrt(squares * (1.0 / width) + EPS)
    for cols in chunks:
        out_ref[:, cols] = (hidden[:, cols] * scale * gain[cols].astype(jnp.float32).reshape(1, step)).astype(jnp.bfloat16)


def lent_kernel(
    count_ref, qkv_hbm, resid_hbm, weight_hbm, bias_hbm, gain_hbm, out_ref,
    qkv, resid, weight, attended, hidden, bias, gain, masks, sems, weight_sems,
):
    width = resid.shape[2]
    at = pl.ds(count_ref[0, 0] - 1, 1)
    step = 2 * LANES
    chunks = [slice(lo, lo + step) for lo in range(0, width, step)]
    parts = [slice(lo, min(lo + 2 * step, width)) for lo in range(0, width, 2 * step)]
    qkv_copy = pltpu.make_async_copy(qkv_hbm.at[at], qkv, sems.at[0])
    weight_copies = [
        pltpu.make_async_copy(weight_hbm.at[part], weight.at[part], weight_sems.at[i]) for i, part in enumerate(parts)
    ]
    pairs = [(resid_hbm.at[at], resid), (bias_hbm, bias), (gain_hbm, gain)]
    other_copies = [pltpu.make_async_copy(a, b, sems.at[i + 1]) for i, (a, b) in enumerate(pairs)]
    for copy in [qkv_copy] + weight_copies[:-1] + other_copies + weight_copies[-1:]:
        copy.start()
    make_masks(masks, width)
    qkv_copy.wait()
    attend(qkv, 0, masks, attended, width)
    for copy, part in list(zip(weight_copies, parts))[:-1]:
        copy.wait()
        for cols in chunks:
            h = dot32(attended[:, part], weight[part, cols])
            hidden[:, cols] = h if part.start == 0 else hidden[:, cols] + h
    for copy in other_copies:
        copy.wait()
    for cols in chunks:
        h = hidden[:, cols] + bias[cols].astype(jnp.float32).reshape(1, step)
        hidden[:, cols] = h + resid[0, :, cols].astype(jnp.float32)
    weight_copies[-1].wait()
    squares = jnp.zeros((WIN, 1), jnp.float32)
    for cols in chunks:
        h = hidden[:, cols] + dot32(attended[:, parts[-1]], weight[parts[-1], cols])
        hidden[:, cols] = h
        squares = squares + jnp.sum(h * h, axis=1, keepdims=True)
    scale = lax.rsqrt(squares * (1.0 / width) + EPS)
    for cols in chunks:
        out_ref[:, cols] = (hidden[:, cols] * scale * gain[cols].astype(jnp.float32).reshape(1, step)).astype(jnp.bfloat16)


def encode(qkv_hbm, resid_hbm, weight_hbm, bias_hbm, gain_hbm, out_ref, qkv, resid, weight, attended, hidden, bias, gain, masks, sems):
    at = pl.ds(0, qkv.shape[0])
    pairs = [(qkv_hbm.at[at], qkv), (weight_hbm, weight), (resid_hbm.at[at], resid), (bias_hbm, bias), (gain_hbm, gain)]
    copies = [pltpu.make_async_copy(a, b, sems.at[i]) for i, (a, b) in enumerate(pairs)]
    for copy in copies:
        copy.start()
    width = resid.shape[2]
    make_masks(masks, width)
    copies[0].wait()
    for b in range(qkv.shape[0]):
        attend(qkv, b, masks, attended, width)
    for copy in copies[1:]:
        copy.wait()
    project(attended, resid, weight, bias, gain, hidden, out_ref)


def split_index(index, n_seq, cap):
    step = index // (GROUP * cap)
    rest = index - step * (GROUP * cap)
    patch = rest // cap
    return step, patch, rest - patch * cap


def own_kernel(
    n_seq, cap, peer, count_ref, send_ref, me_ref, slot_ref, row_ref,
    qkv_hbm, resid_hbm, weight_hbm, bias_hbm, gain_hbm,
    packed_ref, borrow_ref, place_ref, normed, *scratch,
):
    rows = normed.shape[0]
    slots = n_seq * cap
    sent = slots * GROUP
    tokens = rows // GROUP
    me = me_ref[0, 0]
    encode(qkv_hbm, resid_hbm, weight_hbm, bias_hbm, gain_hbm, normed, *scratch)

    step, patch, rank = split_index(lax.broadcasted_iota(jnp.int32, (sent, 1), 0), n_seq, cap)
    row_code = (peer(me, step, 1) * cap + rank) * GROUP + patch
    token = lax.broadcasted_iota(jnp.int32, (tokens, rows), 0)
    column = lax.broadcasted_iota(jnp.int32, (tokens, rows), 1)
    spread = one_hot((column >= token * GROUP) & (column < (token + 1) * GROUP))
    slot = jnp.broadcast_to(slot_ref[...].astype(jnp.float32), (16, tokens)).astype(jnp.bfloat16)
    slot = dot32(slot, spread)[:1].astype(jnp.int32)
    index = lax.broadcasted_iota(jnp.int32, (1, rows), 1)
    col_code = slot * GROUP + jnp.bitwise_and(index, GROUP - 1)
    kept = (count_ref[0, 0] - send_ref[0, 0]) * WIN
    last = rows - WIN
    own = one_hot(row_code == jnp.where(index < kept, col_code, -1))
    packed_ref[...] = dot32(own, normed[...]).astype(jnp.bfloat16)
    borrow_ref[...] = one_hot(row_code == jnp.where(kept > last, -1, col_code[:, last:]))

    step, patch, rank = split_index(lax.broadcasted_iota(jnp.int32, (1, sent), 1), n_seq, cap)
    arrive = peer(me, step, -1) * cap + rank
    pick = one_hot(lax.broadcasted_iota(jnp.int32, (slots, sent), 0) == arrive)
    target = jnp.broadcast_to(row_ref[...].astype(jnp.float32), (16, slots)).astype(jnp.bfloat16)
    target = dot32(target, pick)[:1].astype(jnp.int32)
    out_row = lax.broadcasted_iota(jnp.int32, (tokens, sent), 0)
    for j in range(GROUP):
        place_ref[j * tokens : (j + 1) * tokens, :] = one_hot((target == out_row) & (patch == j))


def in_hbm(*arrays):
    return [pltpu.with_memory_space_constraint(a, pltpu.HBM) for a in arrays]


def encode_call(kernel, blocks, scalars, slots, qkv, resid, weight, bias, gain, out_shape, before=(), after=()):
    width = resid.shape[2]
    rows = blocks * WIN
    vmem = pl.BlockSpec(memory_space=pltpu.VMEM)
    smem = pl.BlockSpec(memory_space=pltpu.SMEM)
    hbm = pl.BlockSpec(memory_space=pltpu.HBM)
    return pl.pallas_call(
        kernel,
        out_shape=out_shape,
        in_specs=[smem] * len(scalars) + [vmem] * len(slots) + [hbm] * 5,
        out_specs=jax.tree.map(lambda _: vmem, out_shape),
        scratch_shapes=[
            *before,
            pltpu.VMEM((blocks, WIN, 3 * width), jnp.bfloat16),
            pltpu.VMEM((blocks, WIN, width), jnp.bfloat16),
            pltpu.VMEM((width, width), jnp.bfloat16),
            pltpu.VMEM((rows, width), jnp.bfloat16),
            pltpu.VMEM((rows, width), jnp.float32),
            pltpu.VMEM((width,), jnp.bfloat16),
            pltpu.VMEM((width,), jnp.bfloat16),
            mask_scratch(width),
            pltpu.SemaphoreType.DMA((5,)),
            *after,
        ],
        compiler_params=pltpu.CompilerParams(vmem_limit_bytes=24 << 20),
        cost_estimate=pl.CostEstimate(
            flops=2 * rows * width * width + 8 * rows * WIN * width,
            bytes_accessed=2 * (width * width + 5 * rows * width),
            transcendentals=rows * WIN * HEADS,
        ),
    )(*scalars, *slots, *in_hbm(qkv, resid, weight, bias, gain))


def pack_kernel(packed_ref, borrow_ref, borrowed_ref, *out_refs):
    total = packed_ref[...].astype(jnp.float32) + dot32(borrow_ref[...], borrowed_ref[...])
    chunk = out_refs[0].shape[0]
    for step, out_ref in enumerate(out_refs):
        out_ref[...] = total[step * chunk : (step + 1) * chunk].astype(jnp.bfloat16)


def place_kernel(place_ref, *refs):
    *in_refs, out_hbm, out, sems = refs
    tokens = out.shape[0]
    chunks = [ref[...].astype(jnp.float32) for ref in in_refs]
    arrived = chunks[0] if len(chunks) == 1 else jnp.concatenate(chunks, axis=0)
    arrived = arrived.astype(jnp.bfloat16)
    width = arrived.shape[1]
    copies = []
    for j in range(GROUP):
        cols = slice(j * width, (j + 1) * width)
        out[:, cols] = dot32(place_ref[j * tokens : (j + 1) * tokens, :], arrived).astype(jnp.bfloat16)
        copies.append(pltpu.make_async_copy(out.at[:, cols], out_hbm.at[:, cols], sems.at[j]))
        copies[-1].start()
    for copy in copies:
        copy.wait()


def exchange_steps(n_seq):
    n_z = n_seq // CORES
    steps = [(dz, dc) for dz in range(n_z) for dc in range(CORES) if (dz, dc) != (0, 0)]
    return [(0, 0)] + sorted(steps, key=lambda s: (abs(s[0] - n_z / 2), s[1], s[0]))


def chip_peer(n_seq, me, step, sign):
    n_z = n_seq // CORES
    offset = jnp.zeros_like(step)
    flip = jnp.zeros_like(step)
    for i, (dz, dc) in enumerate(exchange_steps(n_seq)):
        offset = jnp.where(step == i, dz, offset)
        flip = jnp.where(step == i, dc, flip)
    z = me // CORES + sign * offset
    z = jnp.where(z >= n_z, z - n_z, jnp.where(z < 0, z + n_z, z))
    return z * CORES + jnp.bitwise_xor(jnp.bitwise_and(me, 1), flip)


def per_device(
    qkv, resid, block_count, send_count, send_slot, lm_row, out_weight, out_bias, norm_gain
):
    width = resid.shape[2]
    row_total = send_slot.shape[1]
    tokens = WIN // GROUP
    blocks = row_total // tokens
    n_seq = lax.axis_size("seq")
    n_enc = lax.axis_size("enc")
    slots = lm_row.shape[1]
    cap = slots // n_seq
    chunk = GROUP * cap
    sent = slots * GROUP
    vmem = pl.BlockSpec(memory_space=pltpu.VMEM)
    small = pltpu.CompilerParams(vmem_limit_bytes=16 << 20)

    def rows_of(count, columns=width):
        return jax.ShapeDtypeStruct((count, columns), jnp.bfloat16)

    data = (qkv, resid, out_weight, out_bias, norm_gain)
    weight_parts = [pltpu.SemaphoreType.DMA((-(-width // (4 * LANES)),))]
    lent = encode_call(lent_kernel, 1, [block_count], [], *data, rows_of(WIN), after=weight_parts)
    borrowed = lax.ppermute(lent, "enc", [((i - 1) % n_enc, i) for i in range(n_enc)])

    by_steps = chunk % 8 == 0 and n_seq % CORES == 0
    peer = functools.partial(chip_peer, n_seq) if by_steps else lambda me, step, sign: step
    me = lax.axis_index("seq").astype(jnp.int32).reshape(1, 1)
    packed, borrow, place = encode_call(
        functools.partial(own_kernel, n_seq, cap, peer), blocks,
        [block_count, send_count, me], [send_slot, lm_row], *data,
        (rows_of(sent), rows_of(sent, WIN), rows_of(GROUP * row_total, sent)),
        [pltpu.VMEM((row_total * GROUP, width), jnp.bfloat16)],
    )
    pieces = n_seq if by_steps else 1
    outgoing = pl.pallas_call(
        pack_kernel,
        out_shape=[rows_of(sent // pieces)] * pieces,
        in_specs=[vmem] * 3,
        out_specs=[vmem] * pieces,
        compiler_params=small,
    )(packed, borrow, borrowed)

    if by_steps:
        n_z = n_seq // CORES
        arrived = [outgoing[0]]
        for part, (dz, dc) in list(zip(outgoing, exchange_steps(n_seq)))[1:]:
            route = [(i, (i // CORES + dz) % n_z * CORES + (i + dc) % CORES) for i in range(n_seq)]
            arrived.append(lax.ppermute(part, "seq", route))
    else:
        arrived = [
            lax.all_to_all(
                outgoing[0].reshape(n_seq, chunk, width), "seq", split_axis=0, concat_axis=0, tiled=True
            ).reshape(sent, width)
        ]
    placed = pl.pallas_call(
        place_kernel,
        out_shape=rows_of(row_total, GROUP * width),
        in_specs=[vmem] * (1 + pieces),
        out_specs=pl.BlockSpec(memory_space=pltpu.HBM),
        scratch_shapes=[pltpu.VMEM((row_total, GROUP * width), jnp.bfloat16), pltpu.SemaphoreType.DMA((GROUP,))],
        compiler_params=small,
    )(place, *arrived)
    return placed[None]


def solution(mesh):
    placed = (
        P("enc", "seq", None),
        P("enc", "seq", None),
        P("enc", "seq"),
        P("enc", "seq"),
        P("enc", "seq"),
        P("enc", "seq"),
        P(),
        P(),
        P(),
    )
    return jax.shard_map(
        per_device, mesh=mesh, in_specs=placed, out_specs=P("enc", "seq", None), check_vma=False
    )
```

```python
import functools
import math

import jax
import jax.numpy as jnp
from jax import lax
from jax.experimental import pallas as pl
from jax.experimental.pallas import tpu as pltpu
from jax.sharding import PartitionSpec as P

HEADS = 16
WIN = 64
LANES = 128
GROUP = 4
EPS = 1e-6
CORES = 2

NT = (((1,), (1,)), ((), ()))


def dot32(a, b):
    return jnp.dot(a, b, preferred_element_type=jnp.float32)


def one_hot(match):
    return match.astype(jnp.float32).astype(jnp.bfloat16)


def attend(q, k, v, out_ref, row0, width):
    head = width // HEADS
    rate = 1.0 / math.sqrt(head)
    totals = [None] * (width // LANES)
    sums = [None] * (width // LANES)
    first_half = lax.broadcasted_iota(jnp.int32, (WIN, 2 * WIN), 1) < WIN
    for pair in range(HEADS // 2):
        start = 2 * pair * head
        lo = start // LANES * LANES
        hi = -(-(start + 2 * head) // LANES) * LANES
        column = lax.broadcasted_iota(jnp.int32, (2 * WIN, hi - lo), 1) + lo
        row = lax.broadcasted_iota(jnp.int32, (2 * WIN, hi - lo), 0)
        begin = jnp.where(row < WIN, start, start + head)
        mask = one_hot((column >= begin) & (column < begin + head))
        kw, vw = k(lo, hi), v(lo, hi)
        keys = jnp.concatenate([kw, kw], axis=0) * mask
        values = jnp.concatenate([vw, vw], axis=0) * mask
        scores = lax.dot_general(q(lo, hi), keys, NT, preferred_element_type=jnp.float32)
        top0 = jnp.max(jnp.where(first_half, scores, -jnp.inf), axis=1, keepdims=True)
        top1 = jnp.max(jnp.where(first_half, -jnp.inf, scores), axis=1, keepdims=True)
        raised = jnp.exp((scores - jnp.where(first_half, top0, top1)) * rate).astype(jnp.bfloat16)
        part = dot32(raised, values)
        norm = dot32(raised, mask)
        for tile in range(lo // LANES, hi // LANES):
            at = slice(tile * LANES - lo, (tile + 1) * LANES - lo)
            totals[tile] = part[:, at] if totals[tile] is None else totals[tile] + part[:, at]
            sums[tile] = norm[:, at] if sums[tile] is None else sums[tile] + norm[:, at]
    for tile in range(width // LANES):
        out_ref[row0 : row0 + WIN, tile * LANES : (tile + 1) * LANES] = (totals[tile] / sums[tile]).astype(
            jnp.bfloat16
        )


def encode(
    slot, qkv_hbm, resid_hbm, weight_hbm, bias_hbm, gain_hbm, out_ref,
    qkv, resid, weight, attended, hidden, bias_ref, gain_ref, sems,
):
    blocks = qkv.shape[0]
    width = resid.shape[2]
    at = pl.ds(slot, blocks)
    pairs = [
        (qkv_hbm.at[at], qkv), (weight_hbm, weight), (resid_hbm.at[at], resid), (bias_hbm, bias_ref), (gain_hbm, gain_ref)
    ]
    copies = [pltpu.make_async_copy(a, b, sems.at[i]) for i, (a, b) in enumerate(pairs)]
    for copy in copies:
        copy.start()
    copies[0].wait()
    for b in range(blocks):
        attend(
            lambda lo, hi, b=b: qkv[b, :, lo:hi],
            lambda lo, hi, b=b: qkv[b, :, width + lo : width + hi],
            lambda lo, hi, b=b: qkv[b, :, 2 * width + lo : 2 * width + hi],
            attended, b * WIN, width,
        )
    for copy in copies[1:]:
        copy.wait()
    rows = blocks * WIN
    squares = jnp.zeros((rows, 1), jnp.float32)
    step = 2 * LANES
    for lo in range(0, width, step):
        cols = slice(lo, lo + step)
        h = dot32(attended[...], weight[:, cols])
        h = h + bias_ref[cols].astype(jnp.float32).reshape(1, step)
        h = h + resid[:, :, cols].reshape(rows, step).astype(jnp.float32)
        hidden[:, cols] = h
        squares = squares + jnp.sum(h * h, axis=1, keepdims=True)
    scale = lax.rsqrt(squares * (1.0 / width) + EPS)
    for lo in range(0, width, step):
        cols = slice(lo, lo + step)
        gain = gain_ref[cols].astype(jnp.float32).reshape(1, step)
        out_ref[:, cols] = (hidden[:, cols] * scale * gain).astype(jnp.bfloat16)


def lent_kernel(count_ref, qkv_hbm, resid_hbm, weight_hbm, bias_hbm, gain_hbm, out_ref, *scratch):
    encode(count_ref[0, 0] - 1, qkv_hbm, resid_hbm, weight_hbm, bias_hbm, gain_hbm, out_ref, *scratch)


def split_index(index, n_seq, cap):
    step = index // (GROUP * cap)
    rest = index - step * (GROUP * cap)
    patch = rest // cap
    return step, patch, rest - patch * cap


def own_kernel(
    n_seq, cap, peer, count_ref, send_ref, me_ref, slot_ref, row_ref,
    qkv_hbm, resid_hbm, weight_hbm, bias_hbm, gain_hbm,
    packed_ref, borrow_ref, place_ref, normed, *scratch,
):
    rows = normed.shape[0]
    slots = n_seq * cap
    sent = slots * GROUP
    tokens = rows // GROUP
    me = me_ref[0, 0]
    encode(0, qkv_hbm, resid_hbm, weight_hbm, bias_hbm, gain_hbm, normed, *scratch)

    step, patch, rank = split_index(lax.broadcasted_iota(jnp.int32, (sent, 1), 0), n_seq, cap)
    row_code = (peer(me, step, 1) * cap + rank) * GROUP + patch
    token = lax.broadcasted_iota(jnp.int32, (tokens, rows), 0)
    column = lax.broadcasted_iota(jnp.int32, (tokens, rows), 1)
    spread = one_hot((column >= token * GROUP) & (column < (token + 1) * GROUP))
    slot = jnp.broadcast_to(slot_ref[...].astype(jnp.float32), (16, tokens)).astype(jnp.bfloat16)
    slot = dot32(slot, spread)[:1].astype(jnp.int32)
    index = lax.broadcasted_iota(jnp.int32, (1, rows), 1)
    col_code = slot * GROUP + jnp.bitwise_and(index, GROUP - 1)
    kept = (count_ref[0, 0] - send_ref[0, 0]) * WIN
    last = rows - WIN
    own = one_hot(row_code == jnp.where(index < kept, col_code, -1))
    packed_ref[...] = dot32(own, normed[...]).astype(jnp.bfloat16)
    borrow_ref[...] = one_hot(row_code == jnp.where(kept > last, -1, col_code[:, last:]))

    step, patch, rank = split_index(lax.broadcasted_iota(jnp.int32, (1, sent), 1), n_seq, cap)
    arrive = peer(me, step, -1) * cap + rank
    pick = one_hot(lax.broadcasted_iota(jnp.int32, (slots, sent), 0) == arrive)
    target = jnp.broadcast_to(row_ref[...].astype(jnp.float32), (16, slots)).astype(jnp.bfloat16)
    target = dot32(target, pick)[:1].astype(jnp.int32)
    out_row = lax.broadcasted_iota(jnp.int32, (tokens, sent), 0)
    for j in range(GROUP):
        place_ref[j * tokens : (j + 1) * tokens, :] = one_hot((target == out_row) & (patch == j))


def encode_call(kernel, blocks, scalars, slots, qkv, resid, weight, bias, gain, out_shape, extra):
    width = resid.shape[2]
    rows = blocks * WIN
    vmem = pl.BlockSpec(memory_space=pltpu.VMEM)
    smem = pl.BlockSpec(memory_space=pltpu.SMEM)
    hbm = pl.BlockSpec(memory_space=pltpu.HBM)
    return pl.pallas_call(
        kernel,
        out_shape=out_shape,
        in_specs=[smem] * len(scalars) + [vmem] * len(slots) + [hbm] * 5,
        out_specs=jax.tree.map(lambda _: vmem, out_shape),
        scratch_shapes=extra
        + [
            pltpu.VMEM((blocks, WIN, 3 * width), jnp.bfloat16),
            pltpu.VMEM((blocks, WIN, width), jnp.bfloat16),
            pltpu.VMEM((width, width), jnp.bfloat16),
            pltpu.VMEM((rows, width), jnp.bfloat16),
            pltpu.VMEM((rows, width), jnp.float32),
            pltpu.VMEM((width,), jnp.bfloat16),
            pltpu.VMEM((width,), jnp.bfloat16),
            pltpu.SemaphoreType.DMA((5,)),
        ],
        compiler_params=pltpu.CompilerParams(vmem_limit_bytes=24 << 20),
        cost_estimate=pl.CostEstimate(
            flops=2 * rows * width * width + 8 * rows * WIN * width,
            bytes_accessed=2 * (width * width + 5 * rows * width),
            transcendentals=rows * WIN * HEADS,
        ),
    )(*scalars, *slots, *(pltpu.with_memory_space_constraint(a, pltpu.HBM) for a in (qkv, resid, weight, bias, gain)))


def pack_kernel(packed_ref, borrow_ref, borrowed_ref, *out_refs):
    total = packed_ref[...].astype(jnp.float32) + dot32(borrow_ref[...], borrowed_ref[...])
    chunk = out_refs[0].shape[0]
    for step, out_ref in enumerate(out_refs):
        out_ref[...] = total[step * chunk : (step + 1) * chunk].astype(jnp.bfloat16)


def place_kernel(place_ref, *refs):
    *in_refs, out_hbm, out, sems = refs
    tokens = out.shape[0]
    chunks = [ref[...].astype(jnp.float32) for ref in in_refs]
    arrived = chunks[0] if len(chunks) == 1 else jnp.concatenate(chunks, axis=0)
    arrived = arrived.astype(jnp.bfloat16)
    width = arrived.shape[1]
    copies = []
    for j in range(GROUP):
        cols = slice(j * width, (j + 1) * width)
        out[:, cols] = dot32(place_ref[j * tokens : (j + 1) * tokens, :], arrived).astype(jnp.bfloat16)
        copies.append(pltpu.make_async_copy(out.at[:, cols], out_hbm.at[:, cols], sems.at[j]))
        copies[-1].start()
    for copy in copies:
        copy.wait()


def exchange_steps(n_seq):
    n_z = n_seq // CORES
    steps = [(dz, dc) for dz in range(n_z) for dc in range(CORES) if (dz, dc) != (0, 0)]
    return [(0, 0)] + sorted(steps, key=lambda s: (s != (1, 0), abs(s[0] - n_z / 2), s[1], s[0]))


def chip_peer(n_seq, me, step, sign):
    n_z = n_seq // CORES
    offset = jnp.zeros_like(step)
    flip = jnp.zeros_like(step)
    for i, (dz, dc) in enumerate(exchange_steps(n_seq)):
        offset = jnp.where(step == i, dz, offset)
        flip = jnp.where(step == i, dc, flip)
    z = me // CORES + sign * offset
    z = jnp.where(z >= n_z, z - n_z, jnp.where(z < 0, z + n_z, z))
    return z * CORES + jnp.bitwise_xor(jnp.bitwise_and(me, 1), flip)


def per_device(
    qkv, resid, block_count, send_count, send_slot, lm_row, out_weight, out_bias, norm_gain
):
    width = resid.shape[2]
    row_total = send_slot.shape[1]
    tokens = WIN // GROUP
    blocks = row_total // tokens
    n_seq = lax.axis_size("seq")
    n_enc = lax.axis_size("enc")
    slots = lm_row.shape[1]
    cap = slots // n_seq
    chunk = GROUP * cap
    sent = slots * GROUP
    vmem = pl.BlockSpec(memory_space=pltpu.VMEM)
    small = pltpu.CompilerParams(vmem_limit_bytes=16 << 20)

    def rows_of(count, columns=width):
        return jax.ShapeDtypeStruct((count, columns), jnp.bfloat16)

    data = (qkv, resid, out_weight, out_bias, norm_gain)
    lent = encode_call(lent_kernel, 1, [block_count], [], *data, rows_of(WIN), [])
    borrowed = lax.ppermute(lent, "enc", [((i - 1) % n_enc, i) for i in range(n_enc)])

    by_steps = chunk % 8 == 0 and n_seq % CORES == 0
    peer = functools.partial(chip_peer, n_seq) if by_steps else lambda me, step, sign: step
    me = lax.axis_index("seq").astype(jnp.int32).reshape(1, 1)
    packed, borrow, place = encode_call(
        functools.partial(own_kernel, n_seq, cap, peer), blocks,
        [block_count, send_count, me], [send_slot, lm_row], *data,
        (rows_of(sent), rows_of(sent, WIN), rows_of(GROUP * row_total, sent)),
        [pltpu.VMEM((row_total * GROUP, width), jnp.bfloat16)],
    )
    pieces = n_seq if by_steps else 1
    outgoing = pl.pallas_call(
        pack_kernel,
        out_shape=[rows_of(sent // pieces)] * pieces,
        in_specs=[vmem] * 3,
        out_specs=[vmem] * pieces,
        compiler_params=small,
    )(packed, borrow, borrowed)

    if by_steps:
        n_z = n_seq // CORES
        arrived = [outgoing[0]]
        for part, (dz, dc) in list(zip(outgoing, exchange_steps(n_seq)))[1:]:
            route = [(i, (i // CORES + dz) % n_z * CORES + (i + dc) % CORES) for i in range(n_seq)]
            arrived.append(lax.ppermute(part, "seq", route))
    else:
        arrived = [
            lax.all_to_all(
                outgoing[0].reshape(n_seq, chunk, width), "seq", split_axis=0, concat_axis=0, tiled=True
            ).reshape(sent, width)
        ]
    placed = pl.pallas_call(
        place_kernel,
        out_shape=rows_of(row_total, GROUP * width),
        in_specs=[vmem] * (1 + pieces),
        out_specs=pl.BlockSpec(memory_space=pltpu.HBM),
        scratch_shapes=[pltpu.VMEM((row_total, GROUP * width), jnp.bfloat16), pltpu.SemaphoreType.DMA((GROUP,))],
        compiler_params=small,
    )(place, *arrived)
    return placed[None]


def solution(mesh):
    placed = (
        P("enc", "seq", None),
        P("enc", "seq", None),
        P("enc", "seq"),
        P("enc", "seq"),
        P("enc", "seq"),
        P("enc", "seq"),
        P(),
        P(),
        P(),
    )
    return jax.shard_map(
        per_device, mesh=mesh, in_specs=placed, out_specs=P("enc", "seq", None), check_vma=False
    )
```

```python
import functools
import math

import jax
import jax.numpy as jnp
from jax import lax
from jax.experimental import pallas as pl
from jax.experimental.pallas import tpu as pltpu
from jax.sharding import PartitionSpec as P

HEADS = 16
WIN = 64
LANES = 128
GROUP = 4
EPS = 1e-6
CORES = 2

NT = (((1,), (1,)), ((), ()))


def dot32(a, b):
    return jnp.dot(a, b, preferred_element_type=jnp.float32)


def one_hot(match):
    return match.astype(jnp.float32).astype(jnp.bfloat16)


def attend(q, k, v, out_ref, row0, width):
    head = width // HEADS
    rate = 1.0 / math.sqrt(head)
    totals = [None] * (width // LANES)
    sums = [None] * (width // LANES)
    first_half = lax.broadcasted_iota(jnp.int32, (WIN, 2 * WIN), 1) < WIN
    for pair in range(HEADS // 2):
        start = 2 * pair * head
        lo = start // LANES * LANES
        hi = -(-(start + 2 * head) // LANES) * LANES
        column = lax.broadcasted_iota(jnp.int32, (2 * WIN, hi - lo), 1) + lo
        row = lax.broadcasted_iota(jnp.int32, (2 * WIN, hi - lo), 0)
        begin = jnp.where(row < WIN, start, start + head)
        mask = one_hot((column >= begin) & (column < begin + head))
        kw, vw = k(lo, hi), v(lo, hi)
        keys = jnp.concatenate([kw, kw], axis=0) * mask
        values = jnp.concatenate([vw, vw], axis=0) * mask
        scores = lax.dot_general(q(lo, hi), keys, NT, preferred_element_type=jnp.float32)
        top0 = jnp.max(jnp.where(first_half, scores, -jnp.inf), axis=1, keepdims=True)
        top1 = jnp.max(jnp.where(first_half, -jnp.inf, scores), axis=1, keepdims=True)
        raised = jnp.exp((scores - jnp.where(first_half, top0, top1)) * rate).astype(jnp.bfloat16)
        part = dot32(raised, values)
        norm = dot32(raised, mask)
        for tile in range(lo // LANES, hi // LANES):
            at = slice(tile * LANES - lo, (tile + 1) * LANES - lo)
            totals[tile] = part[:, at] if totals[tile] is None else totals[tile] + part[:, at]
            sums[tile] = norm[:, at] if sums[tile] is None else sums[tile] + norm[:, at]
    for tile in range(width // LANES):
        out_ref[row0 : row0 + WIN, tile * LANES : (tile + 1) * LANES] = (totals[tile] / sums[tile]).astype(
            jnp.bfloat16
        )


def attend_all(qkv, attended, width):
    for b in range(qkv.shape[0]):
        attend(
            lambda lo, hi, b=b: qkv[b, :, lo:hi],
            lambda lo, hi, b=b: qkv[b, :, width + lo : width + hi],
            lambda lo, hi, b=b: qkv[b, :, 2 * width + lo : 2 * width + hi],
            attended, b * WIN, width,
        )


def project(attended, resid, weight, bias, gain, hidden, out_ref):
    rows, width = hidden.shape
    step = 2 * LANES
    chunks = [slice(lo, lo + step) for lo in range(0, width, step)]
    squares = jnp.zeros((rows, 1), jnp.float32)
    for cols in chunks:
        h = dot32(attended[...], weight[:, cols])
        h = h + bias[cols].astype(jnp.float32).reshape(1, step)
        h = h + resid[:, :, cols].reshape(rows, step).astype(jnp.float32)
        hidden[:, cols] = h
        squares = squares + jnp.sum(h * h, axis=1, keepdims=True)
    scale = lax.rsqrt(squares * (1.0 / width) + EPS)
    for cols in chunks:
        out_ref[:, cols] = (hidden[:, cols] * scale * gain[cols].astype(jnp.float32).reshape(1, step)).astype(jnp.bfloat16)


def lent_attention_kernel(count_ref, qkv_hbm, resid_hbm, attended, resid, qkv, sems):
    at = pl.ds(count_ref[0, 0] - 1, 1)
    qkv_copy = pltpu.make_async_copy(qkv_hbm.at[at], qkv, sems.at[0])
    resid_copy = pltpu.make_async_copy(resid_hbm.at[at], resid, sems.at[1])
    qkv_copy.start()
    resid_copy.start()
    qkv_copy.wait()
    attend_all(qkv, attended, resid.shape[2])
    resid_copy.wait()


def lent_project_kernel(attended, resid, weight, bias, gain, out_ref, hidden):
    project(attended, resid, weight, bias, gain, hidden, out_ref)


def encode(qkv_hbm, resid_hbm, weight_hbm, bias_hbm, gain_hbm, out_ref, qkv, resid, weight, attended, hidden, bias, gain, sems):
    at = pl.ds(0, qkv.shape[0])
    pairs = [(qkv_hbm.at[at], qkv), (weight_hbm, weight), (resid_hbm.at[at], resid), (bias_hbm, bias), (gain_hbm, gain)]
    copies = [pltpu.make_async_copy(a, b, sems.at[i]) for i, (a, b) in enumerate(pairs)]
    for copy in copies:
        copy.start()
    copies[0].wait()
    attend_all(qkv, attended, resid.shape[2])
    for copy in copies[1:]:
        copy.wait()
    project(attended, resid, weight, bias, gain, hidden, out_ref)


def split_index(index, n_seq, cap):
    step = index // (GROUP * cap)
    rest = index - step * (GROUP * cap)
    patch = rest // cap
    return step, patch, rest - patch * cap


def own_kernel(
    n_seq, cap, peer, count_ref, send_ref, me_ref, slot_ref, row_ref,
    qkv_hbm, resid_hbm, weight_hbm, bias_hbm, gain_hbm,
    packed_ref, borrow_ref, place_ref, normed, *scratch,
):
    rows = normed.shape[0]
    slots = n_seq * cap
    sent = slots * GROUP
    tokens = rows // GROUP
    me = me_ref[0, 0]
    encode(qkv_hbm, resid_hbm, weight_hbm, bias_hbm, gain_hbm, normed, *scratch)

    step, patch, rank = split_index(lax.broadcasted_iota(jnp.int32, (sent, 1), 0), n_seq, cap)
    row_code = (peer(me, step, 1) * cap + rank) * GROUP + patch
    token = lax.broadcasted_iota(jnp.int32, (tokens, rows), 0)
    column = lax.broadcasted_iota(jnp.int32, (tokens, rows), 1)
    spread = one_hot((column >= token * GROUP) & (column < (token + 1) * GROUP))
    slot = jnp.broadcast_to(slot_ref[...].astype(jnp.float32), (16, tokens)).astype(jnp.bfloat16)
    slot = dot32(slot, spread)[:1].astype(jnp.int32)
    index = lax.broadcasted_iota(jnp.int32, (1, rows), 1)
    col_code = slot * GROUP + jnp.bitwise_and(index, GROUP - 1)
    kept = (count_ref[0, 0] - send_ref[0, 0]) * WIN
    last = rows - WIN
    own = one_hot(row_code == jnp.where(index < kept, col_code, -1))
    packed_ref[...] = dot32(own, normed[...]).astype(jnp.bfloat16)
    borrow_ref[...] = one_hot(row_code == jnp.where(kept > last, -1, col_code[:, last:]))

    step, patch, rank = split_index(lax.broadcasted_iota(jnp.int32, (1, sent), 1), n_seq, cap)
    arrive = peer(me, step, -1) * cap + rank
    pick = one_hot(lax.broadcasted_iota(jnp.int32, (slots, sent), 0) == arrive)
    target = jnp.broadcast_to(row_ref[...].astype(jnp.float32), (16, slots)).astype(jnp.bfloat16)
    target = dot32(target, pick)[:1].astype(jnp.int32)
    out_row = lax.broadcasted_iota(jnp.int32, (tokens, sent), 0)
    for j in range(GROUP):
        place_ref[j * tokens : (j + 1) * tokens, :] = one_hot((target == out_row) & (patch == j))


def in_hbm(*arrays):
    return [pltpu.with_memory_space_constraint(a, pltpu.HBM) for a in arrays]


def encode_lent(count, qkv, resid, weight, bias, gain):
    width = resid.shape[2]
    vmem = pl.BlockSpec(memory_space=pltpu.VMEM)
    hbm = pl.BlockSpec(memory_space=pltpu.HBM)
    small = pltpu.CompilerParams(vmem_limit_bytes=16 << 20)
    attended, rows = pl.pallas_call(
        lent_attention_kernel,
        out_shape=(
            jax.ShapeDtypeStruct((WIN, width), jnp.bfloat16),
            jax.ShapeDtypeStruct((1, WIN, width), jnp.bfloat16),
        ),
        in_specs=[pl.BlockSpec(memory_space=pltpu.SMEM), hbm, hbm],
        out_specs=(vmem, vmem),
        scratch_shapes=[pltpu.VMEM((1, WIN, 3 * width), jnp.bfloat16), pltpu.SemaphoreType.DMA((2,))],
        compiler_params=small,
        cost_estimate=pl.CostEstimate(
            flops=8 << 30, bytes_accessed=16 << 20, transcendentals=WIN * WIN * HEADS
        ),
    )(count, *in_hbm(qkv, resid))
    return pl.pallas_call(
        lent_project_kernel,
        out_shape=jax.ShapeDtypeStruct((WIN, width), jnp.bfloat16),
        in_specs=[vmem] * 5,
        out_specs=vmem,
        scratch_shapes=[pltpu.VMEM((WIN, width), jnp.float32)],
        compiler_params=small,
        cost_estimate=pl.CostEstimate(
            flops=2 * WIN * width * width, bytes_accessed=2 * (width * width + 3 * WIN * width), transcendentals=0
        ),
    )(attended, rows, weight, bias, gain)


def encode_own(kernel, blocks, scalars, slots, qkv, resid, weight, bias, gain, out_shape, extra):
    width = resid.shape[2]
    rows = blocks * WIN
    vmem = pl.BlockSpec(memory_space=pltpu.VMEM)
    smem = pl.BlockSpec(memory_space=pltpu.SMEM)
    hbm = pl.BlockSpec(memory_space=pltpu.HBM)
    return pl.pallas_call(
        kernel,
        out_shape=out_shape,
        in_specs=[smem] * len(scalars) + [vmem] * len(slots) + [hbm] * 5,
        out_specs=jax.tree.map(lambda _: vmem, out_shape),
        scratch_shapes=extra
        + [
            pltpu.VMEM((blocks, WIN, 3 * width), jnp.bfloat16),
            pltpu.VMEM((blocks, WIN, width), jnp.bfloat16),
            pltpu.VMEM((width, width), jnp.bfloat16),
            pltpu.VMEM((rows, width), jnp.bfloat16),
            pltpu.VMEM((rows, width), jnp.float32),
            pltpu.VMEM((width,), jnp.bfloat16),
            pltpu.VMEM((width,), jnp.bfloat16),
            pltpu.SemaphoreType.DMA((5,)),
        ],
        compiler_params=pltpu.CompilerParams(vmem_limit_bytes=24 << 20),
        cost_estimate=pl.CostEstimate(
            flops=2 * rows * width * width + 8 * rows * WIN * width,
            bytes_accessed=2 * (width * width + 5 * rows * width),
            transcendentals=rows * WIN * HEADS,
        ),
    )(*scalars, *slots, *in_hbm(qkv, resid, weight, bias, gain))


def pack_kernel(packed_ref, borrow_ref, borrowed_ref, *out_refs):
    total = packed_ref[...].astype(jnp.float32) + dot32(borrow_ref[...], borrowed_ref[...])
    chunk = out_refs[0].shape[0]
    for step, out_ref in enumerate(out_refs):
        out_ref[...] = total[step * chunk : (step + 1) * chunk].astype(jnp.bfloat16)


def place_kernel(place_ref, *refs):
    *in_refs, out_hbm, out, sems = refs
    tokens = out.shape[0]
    chunks = [ref[...].astype(jnp.float32) for ref in in_refs]
    arrived = chunks[0] if len(chunks) == 1 else jnp.concatenate(chunks, axis=0)
    arrived = arrived.astype(jnp.bfloat16)
    width = arrived.shape[1]
    copies = []
    for j in range(GROUP):
        cols = slice(j * width, (j + 1) * width)
        out[:, cols] = dot32(place_ref[j * tokens : (j + 1) * tokens, :], arrived).astype(jnp.bfloat16)
        copies.append(pltpu.make_async_copy(out.at[:, cols], out_hbm.at[:, cols], sems.at[j]))
        copies[-1].start()
    for copy in copies:
        copy.wait()


def exchange_steps(n_seq):
    n_z = n_seq // CORES
    steps = [(dz, dc) for dz in range(n_z) for dc in range(CORES) if (dz, dc) != (0, 0)]
    return [(0, 0)] + sorted(steps, key=lambda s: (abs(s[0] - n_z / 2), s[1], s[0]))


def chip_peer(n_seq, me, step, sign):
    n_z = n_seq // CORES
    offset = jnp.zeros_like(step)
    flip = jnp.zeros_like(step)
    for i, (dz, dc) in enumerate(exchange_steps(n_seq)):
        offset = jnp.where(step == i, dz, offset)
        flip = jnp.where(step == i, dc, flip)
    z = me // CORES + sign * offset
    z = jnp.where(z >= n_z, z - n_z, jnp.where(z < 0, z + n_z, z))
    return z * CORES + jnp.bitwise_xor(jnp.bitwise_and(me, 1), flip)


def per_device(
    qkv, resid, block_count, send_count, send_slot, lm_row, out_weight, out_bias, norm_gain
):
    width = resid.shape[2]
    row_total = send_slot.shape[1]
    tokens = WIN // GROUP
    blocks = row_total // tokens
    n_seq = lax.axis_size("seq")
    n_enc = lax.axis_size("enc")
    slots = lm_row.shape[1]
    cap = slots // n_seq
    chunk = GROUP * cap
    sent = slots * GROUP
    vmem = pl.BlockSpec(memory_space=pltpu.VMEM)
    small = pltpu.CompilerParams(vmem_limit_bytes=16 << 20)

    def rows_of(count, columns=width):
        return jax.ShapeDtypeStruct((count, columns), jnp.bfloat16)

    data = (qkv, resid, out_weight, out_bias, norm_gain)
    lent = encode_lent(block_count, *data)
    borrowed = lax.ppermute(lent, "enc", [((i - 1) % n_enc, i) for i in range(n_enc)])

    by_steps = chunk % 8 == 0 and n_seq % CORES == 0
    peer = functools.partial(chip_peer, n_seq) if by_steps else lambda me, step, sign: step
    me = lax.axis_index("seq").astype(jnp.int32).reshape(1, 1)
    packed, borrow, place = encode_own(
        functools.partial(own_kernel, n_seq, cap, peer), blocks,
        [block_count, send_count, me], [send_slot, lm_row], *data,
        (rows_of(sent), rows_of(sent, WIN), rows_of(GROUP * row_total, sent)),
        [pltpu.VMEM((row_total * GROUP, width), jnp.bfloat16)],
    )
    pieces = n_seq if by_steps else 1
    outgoing = pl.pallas_call(
        pack_kernel,
        out_shape=[rows_of(sent // pieces)] * pieces,
        in_specs=[vmem] * 3,
        out_specs=[vmem] * pieces,
        compiler_params=small,
    )(packed, borrow, borrowed)

    if by_steps:
        n_z = n_seq // CORES
        arrived = [outgoing[0]]
        for part, (dz, dc) in list(zip(outgoing, exchange_steps(n_seq)))[1:]:
            route = [(i, (i // CORES + dz) % n_z * CORES + (i + dc) % CORES) for i in range(n_seq)]
            arrived.append(lax.ppermute(part, "seq", route))
    else:
        arrived = [
            lax.all_to_all(
                outgoing[0].reshape(n_seq, chunk, width), "seq", split_axis=0, concat_axis=0, tiled=True
            ).reshape(sent, width)
        ]
    placed = pl.pallas_call(
        place_kernel,
        out_shape=rows_of(row_total, GROUP * width),
        in_specs=[vmem] * (1 + pieces),
        out_specs=pl.BlockSpec(memory_space=pltpu.HBM),
        scratch_shapes=[pltpu.VMEM((row_total, GROUP * width), jnp.bfloat16), pltpu.SemaphoreType.DMA((GROUP,))],
        compiler_params=small,
    )(place, *arrived)
    return placed[None]


def solution(mesh):
    placed = (
        P("enc", "seq", None),
        P("enc", "seq", None),
        P("enc", "seq"),
        P("enc", "seq"),
        P("enc", "seq"),
        P("enc", "seq"),
        P(),
        P(),
        P(),
    )
    return jax.shard_map(
        per_device, mesh=mesh, in_specs=placed, out_specs=P("enc", "seq", None), check_vma=False
    )
```

```python
import functools
import math

import jax
import jax.numpy as jnp
from jax import lax
from jax.experimental import pallas as pl
from jax.experimental.pallas import tpu as pltpu
from jax.sharding import PartitionSpec as P

HEADS = 16
WIN = 64
LANES = 128
GROUP = 4
EPS = 1e-6
CORES = 2

NT = (((1,), (1,)), ((), ()))


def dot32(a, b):
    return jnp.dot(a, b, preferred_element_type=jnp.float32)


def one_hot(match):
    return match.astype(jnp.float32).astype(jnp.bfloat16)


def head_pairs(width):
    head = width // HEADS
    spans = []
    for start in range(0, width, 2 * head):
        lo = start // LANES * LANES
        spans.append((start, lo, -(-(start + 2 * head) // LANES) * LANES))
    return spans


def mask_period(width):
    return LANES // math.gcd(LANES, 2 * (width // HEADS))


def mask_scratch(width):
    return pltpu.VMEM((mask_period(width), 2 * WIN, 2 * LANES), jnp.bfloat16)


def make_masks(masks, width):
    head = width // HEADS
    for i in range(masks.shape[0]):
        start, lo, hi = head_pairs(width)[i]
        column = lax.broadcasted_iota(jnp.int32, masks.shape[1:], 1) + lo
        row = lax.broadcasted_iota(jnp.int32, masks.shape[1:], 0)
        begin = jnp.where(row < WIN, start, start + head)
        masks[i] = one_hot((column >= begin) & (column < begin + head))


def attend(qkv, masks, attended, width):
    rate = math.log2(math.e) / math.sqrt(width // HEADS)
    first = lax.broadcasted_iota(jnp.int32, (WIN, 2 * WIN), 1) < WIN
    for b in range(qkv.shape[0]):
        totals = [None] * (width // LANES)
        sums = [None] * (width // LANES)
        for pair, (_, lo, hi) in enumerate(head_pairs(width)):
            mask = masks[pair % masks.shape[0]]
            kw = qkv[b, :, width + lo : width + hi]
            vw = qkv[b, :, 2 * width + lo : 2 * width + hi]
            keys = jnp.concatenate([kw, kw], axis=0) * mask
            values = jnp.concatenate([vw, vw], axis=0) * mask
            scores = lax.dot_general(qkv[b, :, lo:hi], keys, NT, preferred_element_type=jnp.float32)
            top0 = jnp.max(jnp.where(first, scores, -jnp.inf), axis=1, keepdims=True)
            top1 = jnp.max(jnp.where(first, -jnp.inf, scores), axis=1, keepdims=True)
            raised = jnp.exp2((scores - jnp.where(first, top0, top1)) * rate).astype(jnp.bfloat16)
            part = dot32(raised, values)
            norm = dot32(raised, mask)
            for tile in range(lo // LANES, hi // LANES):
                at = slice(tile * LANES - lo, (tile + 1) * LANES - lo)
                totals[tile] = part[:, at] if totals[tile] is None else totals[tile] + part[:, at]
                sums[tile] = norm[:, at] if sums[tile] is None else sums[tile] + norm[:, at]
        for tile in range(width // LANES):
            attended[b * WIN : (b + 1) * WIN, tile * LANES : (tile + 1) * LANES] = (totals[tile] / sums[tile]).astype(
                jnp.bfloat16
            )


def project(attended, resid, weight, bias, gain, hidden, out_ref):
    rows, width = hidden.shape
    step = 2 * LANES
    chunks = [slice(lo, lo + step) for lo in range(0, width, step)]
    squares = jnp.zeros((rows, 1), jnp.float32)
    for cols in chunks:
        h = dot32(attended[...], weight[:, cols])
        h = h + bias[cols].astype(jnp.float32).reshape(1, step)
        h = h + resid[:, :, cols].reshape(rows, step).astype(jnp.float32)
        hidden[:, cols] = h
        squares = squares + jnp.sum(h * h, axis=1, keepdims=True)
    scale = lax.rsqrt(squares * (1.0 / width) + EPS)
    for cols in chunks:
        out_ref[:, cols] = (hidden[:, cols] * scale * gain[cols].astype(jnp.float32).reshape(1, step)).astype(jnp.bfloat16)


def lent_attention_kernel(count_ref, qkv_hbm, resid_hbm, attended, resid, qkv, masks, sems):
    at = pl.ds(count_ref[0, 0] - 1, 1)
    qkv_copy = pltpu.make_async_copy(qkv_hbm.at[at], qkv, sems.at[0])
    resid_copy = pltpu.make_async_copy(resid_hbm.at[at], resid, sems.at[1])
    qkv_copy.start()
    resid_copy.start()
    width = resid.shape[2]
    make_masks(masks, width)
    qkv_copy.wait()
    attend(qkv, masks, attended, width)
    resid_copy.wait()


def lent_project_kernel(attended, resid, weight, bias, gain, out_ref, hidden):
    project(attended, resid, weight, bias, gain, hidden, out_ref)


def encode(qkv_hbm, resid_hbm, weight_hbm, bias_hbm, gain_hbm, out_ref, qkv, resid, weight, attended, hidden, bias, gain, masks, sems):
    at = pl.ds(0, qkv.shape[0])
    pairs = [(qkv_hbm.at[at], qkv), (weight_hbm, weight), (resid_hbm.at[at], resid), (bias_hbm, bias), (gain_hbm, gain)]
    copies = [pltpu.make_async_copy(a, b, sems.at[i]) for i, (a, b) in enumerate(pairs)]
    for copy in copies:
        copy.start()
    width = resid.shape[2]
    make_masks(masks, width)
    copies[0].wait()
    attend(qkv, masks, attended, width)
    for copy in copies[1:]:
        copy.wait()
    project(attended, resid, weight, bias, gain, hidden, out_ref)


def split_index(index, n_seq, cap):
    step = index // (GROUP * cap)
    rest = index - step * (GROUP * cap)
    patch = rest // cap
    return step, patch, rest - patch * cap


def own_kernel(
    n_seq, cap, peer, count_ref, send_ref, me_ref, slot_ref, row_ref,
    qkv_hbm, resid_hbm, weight_hbm, bias_hbm, gain_hbm,
    packed_ref, borrow_ref, place_ref, normed, *scratch,
):
    rows = normed.shape[0]
    slots = n_seq * cap
    sent = slots * GROUP
    tokens = rows // GROUP
    me = me_ref[0, 0]
    encode(qkv_hbm, resid_hbm, weight_hbm, bias_hbm, gain_hbm, normed, *scratch)

    step, patch, rank = split_index(lax.broadcasted_iota(jnp.int32, (sent, 1), 0), n_seq, cap)
    row_code = (peer(me, step, 1) * cap + rank) * GROUP + patch
    token = lax.broadcasted_iota(jnp.int32, (tokens, rows), 0)
    column = lax.broadcasted_iota(jnp.int32, (tokens, rows), 1)
    spread = one_hot((column >= token * GROUP) & (column < (token + 1) * GROUP))
    slot = jnp.broadcast_to(slot_ref[...].astype(jnp.float32), (16, tokens)).astype(jnp.bfloat16)
    slot = dot32(slot, spread)[:1].astype(jnp.int32)
    index = lax.broadcasted_iota(jnp.int32, (1, rows), 1)
    col_code = slot * GROUP + jnp.bitwise_and(index, GROUP - 1)
    kept = (count_ref[0, 0] - send_ref[0, 0]) * WIN
    last = rows - WIN
    own = one_hot(row_code == jnp.where(index < kept, col_code, -1))
    packed_ref[...] = dot32(own, normed[...]).astype(jnp.bfloat16)
    borrow_ref[...] = one_hot(row_code == jnp.where(kept > last, -1, col_code[:, last:]))

    step, patch, rank = split_index(lax.broadcasted_iota(jnp.int32, (1, sent), 1), n_seq, cap)
    arrive = peer(me, step, -1) * cap + rank
    pick = one_hot(lax.broadcasted_iota(jnp.int32, (slots, sent), 0) == arrive)
    target = jnp.broadcast_to(row_ref[...].astype(jnp.float32), (16, slots)).astype(jnp.bfloat16)
    target = dot32(target, pick)[:1].astype(jnp.int32)
    out_row = lax.broadcasted_iota(jnp.int32, (tokens, sent), 0)
    for j in range(GROUP):
        place_ref[j * tokens : (j + 1) * tokens, :] = one_hot((target == out_row) & (patch == j))


def in_hbm(*arrays):
    return [pltpu.with_memory_space_constraint(a, pltpu.HBM) for a in arrays]


def encode_lent(count, qkv, resid, weight, bias, gain):
    width = resid.shape[2]
    vmem = pl.BlockSpec(memory_space=pltpu.VMEM)
    hbm = pl.BlockSpec(memory_space=pltpu.HBM)
    small = pltpu.CompilerParams(vmem_limit_bytes=16 << 20)
    attended, rows = pl.pallas_call(
        lent_attention_kernel,
        out_shape=(
            jax.ShapeDtypeStruct((WIN, width), jnp.bfloat16),
            jax.ShapeDtypeStruct((1, WIN, width), jnp.bfloat16),
        ),
        in_specs=[pl.BlockSpec(memory_space=pltpu.SMEM), hbm, hbm],
        out_specs=(vmem, vmem),
        scratch_shapes=[pltpu.VMEM((1, WIN, 3 * width), jnp.bfloat16), mask_scratch(width), pltpu.SemaphoreType.DMA((2,))],
        compiler_params=small,
        cost_estimate=pl.CostEstimate(
            flops=1 << 30, bytes_accessed=1 << 20, transcendentals=WIN * WIN * HEADS
        ),
    )(count, *in_hbm(qkv, resid))
    return pl.pallas_call(
        lent_project_kernel,
        out_shape=jax.ShapeDtypeStruct((WIN, width), jnp.bfloat16),
        in_specs=[vmem] * 5,
        out_specs=vmem,
        scratch_shapes=[pltpu.VMEM((WIN, width), jnp.float32)],
        compiler_params=small,
        cost_estimate=pl.CostEstimate(
            flops=2 * WIN * width * width, bytes_accessed=2 * (width * width + 3 * WIN * width), transcendentals=0
        ),
    )(attended, rows, weight, bias, gain)


def encode_own(kernel, blocks, scalars, slots, qkv, resid, weight, bias, gain, out_shape, extra):
    width = resid.shape[2]
    rows = blocks * WIN
    vmem = pl.BlockSpec(memory_space=pltpu.VMEM)
    smem = pl.BlockSpec(memory_space=pltpu.SMEM)
    hbm = pl.BlockSpec(memory_space=pltpu.HBM)
    return pl.pallas_call(
        kernel,
        out_shape=out_shape,
        in_specs=[smem] * len(scalars) + [vmem] * len(slots) + [hbm] * 5,
        out_specs=jax.tree.map(lambda _: vmem, out_shape),
        scratch_shapes=extra
        + [
            pltpu.VMEM((blocks, WIN, 3 * width), jnp.bfloat16),
            pltpu.VMEM((blocks, WIN, width), jnp.bfloat16),
            pltpu.VMEM((width, width), jnp.bfloat16),
            pltpu.VMEM((rows, width), jnp.bfloat16),
            pltpu.VMEM((rows, width), jnp.float32),
            pltpu.VMEM((width,), jnp.bfloat16),
            pltpu.VMEM((width,), jnp.bfloat16),
            mask_scratch(width),
            pltpu.SemaphoreType.DMA((5,)),
        ],
        compiler_params=pltpu.CompilerParams(vmem_limit_bytes=24 << 20),
        cost_estimate=pl.CostEstimate(
            flops=2 * rows * width * width + 8 * rows * WIN * width,
            bytes_accessed=2 * (width * width + 5 * rows * width),
            transcendentals=rows * WIN * HEADS,
        ),
    )(*scalars, *slots, *in_hbm(qkv, resid, weight, bias, gain))


def pack_kernel(packed_ref, borrow_ref, borrowed_ref, *out_refs):
    total = packed_ref[...].astype(jnp.float32) + dot32(borrow_ref[...], borrowed_ref[...])
    chunk = out_refs[0].shape[0]
    for step, out_ref in enumerate(out_refs):
        out_ref[...] = total[step * chunk : (step + 1) * chunk].astype(jnp.bfloat16)


def place_kernel(place_ref, *refs):
    *in_refs, out_hbm, out, sems = refs
    tokens = out.shape[0]
    chunks = [ref[...].astype(jnp.float32) for ref in in_refs]
    arrived = chunks[0] if len(chunks) == 1 else jnp.concatenate(chunks, axis=0)
    arrived = arrived.astype(jnp.bfloat16)
    width = arrived.shape[1]
    copies = []
    for j in range(GROUP):
        cols = slice(j * width, (j + 1) * width)
        out[:, cols] = dot32(place_ref[j * tokens : (j + 1) * tokens, :], arrived).astype(jnp.bfloat16)
        copies.append(pltpu.make_async_copy(out.at[:, cols], out_hbm.at[:, cols], sems.at[j]))
        copies[-1].start()
    for copy in copies:
        copy.wait()


def exchange_steps(n_seq):
    n_z = n_seq // CORES
    steps = [(dz, dc) for dz in range(n_z) for dc in range(CORES) if (dz, dc) != (0, 0)]
    return [(0, 0)] + sorted(steps, key=lambda s: (abs(s[0] - n_z / 2), s[1], s[0]))


def chip_peer(n_seq, me, step, sign):
    n_z = n_seq // CORES
    offset = jnp.zeros_like(step)
    flip = jnp.zeros_like(step)
    for i, (dz, dc) in enumerate(exchange_steps(n_seq)):
        offset = jnp.where(step == i, dz, offset)
        flip = jnp.where(step == i, dc, flip)
    z = me // CORES + sign * offset
    z = jnp.where(z >= n_z, z - n_z, jnp.where(z < 0, z + n_z, z))
    return z * CORES + jnp.bitwise_xor(jnp.bitwise_and(me, 1), flip)


def per_device(
    qkv, resid, block_count, send_count, send_slot, lm_row, out_weight, out_bias, norm_gain
):
    width = resid.shape[2]
    row_total = send_slot.shape[1]
    tokens = WIN // GROUP
    blocks = row_total // tokens
    n_seq = lax.axis_size("seq")
    n_enc = lax.axis_size("enc")
    slots = lm_row.shape[1]
    cap = slots // n_seq
    chunk = GROUP * cap
    sent = slots * GROUP
    vmem = pl.BlockSpec(memory_space=pltpu.VMEM)
    small = pltpu.CompilerParams(vmem_limit_bytes=16 << 20)

    def rows_of(count, columns=width):
        return jax.ShapeDtypeStruct((count, columns), jnp.bfloat16)

    data = (qkv, resid, out_weight, out_bias, norm_gain)
    lent = encode_lent(block_count, *data)
    borrowed = lax.ppermute(lent, "enc", [((i - 1) % n_enc, i) for i in range(n_enc)])

    by_steps = chunk % 8 == 0 and n_seq % CORES == 0
    peer = functools.partial(chip_peer, n_seq) if by_steps else lambda me, step, sign: step
    me = lax.axis_index("seq").astype(jnp.int32).reshape(1, 1)
    packed, borrow, place = encode_own(
        functools.partial(own_kernel, n_seq, cap, peer), blocks,
        [block_count, send_count, me], [send_slot, lm_row], *data,
        (rows_of(sent), rows_of(sent, WIN), rows_of(GROUP * row_total, sent)),
        [pltpu.VMEM((row_total * GROUP, width), jnp.bfloat16)],
    )
    pieces = n_seq if by_steps else 1
    outgoing = pl.pallas_call(
        pack_kernel,
        out_shape=[rows_of(sent // pieces)] * pieces,
        in_specs=[vmem] * 3,
        out_specs=[vmem] * pieces,
        compiler_params=small,
    )(packed, borrow, borrowed)

    if by_steps:
        n_z = n_seq // CORES
        arrived = [outgoing[0]]
        for part, (dz, dc) in list(zip(outgoing, exchange_steps(n_seq)))[1:]:
            route = [(i, (i // CORES + dz) % n_z * CORES + (i + dc) % CORES) for i in range(n_seq)]
            arrived.append(lax.ppermute(part, "seq", route))
    else:
        arrived = [
            lax.all_to_all(
                outgoing[0].reshape(n_seq, chunk, width), "seq", split_axis=0, concat_axis=0, tiled=True
            ).reshape(sent, width)
        ]
    placed = pl.pallas_call(
        place_kernel,
        out_shape=rows_of(row_total, GROUP * width),
        in_specs=[vmem] * (1 + pieces),
        out_specs=pl.BlockSpec(memory_space=pltpu.HBM),
        scratch_shapes=[pltpu.VMEM((row_total, GROUP * width), jnp.bfloat16), pltpu.SemaphoreType.DMA((GROUP,))],
        compiler_params=small,
    )(place, *arrived)
    return placed[None]


def solution(mesh):
    placed = (
        P("enc", "seq", None),
        P("enc", "seq", None),
        P("enc", "seq"),
        P("enc", "seq"),
        P("enc", "seq"),
        P("enc", "seq"),
        P(),
        P(),
        P(),
    )
    return jax.shard_map(
        per_device, mesh=mesh, in_specs=placed, out_specs=P("enc", "seq", None), check_vma=False
    )
```

```python
import functools
import math

import jax
import jax.numpy as jnp
from jax import lax
from jax.experimental import pallas as pl
from jax.experimental.pallas import tpu as pltpu
from jax.sharding import PartitionSpec as P

HEADS = 16
WIN = 64
LANES = 128
GROUP = 4
EPS = 1e-6
CORES = 2

NT = (((1,), (1,)), ((), ()))


def dot32(a, b):
    return jnp.dot(a, b, preferred_element_type=jnp.float32)


def one_hot(match):
    return match.astype(jnp.float32).astype(jnp.bfloat16)


def head_pairs(width):
    head = width // HEADS
    spans = []
    for start in range(0, width, 2 * head):
        lo = start // LANES * LANES
        spans.append((start, lo, -(-(start + 2 * head) // LANES) * LANES))
    return spans


def mask_period(width):
    return LANES // math.gcd(LANES, 2 * (width // HEADS))


def mask_scratch(width):
    return pltpu.VMEM((mask_period(width), 2 * WIN, 2 * LANES), jnp.bfloat16)


def make_masks(masks, width):
    head = width // HEADS
    for i in range(masks.shape[0]):
        start, lo, hi = head_pairs(width)[i]
        column = lax.broadcasted_iota(jnp.int32, masks.shape[1:], 1) + lo
        row = lax.broadcasted_iota(jnp.int32, masks.shape[1:], 0)
        begin = jnp.where(row < WIN, start, start + head)
        masks[i] = one_hot((column >= begin) & (column < begin + head))


def attend(qkv, masks, attended, width):
    rate = math.log2(math.e) / math.sqrt(width // HEADS)
    first = lax.broadcasted_iota(jnp.int32, (WIN, 2 * WIN), 1) < WIN
    for b in range(qkv.shape[0]):
        totals = [None] * (width // LANES)
        sums = [None] * (width // LANES)
        for pair, (_, lo, hi) in enumerate(head_pairs(width)):
            mask = masks[pair % masks.shape[0]]
            kw = qkv[b, :, width + lo : width + hi]
            vw = qkv[b, :, 2 * width + lo : 2 * width + hi]
            keys = jnp.concatenate([kw, kw], axis=0) * mask
            values = jnp.concatenate([vw, vw], axis=0) * mask
            scores = lax.dot_general(qkv[b, :, lo:hi], keys, NT, preferred_element_type=jnp.float32)
            top0 = jnp.max(jnp.where(first, scores, -jnp.inf), axis=1, keepdims=True)
            top1 = jnp.max(jnp.where(first, -jnp.inf, scores), axis=1, keepdims=True)
            raised = jnp.exp2((scores - jnp.where(first, top0, top1)) * rate).astype(jnp.bfloat16)
            part = dot32(raised, values)
            norm = dot32(raised, mask)
            for tile in range(lo // LANES, hi // LANES):
                at = slice(tile * LANES - lo, (tile + 1) * LANES - lo)
                totals[tile] = part[:, at] if totals[tile] is None else totals[tile] + part[:, at]
                sums[tile] = norm[:, at] if sums[tile] is None else sums[tile] + norm[:, at]
        for tile in range(width // LANES):
            attended[b * WIN : (b + 1) * WIN, tile * LANES : (tile + 1) * LANES] = (totals[tile] / sums[tile]).astype(
                jnp.bfloat16
            )


def project(attended, resid, weight, bias, gain, hidden, out_ref):
    rows, width = hidden.shape
    step = 2 * LANES
    chunks = [slice(lo, lo + step) for lo in range(0, width, step)]
    squares = jnp.zeros((rows, 1), jnp.float32)
    for cols in chunks:
        h = dot32(attended[...], weight[:, cols])
        h = h + bias[cols].astype(jnp.float32).reshape(1, step)
        h = h + resid[:, :, cols].reshape(rows, step).astype(jnp.float32)
        hidden[:, cols] = h
        squares = squares + jnp.sum(h * h, axis=1, keepdims=True)
    scale = lax.rsqrt(squares * (1.0 / width) + EPS)
    for cols in chunks:
        out_ref[:, cols] = (hidden[:, cols] * scale * gain[cols].astype(jnp.float32).reshape(1, step)).astype(jnp.bfloat16)


def lent_attention_kernel(count_ref, qkv_hbm, resid_hbm, attended, resid, qkv, masks, sems):
    at = pl.ds(count_ref[0, 0] - 1, 1)
    qkv_copy = pltpu.make_async_copy(qkv_hbm.at[at], qkv, sems.at[0])
    resid_copy = pltpu.make_async_copy(resid_hbm.at[at], resid, sems.at[1])
    qkv_copy.start()
    resid_copy.start()
    width = resid.shape[2]
    make_masks(masks, width)
    qkv_copy.wait()
    attend(qkv, masks, attended, width)
    resid_copy.wait()


def lent_project_kernel(attended, resid, weight, bias, gain, out_ref, hidden):
    project(attended, resid, weight, bias, gain, hidden, out_ref)


def encode(qkv_hbm, resid_hbm, weight_hbm, bias_hbm, gain_hbm, out_ref, qkv, resid, weight, attended, hidden, bias, gain, masks, sems):
    at = pl.ds(0, qkv.shape[0])
    pairs = [(qkv_hbm.at[at], qkv), (weight_hbm, weight), (resid_hbm.at[at], resid), (bias_hbm, bias), (gain_hbm, gain)]
    copies = [pltpu.make_async_copy(a, b, sems.at[i]) for i, (a, b) in enumerate(pairs)]
    for copy in copies:
        copy.start()
    width = resid.shape[2]
    make_masks(masks, width)
    copies[0].wait()
    attend(qkv, masks, attended, width)
    for copy in copies[1:]:
        copy.wait()
    project(attended, resid, weight, bias, gain, hidden, out_ref)


def split_index(index, n_seq, cap):
    step = index // (GROUP * cap)
    rest = index - step * (GROUP * cap)
    patch = rest // cap
    return step, patch, rest - patch * cap


def own_kernel(
    n_seq, cap, peer, count_ref, send_ref, me_ref, slot_ref, row_ref,
    qkv_hbm, resid_hbm, weight_hbm, bias_hbm, gain_hbm,
    packed_ref, borrow_ref, place_ref, normed, *scratch,
):
    rows = normed.shape[0]
    slots = n_seq * cap
    sent = slots * GROUP
    tokens = rows // GROUP
    me = me_ref[0, 0]
    encode(qkv_hbm, resid_hbm, weight_hbm, bias_hbm, gain_hbm, normed, *scratch)

    step, patch, rank = split_index(lax.broadcasted_iota(jnp.int32, (sent, 1), 0), n_seq, cap)
    row_code = (peer(me, step, 1) * cap + rank) * GROUP + patch
    token = lax.broadcasted_iota(jnp.int32, (tokens, rows), 0)
    column = lax.broadcasted_iota(jnp.int32, (tokens, rows), 1)
    spread = one_hot((column >= token * GROUP) & (column < (token + 1) * GROUP))
    slot = jnp.broadcast_to(slot_ref[...].astype(jnp.float32), (16, tokens)).astype(jnp.bfloat16)
    slot = dot32(slot, spread)[:1].astype(jnp.int32)
    index = lax.broadcasted_iota(jnp.int32, (1, rows), 1)
    col_code = slot * GROUP + jnp.bitwise_and(index, GROUP - 1)
    kept = (count_ref[0, 0] - send_ref[0, 0]) * WIN
    last = rows - WIN
    own = one_hot(row_code == jnp.where(index < kept, col_code, -1))
    packed_ref[...] = dot32(own, normed[...]).astype(jnp.bfloat16)
    borrow_ref[...] = one_hot(row_code == jnp.where(kept > last, -1, col_code[:, last:]))

    step, patch, rank = split_index(lax.broadcasted_iota(jnp.int32, (1, sent), 1), n_seq, cap)
    arrive = peer(me, step, -1) * cap + rank
    pick = one_hot(lax.broadcasted_iota(jnp.int32, (slots, sent), 0) == arrive)
    target = jnp.broadcast_to(row_ref[...].astype(jnp.float32), (16, slots)).astype(jnp.bfloat16)
    target = dot32(target, pick)[:1].astype(jnp.int32)
    out_row = lax.broadcasted_iota(jnp.int32, (tokens, sent), 0)
    for j in range(GROUP):
        place_ref[j * tokens : (j + 1) * tokens, :] = one_hot((target == out_row) & (patch == j))


def in_hbm(*arrays):
    return [pltpu.with_memory_space_constraint(a, pltpu.HBM) for a in arrays]


def encode_lent(count, qkv, resid, weight, bias, gain):
    width = resid.shape[2]
    vmem = pl.BlockSpec(memory_space=pltpu.VMEM)
    hbm = pl.BlockSpec(memory_space=pltpu.HBM)
    small = pltpu.CompilerParams(vmem_limit_bytes=16 << 20)
    attended, rows = pl.pallas_call(
        lent_attention_kernel,
        out_shape=(
            jax.ShapeDtypeStruct((WIN, width), jnp.bfloat16),
            jax.ShapeDtypeStruct((1, WIN, width), jnp.bfloat16),
        ),
        in_specs=[pl.BlockSpec(memory_space=pltpu.SMEM), hbm, hbm],
        out_specs=(vmem, vmem),
        scratch_shapes=[pltpu.VMEM((1, WIN, 3 * width), jnp.bfloat16), mask_scratch(width), pltpu.SemaphoreType.DMA((2,))],
        compiler_params=small,
        cost_estimate=pl.CostEstimate(
            flops=1 << 30, bytes_accessed=1 << 20, transcendentals=WIN * WIN * HEADS
        ),
    )(count, *in_hbm(qkv, resid))
    return pl.pallas_call(
        lent_project_kernel,
        out_shape=jax.ShapeDtypeStruct((WIN, width), jnp.bfloat16),
        in_specs=[vmem] * 5,
        out_specs=vmem,
        scratch_shapes=[pltpu.VMEM((WIN, width), jnp.float32)],
        compiler_params=small,
        cost_estimate=pl.CostEstimate(
            flops=2 * WIN * width * width, bytes_accessed=2 * (width * width + 3 * WIN * width), transcendentals=0
        ),
    )(attended, rows, weight, bias, gain)


def encode_own(kernel, blocks, scalars, slots, qkv, resid, weight, bias, gain, out_shape, extra):
    width = resid.shape[2]
    rows = blocks * WIN
    vmem = pl.BlockSpec(memory_space=pltpu.VMEM)
    smem = pl.BlockSpec(memory_space=pltpu.SMEM)
    hbm = pl.BlockSpec(memory_space=pltpu.HBM)
    return pl.pallas_call(
        kernel,
        out_shape=out_shape,
        in_specs=[smem] * len(scalars) + [vmem] * len(slots) + [hbm] * 5,
        out_specs=jax.tree.map(lambda _: vmem, out_shape),
        scratch_shapes=extra
        + [
            pltpu.VMEM((blocks, WIN, 3 * width), jnp.bfloat16),
            pltpu.VMEM((blocks, WIN, width), jnp.bfloat16),
            pltpu.VMEM((width, width), jnp.bfloat16),
            pltpu.VMEM((rows, width), jnp.bfloat16),
            pltpu.VMEM((rows, width), jnp.float32),
            pltpu.VMEM((width,), jnp.bfloat16),
            pltpu.VMEM((width,), jnp.bfloat16),
            mask_scratch(width),
            pltpu.SemaphoreType.DMA((5,)),
        ],
        compiler_params=pltpu.CompilerParams(vmem_limit_bytes=24 << 20),
        cost_estimate=pl.CostEstimate(
            flops=2 * rows * width * width + 8 * rows * WIN * width,
            bytes_accessed=2 * (width * width + 5 * rows * width),
            transcendentals=rows * WIN * HEADS,
        ),
    )(*scalars, *slots, *in_hbm(qkv, resid, weight, bias, gain))


def pack_kernel(packed_ref, borrow_ref, borrowed_ref, *out_refs):
    total = packed_ref[...].astype(jnp.float32) + dot32(borrow_ref[...], borrowed_ref[...])
    chunk = out_refs[0].shape[0]
    for step, out_ref in enumerate(out_refs):
        out_ref[...] = total[step * chunk : (step + 1) * chunk].astype(jnp.bfloat16)


def place_kernel(place_ref, *refs):
    *in_refs, out_hbm, out, sems = refs
    tokens = out.shape[0]
    chunks = [ref[...].astype(jnp.float32) for ref in in_refs]
    arrived = chunks[0] if len(chunks) == 1 else jnp.concatenate(chunks, axis=0)
    arrived = arrived.astype(jnp.bfloat16)
    width = arrived.shape[1]
    copies = []
    for j in range(GROUP):
        cols = slice(j * width, (j + 1) * width)
        out[:, cols] = dot32(place_ref[j * tokens : (j + 1) * tokens, :], arrived).astype(jnp.bfloat16)
        copies.append(pltpu.make_async_copy(out.at[:, cols], out_hbm.at[:, cols], sems.at[j]))
        copies[-1].start()
    for copy in copies:
        copy.wait()


def exchange_steps(n_seq):
    return [0] + [dz * CORES + dc for dc in range(CORES) for dz in range(n_seq // CORES - 1, 0, -1)] + [1]


def chip_peer(n_seq, me, step, sign):
    flip = jnp.zeros_like(step)
    for i, bits in enumerate(exchange_steps(n_seq)):
        flip = jnp.where(step == i, bits, flip)
    return jnp.bitwise_xor(me, flip)


def per_device(
    qkv, resid, block_count, send_count, send_slot, lm_row, out_weight, out_bias, norm_gain
):
    width = resid.shape[2]
    row_total = send_slot.shape[1]
    tokens = WIN // GROUP
    blocks = row_total // tokens
    n_seq = lax.axis_size("seq")
    n_enc = lax.axis_size("enc")
    slots = lm_row.shape[1]
    cap = slots // n_seq
    chunk = GROUP * cap
    sent = slots * GROUP
    vmem = pl.BlockSpec(memory_space=pltpu.VMEM)
    small = pltpu.CompilerParams(vmem_limit_bytes=16 << 20)

    def rows_of(count, columns=width):
        return jax.ShapeDtypeStruct((count, columns), jnp.bfloat16)

    data = (qkv, resid, out_weight, out_bias, norm_gain)
    lent = encode_lent(block_count, *data)
    borrowed = lax.ppermute(lent, "enc", [((i - 1) % n_enc, i) for i in range(n_enc)])

    by_steps = chunk % 8 == 0 and n_seq & (n_seq - 1) == 0
    peer = functools.partial(chip_peer, n_seq) if by_steps else lambda me, step, sign: step
    me = lax.axis_index("seq").astype(jnp.int32).reshape(1, 1)
    packed, borrow, place = encode_own(
        functools.partial(own_kernel, n_seq, cap, peer), blocks,
        [block_count, send_count, me], [send_slot, lm_row], *data,
        (rows_of(sent), rows_of(sent, WIN), rows_of(GROUP * row_total, sent)),
        [pltpu.VMEM((row_total * GROUP, width), jnp.bfloat16)],
    )
    pieces = n_seq if by_steps else 1
    outgoing = pl.pallas_call(
        pack_kernel,
        out_shape=[rows_of(sent // pieces)] * pieces,
        in_specs=[vmem] * 3,
        out_specs=[vmem] * pieces,
        compiler_params=small,
    )(packed, borrow, borrowed)

    if by_steps:
        arrived = [outgoing[0]]
        for part, bits in list(zip(outgoing, exchange_steps(n_seq)))[1:]:
            arrived.append(lax.ppermute(part, "seq", [(i, i ^ bits) for i in range(n_seq)]))
    else:
        arrived = [
            lax.all_to_all(
                outgoing[0].reshape(n_seq, chunk, width), "seq", split_axis=0, concat_axis=0, tiled=True
            ).reshape(sent, width)
        ]
    placed = pl.pallas_call(
        place_kernel,
        out_shape=rows_of(row_total, GROUP * width),
        in_specs=[vmem] * (1 + pieces),
        out_specs=pl.BlockSpec(memory_space=pltpu.HBM),
        scratch_shapes=[pltpu.VMEM((row_total, GROUP * width), jnp.bfloat16), pltpu.SemaphoreType.DMA((GROUP,))],
        compiler_params=small,
    )(place, *arrived)
    return placed[None]


def solution(mesh):
    placed = (
        P("enc", "seq", None),
        P("enc", "seq", None),
        P("enc", "seq"),
        P("enc", "seq"),
        P("enc", "seq"),
        P("enc", "seq"),
        P(),
        P(),
        P(),
    )
    return jax.shard_map(
        per_device, mesh=mesh, in_specs=placed, out_specs=P("enc", "seq", None), check_vma=False
    )
```

```python
import functools
import math

import jax
import jax.numpy as jnp
from jax import lax
from jax.experimental import pallas as pl
from jax.experimental.pallas import tpu as pltpu
from jax.sharding import PartitionSpec as P

HEADS = 16
WIN = 64
LANES = 128
GROUP = 4
EPS = 1e-6
CORES = 2

NT = (((1,), (1,)), ((), ()))


def dot32(a, b):
    return jnp.dot(a, b, preferred_element_type=jnp.float32)


def one_hot(match):
    return match.astype(jnp.float32).astype(jnp.bfloat16)


def head_pairs(width):
    head = width // HEADS
    spans = []
    for start in range(0, width, 2 * head):
        lo = start // LANES * LANES
        spans.append((start, lo, -(-(start + 2 * head) // LANES) * LANES))
    return spans


def mask_period(width):
    return LANES // math.gcd(LANES, 2 * (width // HEADS))


def mask_scratch(width):
    return pltpu.VMEM((mask_period(width), 2 * WIN, 2 * LANES), jnp.bfloat16)


def make_masks(masks, width):
    head = width // HEADS
    for i in range(masks.shape[0]):
        start, lo, hi = head_pairs(width)[i]
        column = lax.broadcasted_iota(jnp.int32, masks.shape[1:], 1) + lo
        row = lax.broadcasted_iota(jnp.int32, masks.shape[1:], 0)
        begin = jnp.where(row < WIN, start, start + head)
        masks[i] = one_hot((column >= begin) & (column < begin + head))


def attend(qkv, masks, attended, width):
    rate = math.log2(math.e) / math.sqrt(width // HEADS)
    first = lax.broadcasted_iota(jnp.int32, (WIN, 2 * WIN), 1) < WIN
    for b in range(qkv.shape[0]):
        totals = [None] * (width // LANES)
        sums = [None] * (width // LANES)
        for pair, (_, lo, hi) in enumerate(head_pairs(width)):
            mask = masks[pair % masks.shape[0]]
            kw = qkv[b, :, width + lo : width + hi]
            vw = qkv[b, :, 2 * width + lo : 2 * width + hi]
            keys = jnp.concatenate([kw, kw], axis=0) * mask
            values = jnp.concatenate([vw, vw], axis=0) * mask
            scores = lax.dot_general(qkv[b, :, lo:hi], keys, NT, preferred_element_type=jnp.float32)
            top0 = jnp.max(jnp.where(first, scores, -jnp.inf), axis=1, keepdims=True)
            top1 = jnp.max(jnp.where(first, -jnp.inf, scores), axis=1, keepdims=True)
            raised = jnp.exp2((scores - jnp.where(first, top0, top1)) * rate).astype(jnp.bfloat16)
            part = dot32(raised, values)
            norm = dot32(raised, mask)
            for tile in range(lo // LANES, hi // LANES):
                at = slice(tile * LANES - lo, (tile + 1) * LANES - lo)
                totals[tile] = part[:, at] if totals[tile] is None else totals[tile] + part[:, at]
                sums[tile] = norm[:, at] if sums[tile] is None else sums[tile] + norm[:, at]
        for tile in range(width // LANES):
            attended[b * WIN : (b + 1) * WIN, tile * LANES : (tile + 1) * LANES] = (totals[tile] / sums[tile]).astype(
                jnp.bfloat16
            )


def project(attended, resid, weight, bias, gain, hidden, out_ref):
    rows, width = hidden.shape
    step = 2 * LANES
    chunks = [slice(lo, lo + step) for lo in range(0, width, step)]
    squares = jnp.zeros((rows, 1), jnp.float32)
    for cols in chunks:
        h = dot32(attended[...], weight[:, cols])
        h = h + bias[cols].astype(jnp.float32).reshape(1, step)
        h = h + resid[:, :, cols].reshape(rows, step).astype(jnp.float32)
        hidden[:, cols] = h
        squares = squares + jnp.sum(h * h, axis=1, keepdims=True)
    scale = lax.rsqrt(squares * (1.0 / width) + EPS)
    for cols in chunks:
        out_ref[:, cols] = (hidden[:, cols] * scale * gain[cols].astype(jnp.float32).reshape(1, step)).astype(jnp.bfloat16)


def lent_attention_kernel(count_ref, qkv_hbm, resid_hbm, attended, resid, qkv, masks, sems):
    at = pl.ds(count_ref[0, 0] - 1, 1)
    qkv_copy = pltpu.make_async_copy(qkv_hbm.at[at], qkv, sems.at[0])
    resid_copy = pltpu.make_async_copy(resid_hbm.at[at], resid, sems.at[1])
    qkv_copy.start()
    resid_copy.start()
    width = resid.shape[2]
    make_masks(masks, width)
    qkv_copy.wait()
    attend(qkv, masks, attended, width)
    resid_copy.wait()


def lent_project_kernel(attended, resid, weight, bias, gain, out_ref, hidden):
    project(attended, resid, weight, bias, gain, hidden, out_ref)


def encode(qkv_hbm, resid_hbm, weight_hbm, bias_hbm, gain_hbm, out_ref, qkv, resid, weight, attended, hidden, bias, gain, masks, sems):
    at = pl.ds(0, qkv.shape[0])
    pairs = [(qkv_hbm.at[at], qkv), (weight_hbm, weight), (resid_hbm.at[at], resid), (bias_hbm, bias), (gain_hbm, gain)]
    copies = [pltpu.make_async_copy(a, b, sems.at[i]) for i, (a, b) in enumerate(pairs)]
    for copy in copies:
        copy.start()
    width = resid.shape[2]
    make_masks(masks, width)
    copies[0].wait()
    attend(qkv, masks, attended, width)
    for copy in copies[1:]:
        copy.wait()
    project(attended, resid, weight, bias, gain, hidden, out_ref)


def split_index(index, n_seq, cap):
    step = index // (GROUP * cap)
    rest = index - step * (GROUP * cap)
    patch = rest // cap
    return step, patch, rest - patch * cap


def own_kernel(
    n_seq, cap, peer, count_ref, send_ref, me_ref, slot_ref, row_ref,
    qkv_hbm, resid_hbm, weight_hbm, bias_hbm, gain_hbm,
    packed_ref, borrow_ref, place_ref, normed, *scratch,
):
    rows = normed.shape[0]
    slots = n_seq * cap
    sent = slots * GROUP
    tokens = rows // GROUP
    me = me_ref[0, 0]
    encode(qkv_hbm, resid_hbm, weight_hbm, bias_hbm, gain_hbm, normed, *scratch)

    step, patch, rank = split_index(lax.broadcasted_iota(jnp.int32, (sent, 1), 0), n_seq, cap)
    row_code = (peer(me, step, 1) * cap + rank) * GROUP + patch
    token = lax.broadcasted_iota(jnp.int32, (tokens, rows), 0)
    column = lax.broadcasted_iota(jnp.int32, (tokens, rows), 1)
    spread = one_hot((column >= token * GROUP) & (column < (token + 1) * GROUP))
    slot = jnp.broadcast_to(slot_ref[...].astype(jnp.float32), (16, tokens)).astype(jnp.bfloat16)
    slot = dot32(slot, spread)[:1].astype(jnp.int32)
    index = lax.broadcasted_iota(jnp.int32, (1, rows), 1)
    col_code = slot * GROUP + jnp.bitwise_and(index, GROUP - 1)
    kept = (count_ref[0, 0] - send_ref[0, 0]) * WIN
    last = rows - WIN
    own = one_hot(row_code == jnp.where(index < kept, col_code, -1))
    packed_ref[...] = dot32(own, normed[...]).astype(jnp.bfloat16)
    borrow_ref[...] = one_hot(row_code == jnp.where(kept > last, -1, col_code[:, last:]))

    step, patch, rank = split_index(lax.broadcasted_iota(jnp.int32, (1, sent), 1), n_seq, cap)
    arrive = peer(me, step, -1) * cap + rank
    pick = one_hot(lax.broadcasted_iota(jnp.int32, (slots, sent), 0) == arrive)
    target = jnp.broadcast_to(row_ref[...].astype(jnp.float32), (16, slots)).astype(jnp.bfloat16)
    target = dot32(target, pick)[:1].astype(jnp.int32)
    out_row = lax.broadcasted_iota(jnp.int32, (tokens, sent), 0)
    for j in range(GROUP):
        place_ref[j * tokens : (j + 1) * tokens, :] = one_hot((target == out_row) & (patch == j))


def in_hbm(*arrays):
    return [pltpu.with_memory_space_constraint(a, pltpu.HBM) for a in arrays]


def encode_lent(count, qkv, resid, weight, bias, gain):
    width = resid.shape[2]
    vmem = pl.BlockSpec(memory_space=pltpu.VMEM)
    hbm = pl.BlockSpec(memory_space=pltpu.HBM)
    small = pltpu.CompilerParams(vmem_limit_bytes=16 << 20)
    attended, rows = pl.pallas_call(
        lent_attention_kernel,
        out_shape=(
            jax.ShapeDtypeStruct((WIN, width), jnp.bfloat16),
            jax.ShapeDtypeStruct((1, WIN, width), jnp.bfloat16),
        ),
        in_specs=[pl.BlockSpec(memory_space=pltpu.SMEM), hbm, hbm],
        out_specs=(vmem, vmem),
        scratch_shapes=[pltpu.VMEM((1, WIN, 3 * width), jnp.bfloat16), mask_scratch(width), pltpu.SemaphoreType.DMA((2,))],
        compiler_params=small,
        cost_estimate=pl.CostEstimate(
            flops=1 << 30, bytes_accessed=1 << 20, transcendentals=WIN * WIN * HEADS
        ),
    )(count, *in_hbm(qkv, resid))
    return pl.pallas_call(
        lent_project_kernel,
        out_shape=jax.ShapeDtypeStruct((WIN, width), jnp.bfloat16),
        in_specs=[vmem] * 5,
        out_specs=vmem,
        scratch_shapes=[pltpu.VMEM((WIN, width), jnp.float32)],
        compiler_params=small,
        cost_estimate=pl.CostEstimate(
            flops=2 * WIN * width * width, bytes_accessed=2 * (width * width + 3 * WIN * width), transcendentals=0
        ),
    )(attended, rows, weight, bias, gain)


def encode_own(kernel, blocks, scalars, slots, qkv, resid, weight, bias, gain, out_shape, extra):
    width = resid.shape[2]
    rows = blocks * WIN
    vmem = pl.BlockSpec(memory_space=pltpu.VMEM)
    smem = pl.BlockSpec(memory_space=pltpu.SMEM)
    hbm = pl.BlockSpec(memory_space=pltpu.HBM)
    return pl.pallas_call(
        kernel,
        out_shape=out_shape,
        in_specs=[smem] * len(scalars) + [vmem] * len(slots) + [hbm] * 5,
        out_specs=jax.tree.map(lambda _: vmem, out_shape),
        scratch_shapes=extra
        + [
            pltpu.VMEM((blocks, WIN, 3 * width), jnp.bfloat16),
            pltpu.VMEM((blocks, WIN, width), jnp.bfloat16),
            pltpu.VMEM((width, width), jnp.bfloat16),
            pltpu.VMEM((rows, width), jnp.bfloat16),
            pltpu.VMEM((rows, width), jnp.float32),
            pltpu.VMEM((width,), jnp.bfloat16),
            pltpu.VMEM((width,), jnp.bfloat16),
            mask_scratch(width),
            pltpu.SemaphoreType.DMA((5,)),
        ],
        compiler_params=pltpu.CompilerParams(vmem_limit_bytes=24 << 20),
        cost_estimate=pl.CostEstimate(
            flops=2 * rows * width * width + 8 * rows * WIN * width,
            bytes_accessed=2 * (width * width + 5 * rows * width),
            transcendentals=rows * WIN * HEADS,
        ),
    )(*scalars, *slots, *in_hbm(qkv, resid, weight, bias, gain))


def pack_kernel(packed_ref, borrow_ref, borrowed_ref, *out_refs):
    total = packed_ref[...].astype(jnp.float32) + dot32(borrow_ref[...], borrowed_ref[...])
    chunk = out_refs[0].shape[0]
    for step, out_ref in enumerate(out_refs):
        out_ref[...] = total[step * chunk : (step + 1) * chunk].astype(jnp.bfloat16)


def place_kernel(place_ref, *refs):
    *in_refs, out_hbm, out, sems = refs
    tokens = out.shape[0]
    chunks = [ref[...].astype(jnp.float32) for ref in in_refs]
    arrived = chunks[0] if len(chunks) == 1 else jnp.concatenate(chunks, axis=0)
    arrived = arrived.astype(jnp.bfloat16)
    width = arrived.shape[1]
    copies = []
    for j in range(GROUP):
        cols = slice(j * width, (j + 1) * width)
        out[:, cols] = dot32(place_ref[j * tokens : (j + 1) * tokens, :], arrived).astype(jnp.bfloat16)
        copies.append(pltpu.make_async_copy(out.at[:, cols], out_hbm.at[:, cols], sems.at[j]))
        copies[-1].start()
    for copy in copies:
        copy.wait()


def exchange_steps(n_seq):
    n_z = n_seq // CORES
    return [(0, 0)] + [(dz, dc) for dz in range(1, n_z) for dc in range(CORES)] + [(0, 1)]


def chip_peer(n_seq, me, step, sign):
    n_z = n_seq // CORES
    offset = jnp.zeros_like(step)
    flip = jnp.zeros_like(step)
    for i, (dz, dc) in enumerate(exchange_steps(n_seq)):
        offset = jnp.where(step == i, dz, offset)
        flip = jnp.where(step == i, dc, flip)
    z = me // CORES + sign * offset
    z = jnp.where(z >= n_z, z - n_z, jnp.where(z < 0, z + n_z, z))
    return z * CORES + jnp.bitwise_xor(jnp.bitwise_and(me, 1), flip)


def per_device(
    qkv, resid, block_count, send_count, send_slot, lm_row, out_weight, out_bias, norm_gain
):
    width = resid.shape[2]
    row_total = send_slot.shape[1]
    tokens = WIN // GROUP
    blocks = row_total // tokens
    n_seq = lax.axis_size("seq")
    n_enc = lax.axis_size("enc")
    slots = lm_row.shape[1]
    cap = slots // n_seq
    chunk = GROUP * cap
    sent = slots * GROUP
    vmem = pl.BlockSpec(memory_space=pltpu.VMEM)
    small = pltpu.CompilerParams(vmem_limit_bytes=16 << 20)

    def rows_of(count, columns=width):
        return jax.ShapeDtypeStruct((count, columns), jnp.bfloat16)

    data = (qkv, resid, out_weight, out_bias, norm_gain)
    lent = encode_lent(block_count, *data)
    borrowed = lax.ppermute(lent, "enc", [((i - 1) % n_enc, i) for i in range(n_enc)])

    by_steps = chunk % 8 == 0 and n_seq % CORES == 0
    peer = functools.partial(chip_peer, n_seq) if by_steps else lambda me, step, sign: step
    me = lax.axis_index("seq").astype(jnp.int32).reshape(1, 1)
    packed, borrow, place = encode_own(
        functools.partial(own_kernel, n_seq, cap, peer), blocks,
        [block_count, send_count, me], [send_slot, lm_row], *data,
        (rows_of(sent), rows_of(sent, WIN), rows_of(GROUP * row_total, sent)),
        [pltpu.VMEM((row_total * GROUP, width), jnp.bfloat16)],
    )
    pieces = n_seq if by_steps else 1
    outgoing = pl.pallas_call(
        pack_kernel,
        out_shape=[rows_of(sent // pieces)] * pieces,
        in_specs=[vmem] * 3,
        out_specs=[vmem] * pieces,
        compiler_params=small,
    )(packed, borrow, borrowed)

    if by_steps:
        n_z = n_seq // CORES
        arrived = [outgoing[0]]
        for part, (dz, dc) in list(zip(outgoing, exchange_steps(n_seq)))[1:]:
            route = [(i, (i // CORES + dz) % n_z * CORES + (i + dc) % CORES) for i in range(n_seq)]
            arrived.append(lax.ppermute(part, "seq", route))
    else:
        arrived = [
            lax.all_to_all(
                outgoing[0].reshape(n_seq, chunk, width), "seq", split_axis=0, concat_axis=0, tiled=True
            ).reshape(sent, width)
        ]
    placed = pl.pallas_call(
        place_kernel,
        out_shape=rows_of(row_total, GROUP * width),
        in_specs=[vmem] * (1 + pieces),
        out_specs=pl.BlockSpec(memory_space=pltpu.HBM),
        scratch_shapes=[pltpu.VMEM((row_total, GROUP * width), jnp.bfloat16), pltpu.SemaphoreType.DMA((GROUP,))],
        compiler_params=small,
    )(place, *arrived)
    return placed[None]


def solution(mesh):
    placed = (
        P("enc", "seq", None),
        P("enc", "seq", None),
        P("enc", "seq"),
        P("enc", "seq"),
        P("enc", "seq"),
        P("enc", "seq"),
        P(),
        P(),
        P(),
    )
    return jax.shard_map(
        per_device, mesh=mesh, in_specs=placed, out_specs=P("enc", "seq", None), check_vma=False
    )
```

```python
import functools
import math

import jax
import jax.numpy as jnp
from jax import lax
from jax.experimental import pallas as pl
from jax.experimental.pallas import tpu as pltpu
from jax.sharding import PartitionSpec as P

HEADS = 16
WIN = 64
LANES = 128
GROUP = 4
EPS = 1e-6
CORES = 2

NT = (((1,), (1,)), ((), ()))


def dot32(a, b):
    return jnp.dot(a, b, preferred_element_type=jnp.float32)


def one_hot(match):
    return match.astype(jnp.float32).astype(jnp.bfloat16)


def attend(q, k, v, out_ref, row0, width):
    head = width // HEADS
    rate = 1.0 / math.sqrt(head)
    totals = [None] * (width // LANES)
    sums = [None] * (width // LANES)
    first_half = lax.broadcasted_iota(jnp.int32, (WIN, 2 * WIN), 1) < WIN
    for pair in range(HEADS // 2):
        start = 2 * pair * head
        lo = start // LANES * LANES
        hi = -(-(start + 2 * head) // LANES) * LANES
        column = lax.broadcasted_iota(jnp.int32, (2 * WIN, hi - lo), 1) + lo
        row = lax.broadcasted_iota(jnp.int32, (2 * WIN, hi - lo), 0)
        begin = jnp.where(row < WIN, start, start + head)
        mask = one_hot((column >= begin) & (column < begin + head))
        kw, vw = k(lo, hi), v(lo, hi)
        keys = jnp.concatenate([kw, kw], axis=0) * mask
        values = jnp.concatenate([vw, vw], axis=0) * mask
        scores = lax.dot_general(q(lo, hi), keys, NT, preferred_element_type=jnp.float32)
        top0 = jnp.max(jnp.where(first_half, scores, -jnp.inf), axis=1, keepdims=True)
        top1 = jnp.max(jnp.where(first_half, -jnp.inf, scores), axis=1, keepdims=True)
        raised = jnp.exp((scores - jnp.where(first_half, top0, top1)) * rate).astype(jnp.bfloat16)
        part = dot32(raised, values)
        norm = dot32(raised, mask)
        for tile in range(lo // LANES, hi // LANES):
            at = slice(tile * LANES - lo, (tile + 1) * LANES - lo)
            totals[tile] = part[:, at] if totals[tile] is None else totals[tile] + part[:, at]
            sums[tile] = norm[:, at] if sums[tile] is None else sums[tile] + norm[:, at]
    for tile in range(width // LANES):
        out_ref[row0 : row0 + WIN, tile * LANES : (tile + 1) * LANES] = (totals[tile] / sums[tile]).astype(
            jnp.bfloat16
        )


def encode(
    slot, qkv_hbm, resid_hbm, weight_hbm, bias_hbm, gain_hbm, out_ref,
    qkv, resid, weight, attended, hidden, bias_ref, gain_ref, sems,
):
    blocks = qkv.shape[0]
    width = resid.shape[2]
    at = pl.ds(slot, blocks)
    pairs = [
        (qkv_hbm.at[at], qkv), (weight_hbm, weight), (resid_hbm.at[at], resid), (bias_hbm, bias_ref), (gain_hbm, gain_ref)
    ]
    copies = [pltpu.make_async_copy(a, b, sems.at[i]) for i, (a, b) in enumerate(pairs)]
    for copy in copies:
        copy.start()
    copies[0].wait()
    for b in range(blocks):
        attend(
            lambda lo, hi, b=b: qkv[b, :, lo:hi],
            lambda lo, hi, b=b: qkv[b, :, width + lo : width + hi],
            lambda lo, hi, b=b: qkv[b, :, 2 * width + lo : 2 * width + hi],
            attended, b * WIN, width,
        )
    for copy in copies[1:]:
        copy.wait()
    rows = blocks * WIN
    squares = jnp.zeros((rows, 1), jnp.float32)
    step = 2 * LANES
    for lo in range(0, width, step):
        cols = slice(lo, lo + step)
        h = dot32(attended[...], weight[:, cols])
        h = h + bias_ref[cols].astype(jnp.float32).reshape(1, step)
        h = h + resid[:, :, cols].reshape(rows, step).astype(jnp.float32)
        hidden[:, cols] = h
        squares = squares + jnp.sum(h * h, axis=1, keepdims=True)
    scale = lax.rsqrt(squares * (1.0 / width) + EPS)
    for lo in range(0, width, step):
        cols = slice(lo, lo + step)
        gain = gain_ref[cols].astype(jnp.float32).reshape(1, step)
        out_ref[:, cols] = (hidden[:, cols] * scale * gain).astype(jnp.bfloat16)


def lent_kernel(count_ref, qkv_hbm, resid_hbm, weight_hbm, bias_hbm, gain_hbm, out_ref, *scratch):
    encode(count_ref[0, 0] - 1, qkv_hbm, resid_hbm, weight_hbm, bias_hbm, gain_hbm, out_ref, *scratch)


def split_index(index, n_seq, cap):
    step = index // (GROUP * cap)
    rest = index - step * (GROUP * cap)
    patch = rest // cap
    return step, patch, rest - patch * cap


def own_kernel(
    n_seq, cap, peer, count_ref, send_ref, me_ref, slot_ref, row_ref,
    qkv_hbm, resid_hbm, weight_hbm, bias_hbm, gain_hbm,
    packed_ref, borrow_ref, place_ref, normed, *scratch,
):
    rows = normed.shape[0]
    slots = n_seq * cap
    sent = slots * GROUP
    tokens = rows // GROUP
    me = me_ref[0, 0]
    encode(0, qkv_hbm, resid_hbm, weight_hbm, bias_hbm, gain_hbm, normed, *scratch)

    step, patch, rank = split_index(lax.broadcasted_iota(jnp.int32, (sent, 1), 0), n_seq, cap)
    row_code = (peer(me, step, 1) * cap + rank) * GROUP + patch
    token = lax.broadcasted_iota(jnp.int32, (tokens, rows), 0)
    column = lax.broadcasted_iota(jnp.int32, (tokens, rows), 1)
    spread = one_hot((column >= token * GROUP) & (column < (token + 1) * GROUP))
    slot = jnp.broadcast_to(slot_ref[...].astype(jnp.float32), (16, tokens)).astype(jnp.bfloat16)
    slot = dot32(slot, spread)[:1].astype(jnp.int32)
    index = lax.broadcasted_iota(jnp.int32, (1, rows), 1)
    col_code = slot * GROUP + jnp.bitwise_and(index, GROUP - 1)
    kept = (count_ref[0, 0] - send_ref[0, 0]) * WIN
    last = rows - WIN
    own = one_hot(row_code == jnp.where(index < kept, col_code, -1))
    packed_ref[...] = dot32(own, normed[...]).astype(jnp.bfloat16)
    borrow_ref[...] = one_hot(row_code == jnp.where(kept > last, -1, col_code[:, last:]))

    step, patch, rank = split_index(lax.broadcasted_iota(jnp.int32, (1, sent), 1), n_seq, cap)
    arrive = peer(me, step, -1) * cap + rank
    pick = one_hot(lax.broadcasted_iota(jnp.int32, (slots, sent), 0) == arrive)
    target = jnp.broadcast_to(row_ref[...].astype(jnp.float32), (16, slots)).astype(jnp.bfloat16)
    target = dot32(target, pick)[:1].astype(jnp.int32)
    out_row = lax.broadcasted_iota(jnp.int32, (tokens, sent), 0)
    for j in range(GROUP):
        place_ref[j * tokens : (j + 1) * tokens, :] = one_hot((target == out_row) & (patch == j))


def encode_call(kernel, blocks, scalars, slots, qkv, resid, weight, bias, gain, out_shape, extra):
    width = resid.shape[2]
    rows = blocks * WIN
    vmem = pl.BlockSpec(memory_space=pltpu.VMEM)
    smem = pl.BlockSpec(memory_space=pltpu.SMEM)
    hbm = pl.BlockSpec(memory_space=pltpu.HBM)
    return pl.pallas_call(
        kernel,
        out_shape=out_shape,
        in_specs=[smem] * len(scalars) + [vmem] * len(slots) + [hbm] * 5,
        out_specs=jax.tree.map(lambda _: vmem, out_shape),
        scratch_shapes=extra
        + [
            pltpu.VMEM((blocks, WIN, 3 * width), jnp.bfloat16),
            pltpu.VMEM((blocks, WIN, width), jnp.bfloat16),
            pltpu.VMEM((width, width), jnp.bfloat16),
            pltpu.VMEM((rows, width), jnp.bfloat16),
            pltpu.VMEM((rows, width), jnp.float32),
            pltpu.VMEM((width,), jnp.bfloat16),
            pltpu.VMEM((width,), jnp.bfloat16),
            pltpu.SemaphoreType.DMA((5,)),
        ],
        compiler_params=pltpu.CompilerParams(vmem_limit_bytes=24 << 20),
        cost_estimate=pl.CostEstimate(
            flops=2 * rows * width * width + 8 * rows * WIN * width,
            bytes_accessed=2 * (width * width + 5 * rows * width),
            transcendentals=rows * WIN * HEADS,
        ),
    )(*scalars, *slots, *(pltpu.with_memory_space_constraint(a, pltpu.HBM) for a in (qkv, resid, weight, bias, gain)))


def pack_kernel(packed_ref, borrow_ref, borrowed_ref, *out_refs):
    total = packed_ref[...].astype(jnp.float32) + dot32(borrow_ref[...], borrowed_ref[...])
    chunk = out_refs[0].shape[0]
    for step, out_ref in enumerate(out_refs):
        out_ref[...] = total[step * chunk : (step + 1) * chunk].astype(jnp.bfloat16)


def place_kernel(place_ref, *refs):
    *in_refs, out_hbm, out, sems = refs
    tokens = out.shape[0]
    chunks = [ref[...].astype(jnp.float32) for ref in in_refs]
    arrived = chunks[0] if len(chunks) == 1 else jnp.concatenate(chunks, axis=0)
    arrived = arrived.astype(jnp.bfloat16)
    width = arrived.shape[1]
    copies = []
    for j in range(GROUP):
        cols = slice(j * width, (j + 1) * width)
        out[:, cols] = dot32(place_ref[j * tokens : (j + 1) * tokens, :], arrived).astype(jnp.bfloat16)
        copies.append(pltpu.make_async_copy(out.at[:, cols], out_hbm.at[:, cols], sems.at[j]))
        copies[-1].start()
    for copy in copies:
        copy.wait()


def exchange_steps(n_seq):
    n_z = n_seq // CORES
    offsets = sorted(range(1, n_z), key=lambda dz: (dz != n_z // 2, -dz))
    return [(0, 0)] + [(dz, dc) for dz in offsets for dc in range(CORES)] + [(0, 1)]


def chip_peer(n_seq, me, step, sign):
    n_z = n_seq // CORES
    offset = jnp.zeros_like(step)
    flip = jnp.zeros_like(step)
    for i, (dz, dc) in enumerate(exchange_steps(n_seq)):
        offset = jnp.where(step == i, dz, offset)
        flip = jnp.where(step == i, dc, flip)
    z = me // CORES + sign * offset
    z = jnp.where(z >= n_z, z - n_z, jnp.where(z < 0, z + n_z, z))
    return z * CORES + jnp.bitwise_xor(jnp.bitwise_and(me, 1), flip)


def per_device(
    qkv, resid, block_count, send_count, send_slot, lm_row, out_weight, out_bias, norm_gain
):
    width = resid.shape[2]
    row_total = send_slot.shape[1]
    tokens = WIN // GROUP
    blocks = row_total // tokens
    n_seq = lax.axis_size("seq")
    n_enc = lax.axis_size("enc")
    slots = lm_row.shape[1]
    cap = slots // n_seq
    chunk = GROUP * cap
    sent = slots * GROUP
    vmem = pl.BlockSpec(memory_space=pltpu.VMEM)
    small = pltpu.CompilerParams(vmem_limit_bytes=16 << 20)

    def rows_of(count, columns=width):
        return jax.ShapeDtypeStruct((count, columns), jnp.bfloat16)

    data = (qkv, resid, out_weight, out_bias, norm_gain)
    lent = encode_call(lent_kernel, 1, [block_count], [], *data, rows_of(WIN), [])
    borrowed = lax.ppermute(lent, "enc", [((i - 1) % n_enc, i) for i in range(n_enc)])

    by_steps = chunk % 8 == 0 and n_seq % CORES == 0
    peer = functools.partial(chip_peer, n_seq) if by_steps else lambda me, step, sign: step
    me = lax.axis_index("seq").astype(jnp.int32).reshape(1, 1)
    packed, borrow, place = encode_call(
        functools.partial(own_kernel, n_seq, cap, peer), blocks,
        [block_count, send_count, me], [send_slot, lm_row], *data,
        (rows_of(sent), rows_of(sent, WIN), rows_of(GROUP * row_total, sent)),
        [pltpu.VMEM((row_total * GROUP, width), jnp.bfloat16)],
    )
    pieces = n_seq if by_steps else 1
    outgoing = pl.pallas_call(
        pack_kernel,
        out_shape=[rows_of(sent // pieces)] * pieces,
        in_specs=[vmem] * 3,
        out_specs=[vmem] * pieces,
        compiler_params=small,
    )(packed, borrow, borrowed)

    if by_steps:
        n_z = n_seq // CORES
        arrived = [outgoing[0]]
        for part, (dz, dc) in list(zip(outgoing, exchange_steps(n_seq)))[1:]:
            route = [(i, (i // CORES + dz) % n_z * CORES + (i + dc) % CORES) for i in range(n_seq)]
            arrived.append(lax.ppermute(part, "seq", route))
    else:
        arrived = [
            lax.all_to_all(
                outgoing[0].reshape(n_seq, chunk, width), "seq", split_axis=0, concat_axis=0, tiled=True
            ).reshape(sent, width)
        ]
    placed = pl.pallas_call(
        place_kernel,
        out_shape=rows_of(row_total, GROUP * width),
        in_specs=[vmem] * (1 + pieces),
        out_specs=pl.BlockSpec(memory_space=pltpu.HBM),
        scratch_shapes=[pltpu.VMEM((row_total, GROUP * width), jnp.bfloat16), pltpu.SemaphoreType.DMA((GROUP,))],
        compiler_params=small,
    )(place, *arrived)
    return placed[None]


def solution(mesh):
    placed = (
        P("enc", "seq", None),
        P("enc", "seq", None),
        P("enc", "seq"),
        P("enc", "seq"),
        P("enc", "seq"),
        P("enc", "seq"),
        P(),
        P(),
        P(),
    )
    return jax.shard_map(
        per_device, mesh=mesh, in_specs=placed, out_specs=P("enc", "seq", None), check_vma=False
    )
```

```python
import functools
import math

import jax
import jax.numpy as jnp
from jax import lax
from jax.experimental import pallas as pl
from jax.experimental.pallas import tpu as pltpu
from jax.sharding import PartitionSpec as P

HEADS = 16
WIN = 64
LANES = 128
GROUP = 4
EPS = 1e-6
CORES = 2

NT = (((1,), (1,)), ((), ()))


def dot32(a, b):
    return jnp.dot(a, b, preferred_element_type=jnp.float32)


def one_hot(match):
    return match.astype(jnp.float32).astype(jnp.bfloat16)


def attend(q, k, v, out_ref, row0, width):
    head = width // HEADS
    rate = 1.0 / math.sqrt(head)
    totals = [None] * (width // LANES)
    sums = [None] * (width // LANES)
    first_half = lax.broadcasted_iota(jnp.int32, (WIN, 2 * WIN), 1) < WIN
    for pair in range(HEADS // 2):
        start = 2 * pair * head
        lo = start // LANES * LANES
        hi = -(-(start + 2 * head) // LANES) * LANES
        column = lax.broadcasted_iota(jnp.int32, (2 * WIN, hi - lo), 1) + lo
        row = lax.broadcasted_iota(jnp.int32, (2 * WIN, hi - lo), 0)
        begin = jnp.where(row < WIN, start, start + head)
        mask = one_hot((column >= begin) & (column < begin + head))
        kw, vw = k(lo, hi), v(lo, hi)
        keys = jnp.concatenate([kw, kw], axis=0) * mask
        values = jnp.concatenate([vw, vw], axis=0) * mask
        scores = lax.dot_general(q(lo, hi), keys, NT, preferred_element_type=jnp.float32)
        top0 = jnp.max(jnp.where(first_half, scores, -jnp.inf), axis=1, keepdims=True)
        top1 = jnp.max(jnp.where(first_half, -jnp.inf, scores), axis=1, keepdims=True)
        raised = jnp.exp((scores - jnp.where(first_half, top0, top1)) * rate).astype(jnp.bfloat16)
        part = dot32(raised, values)
        norm = dot32(raised, mask)
        for tile in range(lo // LANES, hi // LANES):
            at = slice(tile * LANES - lo, (tile + 1) * LANES - lo)
            totals[tile] = part[:, at] if totals[tile] is None else totals[tile] + part[:, at]
            sums[tile] = norm[:, at] if sums[tile] is None else sums[tile] + norm[:, at]
    for tile in range(width // LANES):
        out_ref[row0 : row0 + WIN, tile * LANES : (tile + 1) * LANES] = (totals[tile] / sums[tile]).astype(
            jnp.bfloat16
        )


def encode(
    slot, qkv_hbm, resid_hbm, weight_hbm, bias_hbm, gain_hbm, out_ref,
    qkv, resid, weight, attended, hidden, bias_ref, gain_ref, sems,
):
    blocks = qkv.shape[0]
    width = resid.shape[2]
    at = pl.ds(slot, blocks)
    pairs = [
        (qkv_hbm.at[at], qkv), (weight_hbm, weight), (resid_hbm.at[at], resid), (bias_hbm, bias_ref), (gain_hbm, gain_ref)
    ]
    copies = [pltpu.make_async_copy(a, b, sems.at[i]) for i, (a, b) in enumerate(pairs)]
    for copy in copies:
        copy.start()
    copies[0].wait()
    for b in range(blocks):
        attend(
            lambda lo, hi, b=b: qkv[b, :, lo:hi],
            lambda lo, hi, b=b: qkv[b, :, width + lo : width + hi],
            lambda lo, hi, b=b: qkv[b, :, 2 * width + lo : 2 * width + hi],
            attended, b * WIN, width,
        )
    for copy in copies[1:]:
        copy.wait()
    rows = blocks * WIN
    squares = jnp.zeros((rows, 1), jnp.float32)
    step = 2 * LANES
    for lo in range(0, width, step):
        cols = slice(lo, lo + step)
        h = dot32(attended[...], weight[:, cols])
        h = h + bias_ref[cols].astype(jnp.float32).reshape(1, step)
        h = h + resid[:, :, cols].reshape(rows, step).astype(jnp.float32)
        hidden[:, cols] = h
        squares = squares + jnp.sum(h * h, axis=1, keepdims=True)
    scale = lax.rsqrt(squares * (1.0 / width) + EPS)
    for lo in range(0, width, step):
        cols = slice(lo, lo + step)
        gain = gain_ref[cols].astype(jnp.float32).reshape(1, step)
        out_ref[:, cols] = (hidden[:, cols] * scale * gain).astype(jnp.bfloat16)


def lent_kernel(count_ref, qkv_hbm, resid_hbm, weight_hbm, bias_hbm, gain_hbm, out_ref, *scratch):
    encode(count_ref[0, 0] - 1, qkv_hbm, resid_hbm, weight_hbm, bias_hbm, gain_hbm, out_ref, *scratch)


def split_index(index, n_seq, cap):
    step = index // (GROUP * cap)
    rest = index - step * (GROUP * cap)
    patch = rest // cap
    return step, patch, rest - patch * cap


def own_kernel(
    n_seq, cap, peer, count_ref, send_ref, me_ref, slot_ref, row_ref,
    qkv_hbm, resid_hbm, weight_hbm, bias_hbm, gain_hbm,
    packed_ref, borrow_ref, place_ref, normed, *scratch,
):
    rows = normed.shape[0]
    slots = n_seq * cap
    sent = slots * GROUP
    tokens = rows // GROUP
    me = me_ref[0, 0]
    encode(0, qkv_hbm, resid_hbm, weight_hbm, bias_hbm, gain_hbm, normed, *scratch)

    step, patch, rank = split_index(lax.broadcasted_iota(jnp.int32, (sent, 1), 0), n_seq, cap)
    row_code = (peer(me, step, 1) * cap + rank) * GROUP + patch
    token = lax.broadcasted_iota(jnp.int32, (tokens, rows), 0)
    column = lax.broadcasted_iota(jnp.int32, (tokens, rows), 1)
    spread = one_hot((column >= token * GROUP) & (column < (token + 1) * GROUP))
    slot = jnp.broadcast_to(slot_ref[...].astype(jnp.float32), (16, tokens)).astype(jnp.bfloat16)
    slot = dot32(slot, spread)[:1].astype(jnp.int32)
    index = lax.broadcasted_iota(jnp.int32, (1, rows), 1)
    col_code = slot * GROUP + jnp.bitwise_and(index, GROUP - 1)
    kept = (count_ref[0, 0] - send_ref[0, 0]) * WIN
    last = rows - WIN
    own = one_hot(row_code == jnp.where(index < kept, col_code, -1))
    packed_ref[...] = dot32(own, normed[...]).astype(jnp.bfloat16)
    borrow_ref[...] = one_hot(row_code == jnp.where(kept > last, -1, col_code[:, last:]))

    step, patch, rank = split_index(lax.broadcasted_iota(jnp.int32, (1, sent), 1), n_seq, cap)
    arrive = peer(me, step, -1) * cap + rank
    pick = one_hot(lax.broadcasted_iota(jnp.int32, (slots, sent), 0) == arrive)
    target = jnp.broadcast_to(row_ref[...].astype(jnp.float32), (16, slots)).astype(jnp.bfloat16)
    target = dot32(target, pick)[:1].astype(jnp.int32)
    out_row = lax.broadcasted_iota(jnp.int32, (tokens, sent), 0)
    for j in range(GROUP):
        place_ref[j * tokens : (j + 1) * tokens, :] = one_hot((target == out_row) & (patch == j))


def encode_call(kernel, blocks, scalars, slots, qkv, resid, weight, bias, gain, out_shape, extra):
    width = resid.shape[2]
    rows = blocks * WIN
    vmem = pl.BlockSpec(memory_space=pltpu.VMEM)
    smem = pl.BlockSpec(memory_space=pltpu.SMEM)
    hbm = pl.BlockSpec(memory_space=pltpu.HBM)
    return pl.pallas_call(
        kernel,
        out_shape=out_shape,
        in_specs=[smem] * len(scalars) + [vmem] * len(slots) + [hbm] * 5,
        out_specs=jax.tree.map(lambda _: vmem, out_shape),
        scratch_shapes=extra
        + [
            pltpu.VMEM((blocks, WIN, 3 * width), jnp.bfloat16),
            pltpu.VMEM((blocks, WIN, width), jnp.bfloat16),
            pltpu.VMEM((width, width), jnp.bfloat16),
            pltpu.VMEM((rows, width), jnp.bfloat16),
            pltpu.VMEM((rows, width), jnp.float32),
            pltpu.VMEM((width,), jnp.bfloat16),
            pltpu.VMEM((width,), jnp.bfloat16),
            pltpu.SemaphoreType.DMA((5,)),
        ],
        compiler_params=pltpu.CompilerParams(vmem_limit_bytes=24 << 20),
        cost_estimate=pl.CostEstimate(
            flops=2 * rows * width * width + 8 * rows * WIN * width,
            bytes_accessed=2 * (width * width + 5 * rows * width),
            transcendentals=rows * WIN * HEADS,
        ),
    )(*scalars, *slots, *(pltpu.with_memory_space_constraint(a, pltpu.HBM) for a in (qkv, resid, weight, bias, gain)))


def pack_kernel(packed_ref, borrow_ref, borrowed_ref, *out_refs):
    total = packed_ref[...].astype(jnp.float32) + dot32(borrow_ref[...], borrowed_ref[...])
    start = 0
    for out_ref in out_refs:
        stop = start + out_ref.shape[0]
        out_ref[...] = total[start:stop].astype(jnp.bfloat16)
        start = stop


def forward_kernel(double_ref, after_ref, out_ref):
    rows = out_ref.shape[0]
    out_ref[...] = double_ref[...].astype(jnp.float32)[rows:].astype(jnp.bfloat16)


def place_kernel(place_ref, *refs):
    *in_refs, out_hbm, out, sems = refs
    tokens = out.shape[0]
    chunks = [ref[...].astype(jnp.float32) for ref in in_refs]
    if len(chunks) > 1:
        chunks[1] = chunks[1][: chunks[0].shape[0]]
    arrived = chunks[0] if len(chunks) == 1 else jnp.concatenate(chunks, axis=0)
    arrived = arrived.astype(jnp.bfloat16)
    width = arrived.shape[1]
    copies = []
    for j in range(GROUP):
        cols = slice(j * width, (j + 1) * width)
        out[:, cols] = dot32(place_ref[j * tokens : (j + 1) * tokens, :], arrived).astype(jnp.bfloat16)
        copies.append(pltpu.make_async_copy(out.at[:, cols], out_hbm.at[:, cols], sems.at[j]))
        copies[-1].start()
    for copy in copies:
        copy.wait()


def exchange_steps(n_seq):
    n_z = n_seq // CORES
    steps = [(dz, dc) for dz in range(n_z) for dc in range(CORES) if (dz, dc) != (0, 0)]
    return [(0, 0)] + sorted(steps, key=lambda s: (abs(s[0] - n_z / 2), s[1], s[0]))


def chip_peer(n_seq, me, step, sign):
    n_z = n_seq // CORES
    offset = jnp.zeros_like(step)
    flip = jnp.zeros_like(step)
    for i, (dz, dc) in enumerate(exchange_steps(n_seq)):
        offset = jnp.where(step == i, dz, offset)
        flip = jnp.where(step == i, dc, flip)
    z = me // CORES + sign * offset
    z = jnp.where(z >= n_z, z - n_z, jnp.where(z < 0, z + n_z, z))
    return z * CORES + jnp.bitwise_xor(jnp.bitwise_and(me, 1), flip)


def per_device(
    qkv, resid, block_count, send_count, send_slot, lm_row, out_weight, out_bias, norm_gain
):
    width = resid.shape[2]
    row_total = send_slot.shape[1]
    tokens = WIN // GROUP
    blocks = row_total // tokens
    n_seq = lax.axis_size("seq")
    n_enc = lax.axis_size("enc")
    slots = lm_row.shape[1]
    cap = slots // n_seq
    chunk = GROUP * cap
    sent = slots * GROUP
    vmem = pl.BlockSpec(memory_space=pltpu.VMEM)
    small = pltpu.CompilerParams(vmem_limit_bytes=16 << 20)

    def rows_of(count, columns=width):
        return jax.ShapeDtypeStruct((count, columns), jnp.bfloat16)

    data = (qkv, resid, out_weight, out_bias, norm_gain)
    lent = encode_call(lent_kernel, 1, [block_count], [], *data, rows_of(WIN), [])
    borrowed = lax.ppermute(lent, "enc", [((i - 1) % n_enc, i) for i in range(n_enc)])

    by_steps = chunk % 8 == 0 and n_seq % CORES == 0
    peer = functools.partial(chip_peer, n_seq) if by_steps else lambda me, step, sign: step
    me = lax.axis_index("seq").astype(jnp.int32).reshape(1, 1)
    packed, borrow, place = encode_call(
        functools.partial(own_kernel, n_seq, cap, peer), blocks,
        [block_count, send_count, me], [send_slot, lm_row], *data,
        (rows_of(sent), rows_of(sent, WIN), rows_of(GROUP * row_total, sent)),
        [pltpu.VMEM((row_total * GROUP, width), jnp.bfloat16)],
    )
    pieces = [chunk, CORES * chunk] + [chunk] * (n_seq - 1 - CORES) if by_steps else [sent]
    outgoing = pl.pallas_call(
        pack_kernel,
        out_shape=[rows_of(rows) for rows in pieces],
        in_specs=[vmem] * 3,
        out_specs=[vmem] * len(pieces),
        compiler_params=small,
    )(packed, borrow, borrowed)

    if by_steps:
        n_z = n_seq // CORES

        def exchange(part, dz, dc):
            return lax.ppermute(
                part, "seq", [(i, (i // CORES + dz) % n_z * CORES + (i + dc) % CORES) for i in range(n_seq)]
            )

        double = exchange(outgoing[1], n_z // 2, 0)
        rest = [exchange(part, *step) for part, step in zip(outgoing[2:], exchange_steps(n_seq)[1 + CORES :])]
        onward = pl.pallas_call(
            forward_kernel, out_shape=rows_of(chunk), in_specs=[vmem] * 2, out_specs=vmem, compiler_params=small
        )(double, rest[0])
        arrived = [outgoing[0], double, exchange(onward, 0, 1), *rest]
    else:
        arrived = [
            lax.all_to_all(
                outgoing[0].reshape(n_seq, chunk, width), "seq", split_axis=0, concat_axis=0, tiled=True
            ).reshape(sent, width)
        ]
    placed = pl.pallas_call(
        place_kernel,
        out_shape=rows_of(row_total, GROUP * width),
        in_specs=[vmem] * (1 + len(arrived)),
        out_specs=pl.BlockSpec(memory_space=pltpu.HBM),
        scratch_shapes=[pltpu.VMEM((row_total, GROUP * width), jnp.bfloat16), pltpu.SemaphoreType.DMA((GROUP,))],
        compiler_params=small,
    )(place, *arrived)
    return placed[None]


def solution(mesh):
    placed = (
        P("enc", "seq", None),
        P("enc", "seq", None),
        P("enc", "seq"),
        P("enc", "seq"),
        P("enc", "seq"),
        P("enc", "seq"),
        P(),
        P(),
        P(),
    )
    return jax.shard_map(
        per_device, mesh=mesh, in_specs=placed, out_specs=P("enc", "seq", None), check_vma=False
    )
```

```python
import functools
import math

import jax
import jax.numpy as jnp
from jax import lax
from jax.experimental import pallas as pl
from jax.experimental.pallas import tpu as pltpu
from jax.sharding import PartitionSpec as P

HEADS = 16
WIN = 64
LANES = 128
GROUP = 4
EPS = 1e-6
CORES = 2

NT = (((1,), (1,)), ((), ()))


def dot32(a, b):
    return jnp.dot(a, b, preferred_element_type=jnp.float32)


def one_hot(match):
    return match.astype(jnp.float32).astype(jnp.bfloat16)


def attend(q, k, v, out_ref, row0, width):
    head = width // HEADS
    rate = 1.0 / math.sqrt(head)
    totals = [None] * (width // LANES)
    sums = [None] * (width // LANES)
    first_half = lax.broadcasted_iota(jnp.int32, (WIN, 2 * WIN), 1) < WIN
    for pair in range(HEADS // 2):
        start = 2 * pair * head
        lo = start // LANES * LANES
        hi = -(-(start + 2 * head) // LANES) * LANES
        column = lax.broadcasted_iota(jnp.int32, (2 * WIN, hi - lo), 1) + lo
        row = lax.broadcasted_iota(jnp.int32, (2 * WIN, hi - lo), 0)
        begin = jnp.where(row < WIN, start, start + head)
        mask = one_hot((column >= begin) & (column < begin + head))
        kw, vw = k(lo, hi), v(lo, hi)
        keys = jnp.concatenate([kw, kw], axis=0) * mask
        values = jnp.concatenate([vw, vw], axis=0) * mask
        scores = lax.dot_general(q(lo, hi), keys, NT, preferred_element_type=jnp.float32)
        top0 = jnp.max(jnp.where(first_half, scores, -jnp.inf), axis=1, keepdims=True)
        top1 = jnp.max(jnp.where(first_half, -jnp.inf, scores), axis=1, keepdims=True)
        raised = jnp.exp((scores - jnp.where(first_half, top0, top1)) * rate).astype(jnp.bfloat16)
        part = dot32(raised, values)
        norm = dot32(raised, mask)
        for tile in range(lo // LANES, hi // LANES):
            at = slice(tile * LANES - lo, (tile + 1) * LANES - lo)
            totals[tile] = part[:, at] if totals[tile] is None else totals[tile] + part[:, at]
            sums[tile] = norm[:, at] if sums[tile] is None else sums[tile] + norm[:, at]
    for tile in range(width // LANES):
        out_ref[row0 : row0 + WIN, tile * LANES : (tile + 1) * LANES] = (totals[tile] / sums[tile]).astype(
            jnp.bfloat16
        )


def encode(
    slot, qkv_hbm, resid_hbm, weight_hbm, bias_hbm, gain_hbm, out_ref,
    qkv, resid, weight, attended, hidden, bias_ref, gain_ref, sems,
):
    blocks = qkv.shape[0]
    width = resid.shape[2]
    at = pl.ds(slot, blocks)
    pairs = [
        (qkv_hbm.at[at], qkv), (weight_hbm, weight), (resid_hbm.at[at], resid), (bias_hbm, bias_ref), (gain_hbm, gain_ref)
    ]
    copies = [pltpu.make_async_copy(a, b, sems.at[i]) for i, (a, b) in enumerate(pairs)]
    for copy in copies:
        copy.start()
    copies[0].wait()
    for b in range(blocks):
        attend(
            lambda lo, hi, b=b: qkv[b, :, lo:hi],
            lambda lo, hi, b=b: qkv[b, :, width + lo : width + hi],
            lambda lo, hi, b=b: qkv[b, :, 2 * width + lo : 2 * width + hi],
            attended, b * WIN, width,
        )
    for copy in copies[1:]:
        copy.wait()
    rows = blocks * WIN
    squares = jnp.zeros((rows, 1), jnp.float32)
    step = 2 * LANES
    for lo in range(0, width, step):
        cols = slice(lo, lo + step)
        h = dot32(attended[...], weight[:, cols])
        h = h + bias_ref[cols].astype(jnp.float32).reshape(1, step)
        h = h + resid[:, :, cols].reshape(rows, step).astype(jnp.float32)
        hidden[:, cols] = h
        squares = squares + jnp.sum(h * h, axis=1, keepdims=True)
    scale = lax.rsqrt(squares * (1.0 / width) + EPS)
    for lo in range(0, width, step):
        cols = slice(lo, lo + step)
        gain = gain_ref[cols].astype(jnp.float32).reshape(1, step)
        out_ref[:, cols] = (hidden[:, cols] * scale * gain).astype(jnp.bfloat16)


def lent_kernel(count_ref, qkv_hbm, resid_hbm, weight_hbm, bias_hbm, gain_hbm, out_ref, *scratch):
    encode(count_ref[0, 0] - 1, qkv_hbm, resid_hbm, weight_hbm, bias_hbm, gain_hbm, out_ref, *scratch)


def split_index(index, n_seq, cap):
    step = index // (GROUP * cap)
    rest = index - step * (GROUP * cap)
    patch = rest // cap
    return step, patch, rest - patch * cap


def own_kernel(
    n_seq, cap, peer, count_ref, send_ref, me_ref, slot_ref, row_ref,
    qkv_hbm, resid_hbm, weight_hbm, bias_hbm, gain_hbm,
    packed_ref, borrow_ref, place_ref, normed, *scratch,
):
    rows = normed.shape[0]
    slots = n_seq * cap
    sent = slots * GROUP
    tokens = rows // GROUP
    me = me_ref[0, 0]
    encode(0, qkv_hbm, resid_hbm, weight_hbm, bias_hbm, gain_hbm, normed, *scratch)

    step, patch, rank = split_index(lax.broadcasted_iota(jnp.int32, (sent, 1), 0), n_seq, cap)
    row_code = (peer(me, step, 1) * cap + rank) * GROUP + patch
    token = lax.broadcasted_iota(jnp.int32, (tokens, rows), 0)
    column = lax.broadcasted_iota(jnp.int32, (tokens, rows), 1)
    spread = one_hot((column >= token * GROUP) & (column < (token + 1) * GROUP))
    slot = jnp.broadcast_to(slot_ref[...].astype(jnp.float32), (16, tokens)).astype(jnp.bfloat16)
    slot = dot32(slot, spread)[:1].astype(jnp.int32)
    index = lax.broadcasted_iota(jnp.int32, (1, rows), 1)
    col_code = slot * GROUP + jnp.bitwise_and(index, GROUP - 1)
    kept = (count_ref[0, 0] - send_ref[0, 0]) * WIN
    last = rows - WIN
    own = one_hot(row_code == jnp.where(index < kept, col_code, -1))
    packed_ref[...] = dot32(own, normed[...]).astype(jnp.bfloat16)
    borrow_ref[...] = one_hot(row_code == jnp.where(kept > last, -1, col_code[:, last:]))

    step, patch, rank = split_index(lax.broadcasted_iota(jnp.int32, (1, sent), 1), n_seq, cap)
    arrive = peer(me, step, -1) * cap + rank
    pick = one_hot(lax.broadcasted_iota(jnp.int32, (slots, sent), 0) == arrive)
    target = jnp.broadcast_to(row_ref[...].astype(jnp.float32), (16, slots)).astype(jnp.bfloat16)
    target = dot32(target, pick)[:1].astype(jnp.int32)
    out_row = lax.broadcasted_iota(jnp.int32, (tokens, sent), 0)
    for j in range(GROUP):
        place_ref[j * tokens : (j + 1) * tokens, :] = one_hot((target == out_row) & (patch == j))


def encode_call(kernel, blocks, scalars, slots, qkv, resid, weight, bias, gain, out_shape, extra):
    width = resid.shape[2]
    rows = blocks * WIN
    vmem = pl.BlockSpec(memory_space=pltpu.VMEM)
    smem = pl.BlockSpec(memory_space=pltpu.SMEM)
    hbm = pl.BlockSpec(memory_space=pltpu.HBM)
    return pl.pallas_call(
        kernel,
        out_shape=out_shape,
        in_specs=[smem] * len(scalars) + [vmem] * len(slots) + [hbm] * 5,
        out_specs=jax.tree.map(lambda _: vmem, out_shape),
        scratch_shapes=extra
        + [
            pltpu.VMEM((blocks, WIN, 3 * width), jnp.bfloat16),
            pltpu.VMEM((blocks, WIN, width), jnp.bfloat16),
            pltpu.VMEM((width, width), jnp.bfloat16),
            pltpu.VMEM((rows, width), jnp.bfloat16),
            pltpu.VMEM((rows, width), jnp.float32),
            pltpu.VMEM((width,), jnp.bfloat16),
            pltpu.VMEM((width,), jnp.bfloat16),
            pltpu.SemaphoreType.DMA((5,)),
        ],
        compiler_params=pltpu.CompilerParams(vmem_limit_bytes=24 << 20),
        cost_estimate=pl.CostEstimate(
            flops=2 * rows * width * width + 8 * rows * WIN * width,
            bytes_accessed=2 * (width * width + 5 * rows * width),
            transcendentals=rows * WIN * HEADS,
        ),
    )(*scalars, *slots, *(pltpu.with_memory_space_constraint(a, pltpu.HBM) for a in (qkv, resid, weight, bias, gain)))


def pack_kernel(packed_ref, borrow_ref, borrowed_ref, *out_refs):
    total = packed_ref[...].astype(jnp.float32) + dot32(borrow_ref[...], borrowed_ref[...])
    start = 0
    for out_ref in out_refs:
        stop = start + out_ref.shape[0]
        out_ref[...] = total[start:stop].astype(jnp.bfloat16)
        start = stop


def forward_kernel(double_ref, after_ref, out_ref):
    rows = out_ref.shape[0]
    out_ref[...] = double_ref[...].astype(jnp.float32)[rows:].astype(jnp.bfloat16)


def place_kernel(n_double, place_ref, *refs):
    *in_refs, out_hbm, out, sems = refs
    tokens = out.shape[0]
    chunks = [ref[...].astype(jnp.float32) for ref in in_refs]
    if n_double:
        rows = chunks[0].shape[0]
        for i in range(1, 1 + CORES * n_double, CORES):
            chunks[i] = chunks[i][:rows]
    arrived = chunks[0] if len(chunks) == 1 else jnp.concatenate(chunks, axis=0)
    arrived = arrived.astype(jnp.bfloat16)
    width = arrived.shape[1]
    copies = []
    for j in range(GROUP):
        cols = slice(j * width, (j + 1) * width)
        out[:, cols] = dot32(place_ref[j * tokens : (j + 1) * tokens, :], arrived).astype(jnp.bfloat16)
        copies.append(pltpu.make_async_copy(out.at[:, cols], out_hbm.at[:, cols], sems.at[j]))
        copies[-1].start()
    for copy in copies:
        copy.wait()


def double_offsets(n_seq):
    return sorted({1, n_seq // CORES // 2})


def exchange_steps(n_seq):
    doubles = double_offsets(n_seq)
    offsets = doubles + [dz for dz in range(1, n_seq // CORES) if dz not in doubles]
    return [(0, 0)] + [(dz, dc) for dz in offsets for dc in range(CORES)] + [(0, 1)]


def chip_peer(n_seq, me, step, sign):
    n_z = n_seq // CORES
    offset = jnp.zeros_like(step)
    flip = jnp.zeros_like(step)
    for i, (dz, dc) in enumerate(exchange_steps(n_seq)):
        offset = jnp.where(step == i, dz, offset)
        flip = jnp.where(step == i, dc, flip)
    z = me // CORES + sign * offset
    z = jnp.where(z >= n_z, z - n_z, jnp.where(z < 0, z + n_z, z))
    return z * CORES + jnp.bitwise_xor(jnp.bitwise_and(me, 1), flip)


def per_device(
    qkv, resid, block_count, send_count, send_slot, lm_row, out_weight, out_bias, norm_gain
):
    width = resid.shape[2]
    row_total = send_slot.shape[1]
    tokens = WIN // GROUP
    blocks = row_total // tokens
    n_seq = lax.axis_size("seq")
    n_enc = lax.axis_size("enc")
    slots = lm_row.shape[1]
    cap = slots // n_seq
    chunk = GROUP * cap
    sent = slots * GROUP
    vmem = pl.BlockSpec(memory_space=pltpu.VMEM)
    small = pltpu.CompilerParams(vmem_limit_bytes=16 << 20)

    def rows_of(count, columns=width):
        return jax.ShapeDtypeStruct((count, columns), jnp.bfloat16)

    data = (qkv, resid, out_weight, out_bias, norm_gain)
    lent = encode_call(lent_kernel, 1, [block_count], [], *data, rows_of(WIN), [])
    borrowed = lax.ppermute(lent, "enc", [((i - 1) % n_enc, i) for i in range(n_enc)])

    by_steps = chunk % 8 == 0 and n_seq % CORES == 0
    peer = functools.partial(chip_peer, n_seq) if by_steps else lambda me, step, sign: step
    me = lax.axis_index("seq").astype(jnp.int32).reshape(1, 1)
    packed, borrow, place = encode_call(
        functools.partial(own_kernel, n_seq, cap, peer), blocks,
        [block_count, send_count, me], [send_slot, lm_row], *data,
        (rows_of(sent), rows_of(sent, WIN), rows_of(GROUP * row_total, sent)),
        [pltpu.VMEM((row_total * GROUP, width), jnp.bfloat16)],
    )
    n_double = len(double_offsets(n_seq)) if by_steps else 0
    pieces = [sent]
    if by_steps:
        pieces = [chunk] + [CORES * chunk] * n_double + [chunk] * (n_seq - 1 - CORES * n_double)
    outgoing = pl.pallas_call(
        pack_kernel,
        out_shape=[rows_of(rows) for rows in pieces],
        in_specs=[vmem] * 3,
        out_specs=[vmem] * len(pieces),
        compiler_params=small,
    )(packed, borrow, borrowed)

    if by_steps:
        n_z = n_seq // CORES

        def exchange(part, dz, dc):
            return lax.ppermute(
                part, "seq", [(i, (i // CORES + dz) % n_z * CORES + (i + dc) % CORES) for i in range(n_seq)]
            )

        doubles = [exchange(part, dz, 0) for part, dz in zip(outgoing[1:], double_offsets(n_seq))]
        singles = exchange_steps(n_seq)[1 + CORES * n_double : -1]
        singles = [exchange(part, *step) for part, step in zip(outgoing[1 + n_double : -1], singles)]
        arrived = [outgoing[0]]
        for i, double in enumerate(doubles):
            passed = pl.pallas_call(
                forward_kernel, out_shape=rows_of(chunk), in_specs=[vmem] * 2, out_specs=vmem, compiler_params=small
            )(double, singles[0])
            arrived += [double, exchange(passed, 0, 1)]
        arrived += singles + [exchange(outgoing[-1], 0, 1)]
    else:
        arrived = [
            lax.all_to_all(
                outgoing[0].reshape(n_seq, chunk, width), "seq", split_axis=0, concat_axis=0, tiled=True
            ).reshape(sent, width)
        ]
    placed = pl.pallas_call(
        functools.partial(place_kernel, n_double),
        out_shape=rows_of(row_total, GROUP * width),
        in_specs=[vmem] * (1 + len(arrived)),
        out_specs=pl.BlockSpec(memory_space=pltpu.HBM),
        scratch_shapes=[pltpu.VMEM((row_total, GROUP * width), jnp.bfloat16), pltpu.SemaphoreType.DMA((GROUP,))],
        compiler_params=small,
    )(place, *arrived)
    return placed[None]


def solution(mesh):
    placed = (
        P("enc", "seq", None),
        P("enc", "seq", None),
        P("enc", "seq"),
        P("enc", "seq"),
        P("enc", "seq"),
        P("enc", "seq"),
        P(),
        P(),
        P(),
    )
    return jax.shard_map(
        per_device, mesh=mesh, in_specs=placed, out_specs=P("enc", "seq", None), check_vma=False
    )
```

```python
import functools
import math

import jax
import jax.numpy as jnp
from jax import lax
from jax.experimental import pallas as pl
from jax.experimental.pallas import tpu as pltpu
from jax.sharding import PartitionSpec as P

HEADS = 16
WIN = 64
LANES = 128
GROUP = 4
EPS = 1e-6
CORES = 2

NT = (((1,), (1,)), ((), ()))


def dot32(a, b):
    return jnp.dot(a, b, preferred_element_type=jnp.float32)


def one_hot(match):
    return match.astype(jnp.float32).astype(jnp.bfloat16)


def attend(q, k, v, out_ref, row0, width):
    head = width // HEADS
    rate = 1.0 / math.sqrt(head)
    totals = [None] * (width // LANES)
    sums = [None] * (width // LANES)
    first_half = lax.broadcasted_iota(jnp.int32, (WIN, 2 * WIN), 1) < WIN
    for pair in range(HEADS // 2):
        start = 2 * pair * head
        lo = start // LANES * LANES
        hi = -(-(start + 2 * head) // LANES) * LANES
        column = lax.broadcasted_iota(jnp.int32, (2 * WIN, hi - lo), 1) + lo
        row = lax.broadcasted_iota(jnp.int32, (2 * WIN, hi - lo), 0)
        begin = jnp.where(row < WIN, start, start + head)
        mask = one_hot((column >= begin) & (column < begin + head))
        kw, vw = k(lo, hi), v(lo, hi)
        keys = jnp.concatenate([kw, kw], axis=0) * mask
        values = jnp.concatenate([vw, vw], axis=0) * mask
        scores = lax.dot_general(q(lo, hi), keys, NT, preferred_element_type=jnp.float32)
        top0 = jnp.max(jnp.where(first_half, scores, -jnp.inf), axis=1, keepdims=True)
        top1 = jnp.max(jnp.where(first_half, -jnp.inf, scores), axis=1, keepdims=True)
        raised = jnp.exp((scores - jnp.where(first_half, top0, top1)) * rate).astype(jnp.bfloat16)
        part = dot32(raised, values)
        norm = dot32(raised, mask)
        for tile in range(lo // LANES, hi // LANES):
            at = slice(tile * LANES - lo, (tile + 1) * LANES - lo)
            totals[tile] = part[:, at] if totals[tile] is None else totals[tile] + part[:, at]
            sums[tile] = norm[:, at] if sums[tile] is None else sums[tile] + norm[:, at]
    for tile in range(width // LANES):
        out_ref[row0 : row0 + WIN, tile * LANES : (tile + 1) * LANES] = (totals[tile] / sums[tile]).astype(
            jnp.bfloat16
        )


def encode(
    slot, qkv_hbm, resid_hbm, weight_hbm, bias_hbm, gain_hbm, out_ref,
    qkv, resid, weight, attended, hidden, bias_ref, gain_ref, sems,
):
    blocks = qkv.shape[0]
    width = resid.shape[2]
    at = pl.ds(slot, blocks)
    pairs = [
        (qkv_hbm.at[at], qkv), (weight_hbm, weight), (resid_hbm.at[at], resid), (bias_hbm, bias_ref), (gain_hbm, gain_ref)
    ]
    copies = [pltpu.make_async_copy(a, b, sems.at[i]) for i, (a, b) in enumerate(pairs)]
    for copy in copies:
        copy.start()
    copies[0].wait()
    for b in range(blocks):
        attend(
            lambda lo, hi, b=b: qkv[b, :, lo:hi],
            lambda lo, hi, b=b: qkv[b, :, width + lo : width + hi],
            lambda lo, hi, b=b: qkv[b, :, 2 * width + lo : 2 * width + hi],
            attended, b * WIN, width,
        )
    for copy in copies[1:]:
        copy.wait()
    rows = blocks * WIN
    squares = jnp.zeros((rows, 1), jnp.float32)
    step = 2 * LANES
    for lo in range(0, width, step):
        cols = slice(lo, lo + step)
        h = dot32(attended[...], weight[:, cols])
        h = h + bias_ref[cols].astype(jnp.float32).reshape(1, step)
        h = h + resid[:, :, cols].reshape(rows, step).astype(jnp.float32)
        hidden[:, cols] = h
        squares = squares + jnp.sum(h * h, axis=1, keepdims=True)
    scale = lax.rsqrt(squares * (1.0 / width) + EPS)
    for lo in range(0, width, step):
        cols = slice(lo, lo + step)
        gain = gain_ref[cols].astype(jnp.float32).reshape(1, step)
        out_ref[:, cols] = (hidden[:, cols] * scale * gain).astype(jnp.bfloat16)


def lent_kernel(count_ref, qkv_hbm, resid_hbm, weight_hbm, bias_hbm, gain_hbm, out_ref, *scratch):
    encode(count_ref[0, 0] - 1, qkv_hbm, resid_hbm, weight_hbm, bias_hbm, gain_hbm, out_ref, *scratch)


def split_index(index, n_seq, cap):
    step = index // (GROUP * cap)
    rest = index - step * (GROUP * cap)
    patch = rest // cap
    return step, patch, rest - patch * cap


def own_kernel(
    n_seq, cap, peer, count_ref, send_ref, me_ref, slot_ref, row_ref,
    qkv_hbm, resid_hbm, weight_hbm, bias_hbm, gain_hbm,
    packed_ref, borrow_ref, place_ref, normed, *scratch,
):
    rows = normed.shape[0]
    slots = n_seq * cap
    sent = slots * GROUP
    tokens = rows // GROUP
    me = me_ref[0, 0]
    encode(0, qkv_hbm, resid_hbm, weight_hbm, bias_hbm, gain_hbm, normed, *scratch)

    step, patch, rank = split_index(lax.broadcasted_iota(jnp.int32, (sent, 1), 0), n_seq, cap)
    row_code = (peer(me, step, 1) * cap + rank) * GROUP + patch
    token = lax.broadcasted_iota(jnp.int32, (tokens, rows), 0)
    column = lax.broadcasted_iota(jnp.int32, (tokens, rows), 1)
    spread = one_hot((column >= token * GROUP) & (column < (token + 1) * GROUP))
    slot = jnp.broadcast_to(slot_ref[...].astype(jnp.float32), (16, tokens)).astype(jnp.bfloat16)
    slot = dot32(slot, spread)[:1].astype(jnp.int32)
    index = lax.broadcasted_iota(jnp.int32, (1, rows), 1)
    col_code = slot * GROUP + jnp.bitwise_and(index, GROUP - 1)
    kept = (count_ref[0, 0] - send_ref[0, 0]) * WIN
    last = rows - WIN
    own = one_hot(row_code == jnp.where(index < kept, col_code, -1))
    packed_ref[...] = dot32(own, normed[...]).astype(jnp.bfloat16)
    borrow_ref[...] = one_hot(row_code == jnp.where(kept > last, -1, col_code[:, last:]))

    step, patch, rank = split_index(lax.broadcasted_iota(jnp.int32, (1, sent), 1), n_seq, cap)
    arrive = peer(me, step, -1) * cap + rank
    pick = one_hot(lax.broadcasted_iota(jnp.int32, (slots, sent), 0) == arrive)
    target = jnp.broadcast_to(row_ref[...].astype(jnp.float32), (16, slots)).astype(jnp.bfloat16)
    target = dot32(target, pick)[:1].astype(jnp.int32)
    out_row = lax.broadcasted_iota(jnp.int32, (tokens, sent), 0)
    for j in range(GROUP):
        place_ref[j * tokens : (j + 1) * tokens, :] = one_hot((target == out_row) & (patch == j))


def encode_call(kernel, blocks, scalars, slots, qkv, resid, weight, bias, gain, out_shape, extra):
    width = resid.shape[2]
    rows = blocks * WIN
    vmem = pl.BlockSpec(memory_space=pltpu.VMEM)
    smem = pl.BlockSpec(memory_space=pltpu.SMEM)
    hbm = pl.BlockSpec(memory_space=pltpu.HBM)
    return pl.pallas_call(
        kernel,
        out_shape=out_shape,
        in_specs=[smem] * len(scalars) + [vmem] * len(slots) + [hbm] * 5,
        out_specs=jax.tree.map(lambda _: vmem, out_shape),
        scratch_shapes=extra
        + [
            pltpu.VMEM((blocks, WIN, 3 * width), jnp.bfloat16),
            pltpu.VMEM((blocks, WIN, width), jnp.bfloat16),
            pltpu.VMEM((width, width), jnp.bfloat16),
            pltpu.VMEM((rows, width), jnp.bfloat16),
            pltpu.VMEM((rows, width), jnp.float32),
            pltpu.VMEM((width,), jnp.bfloat16),
            pltpu.VMEM((width,), jnp.bfloat16),
            pltpu.SemaphoreType.DMA((5,)),
        ],
        compiler_params=pltpu.CompilerParams(vmem_limit_bytes=24 << 20),
        cost_estimate=pl.CostEstimate(
            flops=2 * rows * width * width + 8 * rows * WIN * width,
            bytes_accessed=2 * (width * width + 5 * rows * width),
            transcendentals=rows * WIN * HEADS,
        ),
    )(*scalars, *slots, *(pltpu.with_memory_space_constraint(a, pltpu.HBM) for a in (qkv, resid, weight, bias, gain)))


def pack_kernel(packed_ref, borrow_ref, borrowed_ref, *out_refs):
    total = packed_ref[...].astype(jnp.float32) + dot32(borrow_ref[...], borrowed_ref[...])
    start = 0
    for out_ref in out_refs:
        stop = start + out_ref.shape[0]
        out_ref[...] = total[start:stop].astype(jnp.bfloat16)
        start = stop


def forward_kernel(double_ref, after_ref, out_ref):
    rows = out_ref.shape[0]
    out_ref[...] = double_ref[...].astype(jnp.float32)[rows:].astype(jnp.bfloat16)


def place_kernel(place_ref, *refs):
    *in_refs, out_hbm, out, sems = refs
    tokens = out.shape[0]
    chunks = [ref[...].astype(jnp.float32) for ref in in_refs]
    if len(chunks) > 1:
        chunks[1] = chunks[1][: chunks[0].shape[0]]
    arrived = chunks[0] if len(chunks) == 1 else jnp.concatenate(chunks, axis=0)
    arrived = arrived.astype(jnp.bfloat16)
    width = arrived.shape[1]
    copies = []
    for j in range(GROUP):
        cols = slice(j * width, (j + 1) * width)
        out[:, cols] = dot32(place_ref[j * tokens : (j + 1) * tokens, :], arrived).astype(jnp.bfloat16)
        copies.append(pltpu.make_async_copy(out.at[:, cols], out_hbm.at[:, cols], sems.at[j]))
        copies[-1].start()
    for copy in copies:
        copy.wait()


def exchange_steps(n_seq):
    return [(0, 0)] + [(dz, dc) for dz in range(1, n_seq // CORES) for dc in range(CORES)] + [(0, 1)]


def chip_peer(n_seq, me, step, sign):
    n_z = n_seq // CORES
    offset = jnp.zeros_like(step)
    flip = jnp.zeros_like(step)
    for i, (dz, dc) in enumerate(exchange_steps(n_seq)):
        offset = jnp.where(step == i, dz, offset)
        flip = jnp.where(step == i, dc, flip)
    z = me // CORES + sign * offset
    z = jnp.where(z >= n_z, z - n_z, jnp.where(z < 0, z + n_z, z))
    return z * CORES + jnp.bitwise_xor(jnp.bitwise_and(me, 1), flip)


def per_device(
    qkv, resid, block_count, send_count, send_slot, lm_row, out_weight, out_bias, norm_gain
):
    width = resid.shape[2]
    row_total = send_slot.shape[1]
    tokens = WIN // GROUP
    blocks = row_total // tokens
    n_seq = lax.axis_size("seq")
    n_enc = lax.axis_size("enc")
    slots = lm_row.shape[1]
    cap = slots // n_seq
    chunk = GROUP * cap
    sent = slots * GROUP
    vmem = pl.BlockSpec(memory_space=pltpu.VMEM)
    small = pltpu.CompilerParams(vmem_limit_bytes=16 << 20)

    def rows_of(count, columns=width):
        return jax.ShapeDtypeStruct((count, columns), jnp.bfloat16)

    data = (qkv, resid, out_weight, out_bias, norm_gain)
    lent = encode_call(lent_kernel, 1, [block_count], [], *data, rows_of(WIN), [])
    borrowed = lax.ppermute(lent, "enc", [((i - 1) % n_enc, i) for i in range(n_enc)])

    by_steps = chunk % 8 == 0 and n_seq % CORES == 0
    peer = functools.partial(chip_peer, n_seq) if by_steps else lambda me, step, sign: step
    me = lax.axis_index("seq").astype(jnp.int32).reshape(1, 1)
    packed, borrow, place = encode_call(
        functools.partial(own_kernel, n_seq, cap, peer), blocks,
        [block_count, send_count, me], [send_slot, lm_row], *data,
        (rows_of(sent), rows_of(sent, WIN), rows_of(GROUP * row_total, sent)),
        [pltpu.VMEM((row_total * GROUP, width), jnp.bfloat16)],
    )
    pieces = [chunk, CORES * chunk] + [chunk] * (n_seq - 1 - CORES) if by_steps else [sent]
    outgoing = pl.pallas_call(
        pack_kernel,
        out_shape=[rows_of(rows) for rows in pieces],
        in_specs=[vmem] * 3,
        out_specs=[vmem] * len(pieces),
        compiler_params=small,
    )(packed, borrow, borrowed)

    if by_steps:
        n_z = n_seq // CORES

        def exchange(part, dz, dc):
            return lax.ppermute(
                part, "seq", [(i, (i // CORES + dz) % n_z * CORES + (i + dc) % CORES) for i in range(n_seq)]
            )

        double = exchange(outgoing[1], 1, 0)
        rest = [exchange(part, *step) for part, step in zip(outgoing[2:], exchange_steps(n_seq)[1 + CORES :])]
        onward = pl.pallas_call(
            forward_kernel, out_shape=rows_of(chunk), in_specs=[vmem] * 2, out_specs=vmem, compiler_params=small
        )(double, rest[0])
        arrived = [outgoing[0], double, exchange(onward, 0, 1), *rest]
    else:
        arrived = [
            lax.all_to_all(
                outgoing[0].reshape(n_seq, chunk, width), "seq", split_axis=0, concat_axis=0, tiled=True
            ).reshape(sent, width)
        ]
    placed = pl.pallas_call(
        place_kernel,
        out_shape=rows_of(row_total, GROUP * width),
        in_specs=[vmem] * (1 + len(arrived)),
        out_specs=pl.BlockSpec(memory_space=pltpu.HBM),
        scratch_shapes=[pltpu.VMEM((row_total, GROUP * width), jnp.bfloat16), pltpu.SemaphoreType.DMA((GROUP,))],
        compiler_params=small,
    )(place, *arrived)
    return placed[None]


def solution(mesh):
    placed = (
        P("enc", "seq", None),
        P("enc", "seq", None),
        P("enc", "seq"),
        P("enc", "seq"),
        P("enc", "seq"),
        P("enc", "seq"),
        P(),
        P(),
        P(),
    )
    return jax.shard_map(
        per_device, mesh=mesh, in_specs=placed, out_specs=P("enc", "seq", None), check_vma=False
    )
```

```python
import functools
import math

import jax
import jax.numpy as jnp
from jax import lax
from jax.experimental import pallas as pl
from jax.experimental.pallas import tpu as pltpu
from jax.sharding import PartitionSpec as P

HEADS = 16
WIN = 64
LANES = 128
GROUP = 4
EPS = 1e-6
CORES = 2

NT = (((1,), (1,)), ((), ()))


def dot32(a, b):
    return jnp.dot(a, b, preferred_element_type=jnp.float32)


def one_hot(match):
    return match.astype(jnp.float32).astype(jnp.bfloat16)


def attend(q, k, v, out_ref, row0, width):
    head = width // HEADS
    rate = 1.0 / math.sqrt(head)
    totals = [None] * (width // LANES)
    sums = [None] * (width // LANES)
    first_half = lax.broadcasted_iota(jnp.int32, (WIN, 2 * WIN), 1) < WIN
    for pair in range(HEADS // 2):
        start = 2 * pair * head
        lo = start // LANES * LANES
        hi = -(-(start + 2 * head) // LANES) * LANES
        column = lax.broadcasted_iota(jnp.int32, (2 * WIN, hi - lo), 1) + lo
        row = lax.broadcasted_iota(jnp.int32, (2 * WIN, hi - lo), 0)
        begin = jnp.where(row < WIN, start, start + head)
        mask = one_hot((column >= begin) & (column < begin + head))
        kw, vw = k(lo, hi), v(lo, hi)
        keys = jnp.concatenate([kw, kw], axis=0) * mask
        values = jnp.concatenate([vw, vw], axis=0) * mask
        scores = lax.dot_general(q(lo, hi), keys, NT, preferred_element_type=jnp.float32)
        top0 = jnp.max(jnp.where(first_half, scores, -jnp.inf), axis=1, keepdims=True)
        top1 = jnp.max(jnp.where(first_half, -jnp.inf, scores), axis=1, keepdims=True)
        raised = jnp.exp((scores - jnp.where(first_half, top0, top1)) * rate).astype(jnp.bfloat16)
        part = dot32(raised, values)
        norm = dot32(raised, mask)
        for tile in range(lo // LANES, hi // LANES):
            at = slice(tile * LANES - lo, (tile + 1) * LANES - lo)
            totals[tile] = part[:, at] if totals[tile] is None else totals[tile] + part[:, at]
            sums[tile] = norm[:, at] if sums[tile] is None else sums[tile] + norm[:, at]
    for tile in range(width // LANES):
        out_ref[row0 : row0 + WIN, tile * LANES : (tile + 1) * LANES] = (totals[tile] / sums[tile]).astype(
            jnp.bfloat16
        )


def encode(
    slot, qkv_hbm, resid_hbm, weight_hbm, bias_hbm, gain_hbm, out_ref,
    qkv, resid, weight, attended, hidden, bias_ref, gain_ref, sems, while_copying=lambda: None,
):
    blocks = qkv.shape[0]
    width = resid.shape[2]
    at = pl.ds(slot, blocks)
    pairs = [
        (qkv_hbm.at[at], qkv), (weight_hbm, weight), (resid_hbm.at[at], resid), (bias_hbm, bias_ref), (gain_hbm, gain_ref)
    ]
    copies = [pltpu.make_async_copy(a, b, sems.at[i]) for i, (a, b) in enumerate(pairs)]
    for copy in copies:
        copy.start()
    while_copying()
    copies[0].wait()
    for b in range(blocks):
        attend(
            lambda lo, hi, b=b: qkv[b, :, lo:hi],
            lambda lo, hi, b=b: qkv[b, :, width + lo : width + hi],
            lambda lo, hi, b=b: qkv[b, :, 2 * width + lo : 2 * width + hi],
            attended, b * WIN, width,
        )
    for copy in copies[1:]:
        copy.wait()
    rows = blocks * WIN
    squares = jnp.zeros((rows, 1), jnp.float32)
    step = 2 * LANES
    for lo in range(0, width, step):
        cols = slice(lo, lo + step)
        h = dot32(attended[...], weight[:, cols])
        h = h + bias_ref[cols].astype(jnp.float32).reshape(1, step)
        h = h + resid[:, :, cols].reshape(rows, step).astype(jnp.float32)
        hidden[:, cols] = h
        squares = squares + jnp.sum(h * h, axis=1, keepdims=True)
    scale = lax.rsqrt(squares * (1.0 / width) + EPS)
    for lo in range(0, width, step):
        cols = slice(lo, lo + step)
        gain = gain_ref[cols].astype(jnp.float32).reshape(1, step)
        out_ref[:, cols] = (hidden[:, cols] * scale * gain).astype(jnp.bfloat16)


def lent_kernel(count_ref, qkv_hbm, resid_hbm, weight_hbm, bias_hbm, gain_hbm, out_ref, *scratch):
    encode(count_ref[0, 0] - 1, qkv_hbm, resid_hbm, weight_hbm, bias_hbm, gain_hbm, out_ref, *scratch)


def split_index(index, n_seq, cap):
    step = index // (GROUP * cap)
    rest = index - step * (GROUP * cap)
    patch = rest // cap
    return step, patch, rest - patch * cap


def own_kernel(
    n_seq, cap, peer, count_ref, send_ref, me_ref, slot_ref, row_ref,
    qkv_hbm, resid_hbm, weight_hbm, bias_hbm, gain_hbm,
    packed_ref, borrow_ref, place_ref, normed, own_ref, *scratch,
):
    rows = normed.shape[0]
    slots = n_seq * cap
    sent = slots * GROUP
    tokens = rows // GROUP
    me = me_ref[0, 0]

    def make_one_hots():
        step, patch, rank = split_index(lax.broadcasted_iota(jnp.int32, (sent, 1), 0), n_seq, cap)
        row_code = (peer(me, step, 1) * cap + rank) * GROUP + patch
        token = lax.broadcasted_iota(jnp.int32, (tokens, rows), 0)
        column = lax.broadcasted_iota(jnp.int32, (tokens, rows), 1)
        spread = one_hot((column >= token * GROUP) & (column < (token + 1) * GROUP))
        slot = jnp.broadcast_to(slot_ref[...].astype(jnp.float32), (16, tokens)).astype(jnp.bfloat16)
        slot = dot32(slot, spread)[:1].astype(jnp.int32)
        index = lax.broadcasted_iota(jnp.int32, (1, rows), 1)
        col_code = slot * GROUP + jnp.bitwise_and(index, GROUP - 1)
        kept = (count_ref[0, 0] - send_ref[0, 0]) * WIN
        last = rows - WIN
        own_ref[...] = one_hot(row_code == jnp.where(index < kept, col_code, -1))
        borrow_ref[...] = one_hot(row_code == jnp.where(kept > last, -1, col_code[:, last:]))

        step, patch, rank = split_index(lax.broadcasted_iota(jnp.int32, (1, sent), 1), n_seq, cap)
        arrive = peer(me, step, -1) * cap + rank
        pick = one_hot(lax.broadcasted_iota(jnp.int32, (slots, sent), 0) == arrive)
        target = jnp.broadcast_to(row_ref[...].astype(jnp.float32), (16, slots)).astype(jnp.bfloat16)
        target = dot32(target, pick)[:1].astype(jnp.int32)
        out_row = lax.broadcasted_iota(jnp.int32, (tokens, sent), 0)
        for j in range(GROUP):
            place_ref[j * tokens : (j + 1) * tokens, :] = one_hot((target == out_row) & (patch == j))

    encode(0, qkv_hbm, resid_hbm, weight_hbm, bias_hbm, gain_hbm, normed, *scratch, while_copying=make_one_hots)
    packed_ref[...] = dot32(own_ref[...], normed[...]).astype(jnp.bfloat16)


def encode_call(kernel, blocks, scalars, slots, qkv, resid, weight, bias, gain, out_shape, extra):
    width = resid.shape[2]
    rows = blocks * WIN
    vmem = pl.BlockSpec(memory_space=pltpu.VMEM)
    smem = pl.BlockSpec(memory_space=pltpu.SMEM)
    hbm = pl.BlockSpec(memory_space=pltpu.HBM)
    return pl.pallas_call(
        kernel,
        out_shape=out_shape,
        in_specs=[smem] * len(scalars) + [vmem] * len(slots) + [hbm] * 5,
        out_specs=jax.tree.map(lambda _: vmem, out_shape),
        scratch_shapes=extra
        + [
            pltpu.VMEM((blocks, WIN, 3 * width), jnp.bfloat16),
            pltpu.VMEM((blocks, WIN, width), jnp.bfloat16),
            pltpu.VMEM((width, width), jnp.bfloat16),
            pltpu.VMEM((rows, width), jnp.bfloat16),
            pltpu.VMEM((rows, width), jnp.float32),
            pltpu.VMEM((width,), jnp.bfloat16),
            pltpu.VMEM((width,), jnp.bfloat16),
            pltpu.SemaphoreType.DMA((5,)),
        ],
        compiler_params=pltpu.CompilerParams(vmem_limit_bytes=24 << 20),
        cost_estimate=pl.CostEstimate(
            flops=2 * rows * width * width + 8 * rows * WIN * width,
            bytes_accessed=2 * (width * width + 5 * rows * width),
            transcendentals=rows * WIN * HEADS,
        ),
    )(*scalars, *slots, *(pltpu.with_memory_space_constraint(a, pltpu.HBM) for a in (qkv, resid, weight, bias, gain)))


def pack_kernel(packed_ref, borrow_ref, borrowed_ref, *out_refs):
    total = packed_ref[...].astype(jnp.float32) + dot32(borrow_ref[...], borrowed_ref[...])
    start = 0
    for out_ref in out_refs:
        stop = start + out_ref.shape[0]
        out_ref[...] = total[start:stop].astype(jnp.bfloat16)
        start = stop


def forward_kernel(double_ref, after_ref, out_ref):
    rows = out_ref.shape[0]
    out_ref[...] = double_ref[...].astype(jnp.float32)[rows:].astype(jnp.bfloat16)


def place_kernel(place_ref, *refs):
    *in_refs, out_hbm, out, sems = refs
    tokens = out.shape[0]
    chunks = [ref[...].astype(jnp.float32) for ref in in_refs]
    if len(chunks) > 1:
        chunks[1] = chunks[1][: chunks[0].shape[0]]
    arrived = chunks[0] if len(chunks) == 1 else jnp.concatenate(chunks, axis=0)
    arrived = arrived.astype(jnp.bfloat16)
    width = arrived.shape[1]
    copies = []
    for j in range(GROUP):
        cols = slice(j * width, (j + 1) * width)
        out[:, cols] = dot32(place_ref[j * tokens : (j + 1) * tokens, :], arrived).astype(jnp.bfloat16)
        copies.append(pltpu.make_async_copy(out.at[:, cols], out_hbm.at[:, cols], sems.at[j]))
        copies[-1].start()
    for copy in copies:
        copy.wait()


def exchange_steps(n_seq):
    return [(0, 0)] + [(dz, dc) for dz in range(1, n_seq // CORES) for dc in range(CORES)] + [(0, 1)]


def chip_peer(n_seq, me, step, sign):
    n_z = n_seq // CORES
    offset = jnp.zeros_like(step)
    flip = jnp.zeros_like(step)
    for i, (dz, dc) in enumerate(exchange_steps(n_seq)):
        offset = jnp.where(step == i, dz, offset)
        flip = jnp.where(step == i, dc, flip)
    z = me // CORES + sign * offset
    z = jnp.where(z >= n_z, z - n_z, jnp.where(z < 0, z + n_z, z))
    return z * CORES + jnp.bitwise_xor(jnp.bitwise_and(me, 1), flip)


def per_device(
    qkv, resid, block_count, send_count, send_slot, lm_row, out_weight, out_bias, norm_gain
):
    width = resid.shape[2]
    row_total = send_slot.shape[1]
    tokens = WIN // GROUP
    blocks = row_total // tokens
    n_seq = lax.axis_size("seq")
    n_enc = lax.axis_size("enc")
    slots = lm_row.shape[1]
    cap = slots // n_seq
    chunk = GROUP * cap
    sent = slots * GROUP
    vmem = pl.BlockSpec(memory_space=pltpu.VMEM)
    small = pltpu.CompilerParams(vmem_limit_bytes=16 << 20)

    def rows_of(count, columns=width):
        return jax.ShapeDtypeStruct((count, columns), jnp.bfloat16)

    data = (qkv, resid, out_weight, out_bias, norm_gain)
    lent = encode_call(lent_kernel, 1, [block_count], [], *data, rows_of(WIN), [])
    borrowed = lax.ppermute(lent, "enc", [((i - 1) % n_enc, i) for i in range(n_enc)])

    by_steps = chunk % 8 == 0 and n_seq % CORES == 0
    peer = functools.partial(chip_peer, n_seq) if by_steps else lambda me, step, sign: step
    me = lax.axis_index("seq").astype(jnp.int32).reshape(1, 1)
    packed, borrow, place = encode_call(
        functools.partial(own_kernel, n_seq, cap, peer), blocks,
        [block_count, send_count, me], [send_slot, lm_row], *data,
        (rows_of(sent), rows_of(sent, WIN), rows_of(GROUP * row_total, sent)),
        [
            pltpu.VMEM((row_total * GROUP, width), jnp.bfloat16),
            pltpu.VMEM((sent, row_total * GROUP), jnp.bfloat16),
        ],
    )
    pieces = [chunk, CORES * chunk] + [chunk] * (n_seq - 1 - CORES) if by_steps else [sent]
    outgoing = pl.pallas_call(
        pack_kernel,
        out_shape=[rows_of(rows) for rows in pieces],
        in_specs=[vmem] * 3,
        out_specs=[vmem] * len(pieces),
        compiler_params=small,
    )(packed, borrow, borrowed)

    if by_steps:
        n_z = n_seq // CORES

        def exchange(part, dz, dc):
            return lax.ppermute(
                part, "seq", [(i, (i // CORES + dz) % n_z * CORES + (i + dc) % CORES) for i in range(n_seq)]
            )

        double = exchange(outgoing[1], 1, 0)
        rest = [exchange(part, *step) for part, step in zip(outgoing[2:], exchange_steps(n_seq)[1 + CORES :])]
        onward = pl.pallas_call(
            forward_kernel, out_shape=rows_of(chunk), in_specs=[vmem] * 2, out_specs=vmem, compiler_params=small
        )(double, rest[0])
        arrived = [outgoing[0], double, exchange(onward, 0, 1), *rest]
    else:
        arrived = [
            lax.all_to_all(
                outgoing[0].reshape(n_seq, chunk, width), "seq", split_axis=0, concat_axis=0, tiled=True
            ).reshape(sent, width)
        ]
    placed = pl.pallas_call(
        place_kernel,
        out_shape=rows_of(row_total, GROUP * width),
        in_specs=[vmem] * (1 + len(arrived)),
        out_specs=pl.BlockSpec(memory_space=pltpu.HBM),
        scratch_shapes=[pltpu.VMEM((row_total, GROUP * width), jnp.bfloat16), pltpu.SemaphoreType.DMA((GROUP,))],
        compiler_params=small,
    )(place, *arrived)
    return placed[None]


def solution(mesh):
    placed = (
        P("enc", "seq", None),
        P("enc", "seq", None),
        P("enc", "seq"),
        P("enc", "seq"),
        P("enc", "seq"),
        P("enc", "seq"),
        P(),
        P(),
        P(),
    )
    return jax.shard_map(
        per_device, mesh=mesh, in_specs=placed, out_specs=P("enc", "seq", None), check_vma=False
    )
```

```python
import functools
import math

import jax
import jax.numpy as jnp
from jax import lax
from jax.experimental import pallas as pl
from jax.experimental.pallas import tpu as pltpu
from jax.sharding import PartitionSpec as P

HEADS = 16
WIN = 64
LANES = 128
GROUP = 4
EPS = 1e-6
CORES = 2

NT = (((1,), (1,)), ((), ()))


def dot32(a, b):
    return jnp.dot(a, b, preferred_element_type=jnp.float32)


def one_hot(match):
    return match.astype(jnp.float32).astype(jnp.bfloat16)


def head_pairs(width):
    head = width // HEADS
    spans = []
    for start in range(0, width, 2 * head):
        lo = start // LANES * LANES
        spans.append((start, lo, -(-(start + 2 * head) // LANES) * LANES))
    return spans


def mask_period(width):
    return LANES // math.gcd(LANES, 2 * (width // HEADS))


def mask_scratch(width):
    return pltpu.VMEM((mask_period(width), 2 * WIN, 2 * LANES), jnp.bfloat16)


def make_masks(masks, width):
    head = width // HEADS
    for i in range(masks.shape[0]):
        start, lo, hi = head_pairs(width)[i]
        column = lax.broadcasted_iota(jnp.int32, masks.shape[1:], 1) + lo
        row = lax.broadcasted_iota(jnp.int32, masks.shape[1:], 0)
        begin = jnp.where(row < WIN, start, start + head)
        masks[i] = one_hot((column >= begin) & (column < begin + head))


def attend(qkv, b, masks, attended, width):
    rate = math.log2(math.e) / math.sqrt(width // HEADS)
    period = masks.shape[0]
    spans = [(lo, hi) for _, lo, hi in head_pairs(width)]
    first = lax.broadcasted_iota(jnp.int32, (WIN, 2 * WIN), 1) < WIN

    def both_heads(part, pair):
        return jnp.concatenate([part, part], axis=0) * masks[pair % period]

    scores = [
        lax.dot_general(
            qkv[b, :, lo:hi], both_heads(qkv[b, :, width + lo : width + hi], pair), NT, preferred_element_type=jnp.float32
        )
        for pair, (lo, hi) in enumerate(spans)
    ]
    tops = [
        (
            jnp.max(jnp.where(first, s, -jnp.inf), axis=1, keepdims=True),
            jnp.max(jnp.where(first, -jnp.inf, s), axis=1, keepdims=True),
        )
        for s in scores
    ]
    raised = [
        jnp.exp2((s - jnp.where(first, top0, top1)) * rate).astype(jnp.bfloat16) for s, (top0, top1) in zip(scores, tops)
    ]
    parts = [
        dot32(raised[pair], both_heads(qkv[b, :, 2 * width + lo : 2 * width + hi], pair))
        for pair, (lo, hi) in enumerate(spans)
    ]
    norms = [None] * len(spans)
    for i in range(period):
        same = range(i, len(spans), period)
        norm = dot32(jnp.concatenate([raised[pair] for pair in same], axis=0), masks[i])
        for n, pair in enumerate(same):
            norms[pair] = norm[n * WIN : (n + 1) * WIN]
    for tile in range(width // LANES):
        at = tile * LANES
        inside = [(pair, slice(at - lo, at - lo + LANES)) for pair, (lo, hi) in enumerate(spans) if lo <= at < hi]
        total = sum(parts[pair][:, cols] for pair, cols in inside)
        norm = sum(norms[pair][:, cols] for pair, cols in inside)
        attended[b * WIN : (b + 1) * WIN, at : at + LANES] = (total / norm).astype(jnp.bfloat16)


def encode(
    slot, qkv_hbm, resid_hbm, weight_hbm, bias_hbm, gain_hbm, out_ref,
    qkv, resid, weight, attended, hidden, bias_ref, gain_ref, masks, sems,
):
    blocks = qkv.shape[0]
    width = resid.shape[2]
    at = pl.ds(slot, blocks)
    pairs = [
        (qkv_hbm.at[at], qkv), (weight_hbm, weight), (resid_hbm.at[at], resid), (bias_hbm, bias_ref), (gain_hbm, gain_ref)
    ]
    copies = [pltpu.make_async_copy(a, b, sems.at[i]) for i, (a, b) in enumerate(pairs)]
    for copy in copies:
        copy.start()
    make_masks(masks, width)
    copies[0].wait()
    for b in range(blocks):
        attend(qkv, b, masks, attended, width)
    for copy in copies[1:]:
        copy.wait()
    rows = blocks * WIN
    squares = jnp.zeros((rows, 1), jnp.float32)
    step = 2 * LANES
    for lo in range(0, width, step):
        cols = slice(lo, lo + step)
        h = dot32(attended[...], weight[:, cols])
        h = h + bias_ref[cols].astype(jnp.float32).reshape(1, step)
        h = h + resid[:, :, cols].reshape(rows, step).astype(jnp.float32)
        hidden[:, cols] = h
        squares = squares + jnp.sum(h * h, axis=1, keepdims=True)
    scale = lax.rsqrt(squares * (1.0 / width) + EPS)
    for lo in range(0, width, step):
        cols = slice(lo, lo + step)
        gain = gain_ref[cols].astype(jnp.float32).reshape(1, step)
        out_ref[:, cols] = (hidden[:, cols] * scale * gain).astype(jnp.bfloat16)


def lent_kernel(count_ref, qkv_hbm, resid_hbm, weight_hbm, bias_hbm, gain_hbm, out_ref, *scratch):
    encode(count_ref[0, 0] - 1, qkv_hbm, resid_hbm, weight_hbm, bias_hbm, gain_hbm, out_ref, *scratch)


def split_index(index, n_seq, cap):
    step = index // (GROUP * cap)
    rest = index - step * (GROUP * cap)
    patch = rest // cap
    return step, patch, rest - patch * cap


def own_kernel(
    n_seq, cap, peer, count_ref, send_ref, me_ref, slot_ref, row_ref,
    qkv_hbm, resid_hbm, weight_hbm, bias_hbm, gain_hbm,
    packed_ref, borrow_ref, place_ref, normed, *scratch,
):
    rows = normed.shape[0]
    slots = n_seq * cap
    sent = slots * GROUP
    tokens = rows // GROUP
    me = me_ref[0, 0]
    encode(0, qkv_hbm, resid_hbm, weight_hbm, bias_hbm, gain_hbm, normed, *scratch)

    step, patch, rank = split_index(lax.broadcasted_iota(jnp.int32, (sent, 1), 0), n_seq, cap)
    row_code = (peer(me, step, 1) * cap + rank) * GROUP + patch
    token = lax.broadcasted_iota(jnp.int32, (tokens, rows), 0)
    column = lax.broadcasted_iota(jnp.int32, (tokens, rows), 1)
    spread = one_hot((column >= token * GROUP) & (column < (token + 1) * GROUP))
    slot = jnp.broadcast_to(slot_ref[...].astype(jnp.float32), (16, tokens)).astype(jnp.bfloat16)
    slot = dot32(slot, spread)[:1].astype(jnp.int32)
    index = lax.broadcasted_iota(jnp.int32, (1, rows), 1)
    col_code = slot * GROUP + jnp.bitwise_and(index, GROUP - 1)
    kept = (count_ref[0, 0] - send_ref[0, 0]) * WIN
    last = rows - WIN
    own = one_hot(row_code == jnp.where(index < kept, col_code, -1))
    packed_ref[...] = dot32(own, normed[...]).astype(jnp.bfloat16)
    borrow_ref[...] = one_hot(row_code == jnp.where(kept > last, -1, col_code[:, last:]))

    step, patch, rank = split_index(lax.broadcasted_iota(jnp.int32, (1, sent), 1), n_seq, cap)
    arrive = peer(me, step, -1) * cap + rank
    pick = one_hot(lax.broadcasted_iota(jnp.int32, (slots, sent), 0) == arrive)
    target = jnp.broadcast_to(row_ref[...].astype(jnp.float32), (16, slots)).astype(jnp.bfloat16)
    target = dot32(target, pick)[:1].astype(jnp.int32)
    out_row = lax.broadcasted_iota(jnp.int32, (tokens, sent), 0)
    for j in range(GROUP):
        place_ref[j * tokens : (j + 1) * tokens, :] = one_hot((target == out_row) & (patch == j))


def encode_call(kernel, blocks, scalars, slots, qkv, resid, weight, bias, gain, out_shape, extra):
    width = resid.shape[2]
    rows = blocks * WIN
    vmem = pl.BlockSpec(memory_space=pltpu.VMEM)
    smem = pl.BlockSpec(memory_space=pltpu.SMEM)
    hbm = pl.BlockSpec(memory_space=pltpu.HBM)
    return pl.pallas_call(
        kernel,
        out_shape=out_shape,
        in_specs=[smem] * len(scalars) + [vmem] * len(slots) + [hbm] * 5,
        out_specs=jax.tree.map(lambda _: vmem, out_shape),
        scratch_shapes=extra
        + [
            pltpu.VMEM((blocks, WIN, 3 * width), jnp.bfloat16),
            pltpu.VMEM((blocks, WIN, width), jnp.bfloat16),
            pltpu.VMEM((width, width), jnp.bfloat16),
            pltpu.VMEM((rows, width), jnp.bfloat16),
            pltpu.VMEM((rows, width), jnp.float32),
            pltpu.VMEM((width,), jnp.bfloat16),
            pltpu.VMEM((width,), jnp.bfloat16),
            mask_scratch(width),
            pltpu.SemaphoreType.DMA((5,)),
        ],
        compiler_params=pltpu.CompilerParams(vmem_limit_bytes=24 << 20),
        cost_estimate=pl.CostEstimate(
            flops=2 * rows * width * width + 8 * rows * WIN * width,
            bytes_accessed=2 * (width * width + 5 * rows * width),
            transcendentals=rows * WIN * HEADS,
        ),
    )(*scalars, *slots, *(pltpu.with_memory_space_constraint(a, pltpu.HBM) for a in (qkv, resid, weight, bias, gain)))


def pack_kernel(packed_ref, borrow_ref, borrowed_ref, *out_refs):
    total = packed_ref[...].astype(jnp.float32) + dot32(borrow_ref[...], borrowed_ref[...])
    start = 0
    for out_ref in out_refs:
        stop = start + out_ref.shape[0]
        out_ref[...] = total[start:stop].astype(jnp.bfloat16)
        start = stop


def forward_kernel(double_ref, after_ref, out_ref):
    rows = out_ref.shape[0]
    out_ref[...] = double_ref[...].astype(jnp.float32)[rows:].astype(jnp.bfloat16)


def place_kernel(place_ref, *refs):
    *in_refs, out_hbm, out, sems = refs
    tokens = out.shape[0]
    chunks = [ref[...].astype(jnp.float32) for ref in in_refs]
    if len(chunks) > 1:
        chunks[1] = chunks[1][: chunks[0].shape[0]]
    arrived = chunks[0] if len(chunks) == 1 else jnp.concatenate(chunks, axis=0)
    arrived = arrived.astype(jnp.bfloat16)
    width = arrived.shape[1]
    copies = []
    for j in range(GROUP):
        cols = slice(j * width, (j + 1) * width)
        out[:, cols] = dot32(place_ref[j * tokens : (j + 1) * tokens, :], arrived).astype(jnp.bfloat16)
        copies.append(pltpu.make_async_copy(out.at[:, cols], out_hbm.at[:, cols], sems.at[j]))
        copies[-1].start()
    for copy in copies:
        copy.wait()


def exchange_steps(n_seq):
    return [(0, 0)] + [(dz, dc) for dz in range(1, n_seq // CORES) for dc in range(CORES)] + [(0, 1)]


def chip_peer(n_seq, me, step, sign):
    n_z = n_seq // CORES
    offset = jnp.zeros_like(step)
    flip = jnp.zeros_like(step)
    for i, (dz, dc) in enumerate(exchange_steps(n_seq)):
        offset = jnp.where(step == i, dz, offset)
        flip = jnp.where(step == i, dc, flip)
    z = me // CORES + sign * offset
    z = jnp.where(z >= n_z, z - n_z, jnp.where(z < 0, z + n_z, z))
    return z * CORES + jnp.bitwise_xor(jnp.bitwise_and(me, 1), flip)


def per_device(
    qkv, resid, block_count, send_count, send_slot, lm_row, out_weight, out_bias, norm_gain
):
    width = resid.shape[2]
    row_total = send_slot.shape[1]
    tokens = WIN // GROUP
    blocks = row_total // tokens
    n_seq = lax.axis_size("seq")
    n_enc = lax.axis_size("enc")
    slots = lm_row.shape[1]
    cap = slots // n_seq
    chunk = GROUP * cap
    sent = slots * GROUP
    vmem = pl.BlockSpec(memory_space=pltpu.VMEM)
    small = pltpu.CompilerParams(vmem_limit_bytes=16 << 20)

    def rows_of(count, columns=width):
        return jax.ShapeDtypeStruct((count, columns), jnp.bfloat16)

    data = (qkv, resid, out_weight, out_bias, norm_gain)
    lent = encode_call(lent_kernel, 1, [block_count], [], *data, rows_of(WIN), [])
    borrowed = lax.ppermute(lent, "enc", [((i - 1) % n_enc, i) for i in range(n_enc)])

    by_steps = chunk % 8 == 0 and n_seq % CORES == 0
    peer = functools.partial(chip_peer, n_seq) if by_steps else lambda me, step, sign: step
    me = lax.axis_index("seq").astype(jnp.int32).reshape(1, 1)
    packed, borrow, place = encode_call(
        functools.partial(own_kernel, n_seq, cap, peer), blocks,
        [block_count, send_count, me], [send_slot, lm_row], *data,
        (rows_of(sent), rows_of(sent, WIN), rows_of(GROUP * row_total, sent)),
        [pltpu.VMEM((row_total * GROUP, width), jnp.bfloat16)],
    )
    pieces = [chunk, CORES * chunk] + [chunk] * (n_seq - 1 - CORES) if by_steps else [sent]
    outgoing = pl.pallas_call(
        pack_kernel,
        out_shape=[rows_of(rows) for rows in pieces],
        in_specs=[vmem] * 3,
        out_specs=[vmem] * len(pieces),
        compiler_params=small,
    )(packed, borrow, borrowed)

    if by_steps:
        n_z = n_seq // CORES

        def exchange(part, dz, dc):
            return lax.ppermute(
                part, "seq", [(i, (i // CORES + dz) % n_z * CORES + (i + dc) % CORES) for i in range(n_seq)]
            )

        double = exchange(outgoing[1], 1, 0)
        rest = [exchange(part, *step) for part, step in zip(outgoing[2:], exchange_steps(n_seq)[1 + CORES :])]
        onward = pl.pallas_call(
            forward_kernel, out_shape=rows_of(chunk), in_specs=[vmem] * 2, out_specs=vmem, compiler_params=small
        )(double, rest[0])
        arrived = [outgoing[0], double, exchange(onward, 0, 1), *rest]
    else:
        arrived = [
            lax.all_to_all(
                outgoing[0].reshape(n_seq, chunk, width), "seq", split_axis=0, concat_axis=0, tiled=True
            ).reshape(sent, width)
        ]
    placed = pl.pallas_call(
        place_kernel,
        out_shape=rows_of(row_total, GROUP * width),
        in_specs=[vmem] * (1 + len(arrived)),
        out_specs=pl.BlockSpec(memory_space=pltpu.HBM),
        scratch_shapes=[pltpu.VMEM((row_total, GROUP * width), jnp.bfloat16), pltpu.SemaphoreType.DMA((GROUP,))],
        compiler_params=small,
    )(place, *arrived)
    return placed[None]


def solution(mesh):
    placed = (
        P("enc", "seq", None),
        P("enc", "seq", None),
        P("enc", "seq"),
        P("enc", "seq"),
        P("enc", "seq"),
        P("enc", "seq"),
        P(),
        P(),
        P(),
    )
    return jax.shard_map(
        per_device, mesh=mesh, in_specs=placed, out_specs=P("enc", "seq", None), check_vma=False
    )
```

```python
import functools
import math

import jax
import jax.numpy as jnp
from jax import lax
from jax.experimental import pallas as pl
from jax.experimental.pallas import tpu as pltpu
from jax.sharding import PartitionSpec as P

HEADS = 16
WIN = 64
LANES = 128
GROUP = 4
EPS = 1e-6
CORES = 2

NT = (((1,), (1,)), ((), ()))


def dot32(a, b):
    return jnp.dot(a, b, preferred_element_type=jnp.float32)


def one_hot(match):
    return match.astype(jnp.float32).astype(jnp.bfloat16)


def head_pairs(width):
    head = width // HEADS
    spans = []
    for start in range(0, width, 2 * head):
        lo = start // LANES * LANES
        spans.append((start, lo, -(-(start + 2 * head) // LANES) * LANES))
    return spans


def mask_period(width):
    return LANES // math.gcd(LANES, 2 * (width // HEADS))


def mask_scratch(width):
    return pltpu.VMEM((mask_period(width), 2 * WIN, 2 * LANES), jnp.bfloat16)


def make_masks(masks, width):
    head = width // HEADS
    for i in range(masks.shape[0]):
        start, lo, hi = head_pairs(width)[i]
        column = lax.broadcasted_iota(jnp.int32, masks.shape[1:], 1) + lo
        row = lax.broadcasted_iota(jnp.int32, masks.shape[1:], 0)
        begin = jnp.where(row < WIN, start, start + head)
        masks[i] = one_hot((column >= begin) & (column < begin + head))


def attend(qkv, b, masks, attended, width):
    rate = math.log2(math.e) / math.sqrt(width // HEADS)
    period = masks.shape[0]
    spans = [(lo, hi) for _, lo, hi in head_pairs(width)]
    first = lax.broadcasted_iota(jnp.int32, (WIN, 2 * WIN), 1) < WIN

    def both_heads(part, pair):
        return jnp.concatenate([part, part], axis=0) * masks[pair % period]

    scores = [
        lax.dot_general(
            qkv[b, :, lo:hi], both_heads(qkv[b, :, width + lo : width + hi], pair), NT, preferred_element_type=jnp.float32
        )
        for pair, (lo, hi) in enumerate(spans)
    ]
    tops = [
        (
            jnp.max(jnp.where(first, s, -jnp.inf), axis=1, keepdims=True),
            jnp.max(jnp.where(first, -jnp.inf, s), axis=1, keepdims=True),
        )
        for s in scores
    ]
    raised = [
        jnp.exp2((s - jnp.where(first, top0, top1)) * rate).astype(jnp.bfloat16) for s, (top0, top1) in zip(scores, tops)
    ]
    parts = [
        dot32(raised[pair], both_heads(qkv[b, :, 2 * width + lo : 2 * width + hi], pair))
        for pair, (lo, hi) in enumerate(spans)
    ]
    norms = [None] * len(spans)
    for i in range(period):
        same = range(i, len(spans), period)
        norm = dot32(jnp.concatenate([raised[pair] for pair in same], axis=0), masks[i])
        for n, pair in enumerate(same):
            norms[pair] = norm[n * WIN : (n + 1) * WIN]
    for tile in range(width // LANES):
        at = tile * LANES
        inside = [(pair, slice(at - lo, at - lo + LANES)) for pair, (lo, hi) in enumerate(spans) if lo <= at < hi]
        total = sum(parts[pair][:, cols] for pair, cols in inside)
        norm = sum(norms[pair][:, cols] for pair, cols in inside)
        attended[b * WIN : (b + 1) * WIN, at : at + LANES] = (total / norm).astype(jnp.bfloat16)


def project(attended, resid, weight, bias, gain, hidden, out_ref):
    rows, width = hidden.shape
    step = 2 * LANES
    chunks = [slice(lo, lo + step) for lo in range(0, width, step)]
    squares = jnp.zeros((rows, 1), jnp.float32)
    for cols in chunks:
        h = dot32(attended[...], weight[:, cols])
        h = h + bias[cols].astype(jnp.float32).reshape(1, step)
        h = h + resid[:, :, cols].reshape(rows, step).astype(jnp.float32)
        hidden[:, cols] = h
        squares = squares + jnp.sum(h * h, axis=1, keepdims=True)
    scale = lax.rsqrt(squares * (1.0 / width) + EPS)
    for cols in chunks:
        out_ref[:, cols] = (hidden[:, cols] * scale * gain[cols].astype(jnp.float32).reshape(1, step)).astype(jnp.bfloat16)


def lent_attention_kernel(count_ref, qkv_hbm, resid_hbm, attended, resid, qkv, masks, sems):
    at = pl.ds(count_ref[0, 0] - 1, 1)
    qkv_copy = pltpu.make_async_copy(qkv_hbm.at[at], qkv, sems.at[0])
    resid_copy = pltpu.make_async_copy(resid_hbm.at[at], resid, sems.at[1])
    qkv_copy.start()
    resid_copy.start()
    width = resid.shape[2]
    make_masks(masks, width)
    qkv_copy.wait()
    for b in range(qkv.shape[0]):
        attend(qkv, b, masks, attended, width)
    resid_copy.wait()


def lent_project_kernel(attended, resid, weight, bias, gain, out_ref, hidden):
    project(attended, resid, weight, bias, gain, hidden, out_ref)


def encode(qkv_hbm, resid_hbm, weight_hbm, bias_hbm, gain_hbm, out_ref, qkv, resid, weight, attended, hidden, bias, gain, masks, sems):
    at = pl.ds(0, qkv.shape[0])
    pairs = [(qkv_hbm.at[at], qkv), (weight_hbm, weight), (resid_hbm.at[at], resid), (bias_hbm, bias), (gain_hbm, gain)]
    copies = [pltpu.make_async_copy(a, b, sems.at[i]) for i, (a, b) in enumerate(pairs)]
    for copy in copies:
        copy.start()
    width = resid.shape[2]
    make_masks(masks, width)
    copies[0].wait()
    for b in range(qkv.shape[0]):
        attend(qkv, b, masks, attended, width)
    for copy in copies[1:]:
        copy.wait()
    project(attended, resid, weight, bias, gain, hidden, out_ref)


def split_index(index, n_seq, cap):
    step = index // (GROUP * cap)
    rest = index - step * (GROUP * cap)
    patch = rest // cap
    return step, patch, rest - patch * cap


def own_kernel(
    n_seq, cap, peer, count_ref, send_ref, me_ref, slot_ref, row_ref,
    qkv_hbm, resid_hbm, weight_hbm, bias_hbm, gain_hbm,
    packed_ref, borrow_ref, place_ref, normed, *scratch,
):
    rows = normed.shape[0]
    slots = n_seq * cap
    sent = slots * GROUP
    tokens = rows // GROUP
    me = me_ref[0, 0]
    encode(qkv_hbm, resid_hbm, weight_hbm, bias_hbm, gain_hbm, normed, *scratch)

    step, patch, rank = split_index(lax.broadcasted_iota(jnp.int32, (sent, 1), 0), n_seq, cap)
    row_code = (peer(me, step, 1) * cap + rank) * GROUP + patch
    token = lax.broadcasted_iota(jnp.int32, (tokens, rows), 0)
    column = lax.broadcasted_iota(jnp.int32, (tokens, rows), 1)
    spread = one_hot((column >= token * GROUP) & (column < (token + 1) * GROUP))
    slot = jnp.broadcast_to(slot_ref[...].astype(jnp.float32), (16, tokens)).astype(jnp.bfloat16)
    slot = dot32(slot, spread)[:1].astype(jnp.int32)
    index = lax.broadcasted_iota(jnp.int32, (1, rows), 1)
    col_code = slot * GROUP + jnp.bitwise_and(index, GROUP - 1)
    kept = (count_ref[0, 0] - send_ref[0, 0]) * WIN
    last = rows - WIN
    own = one_hot(row_code == jnp.where(index < kept, col_code, -1))
    packed_ref[...] = dot32(own, normed[...]).astype(jnp.bfloat16)
    borrow_ref[...] = one_hot(row_code == jnp.where(kept > last, -1, col_code[:, last:]))

    step, patch, rank = split_index(lax.broadcasted_iota(jnp.int32, (1, sent), 1), n_seq, cap)
    arrive = peer(me, step, -1) * cap + rank
    pick = one_hot(lax.broadcasted_iota(jnp.int32, (slots, sent), 0) == arrive)
    target = jnp.broadcast_to(row_ref[...].astype(jnp.float32), (16, slots)).astype(jnp.bfloat16)
    target = dot32(target, pick)[:1].astype(jnp.int32)
    out_row = lax.broadcasted_iota(jnp.int32, (tokens, sent), 0)
    for j in range(GROUP):
        place_ref[j * tokens : (j + 1) * tokens, :] = one_hot((target == out_row) & (patch == j))


def in_hbm(*arrays):
    return [pltpu.with_memory_space_constraint(a, pltpu.HBM) for a in arrays]


def encode_lent(count, qkv, resid, weight, bias, gain):
    width = resid.shape[2]
    vmem = pl.BlockSpec(memory_space=pltpu.VMEM)
    hbm = pl.BlockSpec(memory_space=pltpu.HBM)
    small = pltpu.CompilerParams(vmem_limit_bytes=16 << 20)
    attended, rows = pl.pallas_call(
        lent_attention_kernel,
        out_shape=(
            jax.ShapeDtypeStruct((WIN, width), jnp.bfloat16),
            jax.ShapeDtypeStruct((1, WIN, width), jnp.bfloat16),
        ),
        in_specs=[pl.BlockSpec(memory_space=pltpu.SMEM), hbm, hbm],
        out_specs=(vmem, vmem),
        scratch_shapes=[pltpu.VMEM((1, WIN, 3 * width), jnp.bfloat16), mask_scratch(width), pltpu.SemaphoreType.DMA((2,))],
        compiler_params=small,
        cost_estimate=pl.CostEstimate(
            flops=1 << 30, bytes_accessed=1 << 20, transcendentals=WIN * WIN * HEADS
        ),
    )(count, *in_hbm(qkv, resid))
    return pl.pallas_call(
        lent_project_kernel,
        out_shape=jax.ShapeDtypeStruct((WIN, width), jnp.bfloat16),
        in_specs=[vmem] * 5,
        out_specs=vmem,
        scratch_shapes=[pltpu.VMEM((WIN, width), jnp.float32)],
        compiler_params=small,
        cost_estimate=pl.CostEstimate(
            flops=2 * WIN * width * width, bytes_accessed=2 * (width * width + 3 * WIN * width), transcendentals=0
        ),
    )(attended, rows, weight, bias, gain)


def encode_own(kernel, blocks, scalars, slots, qkv, resid, weight, bias, gain, out_shape, extra):
    width = resid.shape[2]
    rows = blocks * WIN
    vmem = pl.BlockSpec(memory_space=pltpu.VMEM)
    smem = pl.BlockSpec(memory_space=pltpu.SMEM)
    hbm = pl.BlockSpec(memory_space=pltpu.HBM)
    return pl.pallas_call(
        kernel,
        out_shape=out_shape,
        in_specs=[smem] * len(scalars) + [vmem] * len(slots) + [hbm] * 5,
        out_specs=jax.tree.map(lambda _: vmem, out_shape),
        scratch_shapes=extra
        + [
            pltpu.VMEM((blocks, WIN, 3 * width), jnp.bfloat16),
            pltpu.VMEM((blocks, WIN, width), jnp.bfloat16),
            pltpu.VMEM((width, width), jnp.bfloat16),
            pltpu.VMEM((rows, width), jnp.bfloat16),
            pltpu.VMEM((rows, width), jnp.float32),
            pltpu.VMEM((width,), jnp.bfloat16),
            pltpu.VMEM((width,), jnp.bfloat16),
            mask_scratch(width),
            pltpu.SemaphoreType.DMA((5,)),
        ],
        compiler_params=pltpu.CompilerParams(vmem_limit_bytes=24 << 20),
        cost_estimate=pl.CostEstimate(
            flops=2 * rows * width * width + 8 * rows * WIN * width,
            bytes_accessed=2 * (width * width + 5 * rows * width),
            transcendentals=rows * WIN * HEADS,
        ),
    )(*scalars, *slots, *in_hbm(qkv, resid, weight, bias, gain))


def pack_kernel(packed_ref, borrow_ref, borrowed_ref, *out_refs):
    total = packed_ref[...].astype(jnp.float32) + dot32(borrow_ref[...], borrowed_ref[...])
    start = 0
    for out_ref in out_refs:
        stop = start + out_ref.shape[0]
        out_ref[...] = total[start:stop].astype(jnp.bfloat16)
        start = stop


def forward_kernel(double_ref, after_ref, out_ref):
    rows = out_ref.shape[0]
    out_ref[...] = double_ref[...].astype(jnp.float32)[rows:].astype(jnp.bfloat16)


def place_kernel(place_ref, *refs):
    *in_refs, out_hbm, out, sems = refs
    tokens = out.shape[0]
    chunks = [ref[...].astype(jnp.float32) for ref in in_refs]
    if len(chunks) > 1:
        chunks[1] = chunks[1][: chunks[0].shape[0]]
    arrived = chunks[0] if len(chunks) == 1 else jnp.concatenate(chunks, axis=0)
    arrived = arrived.astype(jnp.bfloat16)
    width = arrived.shape[1]
    copies = []
    for j in range(GROUP):
        cols = slice(j * width, (j + 1) * width)
        out[:, cols] = dot32(place_ref[j * tokens : (j + 1) * tokens, :], arrived).astype(jnp.bfloat16)
        copies.append(pltpu.make_async_copy(out.at[:, cols], out_hbm.at[:, cols], sems.at[j]))
        copies[-1].start()
    for copy in copies:
        copy.wait()


def exchange_steps(n_seq):
    return [(0, 0)] + [(dz, dc) for dz in range(1, n_seq // CORES) for dc in range(CORES)] + [(0, 1)]


def chip_peer(n_seq, me, step, sign):
    n_z = n_seq // CORES
    offset = jnp.zeros_like(step)
    flip = jnp.zeros_like(step)
    for i, (dz, dc) in enumerate(exchange_steps(n_seq)):
        offset = jnp.where(step == i, dz, offset)
        flip = jnp.where(step == i, dc, flip)
    z = me // CORES + sign * offset
    z = jnp.where(z >= n_z, z - n_z, jnp.where(z < 0, z + n_z, z))
    return z * CORES + jnp.bitwise_xor(jnp.bitwise_and(me, 1), flip)


def per_device(
    qkv, resid, block_count, send_count, send_slot, lm_row, out_weight, out_bias, norm_gain
):
    width = resid.shape[2]
    row_total = send_slot.shape[1]
    tokens = WIN // GROUP
    blocks = row_total // tokens
    n_seq = lax.axis_size("seq")
    n_enc = lax.axis_size("enc")
    slots = lm_row.shape[1]
    cap = slots // n_seq
    chunk = GROUP * cap
    sent = slots * GROUP
    vmem = pl.BlockSpec(memory_space=pltpu.VMEM)
    small = pltpu.CompilerParams(vmem_limit_bytes=16 << 20)

    def rows_of(count, columns=width):
        return jax.ShapeDtypeStruct((count, columns), jnp.bfloat16)

    data = (qkv, resid, out_weight, out_bias, norm_gain)
    lent = encode_lent(block_count, *data)
    borrowed = lax.ppermute(lent, "enc", [((i - 1) % n_enc, i) for i in range(n_enc)])

    by_steps = chunk % 8 == 0 and n_seq % CORES == 0
    peer = functools.partial(chip_peer, n_seq) if by_steps else lambda me, step, sign: step
    me = lax.axis_index("seq").astype(jnp.int32).reshape(1, 1)
    packed, borrow, place = encode_own(
        functools.partial(own_kernel, n_seq, cap, peer), blocks,
        [block_count, send_count, me], [send_slot, lm_row], *data,
        (rows_of(sent), rows_of(sent, WIN), rows_of(GROUP * row_total, sent)),
        [pltpu.VMEM((row_total * GROUP, width), jnp.bfloat16)],
    )
    pieces = [chunk, CORES * chunk] + [chunk] * (n_seq - 1 - CORES) if by_steps else [sent]
    outgoing = pl.pallas_call(
        pack_kernel,
        out_shape=[rows_of(rows) for rows in pieces],
        in_specs=[vmem] * 3,
        out_specs=[vmem] * len(pieces),
        compiler_params=small,
    )(packed, borrow, borrowed)

    if by_steps:
        n_z = n_seq // CORES

        def exchange(part, dz, dc):
            return lax.ppermute(
                part, "seq", [(i, (i // CORES + dz) % n_z * CORES + (i + dc) % CORES) for i in range(n_seq)]
            )

        double = exchange(outgoing[1], 1, 0)
        rest = [exchange(part, *step) for part, step in zip(outgoing[2:], exchange_steps(n_seq)[1 + CORES :])]
        onward = pl.pallas_call(
            forward_kernel, out_shape=rows_of(chunk), in_specs=[vmem] * 2, out_specs=vmem, compiler_params=small
        )(double, rest[0])
        arrived = [outgoing[0], double, exchange(onward, 0, 1), *rest]
    else:
        arrived = [
            lax.all_to_all(
                outgoing[0].reshape(n_seq, chunk, width), "seq", split_axis=0, concat_axis=0, tiled=True
            ).reshape(sent, width)
        ]
    placed = pl.pallas_call(
        place_kernel,
        out_shape=rows_of(row_total, GROUP * width),
        in_specs=[vmem] * (1 + len(arrived)),
        out_specs=pl.BlockSpec(memory_space=pltpu.HBM),
        scratch_shapes=[pltpu.VMEM((row_total, GROUP * width), jnp.bfloat16), pltpu.SemaphoreType.DMA((GROUP,))],
        compiler_params=small,
    )(place, *arrived)
    return placed[None]


def solution(mesh):
    placed = (
        P("enc", "seq", None),
        P("enc", "seq", None),
        P("enc", "seq"),
        P("enc", "seq"),
        P("enc", "seq"),
        P("enc", "seq"),
        P(),
        P(),
        P(),
    )
    return jax.shard_map(
        per_device, mesh=mesh, in_specs=placed, out_specs=P("enc", "seq", None), check_vma=False
    )
```

```python
import functools
import math

import jax
import jax.numpy as jnp
from jax import lax
from jax.experimental import pallas as pl
from jax.experimental.pallas import tpu as pltpu
from jax.sharding import PartitionSpec as P

HEADS = 16
WIN = 64
LANES = 128
GROUP = 4
EPS = 1e-6
CORES = 2

NT = (((1,), (1,)), ((), ()))


def dot32(a, b):
    return jnp.dot(a, b, preferred_element_type=jnp.float32)


def one_hot(match):
    return match.astype(jnp.float32).astype(jnp.bfloat16)


def attend(q, k, v, out_ref, row0, width):
    head = width // HEADS
    rate = 1.0 / math.sqrt(head)
    totals = [None] * (width // LANES)
    sums = [None] * (width // LANES)
    first_half = lax.broadcasted_iota(jnp.int32, (WIN, 2 * WIN), 1) < WIN
    for pair in range(HEADS // 2):
        start = 2 * pair * head
        lo = start // LANES * LANES
        hi = -(-(start + 2 * head) // LANES) * LANES
        column = lax.broadcasted_iota(jnp.int32, (2 * WIN, hi - lo), 1) + lo
        row = lax.broadcasted_iota(jnp.int32, (2 * WIN, hi - lo), 0)
        begin = jnp.where(row < WIN, start, start + head)
        mask = one_hot((column >= begin) & (column < begin + head))
        kw, vw = k(lo, hi), v(lo, hi)
        keys = jnp.concatenate([kw, kw], axis=0) * mask
        values = jnp.concatenate([vw, vw], axis=0) * mask
        scores = lax.dot_general(q(lo, hi), keys, NT, preferred_element_type=jnp.float32)
        top0 = jnp.max(jnp.where(first_half, scores, -jnp.inf), axis=1, keepdims=True)
        top1 = jnp.max(jnp.where(first_half, -jnp.inf, scores), axis=1, keepdims=True)
        raised = jnp.exp((scores - jnp.where(first_half, top0, top1)) * rate).astype(jnp.bfloat16)
        part = dot32(raised, values)
        norm = dot32(raised, mask)
        for tile in range(lo // LANES, hi // LANES):
            at = slice(tile * LANES - lo, (tile + 1) * LANES - lo)
            totals[tile] = part[:, at] if totals[tile] is None else totals[tile] + part[:, at]
            sums[tile] = norm[:, at] if sums[tile] is None else sums[tile] + norm[:, at]
    for tile in range(width // LANES):
        out_ref[row0 : row0 + WIN, tile * LANES : (tile + 1) * LANES] = (totals[tile] / sums[tile]).astype(
            jnp.bfloat16
        )


def encode(
    slot, qkv_hbm, resid_hbm, weight_hbm, bias_hbm, gain_hbm, out_ref,
    qkv, resid, weight, attended, hidden, bias_ref, gain_ref, gain_row, sems,
):
    blocks = qkv.shape[0]
    width = resid.shape[2]
    at = pl.ds(slot, blocks)
    pairs = [
        (qkv_hbm.at[at], qkv), (bias_hbm, bias_ref), (gain_hbm, gain_ref), (resid_hbm.at[at], resid), (weight_hbm, weight)
    ]
    copies = [pltpu.make_async_copy(a, b, sems.at[i]) for i, (a, b) in enumerate(pairs)]
    for copy in copies:
        copy.start()
    copies[0].wait()
    for b in range(blocks):
        attend(
            lambda lo, hi, b=b: qkv[b, :, lo:hi],
            lambda lo, hi, b=b: qkv[b, :, width + lo : width + hi],
            lambda lo, hi, b=b: qkv[b, :, 2 * width + lo : 2 * width + hi],
            attended, b * WIN, width,
        )
    for copy in copies[1:-1]:
        copy.wait()
    rows = blocks * WIN
    step = 2 * LANES
    chunks = [slice(lo, lo + step) for lo in range(0, width, step)]
    for cols in chunks:
        bias = bias_ref[cols].astype(jnp.float32).reshape(1, step)
        hidden[:, cols] = resid[:, :, cols].reshape(rows, step).astype(jnp.float32) + bias
        gain_row[:, cols] = gain_ref[cols].astype(jnp.float32).reshape(1, step)
    copies[-1].wait()
    squares = jnp.zeros((rows, LANES), jnp.float32)
    for cols in chunks:
        h = hidden[:, cols] + dot32(attended[...], weight[:, cols])
        hidden[:, cols] = h
        h = h * h
        squares = squares + h[:, :LANES] + h[:, LANES:]
    scale = lax.rsqrt(jnp.sum(squares, axis=1, keepdims=True) * (1.0 / width) + EPS)
    for cols in chunks:
        out_ref[:, cols] = (hidden[:, cols] * scale * gain_row[:, cols]).astype(jnp.bfloat16)


def lent_kernel(count_ref, qkv_hbm, resid_hbm, weight_hbm, bias_hbm, gain_hbm, out_ref, *scratch):
    encode(count_ref[0, 0] - 1, qkv_hbm, resid_hbm, weight_hbm, bias_hbm, gain_hbm, out_ref, *scratch)


def split_index(index, n_seq, cap):
    step = index // (GROUP * cap)
    rest = index - step * (GROUP * cap)
    patch = rest // cap
    return step, patch, rest - patch * cap


def own_kernel(
    n_seq, cap, peer, count_ref, send_ref, me_ref, slot_ref, row_ref,
    qkv_hbm, resid_hbm, weight_hbm, bias_hbm, gain_hbm,
    packed_ref, borrow_ref, place_ref, normed, *scratch,
):
    rows = normed.shape[0]
    slots = n_seq * cap
    sent = slots * GROUP
    tokens = rows // GROUP
    me = me_ref[0, 0]
    encode(0, qkv_hbm, resid_hbm, weight_hbm, bias_hbm, gain_hbm, normed, *scratch)

    step, patch, rank = split_index(lax.broadcasted_iota(jnp.int32, (sent, 1), 0), n_seq, cap)
    row_code = (peer(me, step, 1) * cap + rank) * GROUP + patch
    token = lax.broadcasted_iota(jnp.int32, (tokens, rows), 0)
    column = lax.broadcasted_iota(jnp.int32, (tokens, rows), 1)
    spread = one_hot((column >= token * GROUP) & (column < (token + 1) * GROUP))
    slot = jnp.broadcast_to(slot_ref[...].astype(jnp.float32), (16, tokens)).astype(jnp.bfloat16)
    slot = dot32(slot, spread)[:1].astype(jnp.int32)
    index = lax.broadcasted_iota(jnp.int32, (1, rows), 1)
    col_code = slot * GROUP + jnp.bitwise_and(index, GROUP - 1)
    kept = (count_ref[0, 0] - send_ref[0, 0]) * WIN
    last = rows - WIN
    own = one_hot(row_code == jnp.where(index < kept, col_code, -1))
    packed_ref[...] = dot32(own, normed[...]).astype(jnp.bfloat16)
    borrow_ref[...] = one_hot(row_code == jnp.where(kept > last, -1, col_code[:, last:]))

    step, patch, rank = split_index(lax.broadcasted_iota(jnp.int32, (1, sent), 1), n_seq, cap)
    arrive = peer(me, step, -1) * cap + rank
    pick = one_hot(lax.broadcasted_iota(jnp.int32, (slots, sent), 0) == arrive)
    target = jnp.broadcast_to(row_ref[...].astype(jnp.float32), (16, slots)).astype(jnp.bfloat16)
    target = dot32(target, pick)[:1].astype(jnp.int32)
    out_row = lax.broadcasted_iota(jnp.int32, (tokens, sent), 0)
    for j in range(GROUP):
        place_ref[j * tokens : (j + 1) * tokens, :] = one_hot((target == out_row) & (patch == j))


def encode_call(kernel, blocks, scalars, slots, qkv, resid, weight, bias, gain, out_shape, extra):
    width = resid.shape[2]
    rows = blocks * WIN
    vmem = pl.BlockSpec(memory_space=pltpu.VMEM)
    smem = pl.BlockSpec(memory_space=pltpu.SMEM)
    hbm = pl.BlockSpec(memory_space=pltpu.HBM)
    return pl.pallas_call(
        kernel,
        out_shape=out_shape,
        in_specs=[smem] * len(scalars) + [vmem] * len(slots) + [hbm] * 5,
        out_specs=jax.tree.map(lambda _: vmem, out_shape),
        scratch_shapes=extra
        + [
            pltpu.VMEM((blocks, WIN, 3 * width), jnp.bfloat16),
            pltpu.VMEM((blocks, WIN, width), jnp.bfloat16),
            pltpu.VMEM((width, width), jnp.bfloat16),
            pltpu.VMEM((rows, width), jnp.bfloat16),
            pltpu.VMEM((rows, width), jnp.float32),
            pltpu.VMEM((width,), jnp.bfloat16),
            pltpu.VMEM((width,), jnp.bfloat16),
            pltpu.VMEM((1, width), jnp.float32),
            pltpu.SemaphoreType.DMA((5,)),
        ],
        compiler_params=pltpu.CompilerParams(vmem_limit_bytes=24 << 20),
        cost_estimate=pl.CostEstimate(
            flops=2 * rows * width * width + 8 * rows * WIN * width,
            bytes_accessed=2 * (width * width + 5 * rows * width),
            transcendentals=rows * WIN * HEADS,
        ),
    )(*scalars, *slots, *(pltpu.with_memory_space_constraint(a, pltpu.HBM) for a in (qkv, resid, weight, bias, gain)))


def pack_kernel(packed_ref, borrow_ref, borrowed_ref, *out_refs):
    total = packed_ref[...].astype(jnp.float32) + dot32(borrow_ref[...], borrowed_ref[...])
    start = 0
    for out_ref in out_refs:
        stop = start + out_ref.shape[0]
        out_ref[...] = total[start:stop].astype(jnp.bfloat16)
        start = stop


def forward_kernel(double_ref, after_ref, out_ref):
    rows = out_ref.shape[0]
    out_ref[...] = double_ref[...].astype(jnp.float32)[rows:].astype(jnp.bfloat16)


def place_kernel(place_ref, *refs):
    *in_refs, out_hbm, out, sems = refs
    tokens = out.shape[0]
    chunks = [ref[...].astype(jnp.float32) for ref in in_refs]
    if len(chunks) > 1:
        chunks[1] = chunks[1][: chunks[0].shape[0]]
    arrived = chunks[0] if len(chunks) == 1 else jnp.concatenate(chunks, axis=0)
    arrived = arrived.astype(jnp.bfloat16)
    width = arrived.shape[1]
    copies = []
    for j in range(GROUP):
        cols = slice(j * width, (j + 1) * width)
        out[:, cols] = dot32(place_ref[j * tokens : (j + 1) * tokens, :], arrived).astype(jnp.bfloat16)
        copies.append(pltpu.make_async_copy(out.at[:, cols], out_hbm.at[:, cols], sems.at[j]))
        copies[-1].start()
    for copy in copies:
        copy.wait()


def exchange_steps(n_seq):
    return [(0, 0)] + [(dz, dc) for dz in range(1, n_seq // CORES) for dc in range(CORES)] + [(0, 1)]


def chip_peer(n_seq, me, step, sign):
    n_z = n_seq // CORES
    offset = jnp.zeros_like(step)
    flip = jnp.zeros_like(step)
    for i, (dz, dc) in enumerate(exchange_steps(n_seq)):
        offset = jnp.where(step == i, dz, offset)
        flip = jnp.where(step == i, dc, flip)
    z = me // CORES + sign * offset
    z = jnp.where(z >= n_z, z - n_z, jnp.where(z < 0, z + n_z, z))
    return z * CORES + jnp.bitwise_xor(jnp.bitwise_and(me, 1), flip)


def per_device(
    qkv, resid, block_count, send_count, send_slot, lm_row, out_weight, out_bias, norm_gain
):
    width = resid.shape[2]
    row_total = send_slot.shape[1]
    tokens = WIN // GROUP
    blocks = row_total // tokens
    n_seq = lax.axis_size("seq")
    n_enc = lax.axis_size("enc")
    slots = lm_row.shape[1]
    cap = slots // n_seq
    chunk = GROUP * cap
    sent = slots * GROUP
    vmem = pl.BlockSpec(memory_space=pltpu.VMEM)
    small = pltpu.CompilerParams(vmem_limit_bytes=16 << 20)

    def rows_of(count, columns=width):
        return jax.ShapeDtypeStruct((count, columns), jnp.bfloat16)

    data = (qkv, resid, out_weight, out_bias, norm_gain)
    lent = encode_call(lent_kernel, 1, [block_count], [], *data, rows_of(WIN), [])
    borrowed = lax.ppermute(lent, "enc", [((i - 1) % n_enc, i) for i in range(n_enc)])

    by_steps = chunk % 8 == 0 and n_seq % CORES == 0
    peer = functools.partial(chip_peer, n_seq) if by_steps else lambda me, step, sign: step
    me = lax.axis_index("seq").astype(jnp.int32).reshape(1, 1)
    packed, borrow, place = encode_call(
        functools.partial(own_kernel, n_seq, cap, peer), blocks,
        [block_count, send_count, me], [send_slot, lm_row], *data,
        (rows_of(sent), rows_of(sent, WIN), rows_of(GROUP * row_total, sent)),
        [pltpu.VMEM((row_total * GROUP, width), jnp.bfloat16)],
    )
    pieces = [chunk, CORES * chunk] + [chunk] * (n_seq - 1 - CORES) if by_steps else [sent]
    outgoing = pl.pallas_call(
        pack_kernel,
        out_shape=[rows_of(rows) for rows in pieces],
        in_specs=[vmem] * 3,
        out_specs=[vmem] * len(pieces),
        compiler_params=small,
    )(packed, borrow, borrowed)

    if by_steps:
        n_z = n_seq // CORES

        def exchange(part, dz, dc):
            return lax.ppermute(
                part, "seq", [(i, (i // CORES + dz) % n_z * CORES + (i + dc) % CORES) for i in range(n_seq)]
            )

        double = exchange(outgoing[1], 1, 0)
        rest = [exchange(part, *step) for part, step in zip(outgoing[2:], exchange_steps(n_seq)[1 + CORES :])]
        onward = pl.pallas_call(
            forward_kernel, out_shape=rows_of(chunk), in_specs=[vmem] * 2, out_specs=vmem, compiler_params=small
        )(double, rest[0])
        arrived = [outgoing[0], double, exchange(onward, 0, 1), *rest]
    else:
        arrived = [
            lax.all_to_all(
                outgoing[0].reshape(n_seq, chunk, width), "seq", split_axis=0, concat_axis=0, tiled=True
            ).reshape(sent, width)
        ]
    placed = pl.pallas_call(
        place_kernel,
        out_shape=rows_of(row_total, GROUP * width),
        in_specs=[vmem] * (1 + len(arrived)),
        out_specs=pl.BlockSpec(memory_space=pltpu.HBM),
        scratch_shapes=[pltpu.VMEM((row_total, GROUP * width), jnp.bfloat16), pltpu.SemaphoreType.DMA((GROUP,))],
        compiler_params=small,
    )(place, *arrived)
    return placed[None]


def solution(mesh):
    placed = (
        P("enc", "seq", None),
        P("enc", "seq", None),
        P("enc", "seq"),
        P("enc", "seq"),
        P("enc", "seq"),
        P("enc", "seq"),
        P(),
        P(),
        P(),
    )
    return jax.shard_map(
        per_device, mesh=mesh, in_specs=placed, out_specs=P("enc", "seq", None), check_vma=False
    )
```

```python
import functools
import math

import jax
import jax.numpy as jnp
from jax import lax
from jax.experimental import pallas as pl
from jax.experimental.pallas import tpu as pltpu
from jax.sharding import PartitionSpec as P

HEADS = 16
WIN = 64
LANES = 128
GROUP = 4
EPS = 1e-6
CORES = 2

NT = (((1,), (1,)), ((), ()))


def dot32(a, b):
    return jnp.dot(a, b, preferred_element_type=jnp.float32)


def one_hot(match):
    return match.astype(jnp.float32).astype(jnp.bfloat16)


def attend(q, k, v, out_ref, row0, width):
    head = width // HEADS
    rate = 1.0 / math.sqrt(head)
    totals = [None] * (width // LANES)
    sums = [None] * (width // LANES)
    first_half = lax.broadcasted_iota(jnp.int32, (WIN, 2 * WIN), 1) < WIN
    for pair in range(HEADS // 2):
        start = 2 * pair * head
        lo = start // LANES * LANES
        hi = -(-(start + 2 * head) // LANES) * LANES
        column = lax.broadcasted_iota(jnp.int32, (2 * WIN, hi - lo), 1) + lo
        row = lax.broadcasted_iota(jnp.int32, (2 * WIN, hi - lo), 0)
        begin = jnp.where(row < WIN, start, start + head)
        mask = one_hot((column >= begin) & (column < begin + head))
        kw, vw = k(lo, hi), v(lo, hi)
        keys = jnp.concatenate([kw, kw], axis=0) * mask
        values = jnp.concatenate([vw, vw], axis=0) * mask
        scores = lax.dot_general(q(lo, hi), keys, NT, preferred_element_type=jnp.float32)
        top0 = jnp.max(jnp.where(first_half, scores, -jnp.inf), axis=1, keepdims=True)
        top1 = jnp.max(jnp.where(first_half, -jnp.inf, scores), axis=1, keepdims=True)
        raised = jnp.exp((scores - jnp.where(first_half, top0, top1)) * rate).astype(jnp.bfloat16)
        part = dot32(raised, values)
        norm = dot32(raised, mask)
        for tile in range(lo // LANES, hi // LANES):
            at = slice(tile * LANES - lo, (tile + 1) * LANES - lo)
            totals[tile] = part[:, at] if totals[tile] is None else totals[tile] + part[:, at]
            sums[tile] = norm[:, at] if sums[tile] is None else sums[tile] + norm[:, at]
    for tile in range(width // LANES):
        out_ref[row0 : row0 + WIN, tile * LANES : (tile + 1) * LANES] = (totals[tile] / sums[tile]).astype(
            jnp.bfloat16
        )


def encode(
    slot, qkv_hbm, resid_hbm, weight_hbm, bias_hbm, gain_hbm, out_ref,
    qkv, resid, weight, attended, hidden, bias_ref, gain_ref, sems,
):
    blocks = qkv.shape[0]
    width = resid.shape[2]
    at = pl.ds(slot, blocks)
    pairs = [
        (qkv_hbm.at[at], qkv), (weight_hbm, weight), (resid_hbm.at[at], resid), (bias_hbm, bias_ref), (gain_hbm, gain_ref)
    ]
    copies = [pltpu.make_async_copy(a, b, sems.at[i]) for i, (a, b) in enumerate(pairs)]
    for copy in copies:
        copy.start()
    copies[0].wait()
    for b in range(blocks):
        attend(
            lambda lo, hi, b=b: qkv[b, :, lo:hi],
            lambda lo, hi, b=b: qkv[b, :, width + lo : width + hi],
            lambda lo, hi, b=b: qkv[b, :, 2 * width + lo : 2 * width + hi],
            attended, b * WIN, width,
        )
    for copy in copies[1:]:
        copy.wait()
    rows = blocks * WIN
    squares = jnp.zeros((rows, 1), jnp.float32)
    step = 2 * LANES
    for lo in range(0, width, step):
        cols = slice(lo, lo + step)
        h = dot32(attended[...], weight[:, cols])
        h = h + bias_ref[cols].astype(jnp.float32).reshape(1, step)
        h = h + resid[:, :, cols].reshape(rows, step).astype(jnp.float32)
        hidden[:, cols] = h
        squares = squares + jnp.sum(h * h, axis=1, keepdims=True)
    scale = lax.rsqrt(squares * (1.0 / width) + EPS)
    for lo in range(0, width, step):
        cols = slice(lo, lo + step)
        gain = gain_ref[cols].astype(jnp.float32).reshape(1, step)
        out_ref[:, cols] = (hidden[:, cols] * scale * gain).astype(jnp.bfloat16)


def lent_kernel(count_ref, qkv_hbm, resid_hbm, weight_hbm, bias_hbm, gain_hbm, out_ref, *scratch):
    encode(count_ref[0, 0] - 1, qkv_hbm, resid_hbm, weight_hbm, bias_hbm, gain_hbm, out_ref, *scratch)


def split_index(index, n_seq, cap):
    step = index // (GROUP * cap)
    rest = index - step * (GROUP * cap)
    patch = rest // cap
    return step, patch, rest - patch * cap


def own_kernel(
    n_seq, cap, peer, count_ref, send_ref, me_ref, slot_ref, row_ref,
    qkv_hbm, resid_hbm, weight_hbm, bias_hbm, gain_hbm,
    packed_ref, borrow_ref, place_ref, normed, *scratch,
):
    rows = normed.shape[0]
    slots = n_seq * cap
    sent = slots * GROUP
    tokens = rows // GROUP
    me = me_ref[0, 0]
    encode(0, qkv_hbm, resid_hbm, weight_hbm, bias_hbm, gain_hbm, normed, *scratch)

    step, patch, rank = split_index(lax.broadcasted_iota(jnp.int32, (sent, 1), 0), n_seq, cap)
    row_code = (peer(me, step, 1) * cap + rank) * GROUP + patch
    token = lax.broadcasted_iota(jnp.int32, (tokens, rows), 0)
    column = lax.broadcasted_iota(jnp.int32, (tokens, rows), 1)
    spread = one_hot((column >= token * GROUP) & (column < (token + 1) * GROUP))
    slot = jnp.broadcast_to(slot_ref[...].astype(jnp.float32), (16, tokens)).astype(jnp.bfloat16)
    slot = dot32(slot, spread)[:1].astype(jnp.int32)
    index = lax.broadcasted_iota(jnp.int32, (1, rows), 1)
    col_code = slot * GROUP + jnp.bitwise_and(index, GROUP - 1)
    kept = (count_ref[0, 0] - send_ref[0, 0]) * WIN
    last = rows - WIN
    own = one_hot(row_code == jnp.where(index < kept, col_code, -1))
    packed_ref[...] = dot32(own, normed[...]).astype(jnp.bfloat16)
    borrow_ref[...] = one_hot(row_code == jnp.where(kept > last, -1, col_code[:, last:]))

    step, patch, rank = split_index(lax.broadcasted_iota(jnp.int32, (1, sent), 1), n_seq, cap)
    arrive = peer(me, step, -1) * cap + rank
    pick = one_hot(lax.broadcasted_iota(jnp.int32, (slots, sent), 0) == arrive)
    target = jnp.broadcast_to(row_ref[...].astype(jnp.float32), (16, slots)).astype(jnp.bfloat16)
    target = dot32(target, pick)[:1].astype(jnp.int32)
    out_row = lax.broadcasted_iota(jnp.int32, (tokens, sent), 0)
    for j in range(GROUP):
        place_ref[j * tokens : (j + 1) * tokens, :] = one_hot((target == out_row) & (patch == j))


def encode_call(kernel, blocks, scalars, slots, qkv, resid, weight, bias, gain, out_shape, extra):
    width = resid.shape[2]
    rows = blocks * WIN
    vmem = pl.BlockSpec(memory_space=pltpu.VMEM)
    smem = pl.BlockSpec(memory_space=pltpu.SMEM)
    hbm = pl.BlockSpec(memory_space=pltpu.HBM)
    return pl.pallas_call(
        kernel,
        out_shape=out_shape,
        in_specs=[smem] * len(scalars) + [vmem] * len(slots) + [hbm] * 5,
        out_specs=jax.tree.map(lambda _: vmem, out_shape),
        scratch_shapes=extra
        + [
            pltpu.VMEM((blocks, WIN, 3 * width), jnp.bfloat16),
            pltpu.VMEM((blocks, WIN, width), jnp.bfloat16),
            pltpu.VMEM((width, width), jnp.bfloat16),
            pltpu.VMEM((rows, width), jnp.bfloat16),
            pltpu.VMEM((rows, width), jnp.float32),
            pltpu.VMEM((width,), jnp.bfloat16),
            pltpu.VMEM((width,), jnp.bfloat16),
            pltpu.SemaphoreType.DMA((5,)),
        ],
        compiler_params=pltpu.CompilerParams(vmem_limit_bytes=24 << 20),
        cost_estimate=pl.CostEstimate(
            flops=2 * rows * width * width + 8 * rows * WIN * width,
            bytes_accessed=2 * (width * width + 5 * rows * width),
            transcendentals=rows * WIN * HEADS,
        ),
    )(*scalars, *slots, *(pltpu.with_memory_space_constraint(a, pltpu.HBM) for a in (qkv, resid, weight, bias, gain)))


def pack_kernel(packed_ref, borrow_ref, borrowed_ref, *out_refs):
    total = packed_ref[...].astype(jnp.float32) + dot32(borrow_ref[...], borrowed_ref[...])
    start = 0
    for out_ref in out_refs:
        stop = start + out_ref.shape[0]
        out_ref[...] = total[start:stop].astype(jnp.bfloat16)
        start = stop


def forward_kernel(double_ref, out_ref):
    rows = out_ref.shape[0]
    out_ref[...] = double_ref[...].astype(jnp.float32)[rows:].astype(jnp.bfloat16)


def place_kernel(place_ref, *refs):
    *in_refs, out_hbm, out, sems = refs
    tokens = out.shape[0]
    chunks = [ref[...].astype(jnp.float32) for ref in in_refs]
    if len(chunks) > 1:
        chunks[1] = chunks[1][: chunks[0].shape[0]]
    arrived = chunks[0] if len(chunks) == 1 else jnp.concatenate(chunks, axis=0)
    arrived = arrived.astype(jnp.bfloat16)
    width = arrived.shape[1]
    copies = []
    for j in range(GROUP):
        cols = slice(j * width, (j + 1) * width)
        out[:, cols] = dot32(place_ref[j * tokens : (j + 1) * tokens, :], arrived).astype(jnp.bfloat16)
        copies.append(pltpu.make_async_copy(out.at[:, cols], out_hbm.at[:, cols], sems.at[j]))
        copies[-1].start()
    for copy in copies:
        copy.wait()


def exchange_steps(n_seq, enc):
    n_z = n_seq // CORES
    steps = [(dz, dc) for dz in range(1, n_z) for dc in range(CORES)]
    if enc % 2:
        steps.sort(key=lambda s: (abs(s[0] - n_z / 2), s[1], s[0]))
    return [(0, 0)] + steps + [(0, 1)]


def chip_peer(n_seq, place, step, sign):
    n_z = n_seq // CORES
    odd = lax.rem(place // n_seq, 2) == 1
    me = lax.rem(place, n_seq)
    offset = jnp.zeros_like(step)
    flip = jnp.zeros_like(step)
    for i, (even_step, odd_step) in enumerate(zip(exchange_steps(n_seq, 0), exchange_steps(n_seq, 1))):
        offset = jnp.where(step == i, jnp.where(odd, odd_step[0], even_step[0]), offset)
        flip = jnp.where(step == i, jnp.where(odd, odd_step[1], even_step[1]), flip)
    z = me // CORES + sign * offset
    z = jnp.where(z >= n_z, z - n_z, jnp.where(z < 0, z + n_z, z))
    return z * CORES + jnp.bitwise_xor(jnp.bitwise_and(me, 1), flip)


def per_device(
    qkv, resid, block_count, send_count, send_slot, lm_row, out_weight, out_bias, norm_gain
):
    width = resid.shape[2]
    row_total = send_slot.shape[1]
    tokens = WIN // GROUP
    blocks = row_total // tokens
    n_seq = lax.axis_size("seq")
    n_enc = lax.axis_size("enc")
    slots = lm_row.shape[1]
    cap = slots // n_seq
    chunk = GROUP * cap
    sent = slots * GROUP
    vmem = pl.BlockSpec(memory_space=pltpu.VMEM)
    small = pltpu.CompilerParams(vmem_limit_bytes=16 << 20)

    def rows_of(count, columns=width):
        return jax.ShapeDtypeStruct((count, columns), jnp.bfloat16)

    data = (qkv, resid, out_weight, out_bias, norm_gain)
    lent = encode_call(lent_kernel, 1, [block_count], [], *data, rows_of(WIN), [])
    borrowed = lax.ppermute(lent, "enc", [((i - 1) % n_enc, i) for i in range(n_enc)])

    by_steps = chunk % 8 == 0 and n_seq % CORES == 0
    peer = functools.partial(chip_peer, n_seq) if by_steps else lambda me, step, sign: step
    me = (lax.axis_index("enc") * n_seq + lax.axis_index("seq")).astype(jnp.int32).reshape(1, 1)
    packed, borrow, place = encode_call(
        functools.partial(own_kernel, n_seq, cap, peer), blocks,
        [block_count, send_count, me], [send_slot, lm_row], *data,
        (rows_of(sent), rows_of(sent, WIN), rows_of(GROUP * row_total, sent)),
        [pltpu.VMEM((row_total * GROUP, width), jnp.bfloat16)],
    )
    pieces = [chunk, CORES * chunk] + [chunk] * (n_seq - 1 - CORES) if by_steps else [sent]
    outgoing = pl.pallas_call(
        pack_kernel,
        out_shape=[rows_of(rows) for rows in pieces],
        in_specs=[vmem] * 3,
        out_specs=[vmem] * len(pieces),
        compiler_params=small,
    )(packed, borrow, borrowed)

    if by_steps:
        n_z = n_seq // CORES
        steps = [exchange_steps(n_seq, enc) for enc in range(n_enc)]

        def exchange(part, step, flip=True):
            route = []
            for enc in range(n_enc):
                dz, dc = steps[enc][step]
                for i in range(n_seq):
                    to = (i // CORES + dz) % n_z * CORES + (i + (dc if flip else 0)) % CORES
                    route.append((enc * n_seq + i, enc * n_seq + to))
            return lax.ppermute(part, ("enc", "seq"), route)

        double = exchange(outgoing[1], 1, flip=False)
        rest = [exchange(part, 1 + CORES + i) for i, part in enumerate(outgoing[2:])]
        onward = pl.pallas_call(
            forward_kernel, out_shape=rows_of(chunk), in_specs=[vmem], out_specs=vmem, compiler_params=small
        )(double)
        arrived = [outgoing[0], double, exchange(onward, n_seq - 1), *rest]
    else:
        arrived = [
            lax.all_to_all(
                outgoing[0].reshape(n_seq, chunk, width), "seq", split_axis=0, concat_axis=0, tiled=True
            ).reshape(sent, width)
        ]
    placed = pl.pallas_call(
        place_kernel,
        out_shape=rows_of(row_total, GROUP * width),
        in_specs=[vmem] * (1 + len(arrived)),
        out_specs=pl.BlockSpec(memory_space=pltpu.HBM),
        scratch_shapes=[pltpu.VMEM((row_total, GROUP * width), jnp.bfloat16), pltpu.SemaphoreType.DMA((GROUP,))],
        compiler_params=small,
    )(place, *arrived)
    return placed[None]


def solution(mesh):
    placed = (
        P("enc", "seq", None),
        P("enc", "seq", None),
        P("enc", "seq"),
        P("enc", "seq"),
        P("enc", "seq"),
        P("enc", "seq"),
        P(),
        P(),
        P(),
    )
    return jax.shard_map(
        per_device, mesh=mesh, in_specs=placed, out_specs=P("enc", "seq", None), check_vma=False
    )
```

```python
import functools
import math

import jax
import jax.numpy as jnp
from jax import lax
from jax.experimental import pallas as pl
from jax.experimental.pallas import tpu as pltpu
from jax.sharding import PartitionSpec as P

HEADS = 16
WIN = 64
LANES = 128
GROUP = 4
EPS = 1e-6
CORES = 2
CHIP_ROUTES = ((3, 2, 1, 0), (1, 3, 0, 2), (2, 0, 3, 1))

NT = (((1,), (1,)), ((), ()))


def dot32(a, b):
    return jnp.dot(a, b, preferred_element_type=jnp.float32)


def one_hot(match):
    return match.astype(jnp.float32).astype(jnp.bfloat16)


def attend(q, k, v, out_ref, row0, width):
    head = width // HEADS
    rate = 1.0 / math.sqrt(head)
    totals = [None] * (width // LANES)
    sums = [None] * (width // LANES)
    first_half = lax.broadcasted_iota(jnp.int32, (WIN, 2 * WIN), 1) < WIN
    for pair in range(HEADS // 2):
        start = 2 * pair * head
        lo = start // LANES * LANES
        hi = -(-(start + 2 * head) // LANES) * LANES
        column = lax.broadcasted_iota(jnp.int32, (2 * WIN, hi - lo), 1) + lo
        row = lax.broadcasted_iota(jnp.int32, (2 * WIN, hi - lo), 0)
        begin = jnp.where(row < WIN, start, start + head)
        mask = one_hot((column >= begin) & (column < begin + head))
        kw, vw = k(lo, hi), v(lo, hi)
        keys = jnp.concatenate([kw, kw], axis=0) * mask
        values = jnp.concatenate([vw, vw], axis=0) * mask
        scores = lax.dot_general(q(lo, hi), keys, NT, preferred_element_type=jnp.float32)
        top0 = jnp.max(jnp.where(first_half, scores, -jnp.inf), axis=1, keepdims=True)
        top1 = jnp.max(jnp.where(first_half, -jnp.inf, scores), axis=1, keepdims=True)
        raised = jnp.exp((scores - jnp.where(first_half, top0, top1)) * rate).astype(jnp.bfloat16)
        part = dot32(raised, values)
        norm = dot32(raised, mask)
        for tile in range(lo // LANES, hi // LANES):
            at = slice(tile * LANES - lo, (tile + 1) * LANES - lo)
            totals[tile] = part[:, at] if totals[tile] is None else totals[tile] + part[:, at]
            sums[tile] = norm[:, at] if sums[tile] is None else sums[tile] + norm[:, at]
    for tile in range(width // LANES):
        out_ref[row0 : row0 + WIN, tile * LANES : (tile + 1) * LANES] = (totals[tile] / sums[tile]).astype(
            jnp.bfloat16
        )


def encode(
    slot, qkv_hbm, resid_hbm, weight_hbm, bias_hbm, gain_hbm, out_ref,
    qkv, resid, weight, attended, hidden, bias_ref, gain_ref, sems,
):
    blocks = qkv.shape[0]
    width = resid.shape[2]
    at = pl.ds(slot, blocks)
    pairs = [
        (qkv_hbm.at[at], qkv), (weight_hbm, weight), (resid_hbm.at[at], resid), (bias_hbm, bias_ref), (gain_hbm, gain_ref)
    ]
    copies = [pltpu.make_async_copy(a, b, sems.at[i]) for i, (a, b) in enumerate(pairs)]
    for copy in copies:
        copy.start()
    copies[0].wait()
    for b in range(blocks):
        attend(
            lambda lo, hi, b=b: qkv[b, :, lo:hi],
            lambda lo, hi, b=b: qkv[b, :, width + lo : width + hi],
            lambda lo, hi, b=b: qkv[b, :, 2 * width + lo : 2 * width + hi],
            attended, b * WIN, width,
        )
    for copy in copies[1:]:
        copy.wait()
    rows = blocks * WIN
    squares = jnp.zeros((rows, 1), jnp.float32)
    step = 2 * LANES
    for lo in range(0, width, step):
        cols = slice(lo, lo + step)
        h = dot32(attended[...], weight[:, cols])
        h = h + bias_ref[cols].astype(jnp.float32).reshape(1, step)
        h = h + resid[:, :, cols].reshape(rows, step).astype(jnp.float32)
        hidden[:, cols] = h
        squares = squares + jnp.sum(h * h, axis=1, keepdims=True)
    scale = lax.rsqrt(squares * (1.0 / width) + EPS)
    for lo in range(0, width, step):
        cols = slice(lo, lo + step)
        gain = gain_ref[cols].astype(jnp.float32).reshape(1, step)
        out_ref[:, cols] = (hidden[:, cols] * scale * gain).astype(jnp.bfloat16)


def lent_kernel(count_ref, qkv_hbm, resid_hbm, weight_hbm, bias_hbm, gain_hbm, out_ref, *scratch):
    encode(count_ref[0, 0] - 1, qkv_hbm, resid_hbm, weight_hbm, bias_hbm, gain_hbm, out_ref, *scratch)


def split_index(index, n_seq, cap):
    step = index // (GROUP * cap)
    rest = index - step * (GROUP * cap)
    patch = rest // cap
    return step, patch, rest - patch * cap


def own_kernel(
    n_seq, cap, peer, count_ref, send_ref, me_ref, slot_ref, row_ref,
    qkv_hbm, resid_hbm, weight_hbm, bias_hbm, gain_hbm,
    packed_ref, borrow_ref, place_ref, normed, *scratch,
):
    rows = normed.shape[0]
    slots = n_seq * cap
    sent = slots * GROUP
    tokens = rows // GROUP
    me = me_ref[0, 0]
    encode(0, qkv_hbm, resid_hbm, weight_hbm, bias_hbm, gain_hbm, normed, *scratch)

    step, patch, rank = split_index(lax.broadcasted_iota(jnp.int32, (sent, 1), 0), n_seq, cap)
    row_code = (peer(me, step, 1) * cap + rank) * GROUP + patch
    token = lax.broadcasted_iota(jnp.int32, (tokens, rows), 0)
    column = lax.broadcasted_iota(jnp.int32, (tokens, rows), 1)
    spread = one_hot((column >= token * GROUP) & (column < (token + 1) * GROUP))
    slot = jnp.broadcast_to(slot_ref[...].astype(jnp.float32), (16, tokens)).astype(jnp.bfloat16)
    slot = dot32(slot, spread)[:1].astype(jnp.int32)
    index = lax.broadcasted_iota(jnp.int32, (1, rows), 1)
    col_code = slot * GROUP + jnp.bitwise_and(index, GROUP - 1)
    kept = (count_ref[0, 0] - send_ref[0, 0]) * WIN
    last = rows - WIN
    own = one_hot(row_code == jnp.where(index < kept, col_code, -1))
    packed_ref[...] = dot32(own, normed[...]).astype(jnp.bfloat16)
    borrow_ref[...] = one_hot(row_code == jnp.where(kept > last, -1, col_code[:, last:]))

    step, patch, rank = split_index(lax.broadcasted_iota(jnp.int32, (1, sent), 1), n_seq, cap)
    arrive = peer(me, step, -1) * cap + rank
    pick = one_hot(lax.broadcasted_iota(jnp.int32, (slots, sent), 0) == arrive)
    target = jnp.broadcast_to(row_ref[...].astype(jnp.float32), (16, slots)).astype(jnp.bfloat16)
    target = dot32(target, pick)[:1].astype(jnp.int32)
    out_row = lax.broadcasted_iota(jnp.int32, (tokens, sent), 0)
    for j in range(GROUP):
        place_ref[j * tokens : (j + 1) * tokens, :] = one_hot((target == out_row) & (patch == j))


def encode_call(kernel, blocks, scalars, slots, qkv, resid, weight, bias, gain, out_shape, extra):
    width = resid.shape[2]
    rows = blocks * WIN
    vmem = pl.BlockSpec(memory_space=pltpu.VMEM)
    smem = pl.BlockSpec(memory_space=pltpu.SMEM)
    hbm = pl.BlockSpec(memory_space=pltpu.HBM)
    return pl.pallas_call(
        kernel,
        out_shape=out_shape,
        in_specs=[smem] * len(scalars) + [vmem] * len(slots) + [hbm] * 5,
        out_specs=jax.tree.map(lambda _: vmem, out_shape),
        scratch_shapes=extra
        + [
            pltpu.VMEM((blocks, WIN, 3 * width), jnp.bfloat16),
            pltpu.VMEM((blocks, WIN, width), jnp.bfloat16),
            pltpu.VMEM((width, width), jnp.bfloat16),
            pltpu.VMEM((rows, width), jnp.bfloat16),
            pltpu.VMEM((rows, width), jnp.float32),
            pltpu.VMEM((width,), jnp.bfloat16),
            pltpu.VMEM((width,), jnp.bfloat16),
            pltpu.SemaphoreType.DMA((5,)),
        ],
        compiler_params=pltpu.CompilerParams(vmem_limit_bytes=24 << 20),
        cost_estimate=pl.CostEstimate(
            flops=2 * rows * width * width + 8 * rows * WIN * width,
            bytes_accessed=2 * (width * width + 5 * rows * width),
            transcendentals=rows * WIN * HEADS,
        ),
    )(*scalars, *slots, *(pltpu.with_memory_space_constraint(a, pltpu.HBM) for a in (qkv, resid, weight, bias, gain)))


def pack_kernel(packed_ref, borrow_ref, borrowed_ref, *out_refs):
    total = packed_ref[...].astype(jnp.float32) + dot32(borrow_ref[...], borrowed_ref[...])
    start = 0
    for out_ref in out_refs:
        stop = start + out_ref.shape[0]
        out_ref[...] = total[start:stop].astype(jnp.bfloat16)
        start = stop


def forward_kernel(double_ref, out_ref):
    rows = out_ref.shape[0]
    out_ref[...] = double_ref[...].astype(jnp.float32)[rows:].astype(jnp.bfloat16)


def place_kernel(place_ref, *refs):
    *in_refs, out_hbm, out, sems = refs
    tokens = out.shape[0]
    chunks = [ref[...].astype(jnp.float32) for ref in in_refs]
    if len(chunks) > 1:
        chunks[1] = chunks[1][: chunks[0].shape[0]]
    arrived = chunks[0] if len(chunks) == 1 else jnp.concatenate(chunks, axis=0)
    arrived = arrived.astype(jnp.bfloat16)
    width = arrived.shape[1]
    copies = []
    for j in range(GROUP):
        cols = slice(j * width, (j + 1) * width)
        out[:, cols] = dot32(place_ref[j * tokens : (j + 1) * tokens, :], arrived).astype(jnp.bfloat16)
        copies.append(pltpu.make_async_copy(out.at[:, cols], out_hbm.at[:, cols], sems.at[j]))
        copies[-1].start()
    for copy in copies:
        copy.wait()


def exchange_steps():
    stay = tuple(range(len(CHIP_ROUTES[0])))
    return [(stay, 0)] + [(route, dc) for route in CHIP_ROUTES for dc in range(CORES)] + [(stay, 1)]


def chip_peer(me, step, sign):
    z = me // CORES
    peer = jnp.zeros_like(step)
    for i, (route, flip) in enumerate(exchange_steps()):
        chip = sum(
            jnp.where(z == here, there, 0)
            for here, there in ((a, b) if sign > 0 else (b, a) for a, b in enumerate(route))
        )
        peer = jnp.where(step == i, chip * CORES + jnp.bitwise_xor(jnp.bitwise_and(me, 1), flip), peer)
    return peer


def per_device(
    qkv, resid, block_count, send_count, send_slot, lm_row, out_weight, out_bias, norm_gain
):
    width = resid.shape[2]
    row_total = send_slot.shape[1]
    tokens = WIN // GROUP
    blocks = row_total // tokens
    n_seq = lax.axis_size("seq")
    n_enc = lax.axis_size("enc")
    slots = lm_row.shape[1]
    cap = slots // n_seq
    chunk = GROUP * cap
    sent = slots * GROUP
    vmem = pl.BlockSpec(memory_space=pltpu.VMEM)
    small = pltpu.CompilerParams(vmem_limit_bytes=16 << 20)

    def rows_of(count, columns=width):
        return jax.ShapeDtypeStruct((count, columns), jnp.bfloat16)

    data = (qkv, resid, out_weight, out_bias, norm_gain)
    lent = encode_call(lent_kernel, 1, [block_count], [], *data, rows_of(WIN), [])
    borrowed = lax.ppermute(lent, "enc", [((i - 1) % n_enc, i) for i in range(n_enc)])

    by_steps = chunk % 8 == 0 and n_seq == CORES * len(CHIP_ROUTES[0])
    peer = chip_peer if by_steps else lambda me, step, sign: step
    me = lax.axis_index("seq").astype(jnp.int32).reshape(1, 1)
    packed, borrow, place = encode_call(
        functools.partial(own_kernel, n_seq, cap, peer), blocks,
        [block_count, send_count, me], [send_slot, lm_row], *data,
        (rows_of(sent), rows_of(sent, WIN), rows_of(GROUP * row_total, sent)),
        [pltpu.VMEM((row_total * GROUP, width), jnp.bfloat16)],
    )
    pieces = [chunk, CORES * chunk] + [chunk] * (n_seq - 1 - CORES) if by_steps else [sent]
    outgoing = pl.pallas_call(
        pack_kernel,
        out_shape=[rows_of(rows) for rows in pieces],
        in_specs=[vmem] * 3,
        out_specs=[vmem] * len(pieces),
        compiler_params=small,
    )(packed, borrow, borrowed)

    if by_steps:
        steps = exchange_steps()

        def exchange(part, step, flip=True):
            route, dc = steps[step]
            to = [route[i // CORES] * CORES + (i + (dc if flip else 0)) % CORES for i in range(n_seq)]
            return lax.ppermute(part, "seq", list(enumerate(to)))

        double = exchange(outgoing[1], 1, flip=False)
        rest = [exchange(part, 1 + CORES + i) for i, part in enumerate(outgoing[2:])]
        onward = pl.pallas_call(
            forward_kernel, out_shape=rows_of(chunk), in_specs=[vmem], out_specs=vmem, compiler_params=small
        )(double)
        arrived = [outgoing[0], double, exchange(onward, n_seq - 1), *rest]
    else:
        arrived = [
            lax.all_to_all(
                outgoing[0].reshape(n_seq, chunk, width), "seq", split_axis=0, concat_axis=0, tiled=True
            ).reshape(sent, width)
        ]
    placed = pl.pallas_call(
        place_kernel,
        out_shape=rows_of(row_total, GROUP * width),
        in_specs=[vmem] * (1 + len(arrived)),
        out_specs=pl.BlockSpec(memory_space=pltpu.HBM),
        scratch_shapes=[pltpu.VMEM((row_total, GROUP * width), jnp.bfloat16), pltpu.SemaphoreType.DMA((GROUP,))],
        compiler_params=small,
    )(place, *arrived)
    return placed[None]


def solution(mesh):
    placed = (
        P("enc", "seq", None),
        P("enc", "seq", None),
        P("enc", "seq"),
        P("enc", "seq"),
        P("enc", "seq"),
        P("enc", "seq"),
        P(),
        P(),
        P(),
    )
    return jax.shard_map(
        per_device, mesh=mesh, in_specs=placed, out_specs=P("enc", "seq", None), check_vma=False
    )
```

```python
import functools
import math

import jax
import jax.numpy as jnp
from jax import lax
from jax.experimental import pallas as pl
from jax.experimental.pallas import tpu as pltpu
from jax.sharding import PartitionSpec as P

HEADS = 16
WIN = 64
LANES = 128
GROUP = 4
EPS = 1e-6
CORES = 2

NT = (((1,), (1,)), ((), ()))


def dot32(a, b):
    return jnp.dot(a, b, preferred_element_type=jnp.float32)


def one_hot(match):
    return match.astype(jnp.float32).astype(jnp.bfloat16)


def attend(q, k, v, out_ref, row0, width):
    head = width // HEADS
    rate = 1.0 / math.sqrt(head)
    totals = [None] * (width // LANES)
    sums = [None] * (width // LANES)
    first_half = lax.broadcasted_iota(jnp.int32, (WIN, 2 * WIN), 1) < WIN
    for pair in range(HEADS // 2):
        start = 2 * pair * head
        lo = start // LANES * LANES
        hi = -(-(start + 2 * head) // LANES) * LANES
        column = lax.broadcasted_iota(jnp.int32, (2 * WIN, hi - lo), 1) + lo
        row = lax.broadcasted_iota(jnp.int32, (2 * WIN, hi - lo), 0)
        begin = jnp.where(row < WIN, start, start + head)
        mask = one_hot((column >= begin) & (column < begin + head))
        kw, vw = k(lo, hi), v(lo, hi)
        keys = jnp.concatenate([kw, kw], axis=0) * mask
        values = jnp.concatenate([vw, vw], axis=0) * mask
        scores = lax.dot_general(q(lo, hi), keys, NT, preferred_element_type=jnp.float32)
        top0 = jnp.max(jnp.where(first_half, scores, -jnp.inf), axis=1, keepdims=True)
        top1 = jnp.max(jnp.where(first_half, -jnp.inf, scores), axis=1, keepdims=True)
        raised = jnp.exp((scores - jnp.where(first_half, top0, top1)) * rate).astype(jnp.bfloat16)
        part = dot32(raised, values)
        norm = dot32(raised, mask)
        for tile in range(lo // LANES, hi // LANES):
            at = slice(tile * LANES - lo, (tile + 1) * LANES - lo)
            totals[tile] = part[:, at] if totals[tile] is None else totals[tile] + part[:, at]
            sums[tile] = norm[:, at] if sums[tile] is None else sums[tile] + norm[:, at]
    for tile in range(width // LANES):
        out_ref[row0 : row0 + WIN, tile * LANES : (tile + 1) * LANES] = (totals[tile] / sums[tile]).astype(
            jnp.bfloat16
        )


def encode(
    slot, qkv_hbm, resid_hbm, weight_hbm, bias_hbm, gain_hbm, out_ref,
    qkv, resid, weight, attended, hidden, bias_ref, gain_ref, sems,
):
    blocks = qkv.shape[0]
    width = resid.shape[2]
    at = pl.ds(slot, blocks)
    pairs = [
        (qkv_hbm.at[at], qkv), (weight_hbm, weight), (resid_hbm.at[at], resid), (bias_hbm, bias_ref), (gain_hbm, gain_ref)
    ]
    copies = [pltpu.make_async_copy(a, b, sems.at[i]) for i, (a, b) in enumerate(pairs)]
    for copy in copies:
        copy.start()
    copies[0].wait()
    for b in range(blocks):
        attend(
            lambda lo, hi, b=b: qkv[b, :, lo:hi],
            lambda lo, hi, b=b: qkv[b, :, width + lo : width + hi],
            lambda lo, hi, b=b: qkv[b, :, 2 * width + lo : 2 * width + hi],
            attended, b * WIN, width,
        )
    for copy in copies[1:]:
        copy.wait()
    rows = blocks * WIN
    squares = jnp.zeros((rows, 1), jnp.float32)
    step = 2 * LANES
    for lo in range(0, width, step):
        cols = slice(lo, lo + step)
        h = dot32(attended[...], weight[:, cols])
        h = h + bias_ref[cols].astype(jnp.float32).reshape(1, step)
        h = h + resid[:, :, cols].reshape(rows, step).astype(jnp.float32)
        hidden[:, cols] = h
        squares = squares + jnp.sum(h * h, axis=1, keepdims=True)
    scale = lax.rsqrt(squares * (1.0 / width) + EPS)
    for lo in range(0, width, step):
        cols = slice(lo, lo + step)
        gain = gain_ref[cols].astype(jnp.float32).reshape(1, step)
        out_ref[:, cols] = (hidden[:, cols] * scale * gain).astype(jnp.bfloat16)


def lent_kernel(count_ref, qkv_hbm, resid_hbm, weight_hbm, bias_hbm, gain_hbm, out_ref, *scratch):
    encode(count_ref[0, 0] - 1, qkv_hbm, resid_hbm, weight_hbm, bias_hbm, gain_hbm, out_ref, *scratch)


def split_index(index, n_seq, cap):
    step = index // (GROUP * cap)
    rest = index - step * (GROUP * cap)
    patch = rest // cap
    return step, patch, rest - patch * cap


def own_kernel(
    n_seq, cap, peer, count_ref, send_ref, me_ref, slot_ref, row_ref,
    qkv_hbm, resid_hbm, weight_hbm, bias_hbm, gain_hbm,
    packed_ref, borrow_ref, place_ref, normed, *scratch,
):
    rows = normed.shape[0]
    slots = n_seq * cap
    sent = slots * GROUP
    tokens = rows // GROUP
    me = me_ref[0, 0]
    encode(0, qkv_hbm, resid_hbm, weight_hbm, bias_hbm, gain_hbm, normed, *scratch)

    step, patch, rank = split_index(lax.broadcasted_iota(jnp.int32, (sent, 1), 0), n_seq, cap)
    row_code = (peer(me, step, 1) * cap + rank) * GROUP + patch
    token = lax.broadcasted_iota(jnp.int32, (tokens, rows), 0)
    column = lax.broadcasted_iota(jnp.int32, (tokens, rows), 1)
    spread = one_hot((column >= token * GROUP) & (column < (token + 1) * GROUP))
    slot = jnp.broadcast_to(slot_ref[...].astype(jnp.float32), (16, tokens)).astype(jnp.bfloat16)
    slot = dot32(slot, spread)[:1].astype(jnp.int32)
    index = lax.broadcasted_iota(jnp.int32, (1, rows), 1)
    col_code = slot * GROUP + jnp.bitwise_and(index, GROUP - 1)
    kept = (count_ref[0, 0] - send_ref[0, 0]) * WIN
    last = rows - WIN
    own = one_hot(row_code == jnp.where(index < kept, col_code, -1))
    packed_ref[...] = dot32(own, normed[...]).astype(jnp.bfloat16)
    borrow_ref[...] = one_hot(row_code == jnp.where(kept > last, -1, col_code[:, last:]))

    step, patch, rank = split_index(lax.broadcasted_iota(jnp.int32, (1, sent), 1), n_seq, cap)
    arrive = peer(me, step, -1) * cap + rank
    pick = one_hot(lax.broadcasted_iota(jnp.int32, (slots, sent), 0) == arrive)
    target = jnp.broadcast_to(row_ref[...].astype(jnp.float32), (16, slots)).astype(jnp.bfloat16)
    target = dot32(target, pick)[:1].astype(jnp.int32)
    out_row = lax.broadcasted_iota(jnp.int32, (tokens, sent), 0)
    for j in range(GROUP):
        place_ref[j * tokens : (j + 1) * tokens, :] = one_hot((target == out_row) & (patch == j))


def encode_call(kernel, blocks, scalars, slots, qkv, resid, weight, bias, gain, out_shape, extra):
    width = resid.shape[2]
    rows = blocks * WIN
    vmem = pl.BlockSpec(memory_space=pltpu.VMEM)
    smem = pl.BlockSpec(memory_space=pltpu.SMEM)
    hbm = pl.BlockSpec(memory_space=pltpu.HBM)
    return pl.pallas_call(
        kernel,
        out_shape=out_shape,
        in_specs=[smem] * len(scalars) + [vmem] * len(slots) + [hbm] * 5,
        out_specs=jax.tree.map(lambda _: vmem, out_shape),
        scratch_shapes=extra
        + [
            pltpu.VMEM((blocks, WIN, 3 * width), jnp.bfloat16),
            pltpu.VMEM((blocks, WIN, width), jnp.bfloat16),
            pltpu.VMEM((width, width), jnp.bfloat16),
            pltpu.VMEM((rows, width), jnp.bfloat16),
            pltpu.VMEM((rows, width), jnp.float32),
            pltpu.VMEM((width,), jnp.bfloat16),
            pltpu.VMEM((width,), jnp.bfloat16),
            pltpu.SemaphoreType.DMA((5,)),
        ],
        compiler_params=pltpu.CompilerParams(vmem_limit_bytes=24 << 20),
        cost_estimate=pl.CostEstimate(
            flops=2 * rows * width * width + 8 * rows * WIN * width,
            bytes_accessed=2 * (width * width + 5 * rows * width),
            transcendentals=rows * WIN * HEADS,
        ),
    )(*scalars, *slots, *(pltpu.with_memory_space_constraint(a, pltpu.HBM) for a in (qkv, resid, weight, bias, gain)))


def pack_kernel(packed_ref, borrow_ref, borrowed_ref, *out_refs):
    total = packed_ref[...].astype(jnp.float32) + dot32(borrow_ref[...], borrowed_ref[...])
    start = 0
    for out_ref in out_refs:
        stop = start + out_ref.shape[0]
        out_ref[...] = total[start:stop].astype(jnp.bfloat16)
        start = stop


def forward_kernel(double_ref, out_ref):
    rows = out_ref.shape[0]
    out_ref[...] = double_ref[...].astype(jnp.float32)[rows:].astype(jnp.bfloat16)


def place_kernel(place_ref, *refs):
    *in_refs, out_hbm, out, sems = refs
    tokens = out.shape[0]
    chunks = [ref[...].astype(jnp.float32) for ref in in_refs]
    if len(chunks) > 1:
        chunks[1] = chunks[1][: chunks[0].shape[0]]
    arrived = chunks[0] if len(chunks) == 1 else jnp.concatenate(chunks, axis=0)
    arrived = arrived.astype(jnp.bfloat16)
    width = arrived.shape[1]
    copies = []
    for j in range(GROUP):
        cols = slice(j * width, (j + 1) * width)
        out[:, cols] = dot32(place_ref[j * tokens : (j + 1) * tokens, :], arrived).astype(jnp.bfloat16)
        copies.append(pltpu.make_async_copy(out.at[:, cols], out_hbm.at[:, cols], sems.at[j]))
        copies[-1].start()
    for copy in copies:
        copy.wait()


def exchange_steps(n_seq):
    steps = [(dz, dc) for dz in range(1, n_seq // CORES) for dc in range(CORES)]
    return [(0, 0)] + steps[:CORES] + [(0, 1)] + steps[CORES:]


def chip_peer(n_seq, me, step, sign):
    n_z = n_seq // CORES
    offset = jnp.zeros_like(step)
    flip = jnp.zeros_like(step)
    for i, (dz, dc) in enumerate(exchange_steps(n_seq)):
        offset = jnp.where(step == i, dz, offset)
        flip = jnp.where(step == i, dc, flip)
    z = me // CORES + sign * offset
    z = jnp.where(z >= n_z, z - n_z, jnp.where(z < 0, z + n_z, z))
    return z * CORES + jnp.bitwise_xor(jnp.bitwise_and(me, 1), flip)


def per_device(
    qkv, resid, block_count, send_count, send_slot, lm_row, out_weight, out_bias, norm_gain
):
    width = resid.shape[2]
    row_total = send_slot.shape[1]
    tokens = WIN // GROUP
    blocks = row_total // tokens
    n_seq = lax.axis_size("seq")
    n_enc = lax.axis_size("enc")
    slots = lm_row.shape[1]
    cap = slots // n_seq
    chunk = GROUP * cap
    sent = slots * GROUP
    vmem = pl.BlockSpec(memory_space=pltpu.VMEM)
    small = pltpu.CompilerParams(vmem_limit_bytes=16 << 20)

    def rows_of(count, columns=width):
        return jax.ShapeDtypeStruct((count, columns), jnp.bfloat16)

    data = (qkv, resid, out_weight, out_bias, norm_gain)
    lent = encode_call(lent_kernel, 1, [block_count], [], *data, rows_of(WIN), [])
    borrowed = lax.ppermute(lent, "enc", [((i - 1) % n_enc, i) for i in range(n_enc)])

    by_steps = chunk % 8 == 0 and n_seq % CORES == 0
    peer = functools.partial(chip_peer, n_seq) if by_steps else lambda me, step, sign: step
    me = lax.axis_index("seq").astype(jnp.int32).reshape(1, 1)
    packed, borrow, place = encode_call(
        functools.partial(own_kernel, n_seq, cap, peer), blocks,
        [block_count, send_count, me], [send_slot, lm_row], *data,
        (rows_of(sent), rows_of(sent, WIN), rows_of(GROUP * row_total, sent)),
        [pltpu.VMEM((row_total * GROUP, width), jnp.bfloat16)],
    )
    pieces = [chunk, CORES * chunk] + [chunk] * (n_seq - 1 - CORES) if by_steps else [sent]
    outgoing = pl.pallas_call(
        pack_kernel,
        out_shape=[rows_of(rows) for rows in pieces],
        in_specs=[vmem] * 3,
        out_specs=[vmem] * len(pieces),
        compiler_params=small,
    )(packed, borrow, borrowed)

    if by_steps:
        n_z = n_seq // CORES

        def exchange(part, dz, dc):
            return lax.ppermute(
                part, "seq", [(i, (i // CORES + dz) % n_z * CORES + (i + dc) % CORES) for i in range(n_seq)]
            )

        double = exchange(outgoing[1], 1, 0)
        rest = [exchange(part, *step) for part, step in zip(outgoing[2:], exchange_steps(n_seq)[1 + CORES :])]
        onward = pl.pallas_call(
            forward_kernel, out_shape=rows_of(chunk), in_specs=[vmem], out_specs=vmem, compiler_params=small
        )(double)
        arrived = [outgoing[0], double, exchange(onward, 0, 1), *rest]
    else:
        arrived = [
            lax.all_to_all(
                outgoing[0].reshape(n_seq, chunk, width), "seq", split_axis=0, concat_axis=0, tiled=True
            ).reshape(sent, width)
        ]
    placed = pl.pallas_call(
        place_kernel,
        out_shape=rows_of(row_total, GROUP * width),
        in_specs=[vmem] * (1 + len(arrived)),
        out_specs=pl.BlockSpec(memory_space=pltpu.HBM),
        scratch_shapes=[pltpu.VMEM((row_total, GROUP * width), jnp.bfloat16), pltpu.SemaphoreType.DMA((GROUP,))],
        compiler_params=small,
    )(place, *arrived)
    return placed[None]


def solution(mesh):
    placed = (
        P("enc", "seq", None),
        P("enc", "seq", None),
        P("enc", "seq"),
        P("enc", "seq"),
        P("enc", "seq"),
        P("enc", "seq"),
        P(),
        P(),
        P(),
    )
    return jax.shard_map(
        per_device, mesh=mesh, in_specs=placed, out_specs=P("enc", "seq", None), check_vma=False
    )
```

```python
import functools
import math

import jax
import jax.numpy as jnp
from jax import lax
from jax.experimental import pallas as pl
from jax.experimental.pallas import tpu as pltpu
from jax.sharding import PartitionSpec as P

HEADS = 16
WIN = 64
LANES = 128
GROUP = 4
EPS = 1e-6
CORES = 2

NT = (((1,), (1,)), ((), ()))


def dot32(a, b):
    return jnp.dot(a, b, preferred_element_type=jnp.float32)


def one_hot(match):
    return match.astype(jnp.float32).astype(jnp.bfloat16)


def attend(q, k, v, out_ref, row0, width):
    head = width // HEADS
    rate = 1.0 / math.sqrt(head)
    totals = [None] * (width // LANES)
    sums = [None] * (width // LANES)
    first_half = lax.broadcasted_iota(jnp.int32, (WIN, 2 * WIN), 1) < WIN
    for pair in range(HEADS // 2):
        start = 2 * pair * head
        lo = start // LANES * LANES
        hi = -(-(start + 2 * head) // LANES) * LANES
        column = lax.broadcasted_iota(jnp.int32, (2 * WIN, hi - lo), 1) + lo
        row = lax.broadcasted_iota(jnp.int32, (2 * WIN, hi - lo), 0)
        begin = jnp.where(row < WIN, start, start + head)
        mask = one_hot((column >= begin) & (column < begin + head))
        kw, vw = k(lo, hi), v(lo, hi)
        keys = jnp.concatenate([kw, kw], axis=0) * mask
        values = jnp.concatenate([vw, vw], axis=0) * mask
        scores = lax.dot_general(q(lo, hi), keys, NT, preferred_element_type=jnp.float32)
        top0 = jnp.max(jnp.where(first_half, scores, -jnp.inf), axis=1, keepdims=True)
        top1 = jnp.max(jnp.where(first_half, -jnp.inf, scores), axis=1, keepdims=True)
        raised = jnp.exp((scores - jnp.where(first_half, top0, top1)) * rate).astype(jnp.bfloat16)
        part = dot32(raised, values)
        norm = dot32(raised, mask)
        for tile in range(lo // LANES, hi // LANES):
            at = slice(tile * LANES - lo, (tile + 1) * LANES - lo)
            totals[tile] = part[:, at] if totals[tile] is None else totals[tile] + part[:, at]
            sums[tile] = norm[:, at] if sums[tile] is None else sums[tile] + norm[:, at]
    for tile in range(width // LANES):
        out_ref[row0 : row0 + WIN, tile * LANES : (tile + 1) * LANES] = (totals[tile] / sums[tile]).astype(
            jnp.bfloat16
        )


def encode(
    slot, qkv_hbm, resid_hbm, weight_hbm, bias_hbm, gain_hbm, out_ref,
    qkv, resid, weight, attended, hidden, bias_ref, gain_ref, sems,
):
    blocks = qkv.shape[0]
    width = resid.shape[2]
    at = pl.ds(slot, blocks)
    pairs = [
        (qkv_hbm.at[at], qkv), (weight_hbm, weight), (resid_hbm.at[at], resid), (bias_hbm, bias_ref), (gain_hbm, gain_ref)
    ]
    copies = [pltpu.make_async_copy(a, b, sems.at[i]) for i, (a, b) in enumerate(pairs)]
    for copy in copies:
        copy.start()
    copies[0].wait()
    for b in range(blocks):
        attend(
            lambda lo, hi, b=b: qkv[b, :, lo:hi],
            lambda lo, hi, b=b: qkv[b, :, width + lo : width + hi],
            lambda lo, hi, b=b: qkv[b, :, 2 * width + lo : 2 * width + hi],
            attended, b * WIN, width,
        )
    for copy in copies[1:]:
        copy.wait()
    rows = blocks * WIN
    squares = jnp.zeros((rows, 1), jnp.float32)
    step = 2 * LANES
    for lo in range(0, width, step):
        cols = slice(lo, lo + step)
        h = dot32(attended[...], weight[:, cols])
        h = h + bias_ref[cols].astype(jnp.float32).reshape(1, step)
        h = h + resid[:, :, cols].reshape(rows, step).astype(jnp.float32)
        hidden[:, cols] = h
        squares = squares + jnp.sum(h * h, axis=1, keepdims=True)
    scale = lax.rsqrt(squares * (1.0 / width) + EPS)
    for lo in range(0, width, step):
        cols = slice(lo, lo + step)
        gain = gain_ref[cols].astype(jnp.float32).reshape(1, step)
        out_ref[:, cols] = (hidden[:, cols] * scale * gain).astype(jnp.bfloat16)


def lent_kernel(count_ref, qkv_hbm, resid_hbm, weight_hbm, bias_hbm, gain_hbm, out_ref, *scratch):
    encode(count_ref[0, 0] - 1, qkv_hbm, resid_hbm, weight_hbm, bias_hbm, gain_hbm, out_ref, *scratch)


def split_index(index, n_seq, cap):
    step = index // (GROUP * cap)
    rest = index - step * (GROUP * cap)
    patch = rest // cap
    return step, patch, rest - patch * cap


def own_kernel(
    n_seq, cap, peer, count_ref, send_ref, me_ref, slot_ref, row_ref,
    qkv_hbm, resid_hbm, weight_hbm, bias_hbm, gain_hbm,
    packed_ref, borrow_ref, place_ref, normed, *scratch,
):
    rows = normed.shape[0]
    slots = n_seq * cap
    sent = slots * GROUP
    tokens = rows // GROUP
    me = me_ref[0, 0]
    encode(0, qkv_hbm, resid_hbm, weight_hbm, bias_hbm, gain_hbm, normed, *scratch)

    step, patch, rank = split_index(lax.broadcasted_iota(jnp.int32, (sent, 1), 0), n_seq, cap)
    row_code = (peer(me, step, 1) * cap + rank) * GROUP + patch
    token = lax.broadcasted_iota(jnp.int32, (tokens, rows), 0)
    column = lax.broadcasted_iota(jnp.int32, (tokens, rows), 1)
    spread = one_hot((column >= token * GROUP) & (column < (token + 1) * GROUP))
    slot = jnp.broadcast_to(slot_ref[...].astype(jnp.float32), (16, tokens)).astype(jnp.bfloat16)
    slot = dot32(slot, spread)[:1].astype(jnp.int32)
    index = lax.broadcasted_iota(jnp.int32, (1, rows), 1)
    col_code = slot * GROUP + jnp.bitwise_and(index, GROUP - 1)
    kept = (count_ref[0, 0] - send_ref[0, 0]) * WIN
    last = rows - WIN
    own = one_hot(row_code == jnp.where(index < kept, col_code, -1))
    packed_ref[...] = dot32(own, normed[...]).astype(jnp.bfloat16)
    borrow_ref[...] = one_hot(row_code == jnp.where(kept > last, -1, col_code[:, last:]))

    step, patch, rank = split_index(lax.broadcasted_iota(jnp.int32, (1, sent), 1), n_seq, cap)
    arrive = peer(me, step, -1) * cap + rank
    pick = one_hot(lax.broadcasted_iota(jnp.int32, (slots, sent), 0) == arrive)
    target = jnp.broadcast_to(row_ref[...].astype(jnp.float32), (16, slots)).astype(jnp.bfloat16)
    target = dot32(target, pick)[:1].astype(jnp.int32)
    out_row = lax.broadcasted_iota(jnp.int32, (tokens, sent), 0)
    for j in range(GROUP):
        place_ref[j * tokens : (j + 1) * tokens, :] = one_hot((target == out_row) & (patch == j))


def encode_call(kernel, blocks, scalars, slots, qkv, resid, weight, bias, gain, out_shape, extra):
    width = resid.shape[2]
    rows = blocks * WIN
    vmem = pl.BlockSpec(memory_space=pltpu.VMEM)
    smem = pl.BlockSpec(memory_space=pltpu.SMEM)
    hbm = pl.BlockSpec(memory_space=pltpu.HBM)
    return pl.pallas_call(
        kernel,
        out_shape=out_shape,
        in_specs=[smem] * len(scalars) + [vmem] * len(slots) + [hbm] * 5,
        out_specs=jax.tree.map(lambda _: vmem, out_shape),
        scratch_shapes=extra
        + [
            pltpu.VMEM((blocks, WIN, 3 * width), jnp.bfloat16),
            pltpu.VMEM((blocks, WIN, width), jnp.bfloat16),
            pltpu.VMEM((width, width), jnp.bfloat16),
            pltpu.VMEM((rows, width), jnp.bfloat16),
            pltpu.VMEM((rows, width), jnp.float32),
            pltpu.VMEM((width,), jnp.bfloat16),
            pltpu.VMEM((width,), jnp.bfloat16),
            pltpu.SemaphoreType.DMA((5,)),
        ],
        compiler_params=pltpu.CompilerParams(vmem_limit_bytes=24 << 20),
        cost_estimate=pl.CostEstimate(
            flops=2 * rows * width * width + 8 * rows * WIN * width,
            bytes_accessed=2 * (width * width + 5 * rows * width),
            transcendentals=rows * WIN * HEADS,
        ),
    )(*scalars, *slots, *(pltpu.with_memory_space_constraint(a, pltpu.HBM) for a in (qkv, resid, weight, bias, gain)))


def pack_kernel(packed_ref, borrow_ref, borrowed_ref, *out_refs):
    total = packed_ref[...].astype(jnp.float32) + dot32(borrow_ref[...], borrowed_ref[...])
    start = 0
    for out_ref in out_refs:
        stop = start + out_ref.shape[0]
        out_ref[...] = total[start:stop].astype(jnp.bfloat16)
        start = stop


def forward_kernel(double_ref, out_ref):
    rows = out_ref.shape[0]
    out_ref[...] = double_ref[...].astype(jnp.float32)[rows:].astype(jnp.bfloat16)


def place_kernel(place_ref, *refs):
    *in_refs, out_hbm, out, sems = refs
    tokens = out.shape[0]
    chunks = [ref[...].astype(jnp.float32) for ref in in_refs]
    if len(chunks) > 1:
        own, double, passed, partner, *singles = chunks
        chunks = [own, double[: own.shape[0]], passed, *singles, partner]
    arrived = chunks[0] if len(chunks) == 1 else jnp.concatenate(chunks, axis=0)
    arrived = arrived.astype(jnp.bfloat16)
    width = arrived.shape[1]
    copies = []
    for j in range(GROUP):
        cols = slice(j * width, (j + 1) * width)
        out[:, cols] = dot32(place_ref[j * tokens : (j + 1) * tokens, :], arrived).astype(jnp.bfloat16)
        copies.append(pltpu.make_async_copy(out.at[:, cols], out_hbm.at[:, cols], sems.at[j]))
        copies[-1].start()
    for copy in copies:
        copy.wait()


def exchange_steps(n_seq):
    n_z = n_seq // CORES
    offsets = sorted(range(1, n_z), key=lambda dz: (dz != n_z // 2, dz))
    return [(0, 0)] + [(dz, dc) for dz in offsets for dc in range(CORES)] + [(0, 1)]


def chip_peer(n_seq, me, step, sign):
    n_z = n_seq // CORES
    offset = jnp.zeros_like(step)
    flip = jnp.zeros_like(step)
    for i, (dz, dc) in enumerate(exchange_steps(n_seq)):
        offset = jnp.where(step == i, dz, offset)
        flip = jnp.where(step == i, dc, flip)
    z = me // CORES + sign * offset
    z = jnp.where(z >= n_z, z - n_z, jnp.where(z < 0, z + n_z, z))
    return z * CORES + jnp.bitwise_xor(jnp.bitwise_and(me, 1), flip)


def per_device(
    qkv, resid, block_count, send_count, send_slot, lm_row, out_weight, out_bias, norm_gain
):
    width = resid.shape[2]
    row_total = send_slot.shape[1]
    tokens = WIN // GROUP
    blocks = row_total // tokens
    n_seq = lax.axis_size("seq")
    n_enc = lax.axis_size("enc")
    slots = lm_row.shape[1]
    cap = slots // n_seq
    chunk = GROUP * cap
    sent = slots * GROUP
    vmem = pl.BlockSpec(memory_space=pltpu.VMEM)
    small = pltpu.CompilerParams(vmem_limit_bytes=16 << 20)

    def rows_of(count, columns=width):
        return jax.ShapeDtypeStruct((count, columns), jnp.bfloat16)

    data = (qkv, resid, out_weight, out_bias, norm_gain)
    lent = encode_call(lent_kernel, 1, [block_count], [], *data, rows_of(WIN), [])
    borrowed = lax.ppermute(lent, "enc", [((i - 1) % n_enc, i) for i in range(n_enc)])

    by_steps = chunk % 8 == 0 and n_seq % CORES == 0
    peer = functools.partial(chip_peer, n_seq) if by_steps else lambda me, step, sign: step
    me = lax.axis_index("seq").astype(jnp.int32).reshape(1, 1)
    packed, borrow, place = encode_call(
        functools.partial(own_kernel, n_seq, cap, peer), blocks,
        [block_count, send_count, me], [send_slot, lm_row], *data,
        (rows_of(sent), rows_of(sent, WIN), rows_of(GROUP * row_total, sent)),
        [pltpu.VMEM((row_total * GROUP, width), jnp.bfloat16)],
    )
    pieces = [chunk, CORES * chunk] + [chunk] * (n_seq - 1 - CORES) if by_steps else [sent]
    outgoing = pl.pallas_call(
        pack_kernel,
        out_shape=[rows_of(rows) for rows in pieces],
        in_specs=[vmem] * 3,
        out_specs=[vmem] * len(pieces),
        compiler_params=small,
    )(packed, borrow, borrowed)

    if by_steps:
        n_z = n_seq // CORES

        def exchange(part, dz, dc):
            return lax.ppermute(
                part, "seq", [(i, (i // CORES + dz) % n_z * CORES + (i + dc) % CORES) for i in range(n_seq)]
            )

        double = exchange(outgoing[1], n_z // 2, 0)
        rest = [exchange(part, *step) for part, step in zip(outgoing[2:], exchange_steps(n_seq)[1 + CORES :])]
        onward = pl.pallas_call(
            forward_kernel, out_shape=rows_of(chunk), in_specs=[vmem], out_specs=vmem, compiler_params=small
        )(double)
        arrived = [outgoing[0], double, exchange(onward, 0, 1), rest[-1], *rest[:-1]]
    else:
        arrived = [
            lax.all_to_all(
                outgoing[0].reshape(n_seq, chunk, width), "seq", split_axis=0, concat_axis=0, tiled=True
            ).reshape(sent, width)
        ]
    placed = pl.pallas_call(
        place_kernel,
        out_shape=rows_of(row_total, GROUP * width),
        in_specs=[vmem] * (1 + len(arrived)),
        out_specs=pl.BlockSpec(memory_space=pltpu.HBM),
        scratch_shapes=[pltpu.VMEM((row_total, GROUP * width), jnp.bfloat16), pltpu.SemaphoreType.DMA((GROUP,))],
        compiler_params=small,
    )(place, *arrived)
    return placed[None]


def solution(mesh):
    placed = (
        P("enc", "seq", None),
        P("enc", "seq", None),
        P("enc", "seq"),
        P("enc", "seq"),
        P("enc", "seq"),
        P("enc", "seq"),
        P(),
        P(),
        P(),
    )
    return jax.shard_map(
        per_device, mesh=mesh, in_specs=placed, out_specs=P("enc", "seq", None), check_vma=False
    )
```

```python
import functools
import math

import jax
import jax.numpy as jnp
from jax import lax
from jax.experimental import pallas as pl
from jax.experimental.pallas import tpu as pltpu
from jax.sharding import PartitionSpec as P

HEADS = 16
WIN = 64
LANES = 128
GROUP = 4
EPS = 1e-6
CORES = 2

NT = (((1,), (1,)), ((), ()))


def dot32(a, b):
    return jnp.dot(a, b, preferred_element_type=jnp.float32)


def one_hot(match):
    return match.astype(jnp.float32).astype(jnp.bfloat16)


def attend(q, k, v, out_ref, row0, width):
    head = width // HEADS
    rate = 1.0 / math.sqrt(head)
    totals = [None] * (width // LANES)
    sums = [None] * (width // LANES)
    first_half = lax.broadcasted_iota(jnp.int32, (WIN, 2 * WIN), 1) < WIN
    for pair in range(HEADS // 2):
        start = 2 * pair * head
        lo = start // LANES * LANES
        hi = -(-(start + 2 * head) // LANES) * LANES
        column = lax.broadcasted_iota(jnp.int32, (2 * WIN, hi - lo), 1) + lo
        row = lax.broadcasted_iota(jnp.int32, (2 * WIN, hi - lo), 0)
        begin = jnp.where(row < WIN, start, start + head)
        mask = one_hot((column >= begin) & (column < begin + head))
        kw, vw = k(lo, hi), v(lo, hi)
        keys = jnp.concatenate([kw, kw], axis=0) * mask
        values = jnp.concatenate([vw, vw], axis=0) * mask
        scores = lax.dot_general(q(lo, hi), keys, NT, preferred_element_type=jnp.float32)
        top0 = jnp.max(jnp.where(first_half, scores, -jnp.inf), axis=1, keepdims=True)
        top1 = jnp.max(jnp.where(first_half, -jnp.inf, scores), axis=1, keepdims=True)
        raised = jnp.exp((scores - jnp.where(first_half, top0, top1)) * rate).astype(jnp.bfloat16)
        part = dot32(raised, values)
        norm = dot32(raised, mask)
        for tile in range(lo // LANES, hi // LANES):
            at = slice(tile * LANES - lo, (tile + 1) * LANES - lo)
            totals[tile] = part[:, at] if totals[tile] is None else totals[tile] + part[:, at]
            sums[tile] = norm[:, at] if sums[tile] is None else sums[tile] + norm[:, at]
    for tile in range(width // LANES):
        out_ref[row0 : row0 + WIN, tile * LANES : (tile + 1) * LANES] = (totals[tile] / sums[tile]).astype(
            jnp.bfloat16
        )


def encode(
    slot, qkv_hbm, resid_hbm, weight_hbm, bias_hbm, gain_hbm, out_ref,
    qkv, resid, weight, attended, hidden, bias_ref, gain_ref, sems,
):
    blocks = qkv.shape[0]
    width = resid.shape[2]
    at = pl.ds(slot, blocks)
    pairs = [
        (qkv_hbm.at[at], qkv), (weight_hbm, weight), (resid_hbm.at[at], resid), (bias_hbm, bias_ref), (gain_hbm, gain_ref)
    ]
    copies = [pltpu.make_async_copy(a, b, sems.at[i]) for i, (a, b) in enumerate(pairs)]
    for copy in copies:
        copy.start()
    copies[0].wait()
    for b in range(blocks):
        attend(
            lambda lo, hi, b=b: qkv[b, :, lo:hi],
            lambda lo, hi, b=b: qkv[b, :, width + lo : width + hi],
            lambda lo, hi, b=b: qkv[b, :, 2 * width + lo : 2 * width + hi],
            attended, b * WIN, width,
        )
    for copy in copies[1:]:
        copy.wait()
    rows = blocks * WIN
    squares = jnp.zeros((rows, 1), jnp.float32)
    step = 2 * LANES
    for lo in range(0, width, step):
        cols = slice(lo, lo + step)
        h = dot32(attended[...], weight[:, cols])
        h = h + bias_ref[cols].astype(jnp.float32).reshape(1, step)
        h = h + resid[:, :, cols].reshape(rows, step).astype(jnp.float32)
        hidden[:, cols] = h
        squares = squares + jnp.sum(h * h, axis=1, keepdims=True)
    scale = lax.rsqrt(squares * (1.0 / width) + EPS)
    for lo in range(0, width, step):
        cols = slice(lo, lo + step)
        gain = gain_ref[cols].astype(jnp.float32).reshape(1, step)
        out_ref[:, cols] = (hidden[:, cols] * scale * gain).astype(jnp.bfloat16)


def lent_kernel(count_ref, qkv_hbm, resid_hbm, weight_hbm, bias_hbm, gain_hbm, out_ref, *scratch):
    encode(count_ref[0, 0] - 1, qkv_hbm, resid_hbm, weight_hbm, bias_hbm, gain_hbm, out_ref, *scratch)


def split_index(index, n_seq, cap):
    step = index // (GROUP * cap)
    rest = index - step * (GROUP * cap)
    patch = rest // cap
    return step, patch, rest - patch * cap


def own_kernel(
    n_seq, cap, peer, count_ref, send_ref, me_ref, slot_ref, row_ref,
    qkv_hbm, resid_hbm, weight_hbm, bias_hbm, gain_hbm,
    packed_ref, borrow_ref, place_ref, normed, *scratch,
):
    rows = normed.shape[0]
    slots = n_seq * cap
    sent = slots * GROUP
    tokens = rows // GROUP
    me = me_ref[0, 0]
    encode(0, qkv_hbm, resid_hbm, weight_hbm, bias_hbm, gain_hbm, normed, *scratch)

    step, patch, rank = split_index(lax.broadcasted_iota(jnp.int32, (sent, 1), 0), n_seq, cap)
    row_code = (peer(me, step, 1) * cap + rank) * GROUP + patch
    token = lax.broadcasted_iota(jnp.int32, (tokens, rows), 0)
    column = lax.broadcasted_iota(jnp.int32, (tokens, rows), 1)
    spread = one_hot((column >= token * GROUP) & (column < (token + 1) * GROUP))
    slot = jnp.broadcast_to(slot_ref[...].astype(jnp.float32), (16, tokens)).astype(jnp.bfloat16)
    slot = dot32(slot, spread)[:1].astype(jnp.int32)
    index = lax.broadcasted_iota(jnp.int32, (1, rows), 1)
    col_code = slot * GROUP + jnp.bitwise_and(index, GROUP - 1)
    kept = (count_ref[0, 0] - send_ref[0, 0]) * WIN
    last = rows - WIN
    own = one_hot(row_code == jnp.where(index < kept, col_code, -1))
    packed_ref[...] = dot32(own, normed[...]).astype(jnp.bfloat16)
    borrow_ref[...] = one_hot(row_code == jnp.where(kept > last, -1, col_code[:, last:]))

    step, patch, rank = split_index(lax.broadcasted_iota(jnp.int32, (1, sent), 1), n_seq, cap)
    arrive = peer(me, step, -1) * cap + rank
    pick = one_hot(lax.broadcasted_iota(jnp.int32, (slots, sent), 0) == arrive)
    target = jnp.broadcast_to(row_ref[...].astype(jnp.float32), (16, slots)).astype(jnp.bfloat16)
    target = dot32(target, pick)[:1].astype(jnp.int32)
    out_row = lax.broadcasted_iota(jnp.int32, (tokens, sent), 0)
    for j in range(GROUP):
        place_ref[j * tokens : (j + 1) * tokens, :] = one_hot((target == out_row) & (patch == j))


def encode_call(kernel, blocks, scalars, slots, qkv, resid, weight, bias, gain, out_shape, extra):
    width = resid.shape[2]
    rows = blocks * WIN
    vmem = pl.BlockSpec(memory_space=pltpu.VMEM)
    smem = pl.BlockSpec(memory_space=pltpu.SMEM)
    hbm = pl.BlockSpec(memory_space=pltpu.HBM)
    return pl.pallas_call(
        kernel,
        out_shape=out_shape,
        in_specs=[smem] * len(scalars) + [vmem] * len(slots) + [hbm] * 5,
        out_specs=jax.tree.map(lambda _: vmem, out_shape),
        scratch_shapes=extra
        + [
            pltpu.VMEM((blocks, WIN, 3 * width), jnp.bfloat16),
            pltpu.VMEM((blocks, WIN, width), jnp.bfloat16),
            pltpu.VMEM((width, width), jnp.bfloat16),
            pltpu.VMEM((rows, width), jnp.bfloat16),
            pltpu.VMEM((rows, width), jnp.float32),
            pltpu.VMEM((width,), jnp.bfloat16),
            pltpu.VMEM((width,), jnp.bfloat16),
            pltpu.SemaphoreType.DMA((5,)),
        ],
        compiler_params=pltpu.CompilerParams(vmem_limit_bytes=24 << 20),
        cost_estimate=pl.CostEstimate(
            flops=2 * rows * width * width + 8 * rows * WIN * width,
            bytes_accessed=2 * (width * width + 5 * rows * width),
            transcendentals=rows * WIN * HEADS,
        ),
    )(*scalars, *slots, *(pltpu.with_memory_space_constraint(a, pltpu.HBM) for a in (qkv, resid, weight, bias, gain)))


def pack_kernel(packed_ref, borrow_ref, borrowed_ref, *out_refs):
    total = packed_ref[...].astype(jnp.float32) + dot32(borrow_ref[...], borrowed_ref[...])
    start = 0
    for out_ref in out_refs:
        stop = start + out_ref.shape[0]
        out_ref[...] = total[start:stop].astype(jnp.bfloat16)
        start = stop


def forward_kernel(double_ref, out_ref):
    rows = out_ref.shape[0]
    out_ref[...] = double_ref[...].astype(jnp.float32)[rows:].astype(jnp.bfloat16)


def place_kernel(place_ref, *refs):
    *in_refs, out_hbm, out, sems = refs
    tokens = out.shape[0]
    chunks = [ref[...].astype(jnp.float32) for ref in in_refs]
    if len(chunks) > 1:
        chunks[1] = chunks[1][: chunks[0].shape[0]]
    arrived = chunks[0] if len(chunks) == 1 else jnp.concatenate(chunks, axis=0)
    arrived = arrived.astype(jnp.bfloat16)
    width = arrived.shape[1]
    copies = []
    for j in range(GROUP):
        cols = slice(j * width, (j + 1) * width)
        out[:, cols] = dot32(place_ref[j * tokens : (j + 1) * tokens, :], arrived).astype(jnp.bfloat16)
        copies.append(pltpu.make_async_copy(out.at[:, cols], out_hbm.at[:, cols], sems.at[j]))
        copies[-1].start()
    for copy in copies:
        copy.wait()


def exchange_steps(n_seq):
    n_z = n_seq // CORES
    offsets = sorted(range(1, n_z), key=lambda dz: (dz != n_z // 2, dz))
    return [(0, 0)] + [(dz, dc) for dz in offsets for dc in range(CORES)] + [(0, 1)]


def chip_peer(n_seq, me, step, sign):
    n_z = n_seq // CORES
    offset = jnp.zeros_like(step)
    flip = jnp.zeros_like(step)
    for i, (dz, dc) in enumerate(exchange_steps(n_seq)):
        offset = jnp.where(step == i, dz, offset)
        flip = jnp.where(step == i, dc, flip)
    z = me // CORES + sign * offset
    z = jnp.where(z >= n_z, z - n_z, jnp.where(z < 0, z + n_z, z))
    return z * CORES + jnp.bitwise_xor(jnp.bitwise_and(me, 1), flip)


def per_device(
    qkv, resid, block_count, send_count, send_slot, lm_row, out_weight, out_bias, norm_gain
):
    width = resid.shape[2]
    row_total = send_slot.shape[1]
    tokens = WIN // GROUP
    blocks = row_total // tokens
    n_seq = lax.axis_size("seq")
    n_enc = lax.axis_size("enc")
    slots = lm_row.shape[1]
    cap = slots // n_seq
    chunk = GROUP * cap
    sent = slots * GROUP
    vmem = pl.BlockSpec(memory_space=pltpu.VMEM)
    small = pltpu.CompilerParams(vmem_limit_bytes=16 << 20)

    def rows_of(count, columns=width):
        return jax.ShapeDtypeStruct((count, columns), jnp.bfloat16)

    data = (qkv, resid, out_weight, out_bias, norm_gain)
    lent = encode_call(lent_kernel, 1, [block_count], [], *data, rows_of(WIN), [])
    borrowed = lax.ppermute(lent, "enc", [((i - 1) % n_enc, i) for i in range(n_enc)])

    by_steps = chunk % 8 == 0 and n_seq % CORES == 0
    peer = functools.partial(chip_peer, n_seq) if by_steps else lambda me, step, sign: step
    me = lax.axis_index("seq").astype(jnp.int32).reshape(1, 1)
    packed, borrow, place = encode_call(
        functools.partial(own_kernel, n_seq, cap, peer), blocks,
        [block_count, send_count, me], [send_slot, lm_row], *data,
        (rows_of(sent), rows_of(sent, WIN), rows_of(GROUP * row_total, sent)),
        [pltpu.VMEM((row_total * GROUP, width), jnp.bfloat16)],
    )
    pieces = [chunk, CORES * chunk] + [chunk] * (n_seq - 1 - CORES) if by_steps else [sent]
    outgoing = pl.pallas_call(
        pack_kernel,
        out_shape=[rows_of(rows) for rows in pieces],
        in_specs=[vmem] * 3,
        out_specs=[vmem] * len(pieces),
        compiler_params=small,
    )(packed, borrow, borrowed)

    if by_steps:
        n_z = n_seq // CORES

        def exchange(part, dz, dc):
            return lax.ppermute(
                part, "seq", [(i, (i // CORES + dz) % n_z * CORES + (i + dc) % CORES) for i in range(n_seq)]
            )

        double = exchange(outgoing[1], n_z // 2, 0)
        rest = [exchange(part, *step) for part, step in zip(outgoing[2:], exchange_steps(n_seq)[1 + CORES :])]
        onward = pl.pallas_call(
            forward_kernel, out_shape=rows_of(chunk), in_specs=[vmem], out_specs=vmem, compiler_params=small
        )(double)
        arrived = [outgoing[0], double, exchange(onward, 0, 1), *rest]
    else:
        arrived = [
            lax.all_to_all(
                outgoing[0].reshape(n_seq, chunk, width), "seq", split_axis=0, concat_axis=0, tiled=True
            ).reshape(sent, width)
        ]
    placed = pl.pallas_call(
        place_kernel,
        out_shape=rows_of(row_total, GROUP * width),
        in_specs=[vmem] * (1 + len(arrived)),
        out_specs=pl.BlockSpec(memory_space=pltpu.HBM),
        scratch_shapes=[pltpu.VMEM((row_total, GROUP * width), jnp.bfloat16), pltpu.SemaphoreType.DMA((GROUP,))],
        compiler_params=small,
    )(place, *arrived)
    return placed[None]


def solution(mesh):
    placed = (
        P("enc", "seq", None),
        P("enc", "seq", None),
        P("enc", "seq"),
        P("enc", "seq"),
        P("enc", "seq"),
        P("enc", "seq"),
        P(),
        P(),
        P(),
    )
    return jax.shard_map(
        per_device, mesh=mesh, in_specs=placed, out_specs=P("enc", "seq", None), check_vma=False
    )
```

```python
import functools
import math

import jax
import jax.numpy as jnp
from jax import lax
from jax.experimental import pallas as pl
from jax.experimental.pallas import tpu as pltpu
from jax.sharding import PartitionSpec as P

HEADS = 16
WIN = 64
LANES = 128
GROUP = 4
EPS = 1e-6
CORES = 2

NT = (((1,), (1,)), ((), ()))


def dot32(a, b):
    return jnp.dot(a, b, preferred_element_type=jnp.float32)


def one_hot(match):
    return match.astype(jnp.float32).astype(jnp.bfloat16)


def attend(q, k, v, out_ref, row0, width):
    head = width // HEADS
    rate = 1.0 / math.sqrt(head)
    totals = [None] * (width // LANES)
    sums = [None] * (width // LANES)
    first_half = lax.broadcasted_iota(jnp.int32, (WIN, 2 * WIN), 1) < WIN
    for pair in range(HEADS // 2):
        start = 2 * pair * head
        lo = start // LANES * LANES
        hi = -(-(start + 2 * head) // LANES) * LANES
        column = lax.broadcasted_iota(jnp.int32, (2 * WIN, hi - lo), 1) + lo
        row = lax.broadcasted_iota(jnp.int32, (2 * WIN, hi - lo), 0)
        begin = jnp.where(row < WIN, start, start + head)
        mask = one_hot((column >= begin) & (column < begin + head))
        kw, vw = k(lo, hi), v(lo, hi)
        keys = jnp.concatenate([kw, kw], axis=0) * mask
        values = jnp.concatenate([vw, vw], axis=0) * mask
        scores = lax.dot_general(q(lo, hi), keys, NT, preferred_element_type=jnp.float32)
        top0 = jnp.max(jnp.where(first_half, scores, -jnp.inf), axis=1, keepdims=True)
        top1 = jnp.max(jnp.where(first_half, -jnp.inf, scores), axis=1, keepdims=True)
        raised = jnp.exp((scores - jnp.where(first_half, top0, top1)) * rate).astype(jnp.bfloat16)
        part = dot32(raised, values)
        norm = dot32(raised, mask)
        for tile in range(lo // LANES, hi // LANES):
            at = slice(tile * LANES - lo, (tile + 1) * LANES - lo)
            totals[tile] = part[:, at] if totals[tile] is None else totals[tile] + part[:, at]
            sums[tile] = norm[:, at] if sums[tile] is None else sums[tile] + norm[:, at]
    for tile in range(width // LANES):
        out_ref[row0 : row0 + WIN, tile * LANES : (tile + 1) * LANES] = (totals[tile] / sums[tile]).astype(
            jnp.bfloat16
        )


def encode(
    slot, qkv_hbm, resid_hbm, weight_hbm, bias_hbm, gain_hbm, out_ref,
    qkv, resid, weight, attended, hidden, bias_ref, gain_ref, sems,
):
    blocks = qkv.shape[0]
    width = resid.shape[2]
    at = pl.ds(slot, blocks)
    pairs = [
        (qkv_hbm.at[at], qkv), (weight_hbm, weight), (resid_hbm.at[at], resid), (bias_hbm, bias_ref), (gain_hbm, gain_ref)
    ]
    copies = [pltpu.make_async_copy(a, b, sems.at[i]) for i, (a, b) in enumerate(pairs)]
    for copy in copies:
        copy.start()
    copies[0].wait()
    for b in range(blocks):
        attend(
            lambda lo, hi, b=b: qkv[b, :, lo:hi],
            lambda lo, hi, b=b: qkv[b, :, width + lo : width + hi],
            lambda lo, hi, b=b: qkv[b, :, 2 * width + lo : 2 * width + hi],
            attended, b * WIN, width,
        )
    for copy in copies[1:]:
        copy.wait()
    rows = blocks * WIN
    squares = jnp.zeros((rows, 1), jnp.float32)
    step = 2 * LANES
    for lo in range(0, width, step):
        cols = slice(lo, lo + step)
        h = dot32(attended[...], weight[:, cols])
        h = h + bias_ref[cols].astype(jnp.float32).reshape(1, step)
        h = h + resid[:, :, cols].reshape(rows, step).astype(jnp.float32)
        hidden[:, cols] = h
        squares = squares + jnp.sum(h * h, axis=1, keepdims=True)
    scale = lax.rsqrt(squares * (1.0 / width) + EPS)
    for lo in range(0, width, step):
        cols = slice(lo, lo + step)
        gain = gain_ref[cols].astype(jnp.float32).reshape(1, step)
        out_ref[:, cols] = (hidden[:, cols] * scale * gain).astype(jnp.bfloat16)


def lent_kernel(count_ref, qkv_hbm, resid_hbm, weight_hbm, bias_hbm, gain_hbm, out_ref, *scratch):
    encode(count_ref[0, 0] - 1, qkv_hbm, resid_hbm, weight_hbm, bias_hbm, gain_hbm, out_ref, *scratch)


def split_index(index, n_seq, cap):
    step = index // (GROUP * cap)
    rest = index - step * (GROUP * cap)
    patch = rest // cap
    return step, patch, rest - patch * cap


def own_kernel(
    n_seq, cap, peer, count_ref, send_ref, me_ref, slot_ref, row_ref,
    qkv_hbm, resid_hbm, weight_hbm, bias_hbm, gain_hbm,
    packed_ref, borrow_ref, place_ref, normed, *scratch,
):
    rows = normed.shape[0]
    slots = n_seq * cap
    sent = slots * GROUP
    tokens = rows // GROUP
    me = me_ref[0, 0]
    encode(0, qkv_hbm, resid_hbm, weight_hbm, bias_hbm, gain_hbm, normed, *scratch)

    step, patch, rank = split_index(lax.broadcasted_iota(jnp.int32, (sent, 1), 0), n_seq, cap)
    row_code = (peer(me, step, 1) * cap + rank) * GROUP + patch
    token = lax.broadcasted_iota(jnp.int32, (tokens, rows), 0)
    column = lax.broadcasted_iota(jnp.int32, (tokens, rows), 1)
    spread = one_hot((column >= token * GROUP) & (column < (token + 1) * GROUP))
    slot = jnp.broadcast_to(slot_ref[...].astype(jnp.float32), (16, tokens)).astype(jnp.bfloat16)
    slot = dot32(slot, spread)[:1].astype(jnp.int32)
    index = lax.broadcasted_iota(jnp.int32, (1, rows), 1)
    col_code = slot * GROUP + jnp.bitwise_and(index, GROUP - 1)
    kept = (count_ref[0, 0] - send_ref[0, 0]) * WIN
    last = rows - WIN
    own = one_hot(row_code == jnp.where(index < kept, col_code, -1))
    packed_ref[...] = dot32(own, normed[...]).astype(jnp.bfloat16)
    borrow_ref[...] = one_hot(row_code == jnp.where(kept > last, -1, col_code[:, last:]))

    step, patch, rank = split_index(lax.broadcasted_iota(jnp.int32, (1, sent), 1), n_seq, cap)
    arrive = peer(me, step, -1) * cap + rank
    pick = one_hot(lax.broadcasted_iota(jnp.int32, (slots, sent), 0) == arrive)
    target = jnp.broadcast_to(row_ref[...].astype(jnp.float32), (16, slots)).astype(jnp.bfloat16)
    target = dot32(target, pick)[:1].astype(jnp.int32)
    out_row = lax.broadcasted_iota(jnp.int32, (tokens, sent), 0)
    for j in range(GROUP):
        place_ref[j * tokens : (j + 1) * tokens, :] = one_hot((target == out_row) & (patch == j))


def encode_call(kernel, blocks, scalars, slots, qkv, resid, weight, bias, gain, out_shape, extra):
    width = resid.shape[2]
    rows = blocks * WIN
    vmem = pl.BlockSpec(memory_space=pltpu.VMEM)
    smem = pl.BlockSpec(memory_space=pltpu.SMEM)
    hbm = pl.BlockSpec(memory_space=pltpu.HBM)
    return pl.pallas_call(
        kernel,
        out_shape=out_shape,
        in_specs=[smem] * len(scalars) + [vmem] * len(slots) + [hbm] * 5,
        out_specs=jax.tree.map(lambda _: vmem, out_shape),
        scratch_shapes=extra
        + [
            pltpu.VMEM((blocks, WIN, 3 * width), jnp.bfloat16),
            pltpu.VMEM((blocks, WIN, width), jnp.bfloat16),
            pltpu.VMEM((width, width), jnp.bfloat16),
            pltpu.VMEM((rows, width), jnp.bfloat16),
            pltpu.VMEM((rows, width), jnp.float32),
            pltpu.VMEM((width,), jnp.bfloat16),
            pltpu.VMEM((width,), jnp.bfloat16),
            pltpu.SemaphoreType.DMA((5,)),
        ],
        compiler_params=pltpu.CompilerParams(vmem_limit_bytes=24 << 20),
        cost_estimate=pl.CostEstimate(
            flops=2 * rows * width * width + 8 * rows * WIN * width,
            bytes_accessed=2 * (width * width + 5 * rows * width),
            transcendentals=rows * WIN * HEADS,
        ),
    )(*scalars, *slots, *(pltpu.with_memory_space_constraint(a, pltpu.HBM) for a in (qkv, resid, weight, bias, gain)))


def pack_kernel(packed_ref, borrow_ref, borrowed_ref, *out_refs):
    total = packed_ref[...].astype(jnp.float32) + dot32(borrow_ref[...], borrowed_ref[...])
    start = 0
    for out_ref in out_refs:
        stop = start + out_ref.shape[0]
        out_ref[...] = total[start:stop].astype(jnp.bfloat16)
        start = stop


def forward_kernel(double_ref, out_ref):
    rows = out_ref.shape[0]
    out_ref[...] = double_ref[...].astype(jnp.float32)[rows:].astype(jnp.bfloat16)


def place_kernel(place_ref, *refs):
    *in_refs, out_hbm, out, sems = refs
    tokens = out.shape[0]
    chunks = [ref[...].astype(jnp.float32) for ref in in_refs]
    if len(chunks) > 1:
        chunks[1] = chunks[1][: chunks[0].shape[0]]
    arrived = chunks[0] if len(chunks) == 1 else jnp.concatenate(chunks, axis=0)
    arrived = arrived.astype(jnp.bfloat16)
    width = arrived.shape[1]
    copies = []
    for j in range(GROUP):
        cols = slice(j * width, (j + 1) * width)
        out[:, cols] = dot32(place_ref[j * tokens : (j + 1) * tokens, :], arrived).astype(jnp.bfloat16)
        copies.append(pltpu.make_async_copy(out.at[:, cols], out_hbm.at[:, cols], sems.at[j]))
        copies[-1].start()
    for copy in copies:
        copy.wait()


def exchange_steps(n_seq):
    return [(0, 0)] + [(dz, dc) for dz in range(1, n_seq // CORES) for dc in range(CORES)] + [(0, 1)]


def chip_peer(n_seq, me, step, sign):
    n_z = n_seq // CORES
    offset = jnp.zeros_like(step)
    flip = jnp.zeros_like(step)
    for i, (dz, dc) in enumerate(exchange_steps(n_seq)):
        offset = jnp.where(step == i, dz, offset)
        flip = jnp.where(step == i, dc, flip)
    z = me // CORES + sign * offset
    z = jnp.where(z >= n_z, z - n_z, jnp.where(z < 0, z + n_z, z))
    return z * CORES + jnp.bitwise_xor(jnp.bitwise_and(me, 1), flip)


def per_device(
    qkv, resid, block_count, send_count, send_slot, lm_row, out_weight, out_bias, norm_gain
):
    width = resid.shape[2]
    row_total = send_slot.shape[1]
    tokens = WIN // GROUP
    blocks = row_total // tokens
    n_seq = lax.axis_size("seq")
    n_enc = lax.axis_size("enc")
    slots = lm_row.shape[1]
    cap = slots // n_seq
    chunk = GROUP * cap
    sent = slots * GROUP
    vmem = pl.BlockSpec(memory_space=pltpu.VMEM)
    small = pltpu.CompilerParams(vmem_limit_bytes=16 << 20)

    def rows_of(count, columns=width):
        return jax.ShapeDtypeStruct((count, columns), jnp.bfloat16)

    data = (qkv, resid, out_weight, out_bias, norm_gain)
    lent = encode_call(lent_kernel, 1, [block_count], [], *data, rows_of(WIN), [])
    borrowed = lax.ppermute(lent, "enc", [((i - 1) % n_enc, i) for i in range(n_enc)])

    by_steps = chunk % 8 == 0 and n_seq % CORES == 0
    peer = functools.partial(chip_peer, n_seq) if by_steps else lambda me, step, sign: step
    me = lax.axis_index("seq").astype(jnp.int32).reshape(1, 1)
    packed, borrow, place = encode_call(
        functools.partial(own_kernel, n_seq, cap, peer), blocks,
        [block_count, send_count, me], [send_slot, lm_row], *data,
        (rows_of(sent), rows_of(sent, WIN), rows_of(GROUP * row_total, sent)),
        [pltpu.VMEM((row_total * GROUP, width), jnp.bfloat16)],
    )
    pieces = [chunk, CORES * chunk] + [chunk] * (n_seq - 1 - CORES) if by_steps else [sent]
    outgoing = pl.pallas_call(
        pack_kernel,
        out_shape=[rows_of(rows) for rows in pieces],
        in_specs=[vmem] * 3,
        out_specs=[vmem] * len(pieces),
        compiler_params=small,
    )(packed, borrow, borrowed)

    if by_steps:
        n_z = n_seq // CORES

        def exchange(part, dz, dc):
            return lax.ppermute(
                part, "seq", [(i, (i // CORES + dz) % n_z * CORES + (i + dc) % CORES) for i in range(n_seq)]
            )

        double = exchange(outgoing[1], 1, 0)
        rest = [exchange(part, *step) for part, step in zip(outgoing[2:], exchange_steps(n_seq)[1 + CORES :])]
        onward = pl.pallas_call(
            forward_kernel, out_shape=rows_of(chunk), in_specs=[vmem], out_specs=vmem, compiler_params=small
        )(double)
        arrived = [outgoing[0], double, exchange(onward, 0, 1), *rest]
    else:
        arrived = [
            lax.all_to_all(
                outgoing[0].reshape(n_seq, chunk, width), "seq", split_axis=0, concat_axis=0, tiled=True
            ).reshape(sent, width)
        ]
    placed = pl.pallas_call(
        place_kernel,
        out_shape=rows_of(row_total, GROUP * width),
        in_specs=[vmem] * (1 + len(arrived)),
        out_specs=pl.BlockSpec(memory_space=pltpu.HBM),
        scratch_shapes=[pltpu.VMEM((row_total, GROUP * width), jnp.bfloat16), pltpu.SemaphoreType.DMA((GROUP,))],
        compiler_params=small,
    )(place, *arrived)
    return placed[None]


def solution(mesh):
    placed = (
        P("enc", "seq", None),
        P("enc", "seq", None),
        P("enc", "seq"),
        P("enc", "seq"),
        P("enc", "seq"),
        P("enc", "seq"),
        P(),
        P(),
        P(),
    )
    return jax.shard_map(
        per_device, mesh=mesh, in_specs=placed, out_specs=P("enc", "seq", None), check_vma=False
    )
```

```python
import functools
import math

import jax
import jax.numpy as jnp
from jax import lax
from jax.experimental import pallas as pl
from jax.experimental.pallas import tpu as pltpu
from jax.sharding import PartitionSpec as P

HEADS = 16
WIN = 64
LANES = 128
GROUP = 4
EPS = 1e-6
CORES = 2

NT = (((1,), (1,)), ((), ()))


def dot32(a, b):
    return jnp.dot(a, b, preferred_element_type=jnp.float32)


def one_hot(match):
    return match.astype(jnp.float32).astype(jnp.bfloat16)


def attend(q, k, v, out_ref, row0, width):
    head = width // HEADS
    rate = 1.0 / math.sqrt(head)
    totals = [None] * (width // LANES)
    sums = [None] * (width // LANES)
    first_half = lax.broadcasted_iota(jnp.int32, (WIN, 2 * WIN), 1) < WIN
    for pair in range(HEADS // 2):
        start = 2 * pair * head
        lo = start // LANES * LANES
        hi = -(-(start + 2 * head) // LANES) * LANES
        column = lax.broadcasted_iota(jnp.int32, (2 * WIN, hi - lo), 1) + lo
        row = lax.broadcasted_iota(jnp.int32, (2 * WIN, hi - lo), 0)
        begin = jnp.where(row < WIN, start, start + head)
        mask = one_hot((column >= begin) & (column < begin + head))
        kw, vw = k(lo, hi), v(lo, hi)
        keys = jnp.concatenate([kw, kw], axis=0) * mask
        values = jnp.concatenate([vw, vw], axis=0) * mask
        scores = lax.dot_general(q(lo, hi), keys, NT, preferred_element_type=jnp.float32)
        top0 = jnp.max(jnp.where(first_half, scores, -jnp.inf), axis=1, keepdims=True)
        top1 = jnp.max(jnp.where(first_half, -jnp.inf, scores), axis=1, keepdims=True)
        raised = jnp.exp((scores - jnp.where(first_half, top0, top1)) * rate).astype(jnp.bfloat16)
        part = dot32(raised, values)
        norm = dot32(raised, mask)
        for tile in range(lo // LANES, hi // LANES):
            at = slice(tile * LANES - lo, (tile + 1) * LANES - lo)
            totals[tile] = part[:, at] if totals[tile] is None else totals[tile] + part[:, at]
            sums[tile] = norm[:, at] if sums[tile] is None else sums[tile] + norm[:, at]
    for tile in range(width // LANES):
        out_ref[row0 : row0 + WIN, tile * LANES : (tile + 1) * LANES] = (totals[tile] / sums[tile]).astype(
            jnp.bfloat16
        )


def encode(
    slot, qkv_hbm, resid_hbm, weight_hbm, bias_hbm, gain_hbm, out_ref,
    qkv, resid, weight, attended, hidden, bias_ref, gain_ref, sems,
):
    blocks = qkv.shape[0]
    width = resid.shape[2]
    at = pl.ds(slot, blocks)
    pairs = [
        (qkv_hbm.at[at], qkv), (weight_hbm, weight), (resid_hbm.at[at], resid), (bias_hbm, bias_ref), (gain_hbm, gain_ref)
    ]
    copies = [pltpu.make_async_copy(a, b, sems.at[i]) for i, (a, b) in enumerate(pairs)]
    for copy in copies:
        copy.start()
    copies[0].wait()
    for b in range(blocks):
        attend(
            lambda lo, hi, b=b: qkv[b, :, lo:hi],
            lambda lo, hi, b=b: qkv[b, :, width + lo : width + hi],
            lambda lo, hi, b=b: qkv[b, :, 2 * width + lo : 2 * width + hi],
            attended, b * WIN, width,
        )
    for copy in copies[1:]:
        copy.wait()
    rows = blocks * WIN
    squares = jnp.zeros((rows, 1), jnp.float32)
    step = 2 * LANES
    for lo in range(0, width, step):
        cols = slice(lo, lo + step)
        h = dot32(attended[...], weight[:, cols])
        h = h + bias_ref[cols].astype(jnp.float32).reshape(1, step)
        h = h + resid[:, :, cols].reshape(rows, step).astype(jnp.float32)
        hidden[:, cols] = h
        squares = squares + jnp.sum(h * h, axis=1, keepdims=True)
    scale = lax.rsqrt(squares * (1.0 / width) + EPS)
    for lo in range(0, width, step):
        cols = slice(lo, lo + step)
        gain = gain_ref[cols].astype(jnp.float32).reshape(1, step)
        out_ref[:, cols] = (hidden[:, cols] * scale * gain).astype(jnp.bfloat16)


def lent_kernel(count_ref, qkv_hbm, resid_hbm, weight_hbm, bias_hbm, gain_hbm, out_ref, *scratch):
    encode(count_ref[0, 0] - 1, qkv_hbm, resid_hbm, weight_hbm, bias_hbm, gain_hbm, out_ref, *scratch)


def split_index(index, n_seq, cap):
    step = index // (GROUP * cap)
    rest = index - step * (GROUP * cap)
    patch = rest // cap
    return step, patch, rest - patch * cap


def own_kernel(
    n_seq, cap, peer, count_ref, send_ref, me_ref, slot_ref, row_ref,
    qkv_hbm, resid_hbm, weight_hbm, bias_hbm, gain_hbm,
    packed_ref, borrow_ref, place_ref, normed, *scratch,
):
    rows = normed.shape[0]
    slots = n_seq * cap
    sent = slots * GROUP
    tokens = rows // GROUP
    me = me_ref[0, 0]
    encode(0, qkv_hbm, resid_hbm, weight_hbm, bias_hbm, gain_hbm, normed, *scratch)

    step, patch, rank = split_index(lax.broadcasted_iota(jnp.int32, (sent, 1), 0), n_seq, cap)
    row_code = (peer(me, step, 1) * cap + rank) * GROUP + patch
    token = lax.broadcasted_iota(jnp.int32, (tokens, rows), 0)
    column = lax.broadcasted_iota(jnp.int32, (tokens, rows), 1)
    spread = one_hot((column >= token * GROUP) & (column < (token + 1) * GROUP))
    slot = jnp.broadcast_to(slot_ref[...].astype(jnp.float32), (16, tokens)).astype(jnp.bfloat16)
    slot = dot32(slot, spread)[:1].astype(jnp.int32)
    index = lax.broadcasted_iota(jnp.int32, (1, rows), 1)
    col_code = slot * GROUP + jnp.bitwise_and(index, GROUP - 1)
    kept = (count_ref[0, 0] - send_ref[0, 0]) * WIN
    last = rows - WIN
    own = one_hot(row_code == jnp.where(index < kept, col_code, -1))
    packed_ref[...] = dot32(own, normed[...]).astype(jnp.bfloat16)
    borrow_ref[...] = one_hot(row_code == jnp.where(kept > last, -1, col_code[:, last:]))

    step, patch, rank = split_index(lax.broadcasted_iota(jnp.int32, (1, sent), 1), n_seq, cap)
    arrive = peer(me, step, -1) * cap + rank
    pick = one_hot(lax.broadcasted_iota(jnp.int32, (slots, sent), 0) == arrive)
    target = jnp.broadcast_to(row_ref[...].astype(jnp.float32), (16, slots)).astype(jnp.bfloat16)
    target = dot32(target, pick)[:1].astype(jnp.int32)
    out_row = lax.broadcasted_iota(jnp.int32, (tokens, sent), 0)
    for j in range(GROUP):
        place_ref[j * tokens : (j + 1) * tokens, :] = one_hot((target == out_row) & (patch == j))


def encode_call(kernel, blocks, scalars, slots, qkv, resid, weight, bias, gain, out_shape, extra):
    width = resid.shape[2]
    rows = blocks * WIN
    vmem = pl.BlockSpec(memory_space=pltpu.VMEM)
    smem = pl.BlockSpec(memory_space=pltpu.SMEM)
    hbm = pl.BlockSpec(memory_space=pltpu.HBM)
    return pl.pallas_call(
        kernel,
        out_shape=out_shape,
        in_specs=[smem] * len(scalars) + [vmem] * len(slots) + [hbm] * 5,
        out_specs=jax.tree.map(lambda _: vmem, out_shape),
        scratch_shapes=extra
        + [
            pltpu.VMEM((blocks, WIN, 3 * width), jnp.bfloat16),
            pltpu.VMEM((blocks, WIN, width), jnp.bfloat16),
            pltpu.VMEM((width, width), jnp.bfloat16),
            pltpu.VMEM((rows, width), jnp.bfloat16),
            pltpu.VMEM((rows, width), jnp.float32),
            pltpu.VMEM((width,), jnp.bfloat16),
            pltpu.VMEM((width,), jnp.bfloat16),
            pltpu.SemaphoreType.DMA((5,)),
        ],
        compiler_params=pltpu.CompilerParams(vmem_limit_bytes=24 << 20),
        cost_estimate=pl.CostEstimate(
            flops=2 * rows * width * width + 8 * rows * WIN * width,
            bytes_accessed=2 * (width * width + 5 * rows * width),
            transcendentals=rows * WIN * HEADS,
        ),
    )(*scalars, *slots, *(pltpu.with_memory_space_constraint(a, pltpu.HBM) for a in (qkv, resid, weight, bias, gain)))


def pack_kernel(packed_ref, borrow_ref, borrowed_ref, *out_refs):
    total = packed_ref[...].astype(jnp.float32) + dot32(borrow_ref[...], borrowed_ref[...])
    start = 0
    for out_ref in out_refs:
        stop = start + out_ref.shape[0]
        out_ref[...] = total[start:stop].astype(jnp.bfloat16)
        start = stop


def forward_kernel(double_ref, out_ref):
    rows = out_ref.shape[0]
    out_ref[...] = double_ref[...].astype(jnp.float32)[rows:].astype(jnp.bfloat16)


def place_kernel(place_ref, *refs):
    *in_refs, out_hbm, out, sems = refs
    tokens = out.shape[0]
    chunks = [ref[...].astype(jnp.float32) for ref in in_refs]
    if len(chunks) > 1:
        chunks[1] = chunks[1][: chunks[0].shape[0]]
    arrived = chunks[0] if len(chunks) == 1 else jnp.concatenate(chunks, axis=0)
    arrived = arrived.astype(jnp.bfloat16)
    width = arrived.shape[1]
    copies = []
    for j in range(GROUP):
        cols = slice(j * width, (j + 1) * width)
        out[:, cols] = dot32(place_ref[j * tokens : (j + 1) * tokens, :], arrived).astype(jnp.bfloat16)
        copies.append(pltpu.make_async_copy(out.at[:, cols], out_hbm.at[:, cols], sems.at[j]))
        copies[-1].start()
    for copy in copies:
        copy.wait()


def exchange_steps(n_seq):
    n_z = n_seq // CORES
    return [(0, 0), (1, 0), (1, 1)] + [(dz, dc) for dc in range(CORES) for dz in range(2, n_z)] + [(0, 1)]


def chip_peer(n_seq, me, step, sign):
    n_z = n_seq // CORES
    offset = jnp.zeros_like(step)
    flip = jnp.zeros_like(step)
    for i, (dz, dc) in enumerate(exchange_steps(n_seq)):
        offset = jnp.where(step == i, dz, offset)
        flip = jnp.where(step == i, dc, flip)
    z = me // CORES + sign * offset
    z = jnp.where(z >= n_z, z - n_z, jnp.where(z < 0, z + n_z, z))
    return z * CORES + jnp.bitwise_xor(jnp.bitwise_and(me, 1), flip)


def per_device(
    qkv, resid, block_count, send_count, send_slot, lm_row, out_weight, out_bias, norm_gain
):
    width = resid.shape[2]
    row_total = send_slot.shape[1]
    tokens = WIN // GROUP
    blocks = row_total // tokens
    n_seq = lax.axis_size("seq")
    n_enc = lax.axis_size("enc")
    slots = lm_row.shape[1]
    cap = slots // n_seq
    chunk = GROUP * cap
    sent = slots * GROUP
    vmem = pl.BlockSpec(memory_space=pltpu.VMEM)
    small = pltpu.CompilerParams(vmem_limit_bytes=16 << 20)

    def rows_of(count, columns=width):
        return jax.ShapeDtypeStruct((count, columns), jnp.bfloat16)

    data = (qkv, resid, out_weight, out_bias, norm_gain)
    lent = encode_call(lent_kernel, 1, [block_count], [], *data, rows_of(WIN), [])
    borrowed = lax.ppermute(lent, "enc", [((i - 1) % n_enc, i) for i in range(n_enc)])

    by_steps = chunk % 8 == 0 and n_seq % CORES == 0
    peer = functools.partial(chip_peer, n_seq) if by_steps else lambda me, step, sign: step
    me = lax.axis_index("seq").astype(jnp.int32).reshape(1, 1)
    packed, borrow, place = encode_call(
        functools.partial(own_kernel, n_seq, cap, peer), blocks,
        [block_count, send_count, me], [send_slot, lm_row], *data,
        (rows_of(sent), rows_of(sent, WIN), rows_of(GROUP * row_total, sent)),
        [pltpu.VMEM((row_total * GROUP, width), jnp.bfloat16)],
    )
    pieces = [chunk, CORES * chunk] + [chunk] * (n_seq - 1 - CORES) if by_steps else [sent]
    outgoing = pl.pallas_call(
        pack_kernel,
        out_shape=[rows_of(rows) for rows in pieces],
        in_specs=[vmem] * 3,
        out_specs=[vmem] * len(pieces),
        compiler_params=small,
    )(packed, borrow, borrowed)

    if by_steps:
        n_z = n_seq // CORES

        def exchange(part, dz, dc):
            return lax.ppermute(
                part, "seq", [(i, (i // CORES + dz) % n_z * CORES + (i + dc) % CORES) for i in range(n_seq)]
            )

        double = exchange(outgoing[1], 1, 0)
        rest = [exchange(part, *step) for part, step in zip(outgoing[2:], exchange_steps(n_seq)[1 + CORES :])]
        onward = pl.pallas_call(
            forward_kernel, out_shape=rows_of(chunk), in_specs=[vmem], out_specs=vmem, compiler_params=small
        )(double)
        arrived = [outgoing[0], double, exchange(onward, 0, 1), *rest]
    else:
        arrived = [
            lax.all_to_all(
                outgoing[0].reshape(n_seq, chunk, width), "seq", split_axis=0, concat_axis=0, tiled=True
            ).reshape(sent, width)
        ]
    placed = pl.pallas_call(
        place_kernel,
        out_shape=rows_of(row_total, GROUP * width),
        in_specs=[vmem] * (1 + len(arrived)),
        out_specs=pl.BlockSpec(memory_space=pltpu.HBM),
        scratch_shapes=[pltpu.VMEM((row_total, GROUP * width), jnp.bfloat16), pltpu.SemaphoreType.DMA((GROUP,))],
        compiler_params=small,
    )(place, *arrived)
    return placed[None]


def solution(mesh):
    placed = (
        P("enc", "seq", None),
        P("enc", "seq", None),
        P("enc", "seq"),
        P("enc", "seq"),
        P("enc", "seq"),
        P("enc", "seq"),
        P(),
        P(),
        P(),
    )
    return jax.shard_map(
        per_device, mesh=mesh, in_specs=placed, out_specs=P("enc", "seq", None), check_vma=False
    )
```

```python
import functools
import math

import jax
import jax.numpy as jnp
from jax import lax
from jax.experimental import pallas as pl
from jax.experimental.pallas import tpu as pltpu
from jax.sharding import PartitionSpec as P

HEADS = 16
WIN = 64
LANES = 128
GROUP = 4
EPS = 1e-6
CORES = 2

NT = (((1,), (1,)), ((), ()))


def dot32(a, b):
    return jnp.dot(a, b, preferred_element_type=jnp.float32)


def one_hot(match):
    return match.astype(jnp.float32).astype(jnp.bfloat16)


def attend(q, k, v, out_ref, row0, width):
    head = width // HEADS
    rate = 1.0 / math.sqrt(head)
    totals = [None] * (width // LANES)
    sums = [None] * (width // LANES)
    first_half = lax.broadcasted_iota(jnp.int32, (WIN, 2 * WIN), 1) < WIN
    for pair in range(HEADS // 2):
        start = 2 * pair * head
        lo = start // LANES * LANES
        hi = -(-(start + 2 * head) // LANES) * LANES
        column = lax.broadcasted_iota(jnp.int32, (2 * WIN, hi - lo), 1) + lo
        row = lax.broadcasted_iota(jnp.int32, (2 * WIN, hi - lo), 0)
        begin = jnp.where(row < WIN, start, start + head)
        mask = one_hot((column >= begin) & (column < begin + head))
        kw, vw = k(lo, hi), v(lo, hi)
        keys = jnp.concatenate([kw, kw], axis=0) * mask
        values = jnp.concatenate([vw, vw], axis=0) * mask
        scores = lax.dot_general(q(lo, hi), keys, NT, preferred_element_type=jnp.float32)
        top0 = jnp.max(jnp.where(first_half, scores, -jnp.inf), axis=1, keepdims=True)
        top1 = jnp.max(jnp.where(first_half, -jnp.inf, scores), axis=1, keepdims=True)
        raised = jnp.exp((scores - jnp.where(first_half, top0, top1)) * rate).astype(jnp.bfloat16)
        part = dot32(raised, values)
        norm = dot32(raised, mask)
        for tile in range(lo // LANES, hi // LANES):
            at = slice(tile * LANES - lo, (tile + 1) * LANES - lo)
            totals[tile] = part[:, at] if totals[tile] is None else totals[tile] + part[:, at]
            sums[tile] = norm[:, at] if sums[tile] is None else sums[tile] + norm[:, at]
    for tile in range(width // LANES):
        out_ref[row0 : row0 + WIN, tile * LANES : (tile + 1) * LANES] = (totals[tile] / sums[tile]).astype(
            jnp.bfloat16
        )


def encode(
    slot, qkv_hbm, resid_hbm, weight_hbm, bias_hbm, gain_hbm, out_ref,
    qkv, resid, weight, attended, hidden, bias_ref, gain_ref, sems,
):
    blocks = qkv.shape[0]
    width = resid.shape[2]
    at = pl.ds(slot, blocks)
    pairs = [
        (qkv_hbm.at[at], qkv), (weight_hbm, weight), (resid_hbm.at[at], resid), (bias_hbm, bias_ref), (gain_hbm, gain_ref)
    ]
    copies = [pltpu.make_async_copy(a, b, sems.at[i]) for i, (a, b) in enumerate(pairs)]
    for copy in copies:
        copy.start()
    copies[0].wait()
    for b in range(blocks):
        attend(
            lambda lo, hi, b=b: qkv[b, :, lo:hi],
            lambda lo, hi, b=b: qkv[b, :, width + lo : width + hi],
            lambda lo, hi, b=b: qkv[b, :, 2 * width + lo : 2 * width + hi],
            attended, b * WIN, width,
        )
    for copy in copies[1:]:
        copy.wait()
    rows = blocks * WIN
    squares = jnp.zeros((rows, LANES), jnp.float32)
    step = 2 * LANES
    for lo in range(0, width, step):
        cols = slice(lo, lo + step)
        h = dot32(attended[...], weight[:, cols])
        h = h + bias_ref[cols].astype(jnp.float32).reshape(1, step)
        h = h + resid[:, :, cols].reshape(rows, step).astype(jnp.float32)
        hidden[:, cols] = h
        h = h * h
        squares = squares + h[:, :LANES] + h[:, LANES:]
    scale = lax.rsqrt(jnp.sum(squares, axis=1, keepdims=True) * (1.0 / width) + EPS)
    for lo in range(0, width, step):
        cols = slice(lo, lo + step)
        gain = gain_ref[cols].astype(jnp.float32).reshape(1, step)
        out_ref[:, cols] = (hidden[:, cols] * scale * gain).astype(jnp.bfloat16)


def lent_kernel(count_ref, qkv_hbm, resid_hbm, weight_hbm, bias_hbm, gain_hbm, out_ref, *scratch):
    encode(count_ref[0, 0] - 1, qkv_hbm, resid_hbm, weight_hbm, bias_hbm, gain_hbm, out_ref, *scratch)


def split_index(index, n_seq, cap):
    step = index // (GROUP * cap)
    rest = index - step * (GROUP * cap)
    patch = rest // cap
    return step, patch, rest - patch * cap


def own_kernel(
    n_seq, cap, peer, count_ref, send_ref, me_ref, slot_ref, row_ref,
    qkv_hbm, resid_hbm, weight_hbm, bias_hbm, gain_hbm,
    packed_ref, borrow_ref, place_ref, normed, *scratch,
):
    rows = normed.shape[0]
    slots = n_seq * cap
    sent = slots * GROUP
    tokens = rows // GROUP
    me = me_ref[0, 0]
    encode(0, qkv_hbm, resid_hbm, weight_hbm, bias_hbm, gain_hbm, normed, *scratch)

    step, patch, rank = split_index(lax.broadcasted_iota(jnp.int32, (sent, 1), 0), n_seq, cap)
    row_code = (peer(me, step, 1) * cap + rank) * GROUP + patch
    token = lax.broadcasted_iota(jnp.int32, (tokens, rows), 0)
    column = lax.broadcasted_iota(jnp.int32, (tokens, rows), 1)
    spread = one_hot((column >= token * GROUP) & (column < (token + 1) * GROUP))
    slot = jnp.broadcast_to(slot_ref[...].astype(jnp.float32), (16, tokens)).astype(jnp.bfloat16)
    slot = dot32(slot, spread)[:1].astype(jnp.int32)
    index = lax.broadcasted_iota(jnp.int32, (1, rows), 1)
    col_code = slot * GROUP + jnp.bitwise_and(index, GROUP - 1)
    kept = (count_ref[0, 0] - send_ref[0, 0]) * WIN
    last = rows - WIN
    own = one_hot(row_code == jnp.where(index < kept, col_code, -1))
    packed_ref[...] = dot32(own, normed[...]).astype(jnp.bfloat16)
    borrow_ref[...] = one_hot(row_code == jnp.where(kept > last, -1, col_code[:, last:]))

    step, patch, rank = split_index(lax.broadcasted_iota(jnp.int32, (1, sent), 1), n_seq, cap)
    arrive = peer(me, step, -1) * cap + rank
    pick = one_hot(lax.broadcasted_iota(jnp.int32, (slots, sent), 0) == arrive)
    target = jnp.broadcast_to(row_ref[...].astype(jnp.float32), (16, slots)).astype(jnp.bfloat16)
    target = dot32(target, pick)[:1].astype(jnp.int32)
    out_row = lax.broadcasted_iota(jnp.int32, (tokens, sent), 0)
    for j in range(GROUP):
        place_ref[j * tokens : (j + 1) * tokens, :] = one_hot((target == out_row) & (patch == j))


def encode_call(kernel, blocks, scalars, slots, qkv, resid, weight, bias, gain, out_shape, extra):
    width = resid.shape[2]
    rows = blocks * WIN
    vmem = pl.BlockSpec(memory_space=pltpu.VMEM)
    smem = pl.BlockSpec(memory_space=pltpu.SMEM)
    hbm = pl.BlockSpec(memory_space=pltpu.HBM)
    return pl.pallas_call(
        kernel,
        out_shape=out_shape,
        in_specs=[smem] * len(scalars) + [vmem] * len(slots) + [hbm] * 5,
        out_specs=jax.tree.map(lambda _: vmem, out_shape),
        scratch_shapes=extra
        + [
            pltpu.VMEM((blocks, WIN, 3 * width), jnp.bfloat16),
            pltpu.VMEM((blocks, WIN, width), jnp.bfloat16),
            pltpu.VMEM((width, width), jnp.bfloat16),
            pltpu.VMEM((rows, width), jnp.bfloat16),
            pltpu.VMEM((rows, width), jnp.float32),
            pltpu.VMEM((width,), jnp.bfloat16),
            pltpu.VMEM((width,), jnp.bfloat16),
            pltpu.SemaphoreType.DMA((5,)),
        ],
        compiler_params=pltpu.CompilerParams(vmem_limit_bytes=24 << 20),
        cost_estimate=pl.CostEstimate(
            flops=2 * rows * width * width + 8 * rows * WIN * width,
            bytes_accessed=2 * (width * width + 5 * rows * width),
            transcendentals=rows * WIN * HEADS,
        ),
    )(*scalars, *slots, *(pltpu.with_memory_space_constraint(a, pltpu.HBM) for a in (qkv, resid, weight, bias, gain)))


def pack_kernel(packed_ref, borrow_ref, borrowed_ref, *out_refs):
    total = packed_ref[...].astype(jnp.float32) + dot32(borrow_ref[...], borrowed_ref[...])
    start = 0
    for out_ref in out_refs:
        stop = start + out_ref.shape[0]
        out_ref[...] = total[start:stop].astype(jnp.bfloat16)
        start = stop


def forward_kernel(double_ref, out_ref):
    rows = out_ref.shape[0]
    out_ref[...] = double_ref[...].astype(jnp.float32)[rows:].astype(jnp.bfloat16)


def place_kernel(place_ref, *refs):
    *in_refs, out_hbm, out, sems = refs
    tokens = out.shape[0]
    chunks = [ref[...].astype(jnp.float32) for ref in in_refs]
    if len(chunks) > 1:
        chunks[1] = chunks[1][: chunks[0].shape[0]]
    arrived = chunks[0] if len(chunks) == 1 else jnp.concatenate(chunks, axis=0)
    arrived = arrived.astype(jnp.bfloat16)
    width = arrived.shape[1]
    copies = []
    for j in range(GROUP):
        cols = slice(j * width, (j + 1) * width)
        out[:, cols] = dot32(place_ref[j * tokens : (j + 1) * tokens, :], arrived).astype(jnp.bfloat16)
        copies.append(pltpu.make_async_copy(out.at[:, cols], out_hbm.at[:, cols], sems.at[j]))
        copies[-1].start()
    for copy in copies:
        copy.wait()


def exchange_steps(n_seq):
    return [(0, 0)] + [(dz, dc) for dz in range(1, n_seq // CORES) for dc in range(CORES)] + [(0, 1)]


def chip_peer(n_seq, me, step, sign):
    n_z = n_seq // CORES
    offset = jnp.zeros_like(step)
    flip = jnp.zeros_like(step)
    for i, (dz, dc) in enumerate(exchange_steps(n_seq)):
        offset = jnp.where(step == i, dz, offset)
        flip = jnp.where(step == i, dc, flip)
    z = me // CORES + sign * offset
    z = jnp.where(z >= n_z, z - n_z, jnp.where(z < 0, z + n_z, z))
    return z * CORES + jnp.bitwise_xor(jnp.bitwise_and(me, 1), flip)


def per_device(
    qkv, resid, block_count, send_count, send_slot, lm_row, out_weight, out_bias, norm_gain
):
    width = resid.shape[2]
    row_total = send_slot.shape[1]
    tokens = WIN // GROUP
    blocks = row_total // tokens
    n_seq = lax.axis_size("seq")
    n_enc = lax.axis_size("enc")
    slots = lm_row.shape[1]
    cap = slots // n_seq
    chunk = GROUP * cap
    sent = slots * GROUP
    vmem = pl.BlockSpec(memory_space=pltpu.VMEM)
    small = pltpu.CompilerParams(vmem_limit_bytes=16 << 20)

    def rows_of(count, columns=width):
        return jax.ShapeDtypeStruct((count, columns), jnp.bfloat16)

    data = (qkv, resid, out_weight, out_bias, norm_gain)
    lent = encode_call(lent_kernel, 1, [block_count], [], *data, rows_of(WIN), [])
    borrowed = lax.ppermute(lent, "enc", [((i - 1) % n_enc, i) for i in range(n_enc)])

    by_steps = chunk % 8 == 0 and n_seq % CORES == 0
    peer = functools.partial(chip_peer, n_seq) if by_steps else lambda me, step, sign: step
    me = lax.axis_index("seq").astype(jnp.int32).reshape(1, 1)
    packed, borrow, place = encode_call(
        functools.partial(own_kernel, n_seq, cap, peer), blocks,
        [block_count, send_count, me], [send_slot, lm_row], *data,
        (rows_of(sent), rows_of(sent, WIN), rows_of(GROUP * row_total, sent)),
        [pltpu.VMEM((row_total * GROUP, width), jnp.bfloat16)],
    )
    pieces = [chunk, CORES * chunk] + [chunk] * (n_seq - 1 - CORES) if by_steps else [sent]
    outgoing = pl.pallas_call(
        pack_kernel,
        out_shape=[rows_of(rows) for rows in pieces],
        in_specs=[vmem] * 3,
        out_specs=[vmem] * len(pieces),
        compiler_params=small,
    )(packed, borrow, borrowed)

    if by_steps:
        n_z = n_seq // CORES

        def exchange(part, dz, dc):
            return lax.ppermute(
                part, "seq", [(i, (i // CORES + dz) % n_z * CORES + (i + dc) % CORES) for i in range(n_seq)]
            )

        double = exchange(outgoing[1], 1, 0)
        rest = [exchange(part, *step) for part, step in zip(outgoing[2:], exchange_steps(n_seq)[1 + CORES :])]
        onward = pl.pallas_call(
            forward_kernel, out_shape=rows_of(chunk), in_specs=[vmem], out_specs=vmem, compiler_params=small
        )(double)
        arrived = [outgoing[0], double, exchange(onward, 0, 1), *rest]
    else:
        arrived = [
            lax.all_to_all(
                outgoing[0].reshape(n_seq, chunk, width), "seq", split_axis=0, concat_axis=0, tiled=True
            ).reshape(sent, width)
        ]
    placed = pl.pallas_call(
        place_kernel,
        out_shape=rows_of(row_total, GROUP * width),
        in_specs=[vmem] * (1 + len(arrived)),
        out_specs=pl.BlockSpec(memory_space=pltpu.HBM),
        scratch_shapes=[pltpu.VMEM((row_total, GROUP * width), jnp.bfloat16), pltpu.SemaphoreType.DMA((GROUP,))],
        compiler_params=small,
    )(place, *arrived)
    return placed[None]


def solution(mesh):
    placed = (
        P("enc", "seq", None),
        P("enc", "seq", None),
        P("enc", "seq"),
        P("enc", "seq"),
        P("enc", "seq"),
        P("enc", "seq"),
        P(),
        P(),
        P(),
    )
    return jax.shard_map(
        per_device, mesh=mesh, in_specs=placed, out_specs=P("enc", "seq", None), check_vma=False
    )
```

```python
import functools
import math

import jax
import jax.numpy as jnp
from jax import lax
from jax.experimental import pallas as pl
from jax.experimental.pallas import tpu as pltpu
from jax.sharding import PartitionSpec as P

HEADS = 16
WIN = 64
LANES = 128
GROUP = 4
EPS = 1e-6
CORES = 2

NT = (((1,), (1,)), ((), ()))


def dot32(a, b):
    return jnp.dot(a, b, preferred_element_type=jnp.float32)


def one_hot(match):
    return match.astype(jnp.float32).astype(jnp.bfloat16)


def attend(q, k, v, out_ref, row0, width):
    head = width // HEADS
    rate = math.log2(math.e) / math.sqrt(head)
    totals = [None] * (width // LANES)
    sums = [None] * (width // LANES)
    first_half = lax.broadcasted_iota(jnp.int32, (WIN, 2 * WIN), 1) < WIN
    for pair in range(HEADS // 2):
        start = 2 * pair * head
        lo = start // LANES * LANES
        hi = -(-(start + 2 * head) // LANES) * LANES
        column = lax.broadcasted_iota(jnp.int32, (2 * WIN, hi - lo), 1) + lo
        row = lax.broadcasted_iota(jnp.int32, (2 * WIN, hi - lo), 0)
        begin = jnp.where(row < WIN, start, start + head)
        mask = one_hot((column >= begin) & (column < begin + head))
        kw, vw = k(lo, hi), v(lo, hi)
        keys = jnp.concatenate([kw, kw], axis=0) * mask
        values = jnp.concatenate([vw, vw], axis=0) * mask
        scores = lax.dot_general(q(lo, hi), keys, NT, preferred_element_type=jnp.float32)
        top0 = jnp.max(jnp.where(first_half, scores, -jnp.inf), axis=1, keepdims=True)
        top1 = jnp.max(jnp.where(first_half, -jnp.inf, scores), axis=1, keepdims=True)
        raised = jnp.exp2((scores - jnp.where(first_half, top0, top1)) * rate).astype(jnp.bfloat16)
        part = dot32(raised, values)
        norm = dot32(raised, mask)
        for tile in range(lo // LANES, hi // LANES):
            at = slice(tile * LANES - lo, (tile + 1) * LANES - lo)
            totals[tile] = part[:, at] if totals[tile] is None else totals[tile] + part[:, at]
            sums[tile] = norm[:, at] if sums[tile] is None else sums[tile] + norm[:, at]
    for tile in range(width // LANES):
        out_ref[row0 : row0 + WIN, tile * LANES : (tile + 1) * LANES] = (totals[tile] / sums[tile]).astype(
            jnp.bfloat16
        )


def encode(
    slot, qkv_hbm, resid_hbm, weight_hbm, bias_hbm, gain_hbm, out_ref,
    qkv, resid, weight, attended, hidden, bias_ref, gain_ref, sems,
):
    blocks = qkv.shape[0]
    width = resid.shape[2]
    at = pl.ds(slot, blocks)
    pairs = [
        (qkv_hbm.at[at], qkv), (weight_hbm, weight), (resid_hbm.at[at], resid), (bias_hbm, bias_ref), (gain_hbm, gain_ref)
    ]
    copies = [pltpu.make_async_copy(a, b, sems.at[i]) for i, (a, b) in enumerate(pairs)]
    for copy in copies:
        copy.start()
    copies[0].wait()
    for b in range(blocks):
        attend(
            lambda lo, hi, b=b: qkv[b, :, lo:hi],
            lambda lo, hi, b=b: qkv[b, :, width + lo : width + hi],
            lambda lo, hi, b=b: qkv[b, :, 2 * width + lo : 2 * width + hi],
            attended, b * WIN, width,
        )
    for copy in copies[1:]:
        copy.wait()
    rows = blocks * WIN
    squares = jnp.zeros((rows, LANES), jnp.float32)
    step = 2 * LANES
    for lo in range(0, width, step):
        cols = slice(lo, lo + step)
        h = dot32(attended[...], weight[:, cols])
        h = h + bias_ref[cols].astype(jnp.float32).reshape(1, step)
        h = h + resid[:, :, cols].reshape(rows, step).astype(jnp.float32)
        hidden[:, cols] = h
        h = h * h
        squares = squares + h[:, :LANES] + h[:, LANES:]
    scale = lax.rsqrt(jnp.sum(squares, axis=1, keepdims=True) * (1.0 / width) + EPS)
    for lo in range(0, width, step):
        cols = slice(lo, lo + step)
        gain = gain_ref[cols].astype(jnp.float32).reshape(1, step)
        out_ref[:, cols] = (hidden[:, cols] * scale * gain).astype(jnp.bfloat16)


def lent_kernel(count_ref, qkv_hbm, resid_hbm, weight_hbm, bias_hbm, gain_hbm, out_ref, *scratch):
    encode(count_ref[0, 0] - 1, qkv_hbm, resid_hbm, weight_hbm, bias_hbm, gain_hbm, out_ref, *scratch)


def split_index(index, n_seq, cap):
    step = index // (GROUP * cap)
    rest = index - step * (GROUP * cap)
    patch = rest // cap
    return step, patch, rest - patch * cap


def own_kernel(
    n_seq, cap, peer, count_ref, send_ref, me_ref, slot_ref, row_ref,
    qkv_hbm, resid_hbm, weight_hbm, bias_hbm, gain_hbm,
    packed_ref, borrow_ref, place_ref, normed, *scratch,
):
    rows = normed.shape[0]
    slots = n_seq * cap
    sent = slots * GROUP
    tokens = rows // GROUP
    me = me_ref[0, 0]
    encode(0, qkv_hbm, resid_hbm, weight_hbm, bias_hbm, gain_hbm, normed, *scratch)

    step, patch, rank = split_index(lax.broadcasted_iota(jnp.int32, (sent, 1), 0), n_seq, cap)
    row_code = (peer(me, step, 1) * cap + rank) * GROUP + patch
    token = lax.broadcasted_iota(jnp.int32, (tokens, rows), 0)
    column = lax.broadcasted_iota(jnp.int32, (tokens, rows), 1)
    spread = one_hot((column >= token * GROUP) & (column < (token + 1) * GROUP))
    slot = jnp.broadcast_to(slot_ref[...].astype(jnp.float32), (16, tokens)).astype(jnp.bfloat16)
    slot = dot32(slot, spread)[:1].astype(jnp.int32)
    index = lax.broadcasted_iota(jnp.int32, (1, rows), 1)
    col_code = slot * GROUP + jnp.bitwise_and(index, GROUP - 1)
    kept = (count_ref[0, 0] - send_ref[0, 0]) * WIN
    last = rows - WIN
    own = one_hot(row_code == jnp.where(index < kept, col_code, -1))
    packed_ref[...] = dot32(own, normed[...]).astype(jnp.bfloat16)
    borrow_ref[...] = one_hot(row_code == jnp.where(kept > last, -1, col_code[:, last:]))

    step, patch, rank = split_index(lax.broadcasted_iota(jnp.int32, (1, sent), 1), n_seq, cap)
    arrive = peer(me, step, -1) * cap + rank
    pick = one_hot(lax.broadcasted_iota(jnp.int32, (slots, sent), 0) == arrive)
    target = jnp.broadcast_to(row_ref[...].astype(jnp.float32), (16, slots)).astype(jnp.bfloat16)
    target = dot32(target, pick)[:1].astype(jnp.int32)
    out_row = lax.broadcasted_iota(jnp.int32, (tokens, sent), 0)
    for j in range(GROUP):
        place_ref[j * tokens : (j + 1) * tokens, :] = one_hot((target == out_row) & (patch == j))


def encode_call(kernel, blocks, scalars, slots, qkv, resid, weight, bias, gain, out_shape, extra):
    width = resid.shape[2]
    rows = blocks * WIN
    vmem = pl.BlockSpec(memory_space=pltpu.VMEM)
    smem = pl.BlockSpec(memory_space=pltpu.SMEM)
    hbm = pl.BlockSpec(memory_space=pltpu.HBM)
    return pl.pallas_call(
        kernel,
        out_shape=out_shape,
        in_specs=[smem] * len(scalars) + [vmem] * len(slots) + [hbm] * 5,
        out_specs=jax.tree.map(lambda _: vmem, out_shape),
        scratch_shapes=extra
        + [
            pltpu.VMEM((blocks, WIN, 3 * width), jnp.bfloat16),
            pltpu.VMEM((blocks, WIN, width), jnp.bfloat16),
            pltpu.VMEM((width, width), jnp.bfloat16),
            pltpu.VMEM((rows, width), jnp.bfloat16),
            pltpu.VMEM((rows, width), jnp.float32),
            pltpu.VMEM((width,), jnp.bfloat16),
            pltpu.VMEM((width,), jnp.bfloat16),
            pltpu.SemaphoreType.DMA((5,)),
        ],
        compiler_params=pltpu.CompilerParams(vmem_limit_bytes=24 << 20),
        cost_estimate=pl.CostEstimate(
            flops=2 * rows * width * width + 8 * rows * WIN * width,
            bytes_accessed=2 * (width * width + 5 * rows * width),
            transcendentals=rows * WIN * HEADS,
        ),
    )(*scalars, *slots, *(pltpu.with_memory_space_constraint(a, pltpu.HBM) for a in (qkv, resid, weight, bias, gain)))


def pack_kernel(packed_ref, borrow_ref, borrowed_ref, *out_refs):
    total = packed_ref[...].astype(jnp.float32) + dot32(borrow_ref[...], borrowed_ref[...])
    start = 0
    for out_ref in out_refs:
        stop = start + out_ref.shape[0]
        out_ref[...] = total[start:stop].astype(jnp.bfloat16)
        start = stop


def forward_kernel(double_ref, out_ref):
    rows = out_ref.shape[0]
    out_ref[...] = double_ref[...].astype(jnp.float32)[rows:].astype(jnp.bfloat16)


def place_kernel(place_ref, *refs):
    *in_refs, out_hbm, out, sems = refs
    tokens = out.shape[0]
    chunks = [ref[...].astype(jnp.float32) for ref in in_refs]
    if len(chunks) > 1:
        chunks[1] = chunks[1][: chunks[0].shape[0]]
    arrived = chunks[0] if len(chunks) == 1 else jnp.concatenate(chunks, axis=0)
    arrived = arrived.astype(jnp.bfloat16)
    width = arrived.shape[1]
    copies = []
    for j in range(GROUP):
        cols = slice(j * width, (j + 1) * width)
        out[:, cols] = dot32(place_ref[j * tokens : (j + 1) * tokens, :], arrived).astype(jnp.bfloat16)
        copies.append(pltpu.make_async_copy(out.at[:, cols], out_hbm.at[:, cols], sems.at[j]))
        copies[-1].start()
    for copy in copies:
        copy.wait()


def exchange_steps(n_seq):
    return [(0, 0)] + [(dz, dc) for dz in range(1, n_seq // CORES) for dc in range(CORES)] + [(0, 1)]


def chip_peer(n_seq, me, step, sign):
    n_z = n_seq // CORES
    offset = jnp.zeros_like(step)
    flip = jnp.zeros_like(step)
    for i, (dz, dc) in enumerate(exchange_steps(n_seq)):
        offset = jnp.where(step == i, dz, offset)
        flip = jnp.where(step == i, dc, flip)
    z = me // CORES + sign * offset
    z = jnp.where(z >= n_z, z - n_z, jnp.where(z < 0, z + n_z, z))
    return z * CORES + jnp.bitwise_xor(jnp.bitwise_and(me, 1), flip)


def per_device(
    qkv, resid, block_count, send_count, send_slot, lm_row, out_weight, out_bias, norm_gain
):
    width = resid.shape[2]
    row_total = send_slot.shape[1]
    tokens = WIN // GROUP
    blocks = row_total // tokens
    n_seq = lax.axis_size("seq")
    n_enc = lax.axis_size("enc")
    slots = lm_row.shape[1]
    cap = slots // n_seq
    chunk = GROUP * cap
    sent = slots * GROUP
    vmem = pl.BlockSpec(memory_space=pltpu.VMEM)
    small = pltpu.CompilerParams(vmem_limit_bytes=16 << 20)

    def rows_of(count, columns=width):
        return jax.ShapeDtypeStruct((count, columns), jnp.bfloat16)

    data = (qkv, resid, out_weight, out_bias, norm_gain)
    lent = encode_call(lent_kernel, 1, [block_count], [], *data, rows_of(WIN), [])
    borrowed = lax.ppermute(lent, "enc", [((i - 1) % n_enc, i) for i in range(n_enc)])

    by_steps = chunk % 8 == 0 and n_seq % CORES == 0
    peer = functools.partial(chip_peer, n_seq) if by_steps else lambda me, step, sign: step
    me = lax.axis_index("seq").astype(jnp.int32).reshape(1, 1)
    packed, borrow, place = encode_call(
        functools.partial(own_kernel, n_seq, cap, peer), blocks,
        [block_count, send_count, me], [send_slot, lm_row], *data,
        (rows_of(sent), rows_of(sent, WIN), rows_of(GROUP * row_total, sent)),
        [pltpu.VMEM((row_total * GROUP, width), jnp.bfloat16)],
    )
    pieces = [chunk, CORES * chunk] + [chunk] * (n_seq - 1 - CORES) if by_steps else [sent]
    outgoing = pl.pallas_call(
        pack_kernel,
        out_shape=[rows_of(rows) for rows in pieces],
        in_specs=[vmem] * 3,
        out_specs=[vmem] * len(pieces),
        compiler_params=small,
    )(packed, borrow, borrowed)

    if by_steps:
        n_z = n_seq // CORES

        def exchange(part, dz, dc):
            return lax.ppermute(
                part, "seq", [(i, (i // CORES + dz) % n_z * CORES + (i + dc) % CORES) for i in range(n_seq)]
            )

        double = exchange(outgoing[1], 1, 0)
        rest = [exchange(part, *step) for part, step in zip(outgoing[2:], exchange_steps(n_seq)[1 + CORES :])]
        onward = pl.pallas_call(
            forward_kernel, out_shape=rows_of(chunk), in_specs=[vmem], out_specs=vmem, compiler_params=small
        )(double)
        arrived = [outgoing[0], double, exchange(onward, 0, 1), *rest]
    else:
        arrived = [
            lax.all_to_all(
                outgoing[0].reshape(n_seq, chunk, width), "seq", split_axis=0, concat_axis=0, tiled=True
            ).reshape(sent, width)
        ]
    placed = pl.pallas_call(
        place_kernel,
        out_shape=rows_of(row_total, GROUP * width),
        in_specs=[vmem] * (1 + len(arrived)),
        out_specs=pl.BlockSpec(memory_space=pltpu.HBM),
        scratch_shapes=[pltpu.VMEM((row_total, GROUP * width), jnp.bfloat16), pltpu.SemaphoreType.DMA((GROUP,))],
        compiler_params=small,
    )(place, *arrived)
    return placed[None]


def solution(mesh):
    placed = (
        P("enc", "seq", None),
        P("enc", "seq", None),
        P("enc", "seq"),
        P("enc", "seq"),
        P("enc", "seq"),
        P("enc", "seq"),
        P(),
        P(),
        P(),
    )
    return jax.shard_map(
        per_device, mesh=mesh, in_specs=placed, out_specs=P("enc", "seq", None), check_vma=False
    )
```
